32 devices in a mesh: dp: 8 (over y, x, core), tensor: 4 (over z).
Axes of the slice: x: 2, y: 2, z: 4, core: 2. Of those that a mesh axis runs over, the one named last changes fastest.
Arguments:
- tokens: bfloat16 [16384, 2048], P('dp'), may hold values from -6 to 6
- lengths: int32 [8], P('dp'), may hold values from 512 to 2048, as said below
- gains: float32 [2, 2048], P(None, 'dp'), may hold values from 0.5 to 1.5
- w_gelu: float32 [2048, 2560], P('dp', 'tensor'), may hold values from -0.125 to 0.125
- w_rec: float32 [2048, 2560], P('dp', 'tensor'), may hold values from -0.125 to 0.125
- chan: float32 [8, 16, 160], P(None, 'tensor', 'dp'), may hold values from -2 to 9, as said below
- w_lru: float32 [2, 16, 160, 160], P(None, 'tensor', 'dp'), may hold values from -0.5 to 0.5
- w_out: float32 [2560, 2048], P('tensor', 'dp'), may hold values from -0.3125 to 0.3125
- w_mlp_in: float32 [2, 2048, 6144], P(None, 'dp', 'tensor'), may hold values from -0.125 to 0.125
- w_down: float32 [6144, 2048], P('tensor', 'dp'), may hold values from -0.15625 to 0.15625
- cotangent: bfloat16 [16384, 2048], P('dp'), may hold values from -6 to 6
Outputs:
- output: bfloat16 [16384, 2048], P('dp')
- grad_tokens: bfloat16 [16384, 2048], P('dp')
- grad_gain_one: float32 [2048], P('dp')
- grad_gain_two: float32 [2048], P('dp')
- grad_w_gelu: float32 [2048, 2560], P('dp', 'tensor')
- grad_w_rec: float32 [2048, 2560], P('dp', 'tensor')
- grad_chan: float32 [8, 16, 160], P(None, 'tensor', 'dp')
- grad_w_lru: float32 [2, 16, 160, 160], P(None, 'tensor', 'dp')
- grad_w_out: float32 [2560, 2048], P('tensor', 'dp')
- grad_w_mlp_in: float32 [2, 2048, 6144], P(None, 'dp', 'tensor')
- grad_w_down: float32 [6144, 2048], P('tensor', 'dp')
The draws below stay inside these ranges and needn't reach their ends.
Inputs may be any that keep to these rules, and one draw needn't show every extreme that they name: `lengths`: slots at or past a sequence's length are padding; at least one sequence has all 2048 slots live. `chan`: row 7 (the decay parameter) lies from 1 to 9; the other rows lie from -2 to 2.
All inputs are finite; a program needn't handle non-finite values.
Results may differ from the reference program's by a relative error of at most 0.025.
Values may be sent and summed in bfloat16 or wider, within the bound.
No kernel may reach another device: no remote copies, remote signals or barrier semaphores. Data moves between devices by JAX's collectives and lax.ppermute only.
A program may use at most 384 MiB of HBM per device.

```python
import jax
import jax.numpy as jnp
from jax import lax

D = 2048
W = 2560
H = 16
FF = 6144
HEAD = 160
LENGTH = 2048
SEQS = 8
TOKENS = 16384
N_TENSOR = 4


def draw_lengths(key, part):
    key = jax.random.fold_in(key, 5)
    first_key, second_key = jax.random.split(key)
    values = jax.random.randint(first_key, (SEQS,), LENGTH // 4, LENGTH + 1)
    picked = jax.random.randint(second_key, (), 0, SEQS)
    return jnp.where(jnp.arange(SEQS) == picked, LENGTH, values).astype(jnp.int32)


def draw_chan(key, part):
    key = jax.random.fold_in(key, 11)
    tap_key, bias_key, rate_key = jax.random.split(key, 3)
    taps = jnp.clip(0.5 * jax.random.normal(tap_key, (4, H, HEAD), jnp.float32), -2.0, 2.0)
    biases = jnp.clip(0.5 * jax.random.normal(bias_key, (3, H, HEAD), jnp.float32), -2.0, 2.0)
    rates = jax.random.uniform(rate_key, (1, H, HEAD), jnp.float32, 1.0, 9.0)
    return jnp.concatenate([taps, biases, rates], axis=0)


def shard_levels(key, extent, cuts, low, top_value):
    gain, own = 1.0, jax.random.fold_in(key, 6)
    for axis_at, blocks in cuts:
        draws = jnp.exp(jax.random.uniform(jax.random.fold_in(own, axis_at), (blocks,), jnp.float32, low / len(cuts), top_value / len(cuts)))
        gain = gain * jnp.repeat(draws, extent[axis_at] // blocks).reshape([-1 if axis == axis_at else 1 for axis in range(len(extent))])
    return gain


def gaussian(own_key, shape, scale, reach, cuts=(), kind=jnp.bfloat16):
    values = jax.random.normal(own_key, shape, jnp.float32) * scale
    if len(cuts) > 0:
        values = shard_levels(own_key, shape, cuts, -0.22, 0.18) * values
    return jnp.clip(values, min=-reach, max=reach).astype(kind)


def setup_inputs(seed: int = 0) -> dict:
    key_list = jax.random.split(jax.random.key(seed), 12)
    return {
        "tokens": gaussian(key_list[0], (TOKENS, D), 1.0, 6.0, ((0, 8),)),
        "lengths": draw_lengths(jax.random.fold_in(key_list[11], 71), 0),
        "gains": jnp.clip(1.0 + 0.1 * jax.random.normal(key_list[2], (2, D), jnp.float32), 0.5, 1.5),
        "w_gelu": gaussian(key_list[3], (D, W), D ** -0.5, 0.125, ((0, 8), (1, 4)), jnp.float32),
        "w_rec": gaussian(key_list[4], (D, W), D ** -0.5, 0.125, ((0, 8), (1, 4)), jnp.float32),
        "chan": draw_chan(jax.random.fold_in(key_list[11], 71), 0),
        "w_lru": gaussian(key_list[6], (2, H, HEAD, HEAD), HEAD ** -0.5, 0.5, ((1, 4), (2, 8)), jnp.float32),
        "w_out": gaussian(key_list[7], (W, D), (W // 8) ** -0.5, 0.3125, ((0, 4), (1, 8)), jnp.float32),
        "w_mlp_in": gaussian(key_list[8], (2, D, FF), D ** -0.5, 0.125, ((1, 8), (2, 4)), jnp.float32),
        "w_down": gaussian(key_list[9], (FF, D), (FF // 4) ** -0.5, 0.15625, ((0, 4), (1, 8)), jnp.float32),
        "cotangent": gaussian(key_list[10], (TOKENS, D), 1.0, 6.0, ((0, 8),)),
    }


@jax.custom_vjp
def low(v):
    return lax.optimization_barrier(v.astype(jnp.bfloat16)).astype(jnp.float32)

@jax.custom_vjp
def low_back(v):
    return v

def low_keep(v):
    return (low(v), None)

def low_pass(kept, grad):
    return (grad,)

def back_keep(v):
    return (v, None)

def back_low(kept, grad):
    return (low(grad),)
low.defvjp(low_keep, low_pass)
low_back.defvjp(back_keep, back_low)
NORM_EPS = 1e-06
DECAY_FLOOR = 0.05

def norm_scale(values, gain_row):
    return values * lax.rsqrt(lax.optimization_barrier(jnp.mean(values * values, axis=-1, keepdims=True)) + NORM_EPS) * gain_row

def shifted(values, offset):
    padded = jnp.pad(values, ((0, 0), (offset, 0), (0, 0)))
    return padded[:, :values.shape[1], :]

def combine(earlier, later):
    return (earlier[0] * later[0], later[0] * earlier[1] + later[1])

def recurrence(inputs, params, gate_mats, live_mask):
    convolved = params[0] * inputs + params[1] * shifted(inputs, 1) + params[2] * shifted(inputs, 2) + params[3] * shifted(inputs, 3)
    convolved = (convolved + params[4]) * live_mask
    head_count = gate_mats.shape[1]
    head_size = gate_mats.shape[2]
    per_head = convolved.reshape(convolved.shape[0], convolved.shape[1], head_count, head_size)
    input_gate = jnp.einsum('slhj,hjk->slhk', per_head, gate_mats[0], precision=lax.Precision.HIGHEST).reshape(convolved.shape)
    decay_gate = jnp.einsum('slhj,hjk->slhk', per_head, gate_mats[1], precision=lax.Precision.HIGHEST).reshape(convolved.shape)
    input_gate = jax.nn.sigmoid(input_gate + params[5])
    decay_gate = jax.nn.sigmoid(decay_gate + params[6])
    decays = jnp.exp(-8.0 * decay_gate * jax.nn.softplus(-params[7]))
    normalizer = jnp.sqrt(jnp.maximum(1.0 - decays * decays, DECAY_FLOOR))
    driven = normalizer * input_gate * convolved
    _, states = lax.associative_scan(combine, (decays, driven), axis=1)
    return states * live_mask

def project(left, right):
    return jnp.einsum('gld,dw->glw', left, right, precision=lax.Precision.HIGHEST)

def block(tokens_in, live_mask, params):
    gains, w_gelu, w_rec, chan, w_lru, w_out, w_mlp_in, w_down = params
    width_dev = W // N_TENSOR
    hidden_dev = FF // N_TENSOR
    gain_rows = low(gains)
    normed_one = low(norm_scale(tokens_in, gain_rows[0]))
    gelu_w = low(w_gelu)
    rec_w = low(w_rec)
    gelu_parts = []
    rec_parts = []
    for shard in range(N_TENSOR):
        own_rows = low_back(normed_one)
        columns = slice(shard * width_dev, (shard + 1) * width_dev)
        gelu_parts.append(project(own_rows, gelu_w[:, columns]))
        rec_parts.append(project(own_rows, rec_w[:, columns]))
    branch_pre = low_back(jnp.concatenate(gelu_parts, axis=-1))
    rec_in = low_back(jnp.concatenate(rec_parts, axis=-1)) * live_mask
    channel = low(chan).reshape(8, W)
    recurrent = recurrence(rec_in, channel, low(w_lru), live_mask)
    mixed = low(jax.nn.gelu(branch_pre) * recurrent)
    out_w = low(w_out)
    branch_sum = jnp.zeros_like(tokens_in)
    for shard in range(N_TENSOR):
        columns = slice(shard * width_dev, (shard + 1) * width_dev)
        branch_sum = branch_sum + low(project(mixed[..., columns], out_w[columns, :]))
    hidden_res = tokens_in + low_back(branch_sum)
    normed_two = low(norm_scale(hidden_res, gain_rows[1]))
    mlp_w = low(w_mlp_in)
    down_w = low(w_down)
    mlp_sum = jnp.zeros_like(tokens_in)
    for shard in range(N_TENSOR):
        own_rows = low_back(normed_two)
        columns = slice(shard * hidden_dev, (shard + 1) * hidden_dev)
        gate_pre = low_back(project(own_rows, mlp_w[0][:, columns]))
        up_pre = low_back(project(own_rows, mlp_w[1][:, columns]))
        product = low(jax.nn.gelu(gate_pre) * up_pre)
        mlp_sum = mlp_sum + low(project(product, down_w[columns, :]))
    return hidden_res + low_back(mlp_sum)

def reference(tokens, lengths, gains, w_gelu, w_rec, chan, w_lru, w_out, w_mlp_in, w_down, cotangent):
    per_step = 2 if SEQS % 2 == 0 and LENGTH <= 2048 else 1
    step_count = SEQS // per_step
    params = (gains, w_gelu, w_rec, chan, w_lru, w_out, w_mlp_in, w_down)
    inputs = tokens.astype(jnp.float32).reshape(step_count, per_step, LENGTH, D)
    cot_rows = cotangent.astype(jnp.float32).reshape(step_count, per_step, LENGTH, D)
    seq_lengths = lengths.reshape(step_count, per_step)
    positions = jnp.arange(LENGTH, dtype=jnp.int32)

    def advance(totals, item):
        tokens_in, cot_in, lens_in = item
        live_mask = (positions[None, :] < lens_in[:, None]).astype(jnp.float32)[..., None]

        def forward(tokens_arg, params_arg):
            return block(tokens_arg, live_mask, params_arg)
        result, pullback = jax.vjp(forward, tokens_in, params)
        grad_in, grad_params = pullback(cot_in)
        totals = jax.tree.map(lambda first_term, second_term: first_term + second_term, totals, grad_params)
        return (totals, (result, grad_in))
    zeros = jax.tree.map(jnp.zeros_like, params)
    totals, (results, grads) = lax.scan(advance, zeros, (inputs, cot_rows, seq_lengths))
    return (results.reshape(TOKENS, D).astype(jnp.bfloat16), grads.reshape(TOKENS, D).astype(jnp.bfloat16), totals[0][0], totals[0][1], totals[1], totals[2], totals[3], totals[4], totals[5], totals[6], totals[7])
```

```python
import functools

import jax
import jax.numpy as jnp
import numpy as np
from jax import lax
from jax.experimental import pallas as pl
from jax.experimental.pallas import tpu as pltpu
from jax.sharding import PartitionSpec as P

NORM_EPS = 1e-06
DECAY_FLOOR = 0.05
HALO = 16
GROUP = 640
ROWS = 128
SLAB = 8
VMEM = 58 * 1024 * 1024
BF = jnp.bfloat16
F32 = jnp.float32


def dot(left, right, dims=((1,), (0,))):
    return lax.dot_general(left, right, (dims, ((), ())), preferred_element_type=F32)


def exchange(values, bit, size):
    return lax.ppermute(values, "dp", [(k, k ^ (1 << bit)) for k in range(size)])


def orders(size, parts):
    high = list(range(1, size.bit_length() - 1))
    return [high, high[::-1]][:parts]


def parts_of(rows):
    return 2 if rows % 256 == 0 else 1


def spread(own, size):
    parts = parts_of(own.shape[0])
    pieces = jnp.split(own, parts)
    for turn in range(size.bit_length() - 2):
        got = [exchange(p, o[turn], size) for p, o in zip(pieces, orders(size, parts))]
        pieces = [jnp.concatenate([p, g]) for p, g in zip(pieces, got)]
    half = jnp.concatenate(pieces)
    return jnp.concatenate([half, exchange(half, 0, size)])


def add_low(one, two):
    return (one.astype(F32) + two.astype(F32)).astype(BF)


def collect(full, size):
    half = full.shape[0] // 2
    parts = parts_of(full.shape[0] // size)
    kept = add_low(full[:half], exchange(full[half:], 0, size))
    pieces = jnp.split(kept, parts)
    for turn in reversed(range(size.bit_length() - 2)):
        cut = pieces[0].shape[0] // 2
        got = [exchange(p[cut:], o[turn], size) for p, o in zip(pieces, orders(size, parts))]
        pieces = [add_low(p[:cut], g) for p, g in zip(pieces, got)]
    return jnp.concatenate(pieces)


def basis(size, rows, place):
    parts = parts_of(rows)
    count = size // 2
    masks, which = [], []
    for core in range(2):
        for part, order in enumerate(orders(size, parts)):
            for q in range(count):
                masks.append(core | sum(((q >> t) & 1) << b for t, b in enumerate(order)))
                which.append(part)
    table = (place ^ jnp.asarray(np.array(masks, np.int32))) * parts
    table = table + jnp.asarray(np.array(which, np.int32))
    spots = jnp.arange(len(masks), dtype=jnp.int32)
    inverse = jnp.sum(jnp.where(table[None, :] == spots[:, None], spots[None, :], 0), axis=1)
    return table, inverse.astype(jnp.int32)


def copy_kernel(table_ref, in_ref, out_ref):
    out_ref[...] = in_ref[...]


def permute(values, table):
    a, b, r, d = values.shape
    width = d // table.shape[0]
    return pl.pallas_call(
        copy_kernel,
        grid_spec=pltpu.PrefetchScalarGridSpec(
            num_scalar_prefetch=1,
            grid=(b, table.shape[0]),
            in_specs=[
                pl.BlockSpec((a, pl.squeezed, r, width), lambda h, p, tab: (0, h, 0, tab[p]))
            ],
            out_specs=pl.BlockSpec((pl.squeezed, a, r, width), lambda h, p, tab: (h, 0, 0, p)),
        ),
        out_shape=jax.ShapeDtypeStruct((b, a, r, d), values.dtype),
        compiler_params=pltpu.CompilerParams(vmem_limit_bytes=VMEM),
        name="permute",
    )(table, values)


def permute_rows(values, table):
    return permute(values[None, None], table)[0, 0]


def permute_gain(values, table):
    lead = values.shape[0]
    return jnp.take(values.reshape(lead, table.shape[0], -1), table, axis=1).reshape(lead, -1)


def row_ids(count, width, first):
    return lax.broadcasted_iota(jnp.int32, (count, width), 0) + first


def scan_slab(decay, value, back):
    rows = row_ids(SLAB, decay.shape[1], 0)
    for step in (1, 2, 4):
        keep = rows < SLAB - step if back else rows >= step
        shift = SLAB - step if back else step
        moved_decay = pltpu.roll(decay, shift, 0)
        moved_value = pltpu.roll(value, shift, 0)
        value = jnp.where(keep, value + decay * moved_value, value)
        decay = jnp.where(keep, decay * moved_decay, decay)
    return decay, value


def gelu_parts(v):
    c = np.float32(np.sqrt(2 / np.pi))
    return jnp.tanh(c * (v + 0.044715 * v * v * v))


def forward_kernel(live_ref, pre_ref, par_ref, w_ref, conv_ref, decay_ref, ig_ref, dg_ref, state_ref, prod_ref, rec_ref):
    rows, width = conv_ref.shape
    live = live_ref[0]
    rec_ref[...] = jnp.where(row_ids(rows + HALO, width, -HALO) < live, pre_ref[...], 0.0)
    par = [par_ref[k : k + 1, :] for k in range(8)]
    for at in range(0, rows, ROWS):
        span = pl.ds(at, ROWS)
        near = rec_ref[pl.ds(at, ROWS + HALO), :]
        conv = par[4] + par[0] * near[HALO : HALO + ROWS]
        for k in range(1, 4):
            conv = conv + par[k] * near[HALO - k : HALO - k + ROWS]
        conv = jnp.where(row_ids(ROWS, width, at) < live, conv, 0.0)
        conv_ref[span, :] = conv
        gates = dot(conv.astype(BF), w_ref[...])
        ig = lax.logistic(gates[:, :width] + par[5])
        dg = lax.logistic(gates[:, width:] + par[6])
        decay = jnp.exp(dg * par[7])
        ig_ref[span, :] = ig
        dg_ref[span, :] = dg
        decay_ref[span, :] = decay
        state_ref[span, :] = jnp.sqrt(jnp.maximum(1.0 - decay * decay, DECAY_FLOOR)) * ig * conv

    def slab(k, carry):
        state, prod = carry
        for inner in range(4):
            span = pl.ds(pl.multiple_of(k * 4 * SLAB + inner * SLAB, SLAB), SLAB)
            decay, value = scan_slab(decay_ref[span, :], state_ref[span, :], False)
            value = value + decay * state
            decay = decay * prod
            state_ref[span, :] = value
            prod_ref[span, :] = decay
            state = jnp.broadcast_to(value[SLAB - 1 :, :], (SLAB, width))
            prod = jnp.broadcast_to(decay[SLAB - 1 :, :], (SLAB, width))
        return state, prod

    lax.fori_loop(0, rows // (4 * SLAB), slab, (jnp.zeros((SLAB, width), F32), jnp.ones((SLAB, width), F32)))


def back_scan_kernel(live_ref, pre_ref, grad_ref, decay_ref, lam_ref, reach_ref, edge_ref):
    rows, width = grad_ref.shape
    live = live_ref[0]
    for at in range(0, rows, ROWS):
        span = pl.ds(at, ROWS)
        v = pre_ref[pl.ds(at + HALO, ROWS), :]
        act = 0.5 * v * (1.0 + gelu_parts(v))
        lam_ref[span, :] = jnp.where(row_ids(ROWS, width, at) < live, grad_ref[span, :] * act, 0.0)
    last = row_ids(SLAB, width, 0) == SLAB - 1

    def slab(k, carry):
        lam, reach, following, _ = carry
        for inner in range(4):
            span = pl.ds(pl.multiple_of(rows - (k * 4 + inner + 1) * SLAB, SLAB), SLAB)
            own = decay_ref[span, :]
            ahead = jnp.where(last, following, pltpu.roll(own, SLAB - 1, 0))
            decay, value = scan_slab(ahead, lam_ref[span, :], True)
            value = value + decay * lam
            decay = decay * reach
            lam_ref[span, :] = value
            reach_ref[span, :] = decay
            lam = jnp.broadcast_to(value[:1, :], (SLAB, width))
            reach = jnp.broadcast_to(decay[:1, :], (SLAB, width))
            following = jnp.broadcast_to(own[:1, :], (SLAB, width))
        return lam, reach, following, own

    one = jnp.ones((SLAB, width), F32)
    zero = jnp.zeros((SLAB, width), F32)
    lam, _, following, _ = lax.fori_loop(0, rows // (4 * SLAB), slab, (zero, one, one, one))
    edge_ref[...] = lam * following


def backward_kernel(
    live_ref, pre_ref, par_ref, w_ref, lam_ref, reach_ref, edge_ref, decay_ref, conv_ref, ig_ref, dg_ref, state_ref, prod_ref, cin_ref,
    drec_ref, dpar_ref, dw_ref, rec_ref, dconv_ref, full_ref, dw_acc,
):
    rows, width = conv_ref.shape
    live = live_ref[0]
    rec_ref[...] = jnp.where(row_ids(rows + HALO, width, -HALO) < live, pre_ref[...], 0.0)
    par = [par_ref[k : k + 1, :] for k in range(8)]
    cin = cin_ref[:1, :]
    edge = edge_ref[:1, :]
    full_ref[:SLAB, :] = jnp.broadcast_to(cin, (SLAB, width))
    dconv_ref[:HALO, :] = jnp.zeros((HALO, width), F32)
    dconv_ref[rows + HALO :, :] = jnp.zeros((HALO, width), F32)
    sums = [jnp.zeros((1, width), F32) for _ in range(8)]
    for at in range(0, rows, ROWS):
        span = pl.ds(at, ROWS)
        full_ref[pl.ds(at + SLAB, ROWS), :] = state_ref[span, :] + prod_ref[span, :] * cin
        lam = lam_ref[span, :] + reach_ref[span, :] * edge
        decay, conv, ig, dg = decay_ref[span, :], conv_ref[span, :], ig_ref[span, :], dg_ref[span, :]
        before = full_ref[pl.ds(at, ROWS + SLAB), :][SLAB - 1 : SLAB - 1 + ROWS]
        room = 1.0 - decay * decay
        scale = jnp.sqrt(jnp.maximum(room, DECAY_FLOOR))
        lam_conv = lam * conv
        d_decay = lam * before - jnp.where(room > DECAY_FLOOR, lam_conv * ig * decay / scale, 0.0)
        moved = d_decay * decay
        sums[7] = sums[7] + jnp.sum(moved * dg, axis=0, keepdims=True)
        d_ig = lam_conv * scale * ig * (1.0 - ig)
        d_dg = moved * par[7] * dg * (1.0 - dg)
        sums[5] = sums[5] + jnp.sum(d_ig, axis=0, keepdims=True)
        sums[6] = sums[6] + jnp.sum(d_dg, axis=0, keepdims=True)
        both = jnp.concatenate([d_ig.astype(BF), d_dg.astype(BF)], axis=1)
        d_conv = lam * scale * ig + dot(both, w_ref[...], ((1,), (1,)))
        d_conv = jnp.where(row_ids(ROWS, width, at) < live, d_conv, 0.0)
        dconv_ref[pl.ds(at + HALO, ROWS), :] = d_conv
        part = dot(conv.astype(BF), both, ((0,), (0,)))
        dw_acc[...] = part if at == 0 else dw_acc[...] + part
        near = rec_ref[pl.ds(at, ROWS + HALO), :]
        for k in range(4):
            sums[k] = sums[k] + jnp.sum(d_conv * near[HALO - k : HALO - k + ROWS], axis=0, keepdims=True)
        sums[4] = sums[4] + jnp.sum(d_conv, axis=0, keepdims=True)
    for k in range(8):
        dpar_ref[k : k + 1, :] = sums[k]
    dw_ref[...] = dw_acc[...].astype(BF)
    for at in list(range(0, rows, ROWS)) + [rows]:
        count = ROWS if at < rows else HALO
        near = dconv_ref[pl.ds(at, count + SLAB), :]
        total = par[0] * near[:count]
        for k in range(1, 4):
            total = total + par[k] * near[k : k + count]
        drec_ref[pl.ds(at, count), :] = total


def kernel_call(body, live, arrays, offsets, outs, scratch, name):
    width = outs[0][1]
    steps = width // GROUP
    specs = []
    for array, off in zip(arrays, offsets):
        if array.ndim == 3:
            specs.append(pl.BlockSpec((pl.squeezed,) + array.shape[1:], lambda j, s: (j, 0, 0)))
        else:
            specs.append(pl.BlockSpec((array.shape[0], GROUP), lambda j, s, off=off: (0, j + off)))
    out_specs, out_shapes = [], []
    for rows, cols, kind in outs:
        if cols == width:
            out_specs.append(pl.BlockSpec((rows, GROUP), lambda j, s: (0, j)))
            out_shapes.append(jax.ShapeDtypeStruct((rows, cols), kind))
        else:
            out_specs.append(pl.BlockSpec((pl.squeezed, rows, cols), lambda j, s: (j, 0, 0)))
            out_shapes.append(jax.ShapeDtypeStruct((steps, rows, cols), kind))
    return pl.pallas_call(
        body,
        grid_spec=pltpu.PrefetchScalarGridSpec(
            num_scalar_prefetch=1, grid=(steps,), in_specs=specs, out_specs=out_specs,
            scratch_shapes=[pltpu.VMEM(shape, F32) for shape in scratch],
        ),
        out_shape=out_shapes,
        compiler_params=pltpu.CompilerParams(vmem_limit_bytes=VMEM),
        name=name,
    )(live, *arrays)


def norm_rate(values):
    return lax.rsqrt(jnp.mean(values * values, axis=-1, keepdims=True) + NORM_EPS)


def norm_back(grad, unit, rate, gain):
    moved = grad * gain
    return rate * (moved - unit * jnp.mean(moved * unit, axis=-1, keepdims=True))


def gelu_product(gate, up):
    return jax.nn.gelu(gate) * up


def on_device(size, n, tokens, lengths, gains, w_gelu, w_rec, chan, w_lru, w_out, w_mlp_in, w_down, cotangent):
    place = lax.axis_index("dp")
    turn = lax.axis_index("tensor")
    d_model = tokens.shape[1]
    seq_len = tokens.shape[0]
    rows = seq_len // n
    half = rows // 2
    d_own = w_gelu.shape[0]
    heads_own, head = chan.shape[1], w_lru.shape[3]
    heads = heads_own * n
    width = heads * head
    table, inverse = basis(size, d_own, place)
    live_count = (lengths - turn * rows).astype(jnp.int32)
    live = (lax.iota(jnp.int32, rows)[:, None] < live_count).astype(F32)

    gain_rows = lax.all_gather(gains.astype(BF), "dp", axis=1, tiled=True)
    gain = permute_gain(gain_rows, table).astype(F32)

    def wide(parts):
        own = lax.all_gather(jnp.stack(parts).astype(BF), "tensor", axis=0)
        return own.transpose(2, 1, 0, 3).reshape(d_own, -1)

    w_in = spread(wide([w_gelu, w_rec]), size)
    flat = jnp.concatenate([w_lru.reshape(-1), chan.reshape(-1)]).astype(BF)
    flat = lax.all_gather(flat, ("tensor", "dp"), axis=0).reshape(n, size, -1)
    lru = flat[..., : w_lru.size].reshape((n, size) + w_lru.shape)
    lru = lru.transpose(2, 0, 3, 1, 4, 5).reshape(2, heads, head, head)
    chans = flat[..., w_lru.size :].reshape((n, size) + chan.shape)
    chans = chans.transpose(2, 0, 3, 1, 4).reshape(8, width).astype(F32)
    par = jnp.concatenate([chans[:7], -8.0 * jax.nn.softplus(-chans[7:])])
    per = GROUP // head
    groups = width // GROUP
    eye = jnp.eye(per, dtype=BF)[None, None, :, None, :, None]
    dense = lru.reshape(2, groups, per, head, 1, head) * eye
    dense = dense.reshape(2, groups, GROUP, GROUP)
    dense = jnp.concatenate([dense[0], dense[1]], axis=-1)
    w_back = spread(wide([w_out.T]), size)
    w_gu = spread(jnp.concatenate([w_mlp_in[0], w_mlp_in[1]], axis=1).astype(BF), size)
    w_dn = spread(w_down.T.astype(BF), size)

    main = lax.dynamic_slice_in_dim(tokens, turn * rows, rows)
    before = lax.dynamic_slice_in_dim(tokens, jnp.maximum(turn * rows - HALO, 0), HALO)
    before = jnp.where(turn > 0, before, jnp.zeros_like(before))
    extended = permute_rows(jnp.concatenate([before, main]), table).astype(F32)
    first_rate = norm_rate(extended)
    first = (extended * first_rate * gain[0]).astype(BF)
    inputs, first_own, first_rate = extended[HALO:], first[HALO:], first_rate[HALO:]
    cot = permute(cotangent.reshape(n, 2, half, d_model), table)

    pre = dot(first, w_in)
    keep = (rows, width, F32)
    conv, decay, ig, dg, state, prod = kernel_call(
        forward_kernel, live_count, [pre, par, dense], [groups, 0, 0], [keep] * 6,
        [(rows + HALO, GROUP)], "recurrence",
    )
    ends = lax.all_gather(jnp.concatenate([prod[-1:], state[-1:]]), "tensor", axis=0)
    carry = jnp.zeros((1, width), F32)
    for k in range(n - 1):
        carry = jnp.where(k < turn, ends[k, 1:] + ends[k, :1] * carry, carry)
    branch_pre = pre[HALO:, :width]
    recurrent = (state + prod * carry) * live
    activated, gelu_pull = jax.vjp(jax.nn.gelu, branch_pre)
    mixed = (activated * recurrent).astype(BF)
    hidden = inputs + dot(mixed, w_back, ((1,), (1,)))
    second_rate = norm_rate(hidden)
    second_unit = hidden * second_rate
    second_own = (second_unit * gain[1]).astype(BF)

    hidden_units = w_dn.shape[1]
    mlp_sum, grad_second, seconds, products, grads = [], [], [], [], []
    for h in range(2):
        second = lax.all_gather(second_own[h * half : (h + 1) * half], "tensor", axis=0, tiled=True)
        cot_rows = cot[h].reshape(n * half, d_model)
        both = dot(second, w_gu)
        product, pull = jax.vjp(gelu_product, both[:, :hidden_units], both[:, hidden_units:])
        product = product.astype(BF)
        grad_gate, grad_up = pull(dot(cot_rows, w_dn))
        grad = jnp.concatenate([grad_gate.astype(BF), grad_up.astype(BF)], axis=1)
        share = dot(grad, w_gu, ((1,), (1,))).astype(BF)
        grad_second.append(lax.psum_scatter(share, "tensor", scatter_dimension=0, tiled=True))
        share = dot(product, w_dn, ((1,), (1,))).astype(BF)
        mlp_sum.append(lax.psum_scatter(share, "tensor", scatter_dimension=0, tiled=True))
        seconds.append(second)
        products.append(product)
        grads.append(grad)

    def by_rows(lefts, rights):
        part = dot(lefts[0], rights[0], ((0,), (0,))).astype(BF)
        return (part.astype(F32) + dot(lefts[1], rights[1], ((0,), (0,)))).astype(BF)

    cots = [cot[h].reshape(n * half, d_model) for h in range(2)]
    g_gu = collect(by_rows(seconds, grads), size).astype(F32)
    g_dn = collect(by_rows(cots, products), size).astype(F32)
    result = hidden + jnp.concatenate(mlp_sum).astype(F32)
    result = permute_rows(result.astype(BF), inverse)
    output = lax.all_gather(result, "tensor", axis=0, tiled=True)

    grad_second = jnp.concatenate(grad_second).astype(F32)
    cot_own = lax.dynamic_slice_in_dim(cot, turn, 1, axis=1).reshape(rows, d_model).astype(F32)
    gain_two = jnp.sum(grad_second * second_unit, axis=0)
    grad_hidden = cot_own + norm_back(grad_second, second_unit, second_rate, gain[1])
    hidden_low = grad_hidden.astype(BF)

    def to_owner(grad, parts):
        own = collect(grad.astype(BF), size).reshape(d_own, parts, n, -1).transpose(2, 1, 0, 3)
        return lax.psum_scatter(own, "tensor", scatter_dimension=0).astype(F32)

    grad_mixed = dot(hidden_low, w_back)
    lam, reach, edge = kernel_call(
        back_scan_kernel, live_count, [pre, grad_mixed, decay], [0, 0, 0],
        [keep, keep, (SLAB, width, F32)], [], "back_scan",
    )
    edges = lax.all_gather(edge[:1], "tensor", axis=0)
    arriving = jnp.zeros((1, width), F32)
    for k in range(n - 1, 0, -1):
        arriving = jnp.where(k > turn, edges[k] + ends[k, :1] * arriving, arriving)
    (grad_pre,) = gelu_pull(grad_mixed * recurrent)
    g_back = to_owner(dot(hidden_low, mixed, ((0,), (0,))), 1)
    tall = jnp.broadcast_to
    drec, dpar, d_dense = kernel_call(
        backward_kernel, live_count,
        [pre, par, dense, lam, reach, tall(arriving, (SLAB, width)), decay, conv, ig, dg, state, prod, tall(carry, (SLAB, width))],
        [groups] + [0] * 12,
        [(rows + HALO, width, F32), (8, width, F32), (GROUP, 2 * GROUP, BF)],
        [(rows + HALO, GROUP), (rows + 2 * HALO, GROUP), (rows + SLAB, GROUP), (GROUP, 2 * GROUP)], "recurrence_back",
    )
    edge_rows = lax.ppermute(drec[:HALO], "tensor", [(k, k - 1) for k in range(1, n)])
    rec_low = (drec[HALO:] + jnp.pad(edge_rows, ((rows - HALO, 0), (0, 0)))) * live
    grad_in = jnp.concatenate([grad_pre.astype(BF), rec_low.astype(BF)], axis=1)
    g_in = to_owner(dot(first_own, grad_in, ((0,), (0,))), 2)
    grad_first = dot(grad_in, w_in, ((1,), (1,)))
    first_unit = inputs * first_rate
    gain_one = jnp.sum(grad_first * first_unit, axis=0)
    grad_tokens = grad_hidden + norm_back(grad_first, first_unit, first_rate, gain[0])
    grad_tokens = permute_rows(grad_tokens.astype(BF), inverse)
    grad_tokens = lax.all_gather(grad_tokens, "tensor", axis=0, tiled=True)

    d_gain = permute_gain(jnp.stack([gain_one, gain_two]), inverse)
    d_chan = jnp.concatenate([dpar[:7], dpar[7:] * 8.0 * jax.nn.sigmoid(-chans[7:])])
    small = lax.psum(jnp.concatenate([d_gain.reshape(-1), d_chan.reshape(-1)]), ("tensor", "dp"))
    d_gain = small[: d_gain.size].reshape(2, d_model)
    d_gain = lax.dynamic_slice_in_dim(d_gain, place * d_own, d_own, axis=1)
    d_chan = small[d_gain.size * size :].reshape(8, heads, head)
    d_chan = lax.dynamic_slice(d_chan, (0, turn * heads_own, place * chan.shape[2]), chan.shape)
    blocks = [
        d_dense[:, k * head : (k + 1) * head, m * GROUP + k * head : m * GROUP + (k + 1) * head]
        for m in range(2)
        for k in range(per)
    ]
    d_lru = jnp.stack(blocks).reshape(2, per, groups, head, head).transpose(0, 2, 1, 3, 4)
    d_lru = d_lru.reshape(2, n, heads_own, size, head // size, head).transpose(1, 3, 0, 2, 4, 5)
    d_lru = lax.psum_scatter(d_lru.reshape(n * size, -1), ("tensor", "dp"), scatter_dimension=0)
    d_lru = d_lru.reshape(w_lru.shape).astype(F32)
    g_gate, g_up = g_gu[:, :hidden_units], g_gu[:, hidden_units:]
    return (
        output, grad_tokens, d_gain[0], d_gain[1], g_in[0], g_in[1], d_chan, d_lru,
        g_back[0].T, jnp.stack([g_gate, g_up]), g_dn.T,
    )


def solution(mesh):
    in_specs = (
        P("dp", None),
        P("dp"),
        P(None, "dp"),
        P("dp", "tensor"),
        P("dp", "tensor"),
        P(None, "tensor", "dp"),
        P(None, "tensor", "dp", None),
        P("tensor", "dp"),
        P(None, "dp", "tensor"),
        P("tensor", "dp"),
        P("dp", None),
    )
    out_specs = (
        P("dp", None),
        P("dp", None),
        P("dp"),
        P("dp"),
        P("dp", "tensor"),
        P("dp", "tensor"),
        P(None, "tensor", "dp"),
        P(None, "tensor", "dp", None),
        P("tensor", "dp"),
        P(None, "dp", "tensor"),
        P("tensor", "dp"),
    )
    body = functools.partial(on_device, mesh.shape["dp"], mesh.shape["tensor"])
    return jax.shard_map(body, mesh=mesh, in_specs=in_specs, out_specs=out_specs, check_vma=False)
```

```python
import functools

import jax
import jax.numpy as jnp
import numpy as np
from jax import lax
from jax.experimental import pallas as pl
from jax.experimental.pallas import tpu as pltpu
from jax.sharding import PartitionSpec as P

NORM_EPS = 1e-06
DECAY_FLOOR = 0.05
HALO = 16
GROUP = 640
ROWS = 128
SLAB = 8
VMEM = 58 * 1024 * 1024
BF = jnp.bfloat16
F32 = jnp.float32


def dot(left, right, dims=((1,), (0,))):
    return lax.dot_general(left, right, (dims, ((), ())), preferred_element_type=F32)


def tie(values, *others):
    return lax.optimization_barrier((values,) + others)[0]


def exchange(values, bit, size):
    return lax.ppermute(values, "dp", [(k, k ^ (1 << bit)) for k in range(size)])


def orders(size, parts):
    high = list(range(1, size.bit_length() - 1))
    return [high, high[::-1]][:parts]


def parts_of(rows):
    return 2 if rows % 256 == 0 else 1


def spread(own, size):
    parts = parts_of(own.shape[0])
    pieces = jnp.split(own, parts)
    for turn in range(size.bit_length() - 2):
        got = [exchange(p, o[turn], size) for p, o in zip(pieces, orders(size, parts))]
        pieces = [jnp.concatenate([p, g]) for p, g in zip(pieces, got)]
    half = jnp.concatenate(pieces)
    return [half, exchange(half, 0, size)], got[-1][:16, :128]


def add_low(one, two):
    return (one.astype(F32) + two.astype(F32)).astype(BF)


def collect(full, size):
    half = full.shape[0] // 2
    parts = parts_of(full.shape[0] // size)
    kept = add_low(full[:half], exchange(full[half:], 0, size))
    pieces = jnp.split(kept, parts)
    for turn in reversed(range(size.bit_length() - 2)):
        cut = pieces[0].shape[0] // 2
        got = [exchange(p[cut:], o[turn], size) for p, o in zip(pieces, orders(size, parts))]
        pieces = [add_low(p[:cut], g) for p, g in zip(pieces, got)]
    return jnp.concatenate(pieces)


def z_shift(values, by, n, around=True):
    pairs = [(k, (k + by) % n) for k in range(n) if around or 0 <= k + by < n]
    return lax.ppermute(values, "tensor", pairs)


def z_scatter(values, n):
    turn = lax.axis_index("tensor")
    total = lax.dynamic_index_in_dim(values, turn, 0, keepdims=False).astype(F32)
    for k in range(1, n):
        block = lax.dynamic_index_in_dim(values, (turn + k) % n, 0, keepdims=False)
        total = total + z_shift(block, k, n).astype(F32)
    return total


def z_line(own, n):
    turn = lax.axis_index("tensor")
    right, left = [own], [own]
    for k in range(1, n):
        right.append(lax.ppermute(right[-1], "tensor", [(s, s + 1) for s in range(k - 1, n - 1)]))
        left.append(lax.ppermute(left[-1], "tensor", [(s, s - 1) for s in range(1, n - k + 1)]))
    rows = own.shape[0]
    out = jnp.zeros((n * rows, own.shape[1]), own.dtype)
    out = lax.dynamic_update_slice_in_dim(out, own, turn * rows, 0)
    for k in range(1, n):
        out = lax.dynamic_update_slice_in_dim(out, left[k] + right[n - k], (turn + k) % n * rows, 0)
    return out


def small_gather(own, size, n):
    turn, place = lax.axis_index("tensor"), lax.axis_index("dp")
    rows = jnp.stack([own] + [z_shift(own, -k, n) for k in range(1, n)])
    rows = jnp.take(rows, (jnp.arange(n) - turn) % n, axis=0)[None]
    for bit in range(size.bit_length() - 1):
        rows = jnp.concatenate([rows, exchange(rows, bit, size)])
    return jnp.take(rows, jnp.arange(size) ^ place, axis=0).transpose(1, 0, 2)


def small_scatter(values, size, n):
    place = lax.axis_index("dp")
    values = jnp.take(values, jnp.arange(size) ^ place, axis=0)
    for bit in reversed(range(size.bit_length() - 1)):
        half = values.shape[0] // 2
        values = add_low(values[:half], exchange(values[half:], bit, size))
    return z_scatter(values[0], n)


def basis(size, rows, place):
    parts = parts_of(rows)
    count = size // 2
    masks, which = [], []
    for core in range(2):
        for part, order in enumerate(orders(size, parts)):
            for q in range(count):
                masks.append(core | sum(((q >> t) & 1) << b for t, b in enumerate(order)))
                which.append(part)
    table = (place ^ jnp.asarray(np.array(masks, np.int32))) * parts
    table = table + jnp.asarray(np.array(which, np.int32))
    spots = jnp.arange(len(masks), dtype=jnp.int32)
    inverse = jnp.sum(jnp.where(table[None, :] == spots[:, None], spots[None, :], 0), axis=1)
    return table, inverse.astype(jnp.int32)


def copy_kernel(blocks, table_ref, in_ref, out_ref):
    width = in_ref.shape[1] // blocks
    for p in range(blocks):
        start = pl.multiple_of(table_ref[p] * width, width)
        out_ref[:, p * width : (p + 1) * width] = in_ref[:, pl.ds(start, width)]


def permute_rows(values, table):
    rows, d_model = values.shape
    step = max(k for k in range(16, 289, 16) if rows % k == 0)
    spec = pl.BlockSpec((step, d_model), lambda r, tab: (r, 0))
    return pl.pallas_call(
        functools.partial(copy_kernel, table.shape[0]),
        grid_spec=pltpu.PrefetchScalarGridSpec(
            num_scalar_prefetch=1, grid=(rows // step,), in_specs=[spec], out_specs=spec
        ),
        out_shape=jax.ShapeDtypeStruct(values.shape, values.dtype),
        compiler_params=pltpu.CompilerParams(vmem_limit_bytes=VMEM),
        cost_estimate=pl.CostEstimate(flops=0, bytes_accessed=2 * values.nbytes, transcendentals=0),
        name="permute",
    )(table, values)


def permute_gain(values, table):
    lead = values.shape[0]
    return jnp.take(values.reshape(lead, table.shape[0], -1), table, axis=1).reshape(lead, -1)


def row_ids(count, width, first):
    return lax.broadcasted_iota(jnp.int32, (count, width), 0) + first


def scan_slab(decay, value, back):
    rows = row_ids(SLAB, decay.shape[1], 0)
    for step in (1, 2, 4):
        keep = rows < SLAB - step if back else rows >= step
        shift = SLAB - step if back else step
        moved_decay = pltpu.roll(decay, shift, 0)
        moved_value = pltpu.roll(value, shift, 0)
        value = jnp.where(keep, value + decay * moved_value, value)
        decay = jnp.where(keep, decay * moved_decay, decay)
    return decay, value


def gelu_parts(v):
    c = np.float32(np.sqrt(2 / np.pi))
    return jnp.tanh(c * (v + 0.044715 * v * v * v))


def head_mask(head, at, width):
    lanes = lax.broadcasted_iota(jnp.int32, (head, 2 * width), 1)
    lanes = jnp.where(lanes >= width, lanes - width, lanes)
    return (lanes >= at * head) & (lanes < (at + 1) * head)


def fill_dense(w_ref, dense_ref):
    head = w_ref.shape[0]
    blocks = w_ref[...].astype(F32)
    for k in range(dense_ref.shape[0] // head):
        block = jnp.where(head_mask(head, k, dense_ref.shape[0]), blocks, 0.0)
        dense_ref[k * head : (k + 1) * head, :] = block.astype(BF)


def forward_kernel(
    live_ref, pre_ref, par_ref, w_ref, conv_ref, decay_ref, ig_ref, dg_ref, state_ref, prod_ref, rec_ref, dense_ref
):
    rows, width = conv_ref.shape
    fill_dense(w_ref, dense_ref)
    live = live_ref[0]
    rec_ref[...] = jnp.where(row_ids(rows + HALO, width, -HALO) < live, pre_ref[...], 0.0)
    par = [par_ref[k : k + 1, :] for k in range(8)]
    for at in range(0, rows, ROWS):
        span = pl.ds(at, ROWS)
        near = rec_ref[pl.ds(at, ROWS + HALO), :]
        conv = par[4] + par[0] * near[HALO : HALO + ROWS]
        for k in range(1, 4):
            conv = conv + par[k] * near[HALO - k : HALO - k + ROWS]
        conv = jnp.where(row_ids(ROWS, width, at) < live, conv, 0.0)
        conv_ref[span, :] = conv
        gates = dot(conv.astype(BF), dense_ref[...])
        ig = lax.logistic(gates[:, :width] + par[5])
        dg = lax.logistic(gates[:, width:] + par[6])
        decay = jnp.exp(dg * par[7])
        ig_ref[span, :] = ig
        dg_ref[span, :] = dg
        decay_ref[span, :] = decay
        state_ref[span, :] = jnp.sqrt(jnp.maximum(1.0 - decay * decay, DECAY_FLOOR)) * ig * conv

    def slab(k, carry):
        state, prod = carry
        for inner in range(4):
            span = pl.ds(pl.multiple_of(k * 4 * SLAB + inner * SLAB, SLAB), SLAB)
            decay, value = scan_slab(decay_ref[span, :], state_ref[span, :], False)
            value = value + decay * state
            decay = decay * prod
            state_ref[span, :] = value
            prod_ref[span, :] = decay
            state = jnp.broadcast_to(value[SLAB - 1 :, :], (SLAB, width))
            prod = jnp.broadcast_to(decay[SLAB - 1 :, :], (SLAB, width))
        return state, prod

    lax.fori_loop(0, rows // (4 * SLAB), slab, (jnp.zeros((SLAB, width), F32), jnp.ones((SLAB, width), F32)))


def back_scan_kernel(live_ref, pre_ref, grad_ref, decay_ref, lam_ref, reach_ref, edge_ref):
    rows, width = grad_ref.shape
    live = live_ref[0]
    for at in range(0, rows, ROWS):
        span = pl.ds(at, ROWS)
        v = pre_ref[span, :]
        act = 0.5 * v * (1.0 + gelu_parts(v))
        lam_ref[span, :] = jnp.where(row_ids(ROWS, width, at) < live, grad_ref[span, :] * act, 0.0)
    last = row_ids(SLAB, width, 0) == SLAB - 1

    def slab(k, carry):
        lam, reach, following, _ = carry
        for inner in range(4):
            span = pl.ds(pl.multiple_of(rows - (k * 4 + inner + 1) * SLAB, SLAB), SLAB)
            own = decay_ref[span, :]
            ahead = jnp.where(last, following, pltpu.roll(own, SLAB - 1, 0))
            decay, value = scan_slab(ahead, lam_ref[span, :], True)
            value = value + decay * lam
            decay = decay * reach
            lam_ref[span, :] = value
            reach_ref[span, :] = decay
            lam = jnp.broadcast_to(value[:1, :], (SLAB, width))
            reach = jnp.broadcast_to(decay[:1, :], (SLAB, width))
            following = jnp.broadcast_to(own[:1, :], (SLAB, width))
        return lam, reach, following, own

    one = jnp.ones((SLAB, width), F32)
    zero = jnp.zeros((SLAB, width), F32)
    lam, _, following, _ = lax.fori_loop(0, rows // (4 * SLAB), slab, (zero, one, one, one))
    edge_ref[...] = lam * following


def backward_kernel(
    live_ref, pre_ref, par_ref, w_ref, lam_ref, reach_ref, edge_ref, decay_ref, conv_ref, ig_ref, dg_ref, state_ref, prod_ref, cin_ref,
    drec_ref, dpar_ref, dw_ref, rec_ref, dconv_ref, full_ref, dw_acc, dense_ref,
):
    rows, width = conv_ref.shape
    live = live_ref[0]
    rec_ref[...] = jnp.where(row_ids(rows + HALO, width, -HALO) < live, pre_ref[...], 0.0)
    par = [par_ref[k : k + 1, :] for k in range(8)]
    fill_dense(w_ref, dense_ref)
    cin = cin_ref[:1, :]
    edge = edge_ref[:1, :]
    full_ref[:SLAB, :] = jnp.broadcast_to(cin, (SLAB, width))
    dconv_ref[:HALO, :] = jnp.zeros((HALO, width), F32)
    dconv_ref[rows + HALO :, :] = jnp.zeros((HALO, width), F32)
    sums = [jnp.zeros((1, width), F32) for _ in range(8)]
    for at in range(0, rows, ROWS):
        span = pl.ds(at, ROWS)
        full_ref[pl.ds(at + SLAB, ROWS), :] = state_ref[span, :] + prod_ref[span, :] * cin
        lam = lam_ref[span, :] + reach_ref[span, :] * edge
        decay, conv, ig, dg = decay_ref[span, :], conv_ref[span, :], ig_ref[span, :], dg_ref[span, :]
        before = full_ref[pl.ds(at, ROWS + SLAB), :][SLAB - 1 : SLAB - 1 + ROWS]
        room = 1.0 - decay * decay
        scale = jnp.sqrt(jnp.maximum(room, DECAY_FLOOR))
        lam_conv = lam * conv
        d_decay = lam * before - jnp.where(room > DECAY_FLOOR, lam_conv * ig * decay / scale, 0.0)
        moved = d_decay * decay
        sums[7] = sums[7] + jnp.sum(moved * dg, axis=0, keepdims=True)
        d_ig = lam_conv * scale * ig * (1.0 - ig)
        d_dg = moved * par[7] * dg * (1.0 - dg)
        sums[5] = sums[5] + jnp.sum(d_ig, axis=0, keepdims=True)
        sums[6] = sums[6] + jnp.sum(d_dg, axis=0, keepdims=True)
        both = jnp.concatenate([d_ig.astype(BF), d_dg.astype(BF)], axis=1)
        d_conv = lam * scale * ig + dot(both, dense_ref[...], ((1,), (1,)))
        d_conv = jnp.where(row_ids(ROWS, width, at) < live, d_conv, 0.0)
        dconv_ref[pl.ds(at + HALO, ROWS), :] = d_conv
        part = dot(conv.astype(BF), both, ((0,), (0,)))
        dw_acc[...] = part if at == 0 else dw_acc[...] + part
        near = rec_ref[pl.ds(at, ROWS + HALO), :]
        for k in range(4):
            sums[k] = sums[k] + jnp.sum(d_conv * near[HALO - k : HALO - k + ROWS], axis=0, keepdims=True)
        sums[4] = sums[4] + jnp.sum(d_conv, axis=0, keepdims=True)
    for k in range(8):
        dpar_ref[k : k + 1, :] = sums[k]
    head = dw_ref.shape[0]
    total = jnp.zeros((head, 2 * width), F32)
    for k in range(width // head):
        total = total + jnp.where(head_mask(head, k, width), dw_acc[k * head : (k + 1) * head, :], 0.0)
    dw_ref[...] = total.astype(BF)
    for at in list(range(0, rows, ROWS)) + [rows]:
        count = ROWS if at < rows else HALO
        near = dconv_ref[pl.ds(at, count + SLAB), :]
        total = par[0] * near[:count]
        for k in range(1, 4):
            total = total + par[k] * near[k : k + count]
        drec_ref[pl.ds(at, count), :] = total


def kernel_call(body, live, arrays, outs, scratch, name, work):
    width = outs[0][1]
    steps = width // GROUP
    specs = []
    for array in arrays:
        if array.ndim == 3:
            specs.append(pl.BlockSpec((pl.squeezed,) + array.shape[1:], lambda j, s: (j, 0, 0)))
        else:
            specs.append(pl.BlockSpec((array.shape[0], GROUP), lambda j, s: (0, j)))
    out_specs, out_shapes = [], []
    for rows, cols, kind in outs:
        if cols == width:
            out_specs.append(pl.BlockSpec((rows, GROUP), lambda j, s: (0, j)))
            out_shapes.append(jax.ShapeDtypeStruct((rows, cols), kind))
        else:
            out_specs.append(pl.BlockSpec((pl.squeezed, rows, cols), lambda j, s: (j, 0, 0)))
            out_shapes.append(jax.ShapeDtypeStruct((steps, rows, cols), kind))
    moved = sum(a.nbytes for a in arrays) + sum(int(np.prod(o.shape)) * o.dtype.itemsize for o in out_shapes)
    return pl.pallas_call(
        body,
        grid_spec=pltpu.PrefetchScalarGridSpec(
            num_scalar_prefetch=1, grid=(steps,), in_specs=specs, out_specs=out_specs,
            scratch_shapes=[pltpu.VMEM(shape, kind) for shape, kind in scratch],
        ),
        out_shape=out_shapes,
        compiler_params=pltpu.CompilerParams(vmem_limit_bytes=VMEM),
        cost_estimate=pl.CostEstimate(flops=work * outs[0][0] * width, bytes_accessed=moved, transcendentals=0),
        name=name,
    )(live, *arrays)


def norm_rate(values):
    return lax.rsqrt(jnp.mean(values * values, axis=-1, keepdims=True) + NORM_EPS)


def norm_back(grad, unit, rate, gain):
    moved = grad * gain
    return rate * (moved - unit * jnp.mean(moved * unit, axis=-1, keepdims=True))


def gelu_product(gate, up):
    return jax.nn.gelu(gate) * up


def wide_dot(left, halves):
    cut = halves[0].shape[0]
    return dot(left[:, :cut], halves[0]) + dot(left[:, cut:], halves[1])


def wide_back(left, halves):
    return jnp.concatenate([dot(left, h, ((1,), (1,))) for h in halves], axis=1)


def on_device(size, n, tokens, lengths, gains, w_gelu, w_rec, chan, w_lru, w_out, w_mlp_in, w_down, cotangent):
    place = lax.axis_index("dp")
    turn = lax.axis_index("tensor")
    d_model = tokens.shape[1]
    rows = tokens.shape[0] // n
    half = rows // 2
    d_own = w_gelu.shape[0]
    heads_own, part, head = chan.shape[1], chan.shape[2], w_lru.shape[3]
    heads = heads_own * n
    width = heads * head
    groups = width // GROUP
    table, inverse = basis(size, d_own, place)
    live_count = (lengths - turn * rows).astype(jnp.int32)
    live = (lax.iota(jnp.int32, rows)[:, None] < live_count).astype(F32)

    def wide(own):
        own = lax.all_gather(own, "tensor", axis=0)
        return own.transpose(1, 0, 2).reshape(d_own, width)

    z_rec = wide(w_rec.astype(BF))
    small = [w_lru.transpose(2, 0, 1, 3).reshape(-1), chan.reshape(-1), gains.reshape(-1)]
    small = small_gather(jnp.concatenate(small).astype(BF), size, n)
    w_r, token = spread(tie(z_rec, small[0, 0, :128]), size)
    z_gelu = tie(wide(tie(w_gelu.astype(BF), z_rec[:16, :128])), token)
    w_g, token = spread(z_gelu, size)
    z_out = tie(wide(tie(w_out.T.astype(BF), z_gelu[:16, :128])), token)
    w_o, token = spread(z_out, size)
    w_gu = jnp.concatenate([w_mlp_in[0], w_mlp_in[1]], axis=1).astype(BF)
    w_gu, token = spread(tie(w_gu, token), size)
    w_gu = jnp.concatenate(w_gu)
    w_dn = jnp.concatenate(spread(tie(w_down.T.astype(BF), token), size)[0])

    gain = small[0, :, -gains.size :].reshape(size, 2, d_own).transpose(1, 0, 2).reshape(2, d_model)
    gain = permute_gain(gain, table).astype(F32)
    chans = small[..., w_lru.size : w_lru.size + chan.size].reshape((n, size) + chan.shape)
    chans = chans.transpose(2, 0, 3, 1, 4).reshape(8, width).astype(F32)
    par = jnp.concatenate([chans[:7], -8.0 * jax.nn.softplus(-chans[7:])])
    each = n // groups
    lru = small[..., : w_lru.size].reshape(groups, each, head, 2, heads_own * head)
    lru = lru.transpose(0, 2, 3, 1, 4).reshape(groups, head, 2 * GROUP)

    main = lax.dynamic_slice_in_dim(tokens, turn * rows, rows)
    before = lax.dynamic_slice_in_dim(tokens, jnp.maximum(turn * rows - HALO, 0), HALO)
    before = jnp.where(turn > 0, before, jnp.zeros_like(before))
    extended = permute_rows(jnp.concatenate([before, main]), table).astype(F32)
    first_rate = norm_rate(extended)
    first = (extended * first_rate * gain[0]).astype(BF)
    inputs, first_own, first_rate = extended[HALO:], first[HALO:], first_rate[HALO:]
    cot = permute_rows(cotangent, table).reshape(n, 2, half, d_model)
    cots = [cot[:, h].reshape(n * half, d_model) for h in range(2)]

    keep = (rows, width, F32)
    dense = ((GROUP, 2 * GROUP), BF)
    rec_pre = wide_dot(first, w_r)
    conv, decay, ig, dg, state, prod = kernel_call(
        forward_kernel, live_count, [rec_pre, par, lru], [keep] * 6,
        [((rows + HALO, GROUP), F32), dense], "recurrence", 18000,
    )
    ends = jnp.concatenate([prod[-1:], state[-1:]])
    came = [z_shift(ends, k, n, False) for k in range(1, n)]
    carry = jnp.zeros((1, width), F32)
    for end in came[::-1]:
        carry = end[1:] + end[:1] * carry
    branch_pre = wide_dot(first_own, w_g)
    recurrent = (state + prod * carry) * live
    activated, gelu_pull = jax.vjp(jax.nn.gelu, branch_pre)
    mixed = (activated * recurrent).astype(BF)
    hidden = inputs + wide_back(mixed, w_o)
    second_rate = norm_rate(hidden)
    second_unit = hidden * second_rate
    second_own = (second_unit * gain[1]).astype(BF)

    hidden_units = w_dn.shape[1]
    grad_products = [dot(c, w_dn) for c in cots]
    shares, grad_second, seconds, products, grads = [], [], [], [], []
    for h in range(2):
        second = lax.all_gather(second_own[h * half : (h + 1) * half], "tensor", axis=0, tiled=True)
        both = dot(second, w_gu)
        product, pull = jax.vjp(gelu_product, both[:, :hidden_units], both[:, hidden_units:])
        grad_gate, grad_up = pull(grad_products[h])
        product = product.astype(BF)
        grad = jnp.concatenate([grad_gate.astype(BF), grad_up.astype(BF)], axis=1)
        share = dot(grad, w_gu, ((1,), (1,))).astype(BF)
        grad_second.append(lax.psum_scatter(share, "tensor", scatter_dimension=0, tiled=True))
        shares.append(dot(tie(product, share), w_dn, ((1,), (1,))).astype(BF))
        seconds.append(second)
        products.append(product)
        grads.append(grad)

    def by_rows(lefts, rights):
        part = dot(lefts[0], rights[0], ((0,), (0,))).astype(BF)
        return (part.astype(F32) + dot(lefts[1], rights[1], ((0,), (0,)))).astype(BF)

    part_gu = by_rows(seconds, grads)
    part_dn = by_rows(cots, products)
    *grad_second, part_gu, part_dn, share_0, share_1 = lax.optimization_barrier(
        (*grad_second, part_gu, part_dn, *shares)
    )
    g_gu = collect(part_gu, size).astype(F32)
    g_dn = collect(part_dn, size).astype(F32)
    output = jnp.zeros((n, 2, half, d_model), BF)
    for h, share in enumerate([share_0, share_1]):
        mlp_sum = lax.psum_scatter(share, "tensor", scatter_dimension=0, tiled=True).astype(F32)
        result = permute_rows((hidden[h * half : (h + 1) * half] + mlp_sum).astype(BF), inverse)
        result = lax.all_gather(result, "tensor", axis=0)
        output = lax.dynamic_update_slice(output, result[:, None], (0, h, 0, 0))
    output = output.reshape(n * rows, d_model)

    grad_second = jnp.concatenate(grad_second).astype(F32)
    cot_own = lax.dynamic_index_in_dim(cot, turn, 0).reshape(rows, d_model).astype(F32)
    gain_two = jnp.sum(grad_second * second_unit, axis=0)
    grad_hidden = cot_own + norm_back(grad_second, second_unit, second_rate, gain[1])
    hidden_low = grad_hidden.astype(BF)

    def to_owner(left, right):
        own = collect(dot(left, right, ((0,), (0,))).astype(BF), size)
        return z_scatter(own.reshape(d_own, n, width // n).transpose(1, 0, 2), n)

    grad_mixed = wide_dot(hidden_low, w_o)
    lam, reach, edge = kernel_call(
        back_scan_kernel, live_count, [branch_pre, grad_mixed, decay],
        [keep, keep, (SLAB, width, F32)], [], "back_scan", 10000,
    )
    edges = jnp.concatenate([prod[-1:], edge[:1]])
    came = [z_shift(edges, -k, n, False) for k in range(1, n)]
    arriving = jnp.zeros((1, width), F32)
    for end in came[::-1]:
        arriving = end[1:] + end[:1] * arriving
    (grad_pre,) = gelu_pull(grad_mixed * recurrent)
    pre_low = grad_pre.astype(BF)
    first_part = wide_back(pre_low, w_g)
    tall = jnp.broadcast_to
    drec, dpar, d_lru = kernel_call(
        backward_kernel, live_count,
        [rec_pre, par, lru, lam, reach, tall(arriving, (SLAB, width)), decay, conv, ig, dg, state, prod, tall(carry, (SLAB, width))],
        [(rows + HALO, width, F32), (8, width, F32), (head, 2 * GROUP, BF)],
        [((rows + HALO, GROUP), F32), ((rows + 2 * HALO, GROUP), F32), ((rows + SLAB, GROUP), F32), ((GROUP, 2 * GROUP), F32), dense],
        "recurrence_back", 24000,
    )
    edge_rows = z_shift(drec[:HALO], -1, n, False)
    rec_low = (drec[HALO:] + jnp.pad(edge_rows, ((rows - HALO, 0), (0, 0)))) * live
    rec_low = rec_low.astype(BF)
    grad_first = first_part + wide_back(rec_low, w_r)
    first_unit = inputs * first_rate
    gain_one = jnp.sum(grad_first * first_unit, axis=0)
    grad_tokens = grad_hidden + norm_back(grad_first, first_unit, first_rate, gain[0])
    grad_tokens = permute_rows(grad_tokens.astype(BF), inverse)
    g_o = to_owner(hidden_low, mixed)
    g_g = to_owner(first_own, pre_low)
    g_r = to_owner(first_own, rec_low)
    grad_tokens = z_line(grad_tokens, n)

    d_gain = permute_gain(jnp.stack([gain_one, gain_two]), inverse)
    d_chan = jnp.concatenate([dpar[:7], dpar[7:] * 8.0 * jax.nn.sigmoid(-chans[7:])])
    d_lru = d_lru.reshape(groups, size, part, 2, each, -1).transpose(1, 0, 4, 2, 3, 5)
    d_chan = d_chan.reshape(8, n, heads_own, size, part).transpose(3, 1, 0, 2, 4)
    d_gain = d_gain.reshape(2, size, 1, d_own).transpose(1, 2, 0, 3)
    d_gain = jnp.broadcast_to(d_gain, (size, n, 2, d_own))
    small = [v.reshape(size, n, -1).astype(BF) for v in (d_lru, d_chan, d_gain)]
    small = small_scatter(jnp.concatenate(small, axis=2), size, n)
    d_lru = small[: w_lru.size].reshape(part, 2, heads_own, head).transpose(1, 2, 0, 3)
    d_chan = small[w_lru.size : -gains.size].reshape(chan.shape)
    d_gain = small[-gains.size :].reshape(gains.shape)
    g_gate, g_up = g_gu[:, :hidden_units], g_gu[:, hidden_units:]
    return (
        output, grad_tokens, d_gain[0], d_gain[1], g_g, g_r, d_chan, d_lru,
        g_o.T, jnp.stack([g_gate, g_up]), g_dn.T,
    )


def solution(mesh):
    in_specs = (
        P("dp", None),
        P("dp"),
        P(None, "dp"),
        P("dp", "tensor"),
        P("dp", "tensor"),
        P(None, "tensor", "dp"),
        P(None, "tensor", "dp", None),
        P("tensor", "dp"),
        P(None, "dp", "tensor"),
        P("tensor", "dp"),
        P("dp", None),
    )
    out_specs = (
        P("dp", None),
        P("dp", None),
        P("dp"),
        P("dp"),
        P("dp", "tensor"),
        P("dp", "tensor"),
        P(None, "tensor", "dp"),
        P(None, "tensor", "dp", None),
        P("tensor", "dp"),
        P(None, "dp", "tensor"),
        P("tensor", "dp"),
    )
    body = functools.partial(on_device, mesh.shape["dp"], mesh.shape["tensor"])
    return jax.shard_map(body, mesh=mesh, in_specs=in_specs, out_specs=out_specs, check_vma=False)
```

```python
import functools

import jax
import jax.numpy as jnp
import numpy as np
from jax import lax
from jax.experimental import pallas as pl
from jax.experimental.pallas import tpu as pltpu
from jax.sharding import PartitionSpec as P

NORM_EPS = 1e-06
DECAY_FLOOR = 0.05
HALO = 16
GROUP = 640
ROWS = 128
SLAB = 8
VMEM = 58 * 1024 * 1024
BF = jnp.bfloat16
F32 = jnp.float32
LITTLE = pl.CostEstimate(flops=1024, bytes_accessed=1024, transcendentals=0)


def dot(left, right, dims=((1,), (0,))):
    return lax.dot_general(left, right, (dims, ((), ())), preferred_element_type=F32)


def fence(values, *others):
    if not others:
        return list(values)
    place = pl.BlockSpec(memory_space=pl.ANY)
    return pl.pallas_call(
        lambda *refs: None,
        in_specs=[place] * (len(values) + len(others)),
        out_specs=[place] * len(values),
        out_shape=[jax.ShapeDtypeStruct(v.shape, v.dtype) for v in values],
        input_output_aliases={k: k for k in range(len(values))},
        compiler_params=pltpu.CompilerParams(vmem_limit_bytes=VMEM),
        name="fence",
    )(*values, *others)


def exchange(values, bit, size):
    return lax.ppermute(values, "dp", [(k, k ^ (1 << bit)) for k in range(size)])


def orders(size, parts):
    high = list(range(1, size.bit_length() - 1))
    return [high, high[::-1]][:parts]


def parts_of(rows):
    return 2 if rows % 256 == 0 else 1


def hop(pieces, turn, size):
    got = [exchange(p, o[turn], size) for p, o in zip(pieces, orders(size, len(pieces)))]
    return [jnp.concatenate([p, g]) for p, g in zip(pieces, got)], got


def spread_begin(own, size, *before):
    pieces, got = fence(jnp.split(own, parts_of(own.shape[0])), *before), ()
    for turn in range(size.bit_length() - 3):
        pieces, got = hop(pieces, turn, size)
    return pieces, got


def spread_end(pieces, size, before_last, before_core):
    pieces, got = hop(fence(pieces, *before_last), size.bit_length() - 3, size)
    half = jnp.concatenate(fence(pieces, *before_core))
    return [half, exchange(half, 0, size)], got


def add_all(terms):
    total = terms[0].astype(F32)
    for term in terms[1:]:
        total = total + term.astype(F32)
    return total.astype(BF)


class Collect:
    def __init__(self, keep, send, size, d_own):
        self.size = size
        self.parts = parts_of(d_own)
        got = exchange(send, 0, size)
        self.terms = list(zip(jnp.split(keep, self.parts), jnp.split(got, self.parts)))
        self.turn = size.bit_length() - 2

    def sources(self):
        cut = self.terms[0][0].shape[0] // 2
        return [add_all([t[cut:] for t in terms]) for terms in self.terms]

    def hop(self, sources):
        self.turn -= 1
        cut = sources[0].shape[0]
        got = [exchange(v, o[self.turn], self.size) for v, o in zip(sources, orders(self.size, self.parts))]
        self.terms = [[t[:cut] for t in terms] + [g] for terms, g in zip(self.terms, got)]
        return got

    def finish(self):
        while self.turn:
            self.hop(self.sources())
        return jnp.concatenate([add_all(terms) for terms in self.terms])


def z_shift(values, by, n, around=True):
    pairs = [(k, (k + by) % n) for k in range(n) if around or 0 <= k + by < n]
    return lax.ppermute(values, "tensor", pairs)


def z_scatter(values, n):
    turn = lax.axis_index("tensor")
    total = lax.dynamic_index_in_dim(values, turn, 0, keepdims=False).astype(F32)
    for k in range(1, n):
        block = lax.dynamic_index_in_dim(values, (turn + k) % n, 0, keepdims=False)
        total = total + z_shift(block, k, n).astype(F32)
    return total


def line_round(right, left, k, n):
    right = lax.ppermute(right, "tensor", [(s, s + 1) for s in range(k - 1, n - 1)])
    left = lax.ppermute(left, "tensor", [(s, s - 1) for s in range(1, n - k + 1)])
    return right, left


def line_result(own, rounds, n):
    turn = lax.axis_index("tensor")
    rows = own.shape[0]
    out = jnp.zeros((n * rows, own.shape[1]), own.dtype)
    out = lax.dynamic_update_slice_in_dim(out, own, turn * rows, 0)
    for k in range(1, n):
        piece = rounds[k - 1][1] + rounds[n - k - 1][0]
        out = lax.dynamic_update_slice_in_dim(out, piece, (turn + k) % n * rows, 0)
    return out


def small_gather(own, size, n):
    turn, place = lax.axis_index("tensor"), lax.axis_index("dp")
    rows = jnp.stack([own] + [z_shift(own, -k, n) for k in range(1, n)])
    rows = jnp.take(rows, (jnp.arange(n) - turn) % n, axis=0)[None]
    for bit in range(size.bit_length() - 1):
        rows = jnp.concatenate([rows, exchange(rows, bit, size)])
    return jnp.take(rows, jnp.arange(size) ^ place, axis=0).transpose(1, 0, 2)


def small_scatter(values, size, n):
    place = lax.axis_index("dp")
    values = jnp.take(values, jnp.arange(size) ^ place, axis=0)
    for bit in reversed(range(size.bit_length() - 1)):
        half = values.shape[0] // 2
        values = add_all([values[:half], exchange(values[half:], bit, size)])
    return z_scatter(values[0], n)


def basis(size, rows, place):
    parts = parts_of(rows)
    count = size // 2
    masks, which = [], []
    for core in range(2):
        for part, order in enumerate(orders(size, parts)):
            for q in range(count):
                masks.append(core | sum(((q >> t) & 1) << b for t, b in enumerate(order)))
                which.append(part)
    table = (place ^ jnp.asarray(np.array(masks, np.int32))) * parts
    table = table + jnp.asarray(np.array(which, np.int32))
    spots = jnp.arange(len(masks), dtype=jnp.int32)
    inverse = jnp.sum(jnp.where(table[None, :] == spots[:, None], spots[None, :], 0), axis=1)
    return table, inverse.astype(jnp.int32)


def copy_kernel(blocks, table_ref, in_ref, out_ref):
    width = in_ref.shape[1] // blocks
    for p in range(blocks):
        start = pl.multiple_of(table_ref[p] * width, width)
        out_ref[:, p * width : (p + 1) * width] = in_ref[:, pl.ds(start, width)]


def permute_rows(values, table):
    rows, d_model = values.shape
    step = max(k for k in range(16, 289, 16) if rows % k == 0)
    spec = pl.BlockSpec((step, d_model), lambda r, tab: (r, 0))
    return pl.pallas_call(
        functools.partial(copy_kernel, table.shape[0]),
        grid_spec=pltpu.PrefetchScalarGridSpec(
            num_scalar_prefetch=1, grid=(rows // step,), in_specs=[spec], out_specs=spec
        ),
        out_shape=jax.ShapeDtypeStruct(values.shape, values.dtype),
        compiler_params=pltpu.CompilerParams(vmem_limit_bytes=VMEM),
        cost_estimate=LITTLE,
        name="permute",
    )(table, values)


def permute_gain(values, table):
    lead = values.shape[0]
    return jnp.take(values.reshape(lead, table.shape[0], -1), table, axis=1).reshape(lead, -1)


def row_ids(count, width, first):
    return lax.broadcasted_iota(jnp.int32, (count, width), 0) + first


def scan_slab(decay, value, back):
    rows = row_ids(SLAB, decay.shape[1], 0)
    for step in (1, 2, 4):
        keep = rows < SLAB - step if back else rows >= step
        shift = SLAB - step if back else step
        moved_decay = pltpu.roll(decay, shift, 0)
        moved_value = pltpu.roll(value, shift, 0)
        value = jnp.where(keep, value + decay * moved_value, value)
        decay = jnp.where(keep, decay * moved_decay, decay)
    return decay, value


def gelu_parts(v):
    c = np.float32(np.sqrt(2 / np.pi))
    return jnp.tanh(c * (v + 0.044715 * v * v * v))


def head_mask(head, at, width):
    lanes = lax.broadcasted_iota(jnp.int32, (head, 2 * width), 1)
    lanes = jnp.where(lanes >= width, lanes - width, lanes)
    return (lanes >= at * head) & (lanes < (at + 1) * head)


def fill_dense(w_ref, dense_ref):
    head = w_ref.shape[0]
    blocks = w_ref[...].astype(F32)
    for k in range(dense_ref.shape[0] // head):
        block = jnp.where(head_mask(head, k, dense_ref.shape[0]), blocks, 0.0)
        dense_ref[k * head : (k + 1) * head, :] = block.astype(BF)


def forward_kernel(
    live_ref, pre_ref, par_ref, w_ref, conv_ref, decay_ref, ig_ref, dg_ref, state_ref, prod_ref, rec_ref, dense_ref
):
    rows, width = conv_ref.shape
    fill_dense(w_ref, dense_ref)
    live = live_ref[0]
    rec_ref[...] = jnp.where(row_ids(rows + HALO, width, -HALO) < live, pre_ref[...], 0.0)
    par = [par_ref[k : k + 1, :] for k in range(8)]
    for at in range(0, rows, ROWS):
        span = pl.ds(at, ROWS)
        near = rec_ref[pl.ds(at, ROWS + HALO), :]
        conv = par[4] + par[0] * near[HALO : HALO + ROWS]
        for k in range(1, 4):
            conv = conv + par[k] * near[HALO - k : HALO - k + ROWS]
        conv = jnp.where(row_ids(ROWS, width, at) < live, conv, 0.0)
        conv_ref[span, :] = conv
        gates = dot(conv.astype(BF), dense_ref[...])
        ig = lax.logistic(gates[:, :width] + par[5])
        dg = lax.logistic(gates[:, width:] + par[6])
        decay = jnp.exp(dg * par[7])
        ig_ref[span, :] = ig
        dg_ref[span, :] = dg
        decay_ref[span, :] = decay
        state_ref[span, :] = jnp.sqrt(jnp.maximum(1.0 - decay * decay, DECAY_FLOOR)) * ig * conv

    def slab(k, carry):
        state, prod = carry
        for inner in range(4):
            span = pl.ds(pl.multiple_of(k * 4 * SLAB + inner * SLAB, SLAB), SLAB)
            decay, value = scan_slab(decay_ref[span, :], state_ref[span, :], False)
            value = value + decay * state
            decay = decay * prod
            state_ref[span, :] = value
            prod_ref[span, :] = decay
            state = jnp.broadcast_to(value[SLAB - 1 :, :], (SLAB, width))
            prod = jnp.broadcast_to(decay[SLAB - 1 :, :], (SLAB, width))
        return state, prod

    lax.fori_loop(0, rows // (4 * SLAB), slab, (jnp.zeros((SLAB, width), F32), jnp.ones((SLAB, width), F32)))


def back_scan_kernel(live_ref, pre_ref, grad_ref, decay_ref, lam_ref, reach_ref, edge_ref):
    rows, width = grad_ref.shape
    live = live_ref[0]
    for at in range(0, rows, ROWS):
        span = pl.ds(at, ROWS)
        v = pre_ref[span, :]
        act = 0.5 * v * (1.0 + gelu_parts(v))
        lam_ref[span, :] = jnp.where(row_ids(ROWS, width, at) < live, grad_ref[span, :] * act, 0.0)
    last = row_ids(SLAB, width, 0) == SLAB - 1

    def slab(k, carry):
        lam, reach, following, _ = carry
        for inner in range(4):
            span = pl.ds(pl.multiple_of(rows - (k * 4 + inner + 1) * SLAB, SLAB), SLAB)
            own = decay_ref[span, :]
            ahead = jnp.where(last, following, pltpu.roll(own, SLAB - 1, 0))
            decay, value = scan_slab(ahead, lam_ref[span, :], True)
            value = value + decay * lam
            decay = decay * reach
            lam_ref[span, :] = value
            reach_ref[span, :] = decay
            lam = jnp.broadcast_to(value[:1, :], (SLAB, width))
            reach = jnp.broadcast_to(decay[:1, :], (SLAB, width))
            following = jnp.broadcast_to(own[:1, :], (SLAB, width))
        return lam, reach, following, own

    one = jnp.ones((SLAB, width), F32)
    zero = jnp.zeros((SLAB, width), F32)
    lam, _, following, _ = lax.fori_loop(0, rows // (4 * SLAB), slab, (zero, one, one, one))
    edge_ref[...] = lam * following


def backward_kernel(
    live_ref, pre_ref, par_ref, w_ref, lam_ref, reach_ref, edge_ref, decay_ref, conv_ref, ig_ref, dg_ref, state_ref, prod_ref, cin_ref,
    drec_ref, dpar_ref, dw_ref, rec_ref, dconv_ref, full_ref, dw_acc, dense_ref,
):
    rows, width = conv_ref.shape
    live = live_ref[0]
    rec_ref[...] = jnp.where(row_ids(rows + HALO, width, -HALO) < live, pre_ref[...], 0.0)
    par = [par_ref[k : k + 1, :] for k in range(8)]
    fill_dense(w_ref, dense_ref)
    cin = cin_ref[:1, :]
    edge = edge_ref[:1, :]
    full_ref[:SLAB, :] = jnp.broadcast_to(cin, (SLAB, width))
    dconv_ref[:HALO, :] = jnp.zeros((HALO, width), F32)
    dconv_ref[rows + HALO :, :] = jnp.zeros((HALO, width), F32)
    sums = [jnp.zeros((1, width), F32) for _ in range(8)]
    for at in range(0, rows, ROWS):
        span = pl.ds(at, ROWS)
        full_ref[pl.ds(at + SLAB, ROWS), :] = state_ref[span, :] + prod_ref[span, :] * cin
        lam = lam_ref[span, :] + reach_ref[span, :] * edge
        decay, conv, ig, dg = decay_ref[span, :], conv_ref[span, :], ig_ref[span, :], dg_ref[span, :]
        before = full_ref[pl.ds(at, ROWS + SLAB), :][SLAB - 1 : SLAB - 1 + ROWS]
        room = 1.0 - decay * decay
        scale = jnp.sqrt(jnp.maximum(room, DECAY_FLOOR))
        lam_conv = lam * conv
        d_decay = lam * before - jnp.where(room > DECAY_FLOOR, lam_conv * ig * decay / scale, 0.0)
        moved = d_decay * decay
        sums[7] = sums[7] + jnp.sum(moved * dg, axis=0, keepdims=True)
        d_ig = lam_conv * scale * ig * (1.0 - ig)
        d_dg = moved * par[7] * dg * (1.0 - dg)
        sums[5] = sums[5] + jnp.sum(d_ig, axis=0, keepdims=True)
        sums[6] = sums[6] + jnp.sum(d_dg, axis=0, keepdims=True)
        both = jnp.concatenate([d_ig.astype(BF), d_dg.astype(BF)], axis=1)
        d_conv = lam * scale * ig + dot(both, dense_ref[...], ((1,), (1,)))
        d_conv = jnp.where(row_ids(ROWS, width, at) < live, d_conv, 0.0)
        dconv_ref[pl.ds(at + HALO, ROWS), :] = d_conv
        part = dot(conv.astype(BF), both, ((0,), (0,)))
        dw_acc[...] = part if at == 0 else dw_acc[...] + part
        near = rec_ref[pl.ds(at, ROWS + HALO), :]
        for k in range(4):
            sums[k] = sums[k] + jnp.sum(d_conv * near[HALO - k : HALO - k + ROWS], axis=0, keepdims=True)
        sums[4] = sums[4] + jnp.sum(d_conv, axis=0, keepdims=True)
    for k in range(8):
        dpar_ref[k : k + 1, :] = sums[k]
    head = dw_ref.shape[0]
    total = jnp.zeros((head, 2 * width), F32)
    for k in range(width // head):
        total = total + jnp.where(head_mask(head, k, width), dw_acc[k * head : (k + 1) * head, :], 0.0)
    dw_ref[...] = total.astype(BF)
    for at in list(range(0, rows, ROWS)) + [rows]:
        count = ROWS if at < rows else HALO
        near = dconv_ref[pl.ds(at, count + SLAB), :]
        total = par[0] * near[:count]
        for k in range(1, 4):
            total = total + par[k] * near[k : k + count]
        drec_ref[pl.ds(at, count), :] = total


def kernel_call(body, live, arrays, outs, scratch, name):
    width = outs[0][1]
    steps = width // GROUP
    specs = []
    for array in arrays:
        if array.ndim == 3:
            specs.append(pl.BlockSpec((pl.squeezed,) + array.shape[1:], lambda j, s: (j, 0, 0)))
        else:
            specs.append(pl.BlockSpec((array.shape[0], GROUP), lambda j, s: (0, j)))
    out_specs, out_shapes = [], []
    for rows, cols, kind in outs:
        if cols == width:
            out_specs.append(pl.BlockSpec((rows, GROUP), lambda j, s: (0, j)))
            out_shapes.append(jax.ShapeDtypeStruct((rows, cols), kind))
        else:
            out_specs.append(pl.BlockSpec((pl.squeezed, rows, cols), lambda j, s: (j, 0, 0)))
            out_shapes.append(jax.ShapeDtypeStruct((steps, rows, cols), kind))
    return pl.pallas_call(
        body,
        grid_spec=pltpu.PrefetchScalarGridSpec(
            num_scalar_prefetch=1, grid=(steps,), in_specs=specs, out_specs=out_specs,
            scratch_shapes=[pltpu.VMEM(shape, kind) for shape, kind in scratch],
        ),
        out_shape=out_shapes,
        compiler_params=pltpu.CompilerParams(vmem_limit_bytes=VMEM),
        cost_estimate=LITTLE,
        name=name,
    )(live, *arrays)


def norm_rate(values):
    return lax.rsqrt(jnp.mean(values * values, axis=-1, keepdims=True) + NORM_EPS)


def norm_back(grad, unit, rate, gain):
    moved = grad * gain
    return rate * (moved - unit * jnp.mean(moved * unit, axis=-1, keepdims=True))


def gelu_product(gate, up):
    return jax.nn.gelu(gate) * up


def wide_dot(left, halves):
    cut = halves[0].shape[0]
    return dot(left[:, :cut], halves[0]) + dot(left[:, cut:], halves[1])


def wide_back(left, halves):
    return jnp.concatenate([dot(left, h, ((1,), (1,))) for h in halves], axis=1)


def on_device(size, n, tokens, lengths, gains, w_gelu, w_rec, chan, w_lru, w_out, w_mlp_in, w_down, cotangent):
    place = lax.axis_index("dp")
    turn = lax.axis_index("tensor")
    d_model = tokens.shape[1]
    rows = tokens.shape[0] // n
    half = rows // 2
    d_own = w_gelu.shape[0]
    heads_own, part, head = chan.shape[1], chan.shape[2], w_lru.shape[3]
    heads = heads_own * n
    width = heads * head
    groups = width // GROUP
    table, inverse = basis(size, d_own, place)
    live_count = (lengths - turn * rows).astype(jnp.int32)
    live = (lax.iota(jnp.int32, rows)[:, None] < live_count).astype(F32)

    def wide(own):
        own = lax.all_gather(own, "tensor", axis=0)
        return own.transpose(1, 0, 2).reshape(d_own, width)

    z_rec = wide(w_rec.astype(BF))
    own_gu = jnp.concatenate([w_mlp_in[0], w_mlp_in[1]], axis=1).astype(BF)
    own_dn = w_down.T.astype(BF)
    small = [w_lru.transpose(2, 0, 1, 3).reshape(-1), chan.reshape(-1), gains.reshape(-1)]
    small = small_gather(jnp.concatenate(small).astype(BF), size, n)
    z_gelu = wide(*fence([w_gelu.astype(BF)], z_rec))
    z_out = wide(*fence([w_out.T.astype(BF)], z_gelu))
    some_gu, came_gu = spread_begin(own_gu, size)
    some_dn, came_dn = spread_begin(own_dn, size)
    some_r, _ = spread_begin(z_rec, size, *came_gu, *came_dn)

    gain = small[0, :, -gains.size :].reshape(size, 2, d_own).transpose(1, 0, 2).reshape(2, d_model)
    gain = permute_gain(gain, table).astype(F32)
    chans = small[..., w_lru.size : w_lru.size + chan.size].reshape((n, size) + chan.shape)
    chans = chans.transpose(2, 0, 3, 1, 4).reshape(8, width).astype(F32)
    par = jnp.concatenate([chans[:7], -8.0 * jax.nn.softplus(-chans[7:])])
    each = n // groups
    lru = small[..., : w_lru.size].reshape(groups, each, head, 2, heads_own * head)
    lru = lru.transpose(0, 2, 3, 1, 4).reshape(groups, head, 2 * GROUP)

    main = lax.dynamic_slice_in_dim(tokens, turn * rows, rows)
    before = lax.dynamic_slice_in_dim(tokens, jnp.maximum(turn * rows - HALO, 0), HALO)
    before = jnp.where(turn > 0, before, jnp.zeros_like(before))
    extended = permute_rows(jnp.concatenate([before, main]), table).astype(F32)
    first_rate = norm_rate(extended)
    first = (extended * first_rate * gain[0]).astype(BF)
    inputs, first_own, first_rate = extended[HALO:], first[HALO:], first_rate[HALO:]
    cot = permute_rows(cotangent, table).reshape(n, 2, half, d_model)
    cots = [cot[:, h].reshape(n * half, d_model) for h in range(2)]
    cut = d_model // 2

    keep = (rows, width, F32)
    dense = ((GROUP, 2 * GROUP), BF)
    w_r, came_r = spread_end(some_r, size, (), (first, *cots, z_gelu))
    some_g, _ = spread_begin(z_gelu, size, *came_r)
    rec_pre = wide_dot(first, w_r)
    conv, decay, ig, dg, state, prod = kernel_call(
        forward_kernel, live_count, [rec_pre, par, lru], [keep] * 6,
        [((rows + HALO, GROUP), F32), dense], "recurrence",
    )
    ends = jnp.concatenate([prod[-1:], state[-1:]])
    came = [z_shift(ends, k, n, False) for k in range(1, n)]
    carry = jnp.zeros((1, width), F32)
    for end in came[::-1]:
        carry = end[1:] + end[:1] * carry
    w_g, came_g = spread_end(some_g, size, (rec_pre,), (ends,))
    some_o, _ = spread_begin(z_out, size, *came_g, ends)
    branch_pre = wide_dot(first_own, w_g)
    recurrent = (state + prod * carry) * live
    activated, gelu_pull = jax.vjp(jax.nn.gelu, branch_pre)
    mixed = (activated * recurrent).astype(BF)
    w_o, came_o = spread_end(some_o, size, (branch_pre,), (mixed,))
    hidden = inputs + wide_back(mixed, w_o)
    second_rate = norm_rate(hidden)
    second_unit = hidden * second_rate
    second_own = (second_unit * gain[1]).astype(BF)
    w_gu, came_gu = spread_end(some_gu, size, came_o, (second_own,))
    w_dn, _ = spread_end(some_dn, size, came_gu, ())
    w_gu, w_dn = jnp.concatenate(w_gu), jnp.concatenate(w_dn)

    hidden_units = w_dn.shape[1]
    grad_products = [dot(c, w_dn) for c in cots]
    shares, grad_second, seconds, products, grads = [], [], [], [], []
    for h in range(2):
        second = lax.all_gather(second_own[h * half : (h + 1) * half], "tensor", axis=0, tiled=True)
        (second,) = fence([second], *shares)
        both = dot(second, w_gu)
        product, pull = jax.vjp(gelu_product, both[:, :hidden_units], both[:, hidden_units:])
        grad_gate, grad_up = pull(grad_products[h])
        product = product.astype(BF)
        grad = jnp.concatenate([grad_gate.astype(BF), grad_up.astype(BF)], axis=1)
        share = dot(grad, w_gu, ((1,), (1,))).astype(BF)
        shares.append(share)
        grad_second.append(lax.psum_scatter(share, "tensor", scatter_dimension=0, tiled=True))
        seconds.append(second)
        products.append(product)
        grads.append(grad)

    shares = [dot(p, w_dn, ((1,), (1,))).astype(BF) for p in products]

    def by_rows(lefts, rights):
        parts = []
        for span in (slice(cut, None), slice(0, cut)):
            part = dot(lefts[0][:, span], rights[0], ((0,), (0,)))
            parts.append((part + dot(lefts[1][:, span], rights[1], ((0,), (0,)))).astype(BF))
        return Collect(parts[1], parts[0], size, d_own)

    sum_dn = by_rows(cots, products)
    sum_gu = by_rows(seconds, grads)
    sent_dn, sent_gu = sum_dn.sources(), sum_gu.sources()
    grad_second = fence(grad_second, *sent_dn, *sent_gu)
    sum_dn.hop(sent_dn)
    sum_gu.hop(sent_gu)

    def mlp_result(h, mlp_sum):
        return permute_rows((hidden[h * half : (h + 1) * half] + mlp_sum.astype(F32)).astype(BF), inverse)

    (share,) = fence([shares[0]], *grad_second)
    mlp_sum = lax.psum_scatter(share, "tensor", scatter_dimension=0, tiled=True)

    grad_second = jnp.concatenate(grad_second).astype(F32)
    cot_own = lax.dynamic_index_in_dim(cot, turn, 0).reshape(rows, d_model).astype(F32)
    gain_two = jnp.sum(grad_second * second_unit, axis=0)
    grad_hidden = cot_own + norm_back(grad_second, second_unit, second_rate, gain[1])
    hidden_low = grad_hidden.astype(BF)

    def by_cols(left, right):
        parts = [dot(left[:, span], right, ((0,), (0,))).astype(BF) for span in (slice(cut, None), slice(0, cut))]
        return Collect(parts[1], parts[0], size, d_own)

    grad_mixed = wide_dot(hidden_low, w_o)
    lam, reach, edge = kernel_call(
        back_scan_kernel, live_count, [branch_pre, grad_mixed, decay],
        [keep, keep, (SLAB, width, F32)], [], "back_scan",
    )
    edges = jnp.concatenate([prod[-1:], edge[:1]])
    came = [z_shift(edges, -k, n, False) for k in range(1, n)]
    arriving = jnp.zeros((1, width), F32)
    for end in came[::-1]:
        arriving = end[1:] + end[:1] * arriving
    sum_o = by_cols(hidden_low, mixed)
    sent_dn, sent_gu = sum_dn.sources(), sum_gu.sources()
    (lam,) = fence([lam], *sent_dn, *sent_gu)
    sum_dn.hop(sent_dn)
    sum_gu.hop(sent_gu)
    (grad_pre,) = gelu_pull(grad_mixed * recurrent)
    pre_low = grad_pre.astype(BF)
    first_part = wide_back(pre_low, w_g)
    tall = jnp.broadcast_to
    drec, dpar, d_lru = kernel_call(
        backward_kernel, live_count,
        [rec_pre, par, lru, lam, reach, tall(arriving, (SLAB, width)), decay, conv, ig, dg, state, prod, tall(carry, (SLAB, width))],
        [(rows + HALO, width, F32), (8, width, F32), (head, 2 * GROUP, BF)],
        [((rows + HALO, GROUP), F32), ((rows + 2 * HALO, GROUP), F32), ((rows + SLAB, GROUP), F32), ((GROUP, 2 * GROUP), F32), dense],
        "recurrence_back",
    )
    (edge_rows,) = fence([z_shift(drec[:HALO], -1, n, False)], mlp_sum)
    rec_low = (drec[HALO:] + jnp.pad(edge_rows, ((rows - HALO, 0), (0, 0)))) * live
    rec_low = rec_low.astype(BF)
    grad_first = first_part + wide_back(rec_low, w_r)
    first_unit = inputs * first_rate
    gain_one = jnp.sum(grad_first * first_unit, axis=0)
    grad_tokens = grad_hidden + norm_back(grad_first, first_unit, first_rate, gain[0])
    grad_tokens = permute_rows(grad_tokens.astype(BF), inverse)
    result_0 = lax.all_gather(mlp_result(0, mlp_sum), "tensor", axis=0)
    sum_g = by_cols(first_own, pre_low)
    sum_r = by_cols(first_own, rec_low)
    d_lru, dpar = fence([d_lru, dpar], grad_tokens)
    sent = fence(sum_o.sources(), grad_tokens)
    rounds = [line_round(grad_tokens, grad_tokens, 1, n)]
    got_o = sum_o.hop(sent)
    got_g = sum_g.hop(fence(sum_g.sources(), *got_o))
    (share,) = fence([shares[1]], result_0, *rounds[0])
    mlp_sum = lax.psum_scatter(share, "tensor", scatter_dimension=0, tiled=True)
    got_o = sum_o.hop(fence(sum_o.sources(), *rounds[0]))
    rounds.append(line_round(*rounds[0], 2, n))
    got_r = sum_r.hop(fence(sum_r.sources(), *got_o, *got_g))
    (mlp_sum,) = fence([mlp_sum], *rounds[1])
    result_1 = lax.all_gather(mlp_result(1, mlp_sum), "tensor", axis=0)
    got_g = sum_g.hop(fence(sum_g.sources(), *rounds[1]))
    sum_r.hop(fence(sum_r.sources(), *got_r, *got_g))
    for k in range(3, n):
        rounds.append(line_round(*rounds[-1], k, n))
    tokens_out = line_result(grad_tokens, rounds, n)
    output = jnp.zeros((n, 2, half, d_model), BF)
    output = lax.dynamic_update_slice(output, result_0[:, None], (0, 0, 0, 0))
    output = lax.dynamic_update_slice(output, result_1[:, None], (0, 1, 0, 0))
    output = output.reshape(n * rows, d_model)
    g_gu, g_dn = sum_gu.finish().astype(F32), sum_dn.finish().astype(F32)
    owned = jnp.stack([total.finish().reshape(d_own, n, width // n) for total in (sum_o, sum_g, sum_r)])
    owned = lax.psum_scatter(owned.transpose(2, 0, 1, 3), "tensor", scatter_dimension=0).astype(F32)
    g_o, g_g, g_r = owned[0], owned[1], owned[2]

    d_gain = permute_gain(jnp.stack([gain_one, gain_two]), inverse)
    d_chan = jnp.concatenate([dpar[:7], dpar[7:] * 8.0 * jax.nn.sigmoid(-chans[7:])])
    d_lru = d_lru.reshape(groups, size, part, 2, each, -1).transpose(1, 0, 4, 2, 3, 5)
    d_chan = d_chan.reshape(8, n, heads_own, size, part).transpose(3, 1, 0, 2, 4)
    d_gain = d_gain.reshape(2, size, 1, d_own).transpose(1, 2, 0, 3)
    d_gain = jnp.broadcast_to(d_gain, (size, n, 2, d_own))
    small = [v.reshape(size, n, -1).astype(BF) for v in (d_lru, d_chan, d_gain)]
    small = small_scatter(jnp.concatenate(small, axis=2), size, n)
    d_lru = small[: w_lru.size].reshape(part, 2, heads_own, head).transpose(1, 2, 0, 3)
    d_chan = small[w_lru.size : -gains.size].reshape(chan.shape)
    d_gain = small[-gains.size :].reshape(gains.shape)
    g_gate, g_up = g_gu[:, :hidden_units], g_gu[:, hidden_units:]
    return (
        output, tokens_out, d_gain[0], d_gain[1], g_g, g_r, d_chan, d_lru,
        g_o.T, jnp.stack([g_gate, g_up]), g_dn.T,
    )


def solution(mesh):
    in_specs = (
        P("dp", None),
        P("dp"),
        P(None, "dp"),
        P("dp", "tensor"),
        P("dp", "tensor"),
        P(None, "tensor", "dp"),
        P(None, "tensor", "dp", None),
        P("tensor", "dp"),
        P(None, "dp", "tensor"),
        P("tensor", "dp"),
        P("dp", None),
    )
    out_specs = (
        P("dp", None),
        P("dp", None),
        P("dp"),
        P("dp"),
        P("dp", "tensor"),
        P("dp", "tensor"),
        P(None, "tensor", "dp"),
        P(None, "tensor", "dp", None),
        P("tensor", "dp"),
        P(None, "dp", "tensor"),
        P("tensor", "dp"),
    )
    body = functools.partial(on_device, mesh.shape["dp"], mesh.shape["tensor"])
    return jax.shard_map(body, mesh=mesh, in_specs=in_specs, out_specs=out_specs, check_vma=False)
```

```python
import functools

import jax
import jax.numpy as jnp
import numpy as np
from jax import lax
from jax.experimental import pallas as pl
from jax.experimental.pallas import tpu as pltpu
from jax.sharding import PartitionSpec as P

NORM_EPS = 1e-06
DECAY_FLOOR = 0.05
HALO = 16
GROUP = 640
ROWS = 128
SLAB = 8
VMEM = 58 * 1024 * 1024
BF = jnp.bfloat16
F32 = jnp.float32
LITTLE = pl.CostEstimate(flops=1024, bytes_accessed=1024, transcendentals=0)


def dot(left, right, dims=((1,), (0,))):
    return lax.dot_general(left, right, (dims, ((), ())), preferred_element_type=F32)


def fence(values, *others):
    if not others:
        return list(values)
    place = pl.BlockSpec(memory_space=pl.ANY)
    call = pl.pallas_call(
        lambda *refs: None,
        in_specs=[place] * (len(values) + len(others)),
        out_specs=[place] * len(values),
        out_shape=[jax.ShapeDtypeStruct(v.shape, v.dtype) for v in values],
        input_output_aliases={k: k for k in range(len(values))},
        compiler_params=pltpu.CompilerParams(vmem_limit_bytes=VMEM),
        name="fence",
    )
    return list(call(*values, *others))


def exchange(values, bit, size):
    return lax.ppermute(values, "dp", [(k, k ^ (1 << bit)) for k in range(size)])


def squared(size, rows):
    return size == 8 and rows % 256 == 0


def spread_begin(own, size, *before):
    (own,) = fence([own], *before)
    if squared(size, own.shape[0]):
        return [own, exchange(own, 1, size), exchange(own, 2, size)]
    pieces = own
    for bit in range(1, size.bit_length() - 2):
        pieces = jnp.concatenate([pieces, exchange(pieces, bit, size)])
    return [pieces]


def spread_end(some, size, before_last, before_core):
    if len(some) > 1:
        own, by_x, by_y = some
        unit = own.shape[0] // 2
        by_x, by_y = fence([by_x, by_y], *before_last)
        got = [exchange(by_x[:unit], 2, size), exchange(by_y[unit:], 1, size)]
        low, high = fence(got, *before_core)
        half = jnp.concatenate([own, by_x, high, low, by_y])
    else:
        (pieces,) = fence(some, *before_last)
        got = [exchange(pieces, size.bit_length() - 2, size)]
        half = jnp.concatenate([pieces] + fence(got, *before_core))
    return [half, exchange(half, 0, size)], got


def add_all(terms):
    total = terms[0].astype(F32)
    for term in terms[1:]:
        total = total + term.astype(F32)
    return total.astype(BF)


class Collect:
    def __init__(self, keep, send, size, d_own):
        self.size, self.unit = size, d_own // 2
        self.square = squared(size, d_own)
        self.bit = size.bit_length() - 2
        self.terms = [keep, exchange(send, 0, size)]
        self.first = self.last = None

    def rows(self, start, stop):
        return [t[start * self.unit : stop * self.unit] for t in self.terms]

    def sources(self):
        if not self.square:
            cut = self.terms[0].shape[0] // 2
            return [add_all([t[cut:] for t in self.terms])]
        if self.first is None:
            return [add_all(self.rows(3, 5)), add_all(self.rows(5, 7))]
        by_x, by_y = self.first
        return [add_all(self.rows(2, 3) + [by_y[: self.unit]]), add_all(self.rows(7, 8) + [by_x[self.unit :]])]

    def hop(self, sources):
        if not self.square:
            got = exchange(sources[0], self.bit, self.size)
            self.bit -= 1
            self.terms = [t[: got.shape[0]] for t in self.terms] + [got]
            return [got]
        got = [exchange(v, bit, self.size) for v, bit in zip(sources, (1, 2))]
        if self.first is None:
            self.first = got
        else:
            self.last = got
        return got

    def finish(self):
        if not self.square:
            while self.bit:
                self.hop(self.sources())
            return add_all(self.terms)
        low = add_all(self.rows(0, 1) + [self.first[1][self.unit :], self.last[0]])
        high = add_all(self.rows(1, 2) + [self.first[0][: self.unit], self.last[1]])
        return jnp.concatenate([low, high])


def z_shift(values, by, n, around=True):
    pairs = [(k, (k + by) % n) for k in range(n) if around or 0 <= k + by < n]
    return lax.ppermute(values, "tensor", pairs)


def z_scatter(values, n):
    turn = lax.axis_index("tensor")
    total = lax.dynamic_index_in_dim(values, turn, 0, keepdims=False).astype(F32)
    for k in range(1, n):
        block = lax.dynamic_index_in_dim(values, (turn + k) % n, 0, keepdims=False)
        total = total + z_shift(block, k, n).astype(F32)
    return total


def line_round(right, left, k, n):
    right = lax.ppermute(right, "tensor", [(s, s + 1) for s in range(k - 1, n - 1)])
    left = lax.ppermute(left, "tensor", [(s, s - 1) for s in range(1, n - k + 1)])
    return right, left


def line_result(own, rounds, n):
    turn = lax.axis_index("tensor")
    rows = own.shape[0]
    out = jnp.zeros((n * rows, own.shape[1]), own.dtype)
    out = lax.dynamic_update_slice_in_dim(out, own, turn * rows, 0)
    for k in range(1, n):
        piece = rounds[k - 1][1] + rounds[n - k - 1][0]
        out = lax.dynamic_update_slice_in_dim(out, piece, (turn + k) % n * rows, 0)
    return out


def small_gather(own, size, n):
    turn, place = lax.axis_index("tensor"), lax.axis_index("dp")
    rows = jnp.stack([own] + [z_shift(own, -k, n) for k in range(1, n)])
    rows = jnp.take(rows, (jnp.arange(n) - turn) % n, axis=0)[None]
    for bit in range(size.bit_length() - 1):
        rows = jnp.concatenate([rows, exchange(rows, bit, size)])
    return jnp.take(rows, jnp.arange(size) ^ place, axis=0).transpose(1, 0, 2)


def small_scatter(values, size, n):
    place = lax.axis_index("dp")
    values = jnp.take(values, jnp.arange(size) ^ place, axis=0)
    for bit in reversed(range(size.bit_length() - 1)):
        half = values.shape[0] // 2
        values = add_all([values[:half], exchange(values[half:], bit, size)])
    return z_scatter(values[0], n)


def basis(size, rows, place):
    if squared(size, rows):
        parts = 2
        spots = [(core | mask, part) for core in range(2) for mask, part in
                 ((0, 0), (0, 1), (2, 0), (2, 1), (6, 1), (6, 0), (4, 0), (4, 1))]
    else:
        parts = 1
        spots = [(core | q << 1, 0) for core in range(2) for q in range(size // 2)]
    masks, which = (jnp.asarray(np.array(v, np.int32)) for v in zip(*spots))
    table = (place ^ masks) * parts + which
    spots = jnp.arange(table.shape[0], dtype=jnp.int32)
    inverse = jnp.sum(jnp.where(table[None, :] == spots[:, None], spots[None, :], 0), axis=1)
    return table, inverse.astype(jnp.int32)


def copy_kernel(blocks, table_ref, in_ref, out_ref):
    width = in_ref.shape[1] // blocks
    for p in range(blocks):
        start = pl.multiple_of(table_ref[p] * width, width)
        out_ref[:, p * width : (p + 1) * width] = in_ref[:, pl.ds(start, width)]


def permute_rows(values, table):
    rows, d_model = values.shape
    step = max(k for k in range(16, 289, 16) if rows % k == 0)
    spec = pl.BlockSpec((step, d_model), lambda r, tab: (r, 0))
    return pl.pallas_call(
        functools.partial(copy_kernel, table.shape[0]),
        grid_spec=pltpu.PrefetchScalarGridSpec(
            num_scalar_prefetch=1, grid=(rows // step,), in_specs=[spec], out_specs=spec
        ),
        out_shape=jax.ShapeDtypeStruct(values.shape, values.dtype),
        compiler_params=pltpu.CompilerParams(vmem_limit_bytes=VMEM),
        cost_estimate=LITTLE,
        name="permute",
    )(table, values)


def interleave_kernel(one_ref, two_ref, out_ref):
    out_ref[0] = one_ref[...]
    out_ref[1] = two_ref[...]


def interleave(one, two):
    n, rows, d_model = one.shape
    spec = pl.BlockSpec((pl.squeezed, rows, d_model), lambda j: (j, 0, 0))
    return pl.pallas_call(
        interleave_kernel,
        grid=(n,),
        in_specs=[spec, spec],
        out_specs=pl.BlockSpec((pl.squeezed, 2, rows, d_model), lambda j: (j, 0, 0, 0)),
        out_shape=jax.ShapeDtypeStruct((n, 2, rows, d_model), one.dtype),
        compiler_params=pltpu.CompilerParams(vmem_limit_bytes=VMEM),
        cost_estimate=LITTLE,
        name="interleave",
    )(one, two)


def permute_gain(values, table):
    lead = values.shape[0]
    return jnp.take(values.reshape(lead, table.shape[0], -1), table, axis=1).reshape(lead, -1)


def row_ids(count, width, first):
    return lax.broadcasted_iota(jnp.int32, (count, width), 0) + first


def scan_slab(decay, value, back):
    rows = row_ids(SLAB, decay.shape[1], 0)
    for step in (1, 2, 4):
        keep = rows < SLAB - step if back else rows >= step
        shift = SLAB - step if back else step
        moved_decay = pltpu.roll(decay, shift, 0)
        moved_value = pltpu.roll(value, shift, 0)
        value = jnp.where(keep, value + decay * moved_value, value)
        decay = jnp.where(keep, decay * moved_decay, decay)
    return decay, value


def head_mask(head, at, width):
    lanes = lax.broadcasted_iota(jnp.int32, (head, 2 * width), 1)
    lanes = jnp.where(lanes >= width, lanes - width, lanes)
    return (lanes >= at * head) & (lanes < (at + 1) * head)


def fill_dense(w_ref, dense_ref):
    head = w_ref.shape[0]
    blocks = w_ref[...].astype(F32)
    for k in range(dense_ref.shape[0] // head):
        block = jnp.where(head_mask(head, k, dense_ref.shape[0]), blocks, 0.0)
        dense_ref[k * head : (k + 1) * head, :] = block.astype(BF)


def forward_kernel(
    live_ref, pre_ref, par_ref, w_ref, conv_ref, decay_ref, ig_ref, dg_ref, state_ref, prod_ref, rec_ref, dense_ref
):
    rows, width = conv_ref.shape
    fill_dense(w_ref, dense_ref)
    live = live_ref[0]
    rec_ref[...] = jnp.where(row_ids(rows + HALO, width, -HALO) < live, pre_ref[...], 0.0)
    par = [par_ref[k : k + 1, :] for k in range(8)]
    for at in range(0, rows, ROWS):
        span = pl.ds(at, ROWS)
        near = rec_ref[pl.ds(at, ROWS + HALO), :]
        conv = par[4] + par[0] * near[HALO : HALO + ROWS]
        for k in range(1, 4):
            conv = conv + par[k] * near[HALO - k : HALO - k + ROWS]
        conv = jnp.where(row_ids(ROWS, width, at) < live, conv, 0.0)
        conv_ref[span, :] = conv
        gates = dot(conv.astype(BF), dense_ref[...])
        ig = lax.logistic(gates[:, :width] + par[5])
        dg = lax.logistic(gates[:, width:] + par[6])
        decay = jnp.exp(dg * par[7])
        ig_ref[span, :] = ig
        dg_ref[span, :] = dg
        decay_ref[span, :] = decay
        state_ref[span, :] = jnp.sqrt(jnp.maximum(1.0 - decay * decay, DECAY_FLOOR)) * ig * conv

    def slab(k, carry):
        state, prod = carry
        for inner in range(4):
            span = pl.ds(pl.multiple_of(k * 4 * SLAB + inner * SLAB, SLAB), SLAB)
            decay, value = scan_slab(decay_ref[span, :], state_ref[span, :], False)
            value = value + decay * state
            decay = decay * prod
            state_ref[span, :] = value
            prod_ref[span, :] = decay
            state = jnp.broadcast_to(value[SLAB - 1 :, :], (SLAB, width))
            prod = jnp.broadcast_to(decay[SLAB - 1 :, :], (SLAB, width))
        return state, prod

    lax.fori_loop(0, rows // (4 * SLAB), slab, (jnp.zeros((SLAB, width), F32), jnp.ones((SLAB, width), F32)))


def back_scan_kernel(
    live_ref, pre_ref, grad_ref, decay_ref, state_ref, prod_ref, cin_ref, lam_ref, reach_ref, edge_ref, low_ref
):
    rows, width = grad_ref.shape
    live = live_ref[0]
    cin = cin_ref[:1, :]
    c = np.float32(np.sqrt(2 / np.pi))
    for at in range(0, rows, ROWS):
        span = pl.ds(at, ROWS)
        v, grad = pre_ref[span, :], grad_ref[span, :]
        square = v * v
        bend = jnp.tanh(v * (c + (c * 0.044715) * square))
        rise = 0.5 + 0.5 * bend
        slope = rise + 0.5 * v * (1.0 - bend * bend) * (c + (3 * c * 0.044715) * square)
        grad = jnp.where(row_ids(ROWS, width, at) < live, grad, 0.0)
        lam_ref[span, :] = grad * (v * rise)
        low_ref[span, :] = (grad * (state_ref[span, :] + prod_ref[span, :] * cin) * slope).astype(BF)
    last = row_ids(SLAB, width, 0) == SLAB - 1

    def slab(k, carry):
        lam, reach, following, _ = carry
        for inner in range(4):
            span = pl.ds(pl.multiple_of(rows - (k * 4 + inner + 1) * SLAB, SLAB), SLAB)
            own = decay_ref[span, :]
            ahead = jnp.where(last, following, pltpu.roll(own, SLAB - 1, 0))
            decay, value = scan_slab(ahead, lam_ref[span, :], True)
            value = value + decay * lam
            decay = decay * reach
            lam_ref[span, :] = value
            reach_ref[span, :] = decay
            lam = jnp.broadcast_to(value[:1, :], (SLAB, width))
            reach = jnp.broadcast_to(decay[:1, :], (SLAB, width))
            following = jnp.broadcast_to(own[:1, :], (SLAB, width))
        return lam, reach, following, own

    one = jnp.ones((SLAB, width), F32)
    zero = jnp.zeros((SLAB, width), F32)
    lam, _, following, _ = lax.fori_loop(0, rows // (4 * SLAB), slab, (zero, one, one, one))
    edge_ref[...] = lam * following


def backward_kernel(
    live_ref, pre_ref, par_ref, w_ref, lam_ref, reach_ref, edge_ref, decay_ref, conv_ref, ig_ref, dg_ref, state_ref, prod_ref, cin_ref,
    drec_ref, dpar_ref, dw_ref, rec_ref, dconv_ref, full_ref, dw_acc, dense_ref,
):
    rows, width = conv_ref.shape
    live = live_ref[0]
    rec_ref[...] = jnp.where(row_ids(rows + HALO, width, -HALO) < live, pre_ref[...], 0.0)
    par = [par_ref[k : k + 1, :] for k in range(8)]
    fill_dense(w_ref, dense_ref)
    cin = cin_ref[:1, :]
    edge = edge_ref[:1, :]
    full_ref[:SLAB, :] = jnp.broadcast_to(cin, (SLAB, width))
    dconv_ref[:HALO, :] = jnp.zeros((HALO, width), F32)
    dconv_ref[rows + HALO :, :] = jnp.zeros((HALO, width), F32)
    sums = [jnp.zeros((1, width), F32) for _ in range(8)]
    for at in range(0, rows, ROWS):
        span = pl.ds(at, ROWS)
        full_ref[pl.ds(at + SLAB, ROWS), :] = state_ref[span, :] + prod_ref[span, :] * cin
        lam = lam_ref[span, :] + reach_ref[span, :] * edge
        decay, conv, ig, dg = decay_ref[span, :], conv_ref[span, :], ig_ref[span, :], dg_ref[span, :]
        before = full_ref[pl.ds(at, ROWS + SLAB), :][SLAB - 1 : SLAB - 1 + ROWS]
        room = 1.0 - decay * decay
        scale = jnp.sqrt(jnp.maximum(room, DECAY_FLOOR))
        lam_conv = lam * conv
        d_decay = lam * before - jnp.where(room > DECAY_FLOOR, lam_conv * ig * decay / scale, 0.0)
        moved = d_decay * decay
        sums[7] = sums[7] + jnp.sum(moved * dg, axis=0, keepdims=True)
        d_ig = lam_conv * scale * ig * (1.0 - ig)
        d_dg = moved * par[7] * dg * (1.0 - dg)
        sums[5] = sums[5] + jnp.sum(d_ig, axis=0, keepdims=True)
        sums[6] = sums[6] + jnp.sum(d_dg, axis=0, keepdims=True)
        both = jnp.concatenate([d_ig.astype(BF), d_dg.astype(BF)], axis=1)
        d_conv = lam * scale * ig + dot(both, dense_ref[...], ((1,), (1,)))
        d_conv = jnp.where(row_ids(ROWS, width, at) < live, d_conv, 0.0)
        dconv_ref[pl.ds(at + HALO, ROWS), :] = d_conv
        part = dot(conv.astype(BF), both, ((0,), (0,)))
        dw_acc[...] = part if at == 0 else dw_acc[...] + part
        near = rec_ref[pl.ds(at, ROWS + HALO), :]
        for k in range(4):
            sums[k] = sums[k] + jnp.sum(d_conv * near[HALO - k : HALO - k + ROWS], axis=0, keepdims=True)
        sums[4] = sums[4] + jnp.sum(d_conv, axis=0, keepdims=True)
    for k in range(8):
        dpar_ref[k : k + 1, :] = sums[k]
    head = dw_ref.shape[0]
    total = jnp.zeros((head, 2 * width), F32)
    for k in range(width // head):
        total = total + jnp.where(head_mask(head, k, width), dw_acc[k * head : (k + 1) * head, :], 0.0)
    dw_ref[...] = total.astype(BF)
    for at in list(range(0, rows, ROWS)) + [rows]:
        count = ROWS if at < rows else HALO
        near = dconv_ref[pl.ds(at, count + SLAB), :]
        total = par[0] * near[:count]
        for k in range(1, 4):
            total = total + par[k] * near[k : k + count]
        drec_ref[pl.ds(at, count), :] = total


def kernel_call(body, live, arrays, outs, scratch, name):
    width = outs[0][1]
    steps = width // GROUP
    specs = []
    for array in arrays:
        if array.ndim == 3:
            specs.append(pl.BlockSpec((pl.squeezed,) + array.shape[1:], lambda j, s: (j, 0, 0)))
        else:
            specs.append(pl.BlockSpec((array.shape[0], GROUP), lambda j, s: (0, j)))
    out_specs, out_shapes = [], []
    for rows, cols, kind in outs:
        if cols == width:
            out_specs.append(pl.BlockSpec((rows, GROUP), lambda j, s: (0, j)))
            out_shapes.append(jax.ShapeDtypeStruct((rows, cols), kind))
        else:
            out_specs.append(pl.BlockSpec((pl.squeezed, rows, cols), lambda j, s: (j, 0, 0)))
            out_shapes.append(jax.ShapeDtypeStruct((steps, rows, cols), kind))
    return pl.pallas_call(
        body,
        grid_spec=pltpu.PrefetchScalarGridSpec(
            num_scalar_prefetch=1, grid=(steps,), in_specs=specs, out_specs=out_specs,
            scratch_shapes=[pltpu.VMEM(shape, kind) for shape, kind in scratch],
        ),
        out_shape=out_shapes,
        compiler_params=pltpu.CompilerParams(vmem_limit_bytes=VMEM),
        cost_estimate=LITTLE,
        name=name,
    )(live, *arrays)


def norm_rate(values):
    return lax.rsqrt(jnp.mean(values * values, axis=-1, keepdims=True) + NORM_EPS)


def norm_back(grad, unit, rate, gain):
    moved = grad * gain
    return rate * (moved - unit * jnp.mean(moved * unit, axis=-1, keepdims=True))


def gelu_product(gate, up):
    return jax.nn.gelu(gate) * up


def wide_dot(left, halves):
    cut = halves[0].shape[0]
    return dot(left[:, :cut], halves[0]) + dot(left[:, cut:], halves[1])


def wide_back(left, halves):
    return jnp.concatenate([dot(left, h, ((1,), (1,))) for h in halves], axis=1)


def on_device(size, n, tokens, lengths, gains, w_gelu, w_rec, chan, w_lru, w_out, w_mlp_in, w_down, cotangent):
    place = lax.axis_index("dp")
    turn = lax.axis_index("tensor")
    d_model = tokens.shape[1]
    rows = tokens.shape[0] // n
    half = rows // 2
    d_own = w_gelu.shape[0]
    heads_own, part, head = chan.shape[1], chan.shape[2], w_lru.shape[3]
    heads = heads_own * n
    width = heads * head
    groups = width // GROUP
    table, inverse = basis(size, d_own, place)
    live_count = (lengths - turn * rows).astype(jnp.int32)
    live = (lax.iota(jnp.int32, rows)[:, None] < live_count).astype(F32)

    def wide(owns):
        own = lax.all_gather(jnp.stack(owns), "tensor", axis=0)
        return [own[:, k].transpose(1, 0, 2).reshape(d_own, width) for k in range(len(owns))]

    (z_rec,) = wide([w_rec.astype(BF)])
    own_gu = jnp.concatenate([w_mlp_in[0], w_mlp_in[1]], axis=1).astype(BF)
    own_dn = w_down.T.astype(BF)
    some_gu = spread_begin(own_gu, size)
    small = [w_lru.transpose(2, 0, 1, 3).reshape(-1), chan.reshape(-1), gains.reshape(-1)]
    small = small_gather(jnp.concatenate(small).astype(BF), size, n)
    z_gelu, z_out = wide(fence([w_gelu.astype(BF), w_out.T.astype(BF)], z_rec))
    some_r = spread_begin(z_rec, size, *some_gu[1:])

    gain = small[0, :, -gains.size :].reshape(size, 2, d_own).transpose(1, 0, 2).reshape(2, d_model)
    gain = permute_gain(gain, table).astype(F32)
    chans = small[..., w_lru.size : w_lru.size + chan.size].reshape((n, size) + chan.shape)
    chans = chans.transpose(2, 0, 3, 1, 4).reshape(8, width).astype(F32)
    par = jnp.concatenate([chans[:7], -8.0 * jax.nn.softplus(-chans[7:])])
    each = n // groups
    lru = small[..., : w_lru.size].reshape(groups, each, head, 2, heads_own * head)
    lru = lru.transpose(0, 2, 3, 1, 4).reshape(groups, head, 2 * GROUP)

    main = lax.dynamic_slice_in_dim(tokens, turn * rows, rows)
    before = lax.dynamic_slice_in_dim(tokens, jnp.maximum(turn * rows - HALO, 0), HALO)
    before = jnp.where(turn > 0, before, jnp.zeros_like(before))
    extended = permute_rows(jnp.concatenate([before, main]), table).astype(F32)
    first_rate = norm_rate(extended)
    first = (extended * first_rate * gain[0]).astype(BF)
    inputs, first_own, first_rate = extended[HALO:], first[HALO:], first_rate[HALO:]
    cot = permute_rows(cotangent, *fence([table], *some_r[1:])).reshape(n, 2, half, d_model)
    cots = [cot[:, h].reshape(n * half, d_model) for h in range(2)]
    cut = d_model // 2

    keep = (rows, width, F32)
    dense = ((GROUP, 2 * GROUP), BF)
    w_r, came_r = spread_end(some_r, size, (), (first, *cots, lru, par, z_gelu))
    some_g = spread_begin(z_gelu, size, *came_r)
    rec_pre = wide_dot(first, w_r)
    conv, decay, ig, dg, state, prod = kernel_call(
        forward_kernel, live_count, [rec_pre, par, lru], [keep] * 6,
        [((rows + HALO, GROUP), F32), dense], "recurrence",
    )
    ends = jnp.concatenate([prod[-1:], state[-1:]])
    came = [z_shift(ends, k, n, False) for k in range(1, n)]
    carry = jnp.zeros((1, width), F32)
    for end in came[::-1]:
        carry = end[1:] + end[:1] * carry
    w_g, came_g = spread_end(some_g, size, (rec_pre,), (ends,))
    some_o = spread_begin(z_out, size, *came_g, ends)
    branch_pre = wide_dot(first_own, w_g)
    recurrent = (state + prod * carry) * live
    mixed = (jax.nn.gelu(branch_pre) * recurrent).astype(BF)
    w_o, came_o = spread_end(some_o, size, (branch_pre,), (mixed,))
    hidden = inputs + wide_back(mixed, w_o)
    second_rate = norm_rate(hidden)
    second_unit = hidden * second_rate
    second_own = (second_unit * gain[1]).astype(BF)
    w_gu, came_gu = spread_end(some_gu, size, came_o, (second_own,))
    some_dn = spread_begin(own_dn, size, *came_gu)
    w_dn, _ = spread_end(some_dn, size, (), ())
    w_gu, w_dn = jnp.concatenate(w_gu), jnp.concatenate(w_dn)

    hidden_units = w_dn.shape[1]
    grad_products = [dot(c, w_dn) for c in cots]
    shares, grad_second, seconds, products, grads = [], [], [], [], []
    for h in range(2):
        second = lax.all_gather(second_own[h * half : (h + 1) * half], "tensor", axis=0, tiled=True)
        (second,) = fence([second], *shares)
        both = dot(second, w_gu)
        product, pull = jax.vjp(gelu_product, both[:, :hidden_units], both[:, hidden_units:])
        grad_gate, grad_up = pull(grad_products[h])
        product = product.astype(BF)
        grad = jnp.concatenate([grad_gate.astype(BF), grad_up.astype(BF)], axis=1)
        share = dot(grad, w_gu, ((1,), (1,))).astype(BF)
        shares.append(share)
        grad_second.append(lax.psum_scatter(share, "tensor", scatter_dimension=0, tiled=True))
        seconds.append(second)
        products.append(product)
        grads.append(grad)

    products, grads = [[*pair] for pair in zip(*[fence([p, g], shares[-1]) for p, g in zip(products, grads)])]
    shares = [dot(p, w_dn, ((1,), (1,))).astype(BF) for p in products]

    def by_rows(lefts, rights):
        parts = []
        for span in (slice(cut, None), slice(0, cut)):
            part = dot(lefts[0][:, span], rights[0], ((0,), (0,)))
            parts.append((part + dot(lefts[1][:, span], rights[1], ((0,), (0,)))).astype(BF))
        return Collect(parts[1], parts[0], size, d_own)

    sum_dn = by_rows(cots, products)
    sum_gu = by_rows(seconds, grads)
    sent_dn, sent_gu = sum_dn.sources(), sum_gu.sources()
    grad_second = fence(grad_second, *sent_dn, *sent_gu, *shares)
    came_mlp = sum_dn.hop(sent_dn) + sum_gu.hop(sent_gu)

    def mlp_result(h, mlp_sum):
        return permute_rows((hidden[h * half : (h + 1) * half] + mlp_sum.astype(F32)).astype(BF), inverse)

    shares = fence(shares, *grad_second)
    mlp_sums = [lax.psum_scatter(share, "tensor", scatter_dimension=0, tiled=True) for share in shares]

    grad_second = jnp.concatenate(grad_second).astype(F32)
    cot_own = lax.dynamic_index_in_dim(cot, turn, 0).reshape(rows, d_model).astype(F32)
    gain_two = jnp.sum(grad_second * second_unit, axis=0)
    grad_hidden = cot_own + norm_back(grad_second, second_unit, second_rate, gain[1])
    hidden_low = grad_hidden.astype(BF)

    def by_cols(left, right):
        parts = [dot(left[:, span], right, ((0,), (0,))).astype(BF) for span in (slice(cut, None), slice(0, cut))]
        return Collect(parts[1], parts[0], size, d_own)

    grad_mixed = wide_dot(hidden_low, w_o)
    tall = jnp.broadcast_to
    lam, reach, edge, pre_low = kernel_call(
        back_scan_kernel, live_count, [branch_pre, grad_mixed, decay, state, prod, tall(carry, (SLAB, width))],
        [keep, keep, (SLAB, width, F32), (rows, width, BF)], [], "back_scan",
    )
    edges = jnp.concatenate([prod[-1:], edge[:1]])
    came = [z_shift(edges, -k, n, False) for k in range(1, n)]
    arriving = jnp.zeros((1, width), F32)
    for end in came[::-1]:
        arriving = end[1:] + end[:1] * arriving
    (lam,) = fence([lam], *came_mlp)
    drec, dpar, d_lru = kernel_call(
        backward_kernel, live_count,
        [rec_pre, par, lru, lam, reach, tall(arriving, (SLAB, width)), decay, conv, ig, dg, state, prod, tall(carry, (SLAB, width))],
        [(rows + HALO, width, F32), (8, width, F32), (head, 2 * GROUP, BF)],
        [((rows + HALO, GROUP), F32), ((rows + 2 * HALO, GROUP), F32), ((rows + SLAB, GROUP), F32), ((GROUP, 2 * GROUP), F32), dense],
        "recurrence_back",
    )
    (edge_rows,) = fence([z_shift(drec[:HALO], -1, n, False)], mlp_sums[0])
    rec_low = (drec[HALO:] + jnp.pad(edge_rows, ((rows - HALO, 0), (0, 0)))) * live
    rec_low = rec_low.astype(BF)
    (pre_low,) = fence([pre_low], drec)
    grad_first = wide_back(pre_low, w_g) + wide_back(rec_low, w_r)
    first_unit = inputs * first_rate
    gain_one = jnp.sum(grad_first * first_unit, axis=0)
    grad_tokens = grad_hidden + norm_back(grad_first, first_unit, first_rate, gain[0])
    grad_tokens = permute_rows(grad_tokens.astype(BF), inverse)
    rounds = [line_round(grad_tokens, grad_tokens, 1, n)]
    (mixed,) = fence([mixed], grad_tokens)
    sum_o = by_cols(hidden_low, mixed)
    pre_low, rec_low = fence([pre_low, rec_low], sum_o.terms[1])
    sum_g, sum_r = by_cols(first_own, pre_low), by_cols(first_own, rec_low)
    results = [mlp_result(h, mlp_sum) for h, mlp_sum in enumerate(fence(mlp_sums, sum_o.terms[1]))]
    got_o = sum_o.hop(fence(sum_o.sources(), *results))
    result_0, result_1 = (lax.all_gather(result, "tensor", axis=0) for result in results)
    rounds.append(line_round(*fence(rounds[0], *got_o), 2, n))
    sum_o.hop(fence(sum_o.sources(), *rounds[0]))
    got_g = sum_g.hop(fence(sum_g.sources(), *rounds[0]))
    for k in range(3, n):
        rounds.append(line_round(*fence(rounds[-1], result_0, *got_g), k, n))
    sum_g.hop(fence(sum_g.sources(), *rounds[1]))
    got_r = sum_r.hop(fence(sum_r.sources(), *rounds[1], *got_g))
    d_lru, dpar = fence([d_lru, dpar], *rounds[1])
    sum_r.hop(sum_r.sources())
    if sum_dn.square:
        sum_dn.hop(fence(sum_dn.sources(), *rounds[-1]))
        sum_gu.hop(fence(sum_gu.sources(), *rounds[-1]))
    tokens_out = line_result(grad_tokens, rounds, n)
    output = interleave(*fence([result_0, result_1], *rounds[-1])).reshape(n * rows, d_model)
    g_gu, g_dn = sum_gu.finish().astype(F32), sum_dn.finish().astype(F32)
    owned = jnp.stack([total.finish().reshape(d_own, n, width // n) for total in (sum_o, sum_g, sum_r)])
    (owned,) = fence([owned.transpose(2, 0, 1, 3)], result_1)
    owned = lax.psum_scatter(owned, "tensor", scatter_dimension=0).astype(F32)
    g_o, g_g, g_r = owned[0], owned[1], owned[2]

    d_gain = permute_gain(jnp.stack([gain_one, gain_two]), inverse)
    d_chan = jnp.concatenate([dpar[:7], dpar[7:] * 8.0 * jax.nn.sigmoid(-chans[7:])])
    d_lru = d_lru.reshape(groups, size, part, 2, each, -1).transpose(1, 0, 4, 2, 3, 5)
    d_chan = d_chan.reshape(8, n, heads_own, size, part).transpose(3, 1, 0, 2, 4)
    d_gain = d_gain.reshape(2, size, 1, d_own).transpose(1, 2, 0, 3)
    d_gain = jnp.broadcast_to(d_gain, (size, n, 2, d_own))
    small = [v.reshape(size, n, -1).astype(BF) for v in (d_lru, d_chan, d_gain)]
    small = small_scatter(jnp.concatenate(small, axis=2), size, n)
    d_lru = small[: w_lru.size].reshape(part, 2, heads_own, head).transpose(1, 2, 0, 3)
    d_chan = small[w_lru.size : -gains.size].reshape(chan.shape)
    d_gain = small[-gains.size :].reshape(gains.shape)
    g_gate, g_up = g_gu[:, :hidden_units], g_gu[:, hidden_units:]
    return (
        output, tokens_out, d_gain[0], d_gain[1], g_g, g_r, d_chan, d_lru,
        g_o.T, jnp.stack([g_gate, g_up]), g_dn.T,
    )


def solution(mesh):
    in_specs = (
        P("dp", None),
        P("dp"),
        P(None, "dp"),
        P("dp", "tensor"),
        P("dp", "tensor"),
        P(None, "tensor", "dp"),
        P(None, "tensor", "dp", None),
        P("tensor", "dp"),
        P(None, "dp", "tensor"),
        P("tensor", "dp"),
        P("dp", None),
    )
    out_specs = (
        P("dp", None),
        P("dp", None),
        P("dp"),
        P("dp"),
        P("dp", "tensor"),
        P("dp", "tensor"),
        P(None, "tensor", "dp"),
        P(None, "tensor", "dp", None),
        P("tensor", "dp"),
        P(None, "dp", "tensor"),
        P("tensor", "dp"),
    )
    body = functools.partial(on_device, mesh.shape["dp"], mesh.shape["tensor"])
    return jax.shard_map(body, mesh=mesh, in_specs=in_specs, out_specs=out_specs, check_vma=False)
```

```python
import functools

import jax
import jax.numpy as jnp
import numpy as np
from jax import lax
from jax.experimental import pallas as pl
from jax.experimental.pallas import tpu as pltpu
from jax.sharding import PartitionSpec as P

NORM_EPS = 1e-06
DECAY_FLOOR = 0.05
HALO = 16
GROUP = 640
ROWS = 128
SLAB = 8
VMEM = 58 * 1024 * 1024
BF = jnp.bfloat16
F32 = jnp.float32
LITTLE = pl.CostEstimate(flops=1024, bytes_accessed=1024, transcendentals=0)


def dot(left, right, dims=((1,), (0,))):
    return lax.dot_general(left, right, (dims, ((), ())), preferred_element_type=F32)


def fence(values, *others):
    if not others:
        return list(values)
    place = pl.BlockSpec(memory_space=pl.ANY)
    call = pl.pallas_call(
        lambda *refs: None,
        in_specs=[place] * (len(values) + len(others)),
        out_specs=[place] * len(values),
        out_shape=[jax.ShapeDtypeStruct(v.shape, v.dtype) for v in values],
        input_output_aliases={k: k for k in range(len(values))},
        compiler_params=pltpu.CompilerParams(vmem_limit_bytes=VMEM),
        name="fence",
    )
    return list(call(*values, *others))


def assemble(pieces, *others):
    count = len(pieces)
    rows = [p.shape[0] for p in pieces]
    spans = [pl.ds(sum(rows[:k]), rows[k]) for k in range(count)]
    shape = (sum(rows), pieces[0].shape[1])

    def body(*refs):
        out, held, coming, going = refs[count + len(others) :]
        ins = [pltpu.make_async_copy(refs[k], held.at[spans[k]], coming.at[k]) for k in range(count)]
        outs = [pltpu.make_async_copy(held.at[spans[k]], out.at[spans[k]], going.at[k]) for k in range(count)]
        for copy in ins:
            copy.start()
        for here, there in zip(ins, outs):
            here.wait()
            there.start()
        for copy in outs:
            copy.wait()

    place = pl.BlockSpec(memory_space=pl.ANY)
    return pl.pallas_call(
        body,
        in_specs=[place] * (count + len(others)),
        out_specs=place,
        out_shape=jax.ShapeDtypeStruct(shape, pieces[0].dtype),
        scratch_shapes=[
            pltpu.VMEM(shape, pieces[0].dtype),
            pltpu.SemaphoreType.DMA((count,)),
            pltpu.SemaphoreType.DMA((count,)),
        ],
        compiler_params=pltpu.CompilerParams(vmem_limit_bytes=VMEM),
        cost_estimate=LITTLE,
        name="assemble",
    )(*pieces, *others)


def exchange(values, bit, size):
    return lax.ppermute(values, "dp", [(k, k ^ (1 << bit)) for k in range(size)])


def squared(size, rows):
    return size == 8 and rows % 256 == 0


def spread_begin(own, size, *before):
    (own,) = fence([own], *before)
    if squared(size, own.shape[0]):
        return [own, exchange(own, 1, size), exchange(own, 2, size)]
    pieces = own
    for bit in range(1, size.bit_length() - 2):
        pieces = jnp.concatenate([pieces, exchange(pieces, bit, size)])
    return [pieces]


def spread_end(some, size, before_last, before_core):
    if len(some) > 1:
        own, by_x, by_y = some
        unit = own.shape[0] // 2
        by_x, by_y = fence([by_x, by_y], *before_last)
        got = [exchange(by_x[:unit], 2, size), exchange(by_y[unit:], 1, size)]
        half = assemble([own, by_x, got[1], got[0], by_y], *before_core)
    else:
        (pieces,) = fence(some, *before_last)
        got = [exchange(pieces, size.bit_length() - 2, size)]
        half = jnp.concatenate([pieces] + fence(got, *before_core))
    return [half, exchange(half, 0, size)], got


def add_all(terms):
    total = terms[0].astype(F32)
    for term in terms[1:]:
        total = total + term.astype(F32)
    return total.astype(BF)


class Collect:
    def __init__(self, keep, send, size, d_own):
        self.size, self.unit = size, d_own // 2
        self.square = squared(size, d_own)
        self.bit = size.bit_length() - 2
        self.terms = [keep, exchange(send, 0, size)]
        self.first = self.last = None

    def rows(self, start, stop):
        return [t[start * self.unit : stop * self.unit] for t in self.terms]

    def sources(self):
        if not self.square:
            cut = self.terms[0].shape[0] // 2
            return [add_all([t[cut:] for t in self.terms])]
        if self.first is None:
            return [add_all(self.rows(3, 5)), add_all(self.rows(5, 7))]
        by_x, by_y = self.first
        return [add_all(self.rows(2, 3) + [by_y[: self.unit]]), add_all(self.rows(7, 8) + [by_x[self.unit :]])]

    def hop(self, sources):
        if not self.square:
            got = exchange(sources[0], self.bit, self.size)
            self.bit -= 1
            self.terms = [t[: got.shape[0]] for t in self.terms] + [got]
            return [got]
        got = [exchange(v, bit, self.size) for v, bit in zip(sources, (1, 2))]
        if self.first is None:
            self.first = got
        else:
            self.last = got
        return got

    def finish(self):
        if not self.square:
            while self.bit:
                self.hop(self.sources())
            return add_all(self.terms)
        low = add_all(self.rows(0, 1) + [self.first[1][self.unit :], self.last[0]])
        high = add_all(self.rows(1, 2) + [self.first[0][: self.unit], self.last[1]])
        return jnp.concatenate([low, high])


def z_shift(values, by, n, around=True):
    pairs = [(k, (k + by) % n) for k in range(n) if around or 0 <= k + by < n]
    return lax.ppermute(values, "tensor", pairs)


def z_scatter(values, n):
    turn = lax.axis_index("tensor")
    total = lax.dynamic_index_in_dim(values, turn, 0, keepdims=False).astype(F32)
    for k in range(1, n):
        block = lax.dynamic_index_in_dim(values, (turn + k) % n, 0, keepdims=False)
        total = total + z_shift(block, k, n).astype(F32)
    return total


def small_plain(halves, size, n):
    mask = jnp.arange(size) ^ lax.axis_index("dp")
    rows = jnp.concatenate(halves).reshape(size, n, -1)
    return jnp.take(rows, (mask & 1) * (size // 2) + (mask >> 1), axis=0, mode="clip").transpose(1, 0, 2)


def z_gather(own, n):
    turn = lax.axis_index("tensor")
    blocks = jnp.stack([own] + [z_shift(own, -k, n) for k in range(1, n)])
    blocks = jnp.take(blocks, (jnp.arange(n) - turn) % n, axis=0, mode="clip")
    return blocks.transpose(1, 0, 2).reshape(own.shape[0], -1)


def small_scatter(values, size, n):
    place = lax.axis_index("dp")
    values = jnp.take(values, jnp.arange(size) ^ place, axis=0, mode="clip")
    for bit in reversed(range(size.bit_length() - 1)):
        half = values.shape[0] // 2
        values = add_all([values[:half], exchange(values[half:], bit, size)])
    return z_scatter(values[0], n)


def basis(size, rows, place):
    if squared(size, rows):
        parts = 2
        spots = [(core | mask, part) for core in range(2) for mask, part in
                 ((0, 0), (0, 1), (2, 0), (2, 1), (6, 1), (6, 0), (4, 0), (4, 1))]
    else:
        parts = 1
        spots = [(core | q << 1, 0) for core in range(2) for q in range(size // 2)]
    masks, which = (jnp.asarray(np.array(v, np.int32)) for v in zip(*spots))
    table = (place ^ masks) * parts + which
    spots = jnp.arange(table.shape[0], dtype=jnp.int32)
    inverse = jnp.sum(jnp.where(table[None, :] == spots[:, None], spots[None, :], 0), axis=1)
    return table, inverse.astype(jnp.int32)


def copy_kernel(blocks, table_ref, in_ref, out_ref):
    width = in_ref.shape[1] // blocks
    for p in range(blocks):
        start = pl.multiple_of(table_ref[p] * width, width)
        out_ref[:, p * width : (p + 1) * width] = in_ref[:, pl.ds(start, width)]


def permute_rows(values, table, step=0, stride=1, offset=0):
    rows, d_model = values.shape
    step = step or max(k for k in range(16, 289, 16) if rows % k == 0)
    return pl.pallas_call(
        functools.partial(copy_kernel, table.shape[0]),
        grid_spec=pltpu.PrefetchScalarGridSpec(
            num_scalar_prefetch=1,
            grid=(rows // (step * stride),),
            in_specs=[pl.BlockSpec((step, d_model), lambda r, tab: (r * stride + offset, 0))],
            out_specs=pl.BlockSpec((step, d_model), lambda r, tab: (r, 0)),
        ),
        out_shape=jax.ShapeDtypeStruct((rows // stride, d_model), values.dtype),
        compiler_params=pltpu.CompilerParams(vmem_limit_bytes=VMEM),
        cost_estimate=LITTLE,
        name="permute",
    )(table, values)


def interleave_kernel(one_ref, two_ref, out_ref):
    out_ref[0] = one_ref[...]
    out_ref[1] = two_ref[...]


def interleave(one, two):
    n, rows, d_model = one.shape
    spec = pl.BlockSpec((pl.squeezed, rows, d_model), lambda j: (j, 0, 0))
    return pl.pallas_call(
        interleave_kernel,
        grid=(n,),
        in_specs=[spec, spec],
        out_specs=pl.BlockSpec((pl.squeezed, 2, rows, d_model), lambda j: (j, 0, 0, 0)),
        out_shape=jax.ShapeDtypeStruct((n, 2, rows, d_model), one.dtype),
        compiler_params=pltpu.CompilerParams(vmem_limit_bytes=VMEM),
        cost_estimate=LITTLE,
        name="interleave",
    )(one, two)


def permute_gain(values, table):
    lead = values.shape[0]
    return jnp.take(values.reshape(lead, table.shape[0], -1), table, axis=1, mode="clip").reshape(lead, -1)


def row_ids(count, width, first):
    return lax.broadcasted_iota(jnp.int32, (count, width), 0) + first


def scan_slab(decay, value, back):
    rows = row_ids(SLAB, decay.shape[1], 0)
    for step in (1, 2, 4):
        keep = rows < SLAB - step if back else rows >= step
        shift = SLAB - step if back else step
        moved_decay = pltpu.roll(decay, shift, 0)
        moved_value = pltpu.roll(value, shift, 0)
        value = jnp.where(keep, value + decay * moved_value, value)
        decay = jnp.where(keep, decay * moved_decay, decay)
    return decay, value


def head_mask(head, at, width):
    lanes = lax.broadcasted_iota(jnp.int32, (head, 2 * width), 1)
    lanes = jnp.where(lanes >= width, lanes - width, lanes)
    return (lanes >= at * head) & (lanes < (at + 1) * head)


def fill_dense(w_ref, dense_ref):
    head = w_ref.shape[0]
    blocks = w_ref[...].astype(F32)
    for k in range(dense_ref.shape[0] // head):
        block = jnp.where(head_mask(head, k, dense_ref.shape[0]), blocks, 0.0)
        dense_ref[k * head : (k + 1) * head, :] = block.astype(BF)


def forward_kernel(
    live_ref, pre_ref, par_ref, w_ref, conv_ref, decay_ref, ig_ref, dg_ref, state_ref, prod_ref, rec_ref, dense_ref
):
    rows, width = conv_ref.shape
    fill_dense(w_ref, dense_ref)
    live = live_ref[0]
    rec_ref[...] = jnp.where(row_ids(rows + HALO, width, -HALO) < live, pre_ref[...], 0.0)
    par = [par_ref[k : k + 1, :] for k in range(8)]
    for at in range(0, rows, ROWS):
        span = pl.ds(at, ROWS)
        near = rec_ref[pl.ds(at, ROWS + HALO), :]
        conv = par[4] + par[0] * near[HALO : HALO + ROWS]
        for k in range(1, 4):
            conv = conv + par[k] * near[HALO - k : HALO - k + ROWS]
        conv = jnp.where(row_ids(ROWS, width, at) < live, conv, 0.0)
        conv_ref[span, :] = conv
        gates = dot(conv.astype(BF), dense_ref[...])
        ig = lax.logistic(gates[:, :width] + par[5])
        dg = lax.logistic(gates[:, width:] + par[6])
        decay = jnp.exp(dg * par[7])
        ig_ref[span, :] = ig
        dg_ref[span, :] = dg
        decay_ref[span, :] = decay
        state_ref[span, :] = jnp.sqrt(jnp.maximum(1.0 - decay * decay, DECAY_FLOOR)) * ig * conv

    def slab(k, carry):
        state, prod = carry
        for inner in range(4):
            span = pl.ds(pl.multiple_of(k * 4 * SLAB + inner * SLAB, SLAB), SLAB)
            decay, value = scan_slab(decay_ref[span, :], state_ref[span, :], False)
            value = value + decay * state
            decay = decay * prod
            state_ref[span, :] = value
            prod_ref[span, :] = decay
            state = jnp.broadcast_to(value[SLAB - 1 :, :], (SLAB, width))
            prod = jnp.broadcast_to(decay[SLAB - 1 :, :], (SLAB, width))
        return state, prod

    lax.fori_loop(0, rows // (4 * SLAB), slab, (jnp.zeros((SLAB, width), F32), jnp.ones((SLAB, width), F32)))


def back_scan_kernel(
    live_ref, pre_ref, grad_ref, decay_ref, state_ref, prod_ref, cin_ref, lam_ref, reach_ref, edge_ref, low_ref
):
    rows, width = grad_ref.shape
    live = live_ref[0]
    cin = cin_ref[:1, :]
    c = np.float32(np.sqrt(2 / np.pi))
    for at in range(0, rows, ROWS):
        span = pl.ds(at, ROWS)
        v, grad = pre_ref[span, :], grad_ref[span, :]
        square = v * v
        bend = jnp.tanh(v * (c + (c * 0.044715) * square))
        rise = 0.5 + 0.5 * bend
        slope = rise + 0.5 * v * (1.0 - bend * bend) * (c + (3 * c * 0.044715) * square)
        grad = jnp.where(row_ids(ROWS, width, at) < live, grad, 0.0)
        lam_ref[span, :] = grad * (v * rise)
        low_ref[span, :] = (grad * (state_ref[span, :] + prod_ref[span, :] * cin) * slope).astype(BF)
    last = row_ids(SLAB, width, 0) == SLAB - 1

    def slab(k, carry):
        lam, reach, following, _ = carry
        for inner in range(4):
            span = pl.ds(pl.multiple_of(rows - (k * 4 + inner + 1) * SLAB, SLAB), SLAB)
            own = decay_ref[span, :]
            ahead = jnp.where(last, following, pltpu.roll(own, SLAB - 1, 0))
            decay, value = scan_slab(ahead, lam_ref[span, :], True)
            value = value + decay * lam
            decay = decay * reach
            lam_ref[span, :] = value
            reach_ref[span, :] = decay
            lam = jnp.broadcast_to(value[:1, :], (SLAB, width))
            reach = jnp.broadcast_to(decay[:1, :], (SLAB, width))
            following = jnp.broadcast_to(own[:1, :], (SLAB, width))
        return lam, reach, following, own

    one = jnp.ones((SLAB, width), F32)
    zero = jnp.zeros((SLAB, width), F32)
    lam, _, following, _ = lax.fori_loop(0, rows // (4 * SLAB), slab, (zero, one, one, one))
    edge_ref[...] = lam * following


def backward_kernel(
    live_ref, pre_ref, par_ref, w_ref, lam_ref, reach_ref, edge_ref, decay_ref, conv_ref, ig_ref, dg_ref, state_ref, prod_ref, cin_ref,
    drec_ref, dpar_ref, dw_ref, rec_ref, dconv_ref, full_ref, dw_acc, dense_ref,
):
    rows, width = conv_ref.shape
    live = live_ref[0]
    rec_ref[...] = jnp.where(row_ids(rows + HALO, width, -HALO) < live, pre_ref[...], 0.0)
    par = [par_ref[k : k + 1, :] for k in range(8)]
    fill_dense(w_ref, dense_ref)
    cin = cin_ref[:1, :]
    edge = edge_ref[:1, :]
    full_ref[:SLAB, :] = jnp.broadcast_to(cin, (SLAB, width))
    dconv_ref[:HALO, :] = jnp.zeros((HALO, width), F32)
    dconv_ref[rows + HALO :, :] = jnp.zeros((HALO, width), F32)
    sums = [jnp.zeros((1, width), F32) for _ in range(8)]
    for at in range(0, rows, ROWS):
        span = pl.ds(at, ROWS)
        full_ref[pl.ds(at + SLAB, ROWS), :] = state_ref[span, :] + prod_ref[span, :] * cin
        lam = lam_ref[span, :] + reach_ref[span, :] * edge
        decay, conv, ig, dg = decay_ref[span, :], conv_ref[span, :], ig_ref[span, :], dg_ref[span, :]
        before = full_ref[pl.ds(at, ROWS + SLAB), :][SLAB - 1 : SLAB - 1 + ROWS]
        room = 1.0 - decay * decay
        scale = jnp.sqrt(jnp.maximum(room, DECAY_FLOOR))
        lam_conv = lam * conv
        d_decay = lam * before - jnp.where(room > DECAY_FLOOR, lam_conv * ig * decay / scale, 0.0)
        moved = d_decay * decay
        sums[7] = sums[7] + jnp.sum(moved * dg, axis=0, keepdims=True)
        d_ig = lam_conv * scale * ig * (1.0 - ig)
        d_dg = moved * par[7] * dg * (1.0 - dg)
        sums[5] = sums[5] + jnp.sum(d_ig, axis=0, keepdims=True)
        sums[6] = sums[6] + jnp.sum(d_dg, axis=0, keepdims=True)
        both = jnp.concatenate([d_ig.astype(BF), d_dg.astype(BF)], axis=1)
        d_conv = lam * scale * ig + dot(both, dense_ref[...], ((1,), (1,)))
        d_conv = jnp.where(row_ids(ROWS, width, at) < live, d_conv, 0.0)
        dconv_ref[pl.ds(at + HALO, ROWS), :] = d_conv
        part = dot(conv.astype(BF), both, ((0,), (0,)))
        dw_acc[...] = part if at == 0 else dw_acc[...] + part
        near = rec_ref[pl.ds(at, ROWS + HALO), :]
        for k in range(4):
            sums[k] = sums[k] + jnp.sum(d_conv * near[HALO - k : HALO - k + ROWS], axis=0, keepdims=True)
        sums[4] = sums[4] + jnp.sum(d_conv, axis=0, keepdims=True)
    for k in range(8):
        dpar_ref[k : k + 1, :] = sums[k]
    head = dw_ref.shape[0]
    total = jnp.zeros((head, 2 * width), F32)
    for k in range(width // head):
        total = total + jnp.where(head_mask(head, k, width), dw_acc[k * head : (k + 1) * head, :], 0.0)
    dw_ref[...] = total.astype(BF)
    for at in list(range(0, rows, ROWS)) + [rows]:
        count = ROWS if at < rows else HALO
        near = dconv_ref[pl.ds(at, count + SLAB), :]
        total = par[0] * near[:count]
        for k in range(1, 4):
            total = total + par[k] * near[k : k + count]
        drec_ref[pl.ds(at, count), :] = total


def kernel_call(body, live, arrays, outs, scratch, name):
    width = outs[0][1]
    steps = width // GROUP
    specs = []
    for array in arrays:
        if array.ndim == 3:
            specs.append(pl.BlockSpec((pl.squeezed,) + array.shape[1:], lambda j, s: (j, 0, 0)))
        else:
            specs.append(pl.BlockSpec((array.shape[0], GROUP), lambda j, s: (0, j)))
    out_specs, out_shapes = [], []
    for rows, cols, kind in outs:
        if cols == width:
            out_specs.append(pl.BlockSpec((rows, GROUP), lambda j, s: (0, j)))
            out_shapes.append(jax.ShapeDtypeStruct((rows, cols), kind))
        else:
            out_specs.append(pl.BlockSpec((pl.squeezed, rows, cols), lambda j, s: (j, 0, 0)))
            out_shapes.append(jax.ShapeDtypeStruct((steps, rows, cols), kind))
    return pl.pallas_call(
        body,
        grid_spec=pltpu.PrefetchScalarGridSpec(
            num_scalar_prefetch=1, grid=(steps,), in_specs=specs, out_specs=out_specs,
            scratch_shapes=[pltpu.VMEM(shape, kind) for shape, kind in scratch],
        ),
        out_shape=out_shapes,
        compiler_params=pltpu.CompilerParams(vmem_limit_bytes=VMEM),
        cost_estimate=LITTLE,
        name=name,
    )(live, *arrays)


def norm_rate(values):
    return lax.rsqrt(jnp.mean(values * values, axis=-1, keepdims=True) + NORM_EPS)


def norm_back(grad, unit, rate, gain):
    moved = grad * gain
    return rate * (moved - unit * jnp.mean(moved * unit, axis=-1, keepdims=True))


def gelu_product(gate, up):
    return jax.nn.gelu(gate) * up


def wide_dot(left, halves):
    cut = halves[0].shape[0]
    return dot(left[:, :cut], halves[0]) + dot(left[:, cut:], halves[1])


def wide_back(left, halves):
    return jnp.concatenate([dot(left, h, ((1,), (1,))) for h in halves], axis=1)


def on_device(size, n, tokens, lengths, gains, w_gelu, w_rec, chan, w_lru, w_out, w_mlp_in, w_down, cotangent):
    place = lax.axis_index("dp")
    turn = lax.axis_index("tensor")
    d_model = tokens.shape[1]
    rows = tokens.shape[0] // n
    half = rows // 2
    d_own = w_gelu.shape[0]
    heads_own, part, head = chan.shape[1], chan.shape[2], w_lru.shape[3]
    heads = heads_own * n
    width = heads * head
    groups = width // GROUP
    table, inverse = basis(size, d_own, place)
    live_count = (lengths - turn * rows).astype(jnp.int32)
    live = (lax.iota(jnp.int32, rows)[:, None] < live_count).astype(F32)

    small = [w_lru.transpose(2, 0, 1, 3).reshape(-1), chan.reshape(-1), gains.reshape(-1)]
    small = jnp.concatenate(small).astype(BF)
    count, cols = small.shape[0], w_gelu.shape[1]
    small = jnp.pad(small, (0, -count % (16 * cols))).reshape(-1, cols)
    whole = jnp.concatenate([w_rec.astype(BF), w_gelu.astype(BF), small])
    own_dn = w_down.T.astype(BF)
    own_gu = jnp.concatenate([w_mlp_in[0], w_mlp_in[1]], axis=1).astype(BF)
    some_dn = spread_begin(own_dn, size)
    whole = lax.all_gather(whole, "tensor", axis=0)
    z_rec, z_gelu = (
        whole[:, k * d_own : (k + 1) * d_own].transpose(1, 0, 2).reshape(d_own, width) for k in range(2)
    )
    some_r = spread_begin(z_rec, size, *some_dn[1:])
    some_small = spread_begin(whole[:, 2 * d_own :].reshape(n, -1), size)
    z_out = z_gather(*fence([w_out.T.astype(BF)], z_rec), n)
    w_r, came_r = spread_end(some_r, size, (), ())
    small, _ = spread_end(some_small, size, (), ())
    small = small_plain(fence(small, *came_r), size, n)[..., :count]

    gain = small[0, :, -gains.size :].reshape(size, 2, d_own).transpose(1, 0, 2).reshape(2, d_model)
    gain = permute_gain(gain, table).astype(F32)
    chans = small[..., w_lru.size : w_lru.size + chan.size].reshape((n, size) + chan.shape)
    chans = chans.transpose(2, 0, 3, 1, 4).reshape(8, width).astype(F32)
    par = jnp.concatenate([chans[:7], -8.0 * jax.nn.softplus(-chans[7:])])
    each = n // groups
    lru = small[..., : w_lru.size].reshape(groups, each, head, 2, heads_own * head)
    lru = lru.transpose(0, 2, 3, 1, 4).reshape(groups, head, 2 * GROUP)

    main = lax.dynamic_slice_in_dim(tokens, turn * rows, rows)
    before = lax.dynamic_slice_in_dim(tokens, jnp.maximum(turn * rows - HALO, 0), HALO)
    before = jnp.where(turn > 0, before, jnp.zeros_like(before))
    extended = permute_rows(jnp.concatenate([before, main]), table).astype(F32)
    first_rate = norm_rate(extended)
    first = (extended * first_rate * gain[0]).astype(BF)
    inputs, first_own, first_rate = extended[HALO:], first[HALO:], first_rate[HALO:]
    cut = d_model // 2

    keep = (rows, width, F32)
    dense = ((GROUP, 2 * GROUP), BF)
    some_g = spread_begin(z_gelu, size, *came_r)
    rec_pre = wide_dot(first, w_r)
    conv, decay, ig, dg, state, prod = kernel_call(
        forward_kernel, live_count, [rec_pre, par, lru], [keep] * 6,
        [((rows + HALO, GROUP), F32), dense], "recurrence",
    )
    ends = jnp.concatenate([prod[-1:], state[-1:]])
    came = [z_shift(ends, k, n, False) for k in range(1, n)]
    carry = jnp.zeros((1, width), F32)
    for end in came[::-1]:
        carry = end[1:] + end[:1] * carry
    w_g, came_g = spread_end(some_g, size, (rec_pre, z_out), (ends,))
    some_o = spread_begin(z_out, size, *came_g, ends)
    branch_pre = wide_dot(first_own, w_g)
    recurrent = (state + prod * carry) * live
    mixed = (jax.nn.gelu(branch_pre) * recurrent).astype(BF)
    w_o, came_o = spread_end(some_o, size, (branch_pre,), (mixed,))
    hidden = inputs + wide_back(mixed, w_o)
    second_rate = norm_rate(hidden)
    second_unit = hidden * second_rate
    second_own = (second_unit * gain[1]).astype(BF)
    some_gu = spread_begin(own_gu, size, *came_o)
    w_gu, came_gu = spread_end(some_gu, size, (), (second_own,))
    w_dn, _ = spread_end(some_dn, size, came_gu, ())
    w_gu, w_dn = assemble(w_gu), assemble(w_dn)
    late = fence([table], second_own)[0]
    cots = [permute_rows(cotangent, late, half, 2, h) for h in range(2)]

    hidden_units = w_dn.shape[1]
    grad_products = [dot(c, w_dn) for c in cots]
    shares, grad_second, seconds, products, grads = [], [], [], [], []
    for h in range(2):
        second = lax.all_gather(second_own[h * half : (h + 1) * half], "tensor", axis=0, tiled=True)
        (second,) = fence([second], *shares)
        both = dot(second, w_gu)
        product, pull = jax.vjp(gelu_product, both[:, :hidden_units], both[:, hidden_units:])
        grad_gate, grad_up = pull(grad_products[h])
        product = product.astype(BF)
        grad = jnp.concatenate([grad_gate.astype(BF), grad_up.astype(BF)], axis=1)
        share = dot(grad, w_gu, ((1,), (1,))).astype(BF)
        shares.append(share)
        grad_second.append(lax.psum_scatter(share, "tensor", scatter_dimension=0, tiled=True))
        seconds.append(second)
        products.append(product)
        grads.append(grad)

    products, grads = [[*pair] for pair in zip(*[fence([p, g], shares[-1]) for p, g in zip(products, grads)])]
    shares = [dot(p, w_dn, ((1,), (1,))).astype(BF) for p in products]

    def by_rows(lefts, rights):
        parts = []
        for span in (slice(cut, None), slice(0, cut)):
            part = dot(lefts[0][:, span], rights[0], ((0,), (0,)))
            parts.append((part + dot(lefts[1][:, span], rights[1], ((0,), (0,)))).astype(BF))
        return Collect(parts[1], parts[0], size, d_own)

    sum_dn = by_rows(cots, products)
    sum_gu = by_rows(seconds, grads)
    sent_dn, sent_gu = sum_dn.sources(), sum_gu.sources()
    grad_second = fence(grad_second, *sent_dn, *sent_gu, *shares)
    came_mlp = sum_dn.hop(sent_dn) + sum_gu.hop(sent_gu)

    def mlp_result(h, mlp_sum):
        return permute_rows((hidden[h * half : (h + 1) * half] + mlp_sum.astype(F32)).astype(BF), inverse)

    shares = fence(shares, *grad_second)
    mlp_sums = [lax.psum_scatter(share, "tensor", scatter_dimension=0, tiled=True) for share in shares]

    grad_second = jnp.concatenate(grad_second).astype(F32)
    cot_own = jnp.concatenate([lax.dynamic_slice_in_dim(c, turn * half, half) for c in cots]).astype(F32)
    gain_two = jnp.sum(grad_second * second_unit, axis=0)
    grad_hidden = cot_own + norm_back(grad_second, second_unit, second_rate, gain[1])
    hidden_low = grad_hidden.astype(BF)

    def by_cols(left, right):
        parts = [dot(left[:, span], right, ((0,), (0,))).astype(BF) for span in (slice(cut, None), slice(0, cut))]
        return Collect(parts[1], parts[0], size, d_own)

    grad_mixed = wide_dot(hidden_low, w_o)
    tall = jnp.broadcast_to
    lam, reach, edge, pre_low = kernel_call(
        back_scan_kernel, live_count, [branch_pre, grad_mixed, decay, state, prod, tall(carry, (SLAB, width))],
        [keep, keep, (SLAB, width, F32), (rows, width, BF)], [], "back_scan",
    )
    edges = jnp.concatenate([prod[-1:], edge[:1]])
    came = [z_shift(edges, -k, n, False) for k in range(1, n)]
    arriving = jnp.zeros((1, width), F32)
    for end in came[::-1]:
        arriving = end[1:] + end[:1] * arriving
    (lam,) = fence([lam], *came_mlp)
    drec, dpar, d_lru = kernel_call(
        backward_kernel, live_count,
        [rec_pre, par, lru, lam, reach, tall(arriving, (SLAB, width)), decay, conv, ig, dg, state, prod, tall(carry, (SLAB, width))],
        [(rows + HALO, width, F32), (8, width, F32), (head, 2 * GROUP, BF)],
        [((rows + HALO, GROUP), F32), ((rows + 2 * HALO, GROUP), F32), ((rows + SLAB, GROUP), F32), ((GROUP, 2 * GROUP), F32), dense],
        "recurrence_back",
    )
    (edge_rows,) = fence([z_shift(drec[:HALO], -1, n, False)], mlp_sums[0])
    rec_low = (drec[HALO:] + jnp.pad(edge_rows, ((rows - HALO, 0), (0, 0)))) * live
    rec_low = rec_low.astype(BF)
    (pre_low,) = fence([pre_low], drec)
    grad_first = wide_back(pre_low, w_g) + wide_back(rec_low, w_r)
    first_unit = inputs * first_rate
    gain_one = jnp.sum(grad_first * first_unit, axis=0)
    grad_tokens = grad_hidden + norm_back(grad_first, first_unit, first_rate, gain[0])
    grad_tokens = permute_rows(grad_tokens.astype(BF), inverse)
    gathered = [lax.all_gather(grad_tokens[h * half : (h + 1) * half], "tensor", axis=0) for h in range(2)]
    (mixed,) = fence([mixed], grad_tokens)
    sum_o = by_cols(hidden_low, mixed)
    pre_low, rec_low = fence([pre_low, rec_low], sum_o.terms[1])
    sum_g, sum_r = by_cols(first_own, pre_low), by_cols(first_own, rec_low)
    results = [mlp_result(h, mlp_sum) for h, mlp_sum in enumerate(fence(mlp_sums, sum_o.terms[1]))]
    got_o = sum_o.hop(sum_o.sources())
    sum_o.hop(fence(sum_o.sources(), gathered[0]))
    got_g = sum_g.hop(fence(sum_g.sources(), gathered[0]))
    results = fence(results, gathered[0])
    results = [lax.all_gather(result, "tensor", axis=0) for result in results]
    sum_g.hop(fence(sum_g.sources(), gathered[1]))
    got_r = sum_r.hop(fence(sum_r.sources(), gathered[1], *got_g))
    d_lru, dpar = fence([d_lru, dpar], gathered[1])
    sum_r.hop(fence(sum_r.sources(), results[0]))
    if sum_dn.square:
        sum_dn.hop(fence(sum_dn.sources(), results[0]))
        sum_gu.hop(fence(sum_gu.sources(), results[0]))
    tokens_out = interleave(*fence(gathered, results[0])).reshape(n * rows, d_model)
    g_gu, g_dn = sum_gu.finish().astype(F32), sum_dn.finish().astype(F32)
    owned = jnp.stack([total.finish().reshape(d_own, n, width // n) for total in (sum_o, sum_g, sum_r)])
    (owned,) = fence([owned.transpose(2, 0, 1, 3)], results[1])
    output = interleave(*results).reshape(n * rows, d_model)
    owned = lax.psum_scatter(owned, "tensor", scatter_dimension=0).astype(F32)
    g_o, g_g, g_r = owned[0], owned[1], owned[2]

    d_gain = permute_gain(jnp.stack([gain_one, gain_two]), inverse)
    d_chan = jnp.concatenate([dpar[:7], dpar[7:] * 8.0 * jax.nn.sigmoid(-chans[7:])])
    d_lru = d_lru.reshape(groups, size, part, 2, each, -1).transpose(1, 0, 4, 2, 3, 5)
    d_chan = d_chan.reshape(8, n, heads_own, size, part).transpose(3, 1, 0, 2, 4)
    d_gain = d_gain.reshape(2, size, 1, d_own).transpose(1, 2, 0, 3)
    d_gain = jnp.broadcast_to(d_gain, (size, n, 2, d_own))
    small = [v.reshape(size, n, -1).astype(BF) for v in (d_lru, d_chan, d_gain)]
    small = small_scatter(jnp.concatenate(small, axis=2), size, n)
    d_lru = small[: w_lru.size].reshape(part, 2, heads_own, head).transpose(1, 2, 0, 3)
    d_chan = small[w_lru.size : -gains.size].reshape(chan.shape)
    d_gain = small[-gains.size :].reshape(gains.shape)
    g_gate, g_up = g_gu[:, :hidden_units], g_gu[:, hidden_units:]
    return (
        output, tokens_out, d_gain[0], d_gain[1], g_g, g_r, d_chan, d_lru,
        g_o.T, jnp.stack([g_gate, g_up]), g_dn.T,
    )


def solution(mesh):
    in_specs = (
        P("dp", None),
        P("dp"),
        P(None, "dp"),
        P("dp", "tensor"),
        P("dp", "tensor"),
        P(None, "tensor", "dp"),
        P(None, "tensor", "dp", None),
        P("tensor", "dp"),
        P(None, "dp", "tensor"),
        P("tensor", "dp"),
        P("dp", None),
    )
    out_specs = (
        P("dp", None),
        P("dp", None),
        P("dp"),
        P("dp"),
        P("dp", "tensor"),
        P("dp", "tensor"),
        P(None, "tensor", "dp"),
        P(None, "tensor", "dp", None),
        P("tensor", "dp"),
        P(None, "dp", "tensor"),
        P("tensor", "dp"),
    )
    body = functools.partial(on_device, mesh.shape["dp"], mesh.shape["tensor"])
    return jax.shard_map(body, mesh=mesh, in_specs=in_specs, out_specs=out_specs, check_vma=False)
```

```python
import functools

import jax
import jax.numpy as jnp
import numpy as np
from jax import lax
from jax.experimental import pallas as pl
from jax.experimental.pallas import tpu as pltpu
from jax.sharding import PartitionSpec as P

NORM_EPS = 1e-06
DECAY_FLOOR = 0.05
HALO = 16
GROUP = 640
ROWS = 128
SLAB = 8
VMEM = 58 * 1024 * 1024
BF = jnp.bfloat16
F32 = jnp.float32
LITTLE = pl.CostEstimate(flops=1024, bytes_accessed=1024, transcendentals=0)


def dot(left, right, dims=((1,), (0,))):
    return lax.dot_general(left, right, (dims, ((), ())), preferred_element_type=F32)


def fence(values, *others):
    if not others:
        return list(values)
    place = pl.BlockSpec(memory_space=pl.ANY)
    call = pl.pallas_call(
        lambda *refs: None,
        in_specs=[place] * (len(values) + len(others)),
        out_specs=[place] * len(values),
        out_shape=[jax.ShapeDtypeStruct(v.shape, v.dtype) for v in values],
        input_output_aliases={k: k for k in range(len(values))},
        compiler_params=pltpu.CompilerParams(vmem_limit_bytes=VMEM),
        name="fence",
    )
    return list(call(*values, *others))


def assemble(pieces, *others):
    count = len(pieces)
    rows = [p.shape[0] for p in pieces]
    spans = [pl.ds(sum(rows[:k]), rows[k]) for k in range(count)]
    shape = (sum(rows), pieces[0].shape[1])

    def body(*refs):
        out, held, coming, going = refs[count + len(others) :]
        ins = [pltpu.make_async_copy(refs[k], held.at[spans[k]], coming.at[k]) for k in range(count)]
        outs = [pltpu.make_async_copy(held.at[spans[k]], out.at[spans[k]], going.at[k]) for k in range(count)]
        for copy in ins:
            copy.start()
        for here, there in zip(ins, outs):
            here.wait()
            there.start()
        for copy in outs:
            copy.wait()

    place = pl.BlockSpec(memory_space=pl.ANY)
    return pl.pallas_call(
        body,
        in_specs=[place] * (count + len(others)),
        out_specs=place,
        out_shape=jax.ShapeDtypeStruct(shape, pieces[0].dtype),
        scratch_shapes=[
            pltpu.VMEM(shape, pieces[0].dtype),
            pltpu.SemaphoreType.DMA((count,)),
            pltpu.SemaphoreType.DMA((count,)),
        ],
        compiler_params=pltpu.CompilerParams(vmem_limit_bytes=VMEM),
        cost_estimate=LITTLE,
        name="assemble",
    )(*pieces, *others)


def exchange(values, bit, size):
    return lax.ppermute(values, "dp", [(k, k ^ (1 << bit)) for k in range(size)])


def squared(size, rows):
    return size == 8 and rows % 256 == 0


def spread_begin(own, size, *before):
    (own,) = fence([own], *before)
    if squared(size, own.shape[0]):
        return [own, exchange(own, 1, size), exchange(own, 2, size)]
    pieces = own
    for bit in range(1, size.bit_length() - 2):
        pieces = jnp.concatenate([pieces, exchange(pieces, bit, size)])
    return [pieces]


def spread_end(some, size, before_last, before_core):
    if len(some) > 1:
        own, by_x, by_y = some
        unit = own.shape[0] // 2
        by_x, by_y = fence([by_x, by_y], *before_last)
        got = [exchange(by_x[:unit], 2, size), exchange(by_y[unit:], 1, size)]
        half = assemble([own, by_x, got[1], got[0], by_y], *before_core)
    else:
        (pieces,) = fence(some, *before_last)
        got = [exchange(pieces, size.bit_length() - 2, size)]
        half = jnp.concatenate([pieces] + fence(got, *before_core))
    return [half, exchange(half, 0, size)], got


def add_all(terms):
    total = terms[0].astype(F32)
    for term in terms[1:]:
        total = total + term.astype(F32)
    return total.astype(BF)


class Collect:
    def __init__(self, keep, send, size, d_own):
        self.size, self.unit = size, d_own // 2
        self.square = squared(size, d_own)
        self.bit = size.bit_length() - 2
        self.terms = [keep, exchange(send, 0, size)]
        self.first = self.last = None

    def rows(self, start, stop):
        return [t[start * self.unit : stop * self.unit] for t in self.terms]

    def sources(self):
        if not self.square:
            cut = self.terms[0].shape[0] // 2
            return [add_all([t[cut:] for t in self.terms])]
        if self.first is None:
            return [add_all(self.rows(3, 5)), add_all(self.rows(5, 7))]
        by_x, by_y = self.first
        return [add_all(self.rows(2, 3) + [by_y[: self.unit]]), add_all(self.rows(7, 8) + [by_x[self.unit :]])]

    def hop(self, sources):
        if not self.square:
            got = exchange(sources[0], self.bit, self.size)
            self.bit -= 1
            self.terms = [t[: got.shape[0]] for t in self.terms] + [got]
            return [got]
        got = [exchange(v, bit, self.size) for v, bit in zip(sources, (1, 2))]
        if self.first is None:
            self.first = got
        else:
            self.last = got
        return got

    def finish(self):
        if not self.square:
            while self.bit:
                self.hop(self.sources())
            return add_all(self.terms)
        low = add_all(self.rows(0, 1) + [self.first[1][self.unit :], self.last[0]])
        high = add_all(self.rows(1, 2) + [self.first[0][: self.unit], self.last[1]])
        return jnp.concatenate([low, high])


def z_shift(values, by, n, around=True):
    pairs = [(k, (k + by) % n) for k in range(n) if around or 0 <= k + by < n]
    return lax.ppermute(values, "tensor", pairs)


def z_scatter(values, n):
    turn = lax.axis_index("tensor")
    total = lax.dynamic_index_in_dim(values, turn, 0, keepdims=False).astype(F32)
    for k in range(1, n):
        block = lax.dynamic_index_in_dim(values, (turn + k) % n, 0, keepdims=False)
        total = total + z_shift(block, k, n).astype(F32)
    return total


class Line:
    def __init__(self, own, n):
        self.own, self.n, self.rounds = own, n, []

    def go(self, *others):
        k = len(self.rounds) + 1
        if k >= self.n:
            return ()
        right, left = fence(self.rounds[-1], *others) if self.rounds else (self.own, self.own)
        right = lax.ppermute(right, "tensor", [(s, s + 1) for s in range(k - 1, self.n - 1)])
        left = lax.ppermute(left, "tensor", [(s, s - 1) for s in range(1, self.n - k + 1)])
        self.rounds.append((right, left))
        return self.rounds[-1]

    def place(self, out, at):
        turn = lax.axis_index("tensor")
        out = lax.dynamic_update_slice(out, self.own[None, None], (turn, at, 0, 0))
        while len(self.rounds) < self.n - 1:
            self.go()
        for k in range(1, self.n):
            piece = self.rounds[k - 1][1] + self.rounds[self.n - k - 1][0]
            out = lax.dynamic_update_slice(out, piece[None, None], ((turn + k) % self.n, at, 0, 0))
        return out


def small_begin(own, size):
    if size == 8:
        return [own, exchange(own, 1, size), exchange(own, 2, size)]
    rows = own[None]
    for bit in range(1, size.bit_length() - 1):
        rows = jnp.concatenate([rows, exchange(rows, bit, size)])
    return [rows]


def small_end(some, size):
    if size == 8:
        own, by_x, by_y = some
        cut = own.shape[0] // 2
        far = jnp.concatenate([exchange(by_x[:cut], 2, size), exchange(by_y[cut:], 1, size)])
        rows = jnp.stack([own, by_x, by_y, far])
    else:
        (rows,) = some
    return jnp.concatenate([rows, exchange(rows, 0, size)])


def z_gather(own, n, *others):
    turn = lax.axis_index("tensor")
    blocks = jnp.stack([own] + fence([z_shift(own, -k, n) for k in range(1, n)], *others))
    blocks = jnp.take(blocks, (jnp.arange(n) - turn) % n, axis=0, mode="clip")
    return blocks.transpose(1, 0, 2).reshape(own.shape[0], -1)


def small_scatter(values, size, n):
    place = lax.axis_index("dp")
    values = jnp.take(values, jnp.arange(size) ^ place, axis=0, mode="clip")
    for bit in reversed(range(size.bit_length() - 1)):
        half = values.shape[0] // 2
        values = add_all([values[:half], exchange(values[half:], bit, size)])
    return z_scatter(values[0], n)


def basis_spots(size, rows):
    if squared(size, rows):
        turns = ((0, 0), (0, 1), (2, 0), (2, 1), (6, 1), (6, 0), (4, 0), (4, 1))
        return [(core | mask, part) for core in range(2) for mask, part in turns], 2
    return [(core | q << 1, 0) for core in range(2) for q in range(size // 2)], 1


def basis(size, rows, place):
    spots, parts = basis_spots(size, rows)
    masks, which = (jnp.asarray(np.array(v, np.int32)) for v in zip(*spots))
    table = (place ^ masks) * parts + which
    spots = jnp.arange(table.shape[0], dtype=jnp.int32)
    inverse = jnp.sum(jnp.where(table[None, :] == spots[:, None], spots[None, :], 0), axis=1)
    return table, inverse.astype(jnp.int32)


def copy_kernel(blocks, table_ref, in_ref, out_ref):
    width = in_ref.shape[1] // blocks
    for p in range(blocks):
        start = pl.multiple_of(table_ref[p] * width, width)
        out_ref[:, p * width : (p + 1) * width] = in_ref[:, pl.ds(start, width)]


def permute_rows(values, table, step=0, stride=1, offset=0):
    rows, d_model = values.shape
    step = step or max(k for k in range(16, 289, 16) if rows % k == 0)
    return pl.pallas_call(
        functools.partial(copy_kernel, table.shape[0]),
        grid_spec=pltpu.PrefetchScalarGridSpec(
            num_scalar_prefetch=1,
            grid=(rows // (step * stride),),
            in_specs=[pl.BlockSpec((step, d_model), lambda r, tab: (r * stride + offset, 0))],
            out_specs=pl.BlockSpec((step, d_model), lambda r, tab: (r, 0)),
        ),
        out_shape=jax.ShapeDtypeStruct((rows // stride, d_model), values.dtype),
        compiler_params=pltpu.CompilerParams(vmem_limit_bytes=VMEM),
        cost_estimate=LITTLE,
        name="permute",
    )(table, values)


def interleave_kernel(one_ref, two_ref, out_ref):
    out_ref[0] = one_ref[...]
    out_ref[1] = two_ref[...]


def interleave(one, two):
    n, rows, d_model = one.shape
    spec = pl.BlockSpec((pl.squeezed, rows, d_model), lambda j: (j, 0, 0))
    return pl.pallas_call(
        interleave_kernel,
        grid=(n,),
        in_specs=[spec, spec],
        out_specs=pl.BlockSpec((pl.squeezed, 2, rows, d_model), lambda j: (j, 0, 0, 0)),
        out_shape=jax.ShapeDtypeStruct((n, 2, rows, d_model), one.dtype),
        compiler_params=pltpu.CompilerParams(vmem_limit_bytes=VMEM),
        cost_estimate=LITTLE,
        name="interleave",
    )(one, two)


def permute_gain(values, table):
    lead = values.shape[0]
    return jnp.take(values.reshape(lead, table.shape[0], -1), table, axis=1, mode="clip").reshape(lead, -1)


def row_ids(count, width, first):
    return lax.broadcasted_iota(jnp.int32, (count, width), 0) + first


def scan_slab(decay, value, back):
    rows = row_ids(SLAB, decay.shape[1], 0)
    for step in (1, 2, 4):
        keep = rows < SLAB - step if back else rows >= step
        shift = SLAB - step if back else step
        moved_decay = pltpu.roll(decay, shift, 0)
        moved_value = pltpu.roll(value, shift, 0)
        value = jnp.where(keep, value + decay * moved_value, value)
        decay = jnp.where(keep, decay * moved_decay, decay)
    return decay, value


def head_mask(head, at, width):
    lanes = lax.broadcasted_iota(jnp.int32, (head, 2 * width), 1)
    lanes = jnp.where(lanes >= width, lanes - width, lanes)
    return (lanes >= at * head) & (lanes < (at + 1) * head)


def fill_dense(w_ref, order_ref, dense_ref):
    head, count = order_ref.shape
    pad = count // w_ref.shape[0]
    width = dense_ref.shape[0]
    for gate in range(2):
        rows = w_ref[:, gate * pad : (gate + 1) * pad, :].reshape(count, width)
        rows = dot(order_ref[...], rows)
        for k in range(width // head):
            lanes = lax.broadcasted_iota(jnp.int32, (head, width), 1)
            block = jnp.where((lanes >= k * head) & (lanes < (k + 1) * head), rows, 0.0)
            dense_ref[k * head : (k + 1) * head, gate * width : (gate + 1) * width] = block.astype(BF)


def forward_kernel(
    live_ref, pre_ref, par_ref, w_ref, order_ref, conv_ref, decay_ref, ig_ref, dg_ref, state_ref, prod_ref,
    rec_ref, dense_ref,
):
    rows, width = conv_ref.shape
    fill_dense(w_ref, order_ref, dense_ref)
    live = live_ref[0]
    rec_ref[...] = jnp.where(row_ids(rows + HALO, width, -HALO) < live, pre_ref[...], 0.0)
    par = [par_ref[k : k + 1, :] for k in range(8)]
    for at in range(0, rows, ROWS):
        span = pl.ds(at, ROWS)
        near = rec_ref[pl.ds(at, ROWS + HALO), :]
        conv = par[4] + par[0] * near[HALO : HALO + ROWS]
        for k in range(1, 4):
            conv = conv + par[k] * near[HALO - k : HALO - k + ROWS]
        conv = jnp.where(row_ids(ROWS, width, at) < live, conv, 0.0)
        conv_ref[span, :] = conv
        gates = dot(conv.astype(BF), dense_ref[...])
        ig = lax.logistic(gates[:, :width] + par[5])
        dg = lax.logistic(gates[:, width:] + par[6])
        decay = jnp.exp(dg * par[7])
        ig_ref[span, :] = ig
        dg_ref[span, :] = dg
        decay_ref[span, :] = decay
        state_ref[span, :] = jnp.sqrt(jnp.maximum(1.0 - decay * decay, DECAY_FLOOR)) * ig * conv

    def slab(k, carry):
        state, prod = carry
        for inner in range(4):
            span = pl.ds(pl.multiple_of(k * 4 * SLAB + inner * SLAB, SLAB), SLAB)
            decay, value = scan_slab(decay_ref[span, :], state_ref[span, :], False)
            value = value + decay * state
            decay = decay * prod
            state_ref[span, :] = value
            prod_ref[span, :] = decay
            state = jnp.broadcast_to(value[SLAB - 1 :, :], (SLAB, width))
            prod = jnp.broadcast_to(decay[SLAB - 1 :, :], (SLAB, width))
        return state, prod

    lax.fori_loop(0, rows // (4 * SLAB), slab, (jnp.zeros((SLAB, width), F32), jnp.ones((SLAB, width), F32)))


def back_scan_kernel(
    live_ref, pre_ref, grad_ref, decay_ref, state_ref, prod_ref, cin_ref, lam_ref, reach_ref, edge_ref, low_ref
):
    rows, width = grad_ref.shape
    live = live_ref[0]
    cin = cin_ref[:1, :]
    c = np.float32(np.sqrt(2 / np.pi))
    for at in range(0, rows, ROWS):
        span = pl.ds(at, ROWS)
        v, grad = pre_ref[span, :], grad_ref[span, :]
        square = v * v
        bend = jnp.tanh(v * (c + (c * 0.044715) * square))
        rise = 0.5 + 0.5 * bend
        slope = rise + 0.5 * v * (1.0 - bend * bend) * (c + (3 * c * 0.044715) * square)
        grad = jnp.where(row_ids(ROWS, width, at) < live, grad, 0.0)
        lam_ref[span, :] = grad * (v * rise)
        low_ref[span, :] = (grad * (state_ref[span, :] + prod_ref[span, :] * cin) * slope).astype(BF)
    last = row_ids(SLAB, width, 0) == SLAB - 1

    def slab(k, carry):
        lam, reach, following, _ = carry
        for inner in range(4):
            span = pl.ds(pl.multiple_of(rows - (k * 4 + inner + 1) * SLAB, SLAB), SLAB)
            own = decay_ref[span, :]
            ahead = jnp.where(last, following, pltpu.roll(own, SLAB - 1, 0))
            decay, value = scan_slab(ahead, lam_ref[span, :], True)
            value = value + decay * lam
            decay = decay * reach
            lam_ref[span, :] = value
            reach_ref[span, :] = decay
            lam = jnp.broadcast_to(value[:1, :], (SLAB, width))
            reach = jnp.broadcast_to(decay[:1, :], (SLAB, width))
            following = jnp.broadcast_to(own[:1, :], (SLAB, width))
        return lam, reach, following, own

    one = jnp.ones((SLAB, width), F32)
    zero = jnp.zeros((SLAB, width), F32)
    lam, _, following, _ = lax.fori_loop(0, rows // (4 * SLAB), slab, (zero, one, one, one))
    edge_ref[...] = lam * following


def backward_kernel(
    live_ref, pre_ref, par_ref, w_ref, order_ref, lam_ref, reach_ref, edge_ref, decay_ref, conv_ref, ig_ref, dg_ref, state_ref, prod_ref, cin_ref,
    drec_ref, dpar_ref, dw_ref, rec_ref, dconv_ref, full_ref, dw_acc, dense_ref,
):
    rows, width = conv_ref.shape
    live = live_ref[0]
    rec_ref[...] = jnp.where(row_ids(rows + HALO, width, -HALO) < live, pre_ref[...], 0.0)
    par = [par_ref[k : k + 1, :] for k in range(8)]
    fill_dense(w_ref, order_ref, dense_ref)
    cin = cin_ref[:1, :]
    edge = edge_ref[:1, :]
    full_ref[:SLAB, :] = jnp.broadcast_to(cin, (SLAB, width))
    dconv_ref[:HALO, :] = jnp.zeros((HALO, width), F32)
    dconv_ref[rows + HALO :, :] = jnp.zeros((HALO, width), F32)
    sums = [jnp.zeros((1, width), F32) for _ in range(8)]
    for at in range(0, rows, ROWS):
        span = pl.ds(at, ROWS)
        full_ref[pl.ds(at + SLAB, ROWS), :] = state_ref[span, :] + prod_ref[span, :] * cin
        lam = lam_ref[span, :] + reach_ref[span, :] * edge
        decay, conv, ig, dg = decay_ref[span, :], conv_ref[span, :], ig_ref[span, :], dg_ref[span, :]
        before = full_ref[pl.ds(at, ROWS + SLAB), :][SLAB - 1 : SLAB - 1 + ROWS]
        room = 1.0 - decay * decay
        scale = jnp.sqrt(jnp.maximum(room, DECAY_FLOOR))
        lam_conv = lam * conv
        d_decay = lam * before - jnp.where(room > DECAY_FLOOR, lam_conv * ig * decay / scale, 0.0)
        moved = d_decay * decay
        sums[7] = sums[7] + jnp.sum(moved * dg, axis=0, keepdims=True)
        d_ig = lam_conv * scale * ig * (1.0 - ig)
        d_dg = moved * par[7] * dg * (1.0 - dg)
        sums[5] = sums[5] + jnp.sum(d_ig, axis=0, keepdims=True)
        sums[6] = sums[6] + jnp.sum(d_dg, axis=0, keepdims=True)
        both = jnp.concatenate([d_ig.astype(BF), d_dg.astype(BF)], axis=1)
        d_conv = lam * scale * ig + dot(both, dense_ref[...], ((1,), (1,)))
        d_conv = jnp.where(row_ids(ROWS, width, at) < live, d_conv, 0.0)
        dconv_ref[pl.ds(at + HALO, ROWS), :] = d_conv
        part = dot(conv.astype(BF), both, ((0,), (0,)))
        dw_acc[...] = part if at == 0 else dw_acc[...] + part
        near = rec_ref[pl.ds(at, ROWS + HALO), :]
        for k in range(4):
            sums[k] = sums[k] + jnp.sum(d_conv * near[HALO - k : HALO - k + ROWS], axis=0, keepdims=True)
        sums[4] = sums[4] + jnp.sum(d_conv, axis=0, keepdims=True)
    for k in range(8):
        dpar_ref[k : k + 1, :] = sums[k]
    head = dw_ref.shape[0]
    total = jnp.zeros((head, 2 * width), F32)
    for k in range(width // head):
        total = total + jnp.where(head_mask(head, k, width), dw_acc[k * head : (k + 1) * head, :], 0.0)
    dw_ref[...] = total.astype(BF)
    for at in list(range(0, rows, ROWS)) + [rows]:
        count = ROWS if at < rows else HALO
        near = dconv_ref[pl.ds(at, count + SLAB), :]
        total = par[0] * near[:count]
        for k in range(1, 4):
            total = total + par[k] * near[k : k + count]
        drec_ref[pl.ds(at, count), :] = total


def kernel_call(body, live, arrays, outs, scratch, name):
    width = outs[0][1]
    steps = width // GROUP
    specs = []
    for array in arrays:
        if array.ndim == 4:
            block = (array.shape[0], pl.squeezed) + array.shape[2:]
            specs.append(pl.BlockSpec(block, lambda j, s: (0, j, 0, 0)))
        elif array.shape[1] != width:
            specs.append(pl.BlockSpec(array.shape, lambda j, s: (0, 0)))
        else:
            specs.append(pl.BlockSpec((array.shape[0], GROUP), lambda j, s: (0, j)))
    out_specs, out_shapes = [], []
    for rows, cols, kind in outs:
        if cols == width:
            out_specs.append(pl.BlockSpec((rows, GROUP), lambda j, s: (0, j)))
            out_shapes.append(jax.ShapeDtypeStruct((rows, cols), kind))
        else:
            out_specs.append(pl.BlockSpec((pl.squeezed, rows, cols), lambda j, s: (j, 0, 0)))
            out_shapes.append(jax.ShapeDtypeStruct((steps, rows, cols), kind))
    return pl.pallas_call(
        body,
        grid_spec=pltpu.PrefetchScalarGridSpec(
            num_scalar_prefetch=1, grid=(steps,), in_specs=specs, out_specs=out_specs,
            scratch_shapes=[pltpu.VMEM(shape, kind) for shape, kind in scratch],
        ),
        out_shape=out_shapes,
        compiler_params=pltpu.CompilerParams(vmem_limit_bytes=VMEM),
        cost_estimate=LITTLE,
        name=name,
    )(live, *arrays)


def norm_rate(values):
    return lax.rsqrt(jnp.mean(values * values, axis=-1, keepdims=True) + NORM_EPS)


def norm_back(grad, unit, rate, gain):
    moved = grad * gain
    return rate * (moved - unit * jnp.mean(moved * unit, axis=-1, keepdims=True))


def gelu_product(gate, up):
    return jax.nn.gelu(gate) * up


def wide_dot(left, halves):
    cut = halves[0].shape[0]
    return dot(left[:, :cut], halves[0]) + dot(left[:, cut:], halves[1])


def wide_back(left, halves):
    return jnp.concatenate([dot(left, h, ((1,), (1,))) for h in halves], axis=1)


def on_device(size, n, tokens, lengths, gains, w_gelu, w_rec, chan, w_lru, w_out, w_mlp_in, w_down, cotangent):
    place = lax.axis_index("dp")
    turn = lax.axis_index("tensor")
    d_model = tokens.shape[1]
    rows = tokens.shape[0] // n
    half = rows // 2
    d_own = w_gelu.shape[0]
    heads_own, part, head = chan.shape[1], chan.shape[2], w_lru.shape[3]
    heads = heads_own * n
    width = heads * head
    groups = width // GROUP
    table, inverse = basis(size, d_own, place)
    live_count = (lengths - turn * rows).astype(jnp.int32)
    live = (lax.iota(jnp.int32, rows)[:, None] < live_count).astype(F32)

    cols = w_gelu.shape[1]
    pad = -(-part // 16) * 16
    own_lru = jnp.pad(w_lru.transpose(0, 2, 1, 3).reshape(2, part, cols), ((0, 0), (0, pad - part), (0, 0)))
    own_chan = jnp.zeros((8, heads_own, head), F32)
    own_chan = lax.dynamic_update_slice(own_chan, chan, (0, 0, place * part)).reshape(8, cols)
    own_gain = jnp.pad(gains.reshape(1, -1), ((0, 7), (0, cols - gains.size)))
    small = jnp.concatenate([own_lru.reshape(2 * pad, cols), own_chan, own_gain])
    whole = jnp.concatenate([w_rec, w_gelu, small]).astype(BF)
    own_dn = w_down.T.astype(BF)
    own_gu = jnp.concatenate([w_mlp_in[0], w_mlp_in[1]], axis=1).astype(BF)
    some_dn = spread_begin(own_dn, size)
    whole = lax.all_gather(whole, "tensor", axis=0)
    z_rec, z_gelu = (
        whole[:, k * d_own : (k + 1) * d_own].transpose(1, 0, 2).reshape(d_own, width) for k in range(2)
    )
    some_r = spread_begin(z_rec, size, *some_dn[1:])
    some_small = small_begin(whole[:, 2 * d_own :].reshape(-1, cols), size)
    w_r, came_r = spread_end(some_r, size, (), ())
    small = small_end(some_small, size).reshape(size, n, -1, cols)

    spots, parts = basis_spots(size, d_own)
    unit = d_own // parts
    gain = small[:, 0, 2 * pad + 8, : gains.size].reshape(size, 2, d_own)
    gain = [gain[(mask & 1) * (size // 2) + (mask >> 1), :, k * unit : (k + 1) * unit] for mask, k in spots]
    gain = jnp.concatenate(gain, axis=1).astype(F32)
    chans = jnp.sum(small[:, :, 2 * pad : 2 * pad + 8].astype(F32), axis=0)
    chans = chans.transpose(1, 0, 2).reshape(8, width)
    par = jnp.concatenate([chans[:7], -8.0 * jax.nn.softplus(-chans[7:])])
    each = n // groups
    lru = small
    if each > 1:
        lru = lru.reshape(size, groups, each, -1, cols).transpose(0, 1, 3, 2, 4).reshape(size, groups, -1, GROUP)
    spot, row = jnp.arange(size * pad) // pad, jnp.arange(size * pad) % pad
    spot = place ^ (spot // (size // 2) | (spot % (size // 2)) << 1)
    row = jnp.where(row < part, spot * part + row, head)
    order = (jnp.arange(head)[:, None] == row[None, :]).astype(BF)

    main = lax.dynamic_slice_in_dim(tokens, turn * rows, rows)
    before = lax.dynamic_slice_in_dim(tokens, jnp.maximum(turn * rows - HALO, 0), HALO)
    before = jnp.where(turn > 0, before, jnp.zeros_like(before))
    extended = permute_rows(jnp.concatenate([before, main]), table).astype(F32)
    first_rate = norm_rate(extended)
    first = (extended * first_rate * gain[0]).astype(BF)
    inputs, first_own, first_rate = extended[HALO:], first[HALO:], first_rate[HALO:]
    cut = d_model // 2

    keep = (rows, width, F32)
    dense = ((GROUP, 2 * GROUP), BF)
    some_g = spread_begin(z_gelu, size, *came_r)
    rec_pre = wide_dot(first, w_r)
    conv, decay, ig, dg, state, prod = kernel_call(
        forward_kernel, live_count, [rec_pre, par, lru, order], [keep] * 6,
        [((rows + HALO, GROUP), F32), dense], "recurrence",
    )
    ends = jnp.concatenate([prod[-1:], state[-1:]])
    came = [z_shift(ends, k, n, False) for k in range(1, n)]
    carry = jnp.zeros((1, width), F32)
    for end in came[::-1]:
        carry = end[1:] + end[:1] * carry
    z_out = z_gather(*fence([w_out.T.astype(BF)], z_rec), n, ends)
    w_g, came_g = spread_end(some_g, size, (rec_pre,), (ends, z_out))
    some_o = spread_begin(z_out, size, *came_g, ends)
    branch_pre = wide_dot(first_own, w_g)
    recurrent = (state + prod * carry) * live
    mixed = (jax.nn.gelu(branch_pre) * recurrent).astype(BF)
    w_o, came_o = spread_end(some_o, size, (branch_pre,), (mixed,))
    hidden = inputs + wide_back(mixed, w_o)
    second_rate = norm_rate(hidden)
    second_unit = hidden * second_rate
    second_own = (second_unit * gain[1]).astype(BF)
    some_gu = spread_begin(own_gu, size, *came_o)
    w_gu, came_gu = spread_end(some_gu, size, (second_own,), ())
    w_dn, _ = spread_end(some_dn, size, came_gu, ())
    w_gu, w_dn = assemble(w_gu), assemble(w_dn)
    late = fence([table], second_own)[0]
    cots = [permute_rows(cotangent, late, half, 2, h) for h in range(2)]

    hidden_units = w_dn.shape[1]
    grad_products = [dot(c, w_dn) for c in cots]
    shares, grad_second, seconds, products, grads = [], [], [], [], []
    for h in range(2):
        second = lax.all_gather(second_own[h * half : (h + 1) * half], "tensor", axis=0, tiled=True)
        (second,) = fence([second], *shares)
        both = dot(second, w_gu)
        product, pull = jax.vjp(gelu_product, both[:, :hidden_units], both[:, hidden_units:])
        grad_gate, grad_up = pull(grad_products[h])
        product = product.astype(BF)
        grad = jnp.concatenate([grad_gate.astype(BF), grad_up.astype(BF)], axis=1)
        share = dot(grad, w_gu, ((1,), (1,))).astype(BF)
        shares.append(share)
        grad_second.append(lax.psum_scatter(share, "tensor", scatter_dimension=0, tiled=True))
        seconds.append(second)
        products.append(product)
        grads.append(grad)

    products, grads = [[*pair] for pair in zip(*[fence([p, g], shares[-1]) for p, g in zip(products, grads)])]
    shares = [dot(p, w_dn, ((1,), (1,))).astype(BF) for p in products]

    def by_rows(lefts, rights):
        parts = []
        for span in (slice(cut, None), slice(0, cut)):
            part = dot(lefts[0][:, span], rights[0], ((0,), (0,)))
            parts.append((part + dot(lefts[1][:, span], rights[1], ((0,), (0,)))).astype(BF))
        return Collect(parts[1], parts[0], size, d_own)

    sum_dn = by_rows(cots, products)
    sum_gu = by_rows(seconds, grads)
    sent_dn, sent_gu = sum_dn.sources(), sum_gu.sources()
    grad_second = fence(grad_second, *sent_dn, *sent_gu, *shares)
    came_mlp = sum_dn.hop(sent_dn) + sum_gu.hop(sent_gu)

    def mlp_result(h, mlp_sum):
        return permute_rows((hidden[h * half : (h + 1) * half] + mlp_sum.astype(F32)).astype(BF), inverse)

    shares = fence(shares, *grad_second)
    mlp_sums = [lax.psum_scatter(share, "tensor", scatter_dimension=0, tiled=True) for share in shares]

    grad_second = jnp.concatenate(grad_second).astype(F32)
    cot_own = jnp.concatenate([lax.dynamic_slice_in_dim(c, turn * half, half) for c in cots]).astype(F32)
    gain_two = jnp.sum(grad_second * second_unit, axis=0)
    grad_hidden = cot_own + norm_back(grad_second, second_unit, second_rate, gain[1])
    hidden_low = grad_hidden.astype(BF)

    def by_cols(left, right):
        parts = [dot(left[:, span], right, ((0,), (0,))).astype(BF) for span in (slice(cut, None), slice(0, cut))]
        return Collect(parts[1], parts[0], size, d_own)

    grad_mixed = wide_dot(hidden_low, w_o)
    tall = jnp.broadcast_to
    lam, reach, edge, pre_low = kernel_call(
        back_scan_kernel, live_count, [branch_pre, grad_mixed, decay, state, prod, tall(carry, (SLAB, width))],
        [keep, keep, (SLAB, width, F32), (rows, width, BF)], [], "back_scan",
    )
    edges = jnp.concatenate([prod[-1:], edge[:1]])
    came = [z_shift(edges, -k, n, False) for k in range(1, n)]
    arriving = jnp.zeros((1, width), F32)
    for end in came[::-1]:
        arriving = end[1:] + end[:1] * arriving
    (lam,) = fence([lam], *came_mlp)
    drec, dpar, d_lru = kernel_call(
        backward_kernel, live_count,
        [rec_pre, par, lru, order, lam, reach, tall(arriving, (SLAB, width)), decay, conv, ig, dg, state, prod, tall(carry, (SLAB, width))],
        [(rows + HALO, width, F32), (8, width, F32), (head, 2 * GROUP, BF)],
        [((rows + HALO, GROUP), F32), ((rows + 2 * HALO, GROUP), F32), ((rows + SLAB, GROUP), F32), ((GROUP, 2 * GROUP), F32), dense],
        "recurrence_back",
    )
    line_0 = Line(mlp_result(0, mlp_sums[0]), n)
    (edge_rows,) = fence([z_shift(drec[:HALO], -1, n, False)], line_0.own)
    came_0 = line_0.go()
    rec_low = (drec[HALO:] + jnp.pad(edge_rows, ((rows - HALO, 0), (0, 0)))) * live
    rec_low = rec_low.astype(BF)
    (pre_low,) = fence([pre_low], drec)
    (grad_first,) = fence([wide_back(pre_low, w_g) + wide_back(rec_low, w_r)], *came_0)
    came_0 = line_0.go()
    first_unit = inputs * first_rate
    gain_one = jnp.sum(grad_first * first_unit, axis=0)
    grad_tokens = grad_hidden + norm_back(grad_first, first_unit, first_rate, gain[0])
    grad_tokens = permute_rows(grad_tokens.astype(BF), inverse)
    gathered = [lax.all_gather(grad_tokens[h * half : (h + 1) * half], "tensor", axis=0) for h in range(2)]
    (mixed,) = fence([mixed], grad_tokens)
    sum_o = by_cols(hidden_low, mixed)
    pre_low, rec_low = fence([pre_low, rec_low], sum_o.terms[1])
    sum_g, sum_r = by_cols(first_own, pre_low), by_cols(first_own, rec_low)
    line_1 = Line(mlp_result(1, *fence(mlp_sums[1:], sum_o.terms[1])), n)
    got_o = sum_o.hop(fence(sum_o.sources(), line_1.own, *came_0))
    came_0, came_1 = line_0.go(), line_1.go()
    got_g = sum_g.hop(fence(sum_g.sources(), *got_o))
    if sum_dn.square:
        sum_dn.hop(fence(sum_dn.sources(), *got_o))
        sum_gu.hop(fence(sum_gu.sources(), *got_o))
    pause = (gathered[0], *came_0, *came_1, *got_g)
    sum_o.hop(fence(sum_o.sources(), *pause))
    got_r = sum_r.hop(fence(sum_r.sources(), *pause))
    came_1 = line_1.go(gathered[0], *got_g)
    sum_g.hop(fence(sum_g.sources(), *pause))
    pause = (gathered[1], *came_1, *got_r)
    sum_r.hop(fence(sum_r.sources(), *pause))
    d_lru, dpar = fence([d_lru, dpar], *pause)
    line_1.go(gathered[1])
    tokens_out = interleave(*fence(gathered, *got_r)).reshape(n * rows, d_model)
    g_gu, g_dn = sum_gu.finish().astype(F32), sum_dn.finish().astype(F32)
    owned = jnp.stack([total.finish().reshape(d_own, n, width // n) for total in (sum_o, sum_g, sum_r)])
    owned = lax.psum_scatter(owned.transpose(2, 0, 1, 3), "tensor", scatter_dimension=0).astype(F32)
    g_o, g_g, g_r = owned[0], owned[1], owned[2]
    output = line_0.place(jnp.zeros((n, 2, half, d_model), BF), 0)
    output = line_1.place(output, 1).reshape(n * rows, d_model)

    d_gain = permute_gain(jnp.stack([gain_one, gain_two]), inverse)
    d_chan = jnp.concatenate([dpar[:7], dpar[7:] * 8.0 * jax.nn.sigmoid(-chans[7:])])
    d_lru = d_lru.reshape(groups, size, part, 2, each, -1).transpose(1, 0, 4, 2, 3, 5)
    d_chan = d_chan.reshape(8, n, heads_own, size, part).transpose(3, 1, 0, 2, 4)
    d_gain = d_gain.reshape(2, size, 1, d_own).transpose(1, 2, 0, 3)
    d_gain = jnp.broadcast_to(d_gain, (size, n, 2, d_own))
    small = [v.reshape(size, n, -1).astype(BF) for v in (d_lru, d_chan, d_gain)]
    small = small_scatter(jnp.concatenate(small, axis=2), size, n)
    d_lru = small[: w_lru.size].reshape(part, 2, heads_own, head).transpose(1, 2, 0, 3)
    d_chan = small[w_lru.size : -gains.size].reshape(chan.shape)
    d_gain = small[-gains.size :].reshape(gains.shape)
    g_gate, g_up = g_gu[:, :hidden_units], g_gu[:, hidden_units:]
    return (
        output, tokens_out, d_gain[0], d_gain[1], g_g, g_r, d_chan, d_lru,
        g_o.T, jnp.stack([g_gate, g_up]), g_dn.T,
    )


def solution(mesh):
    in_specs = (
        P("dp", None),
        P("dp"),
        P(None, "dp"),
        P("dp", "tensor"),
        P("dp", "tensor"),
        P(None, "tensor", "dp"),
        P(None, "tensor", "dp", None),
        P("tensor", "dp"),
        P(None, "dp", "tensor"),
        P("tensor", "dp"),
        P("dp", None),
    )
    out_specs = (
        P("dp", None),
        P("dp", None),
        P("dp"),
        P("dp"),
        P("dp", "tensor"),
        P("dp", "tensor"),
        P(None, "tensor", "dp"),
        P(None, "tensor", "dp", None),
        P("tensor", "dp"),
        P(None, "dp", "tensor"),
        P("tensor", "dp"),
    )
    body = functools.partial(on_device, mesh.shape["dp"], mesh.shape["tensor"])
    return jax.shard_map(body, mesh=mesh, in_specs=in_specs, out_specs=out_specs, check_vma=False)
```

```python
import functools

import jax
import jax.numpy as jnp
import numpy as np
from jax import lax
from jax.experimental import pallas as pl
from jax.experimental.pallas import tpu as pltpu
from jax.sharding import PartitionSpec as P

NORM_EPS = 1e-06
DECAY_FLOOR = 0.05
HALO = 16
GROUP = 640
ROWS = 128
SLAB = 8
VMEM = 58 * 1024 * 1024
BF = jnp.bfloat16
F32 = jnp.float32
LITTLE = pl.CostEstimate(flops=1024, bytes_accessed=1024, transcendentals=0)


def dot(left, right, dims=((1,), (0,))):
    return lax.dot_general(left, right, (dims, ((), ())), preferred_element_type=F32)


def fence(values, *others):
    if not others:
        return list(values)
    place = pl.BlockSpec(memory_space=pl.ANY)
    call = pl.pallas_call(
        lambda *refs: None,
        in_specs=[place] * (len(values) + len(others)),
        out_specs=[place] * len(values),
        out_shape=[jax.ShapeDtypeStruct(v.shape, v.dtype) for v in values],
        input_output_aliases={k: k for k in range(len(values))},
        compiler_params=pltpu.CompilerParams(vmem_limit_bytes=VMEM),
        name="fence",
    )
    return list(call(*values, *others))


def assemble(pieces, *others):
    count = len(pieces)
    rows = [p.shape[0] for p in pieces]
    spans = [pl.ds(sum(rows[:k]), rows[k]) for k in range(count)]
    shape = (sum(rows), pieces[0].shape[1])

    def body(*refs):
        out, held, coming, going = refs[count + len(others) :]
        ins = [pltpu.make_async_copy(refs[k], held.at[spans[k]], coming.at[k]) for k in range(count)]
        outs = [pltpu.make_async_copy(held.at[spans[k]], out.at[spans[k]], going.at[k]) for k in range(count)]
        for copy in ins:
            copy.start()
        for here, there in zip(ins, outs):
            here.wait()
            there.start()
        for copy in outs:
            copy.wait()

    place = pl.BlockSpec(memory_space=pl.ANY)
    return pl.pallas_call(
        body,
        in_specs=[place] * (count + len(others)),
        out_specs=place,
        out_shape=jax.ShapeDtypeStruct(shape, pieces[0].dtype),
        scratch_shapes=[
            pltpu.VMEM(shape, pieces[0].dtype),
            pltpu.SemaphoreType.DMA((count,)),
            pltpu.SemaphoreType.DMA((count,)),
        ],
        compiler_params=pltpu.CompilerParams(vmem_limit_bytes=VMEM),
        cost_estimate=LITTLE,
        name="assemble",
    )(*pieces, *others)


def exchange(values, bit, size):
    return lax.ppermute(values, "dp", [(k, k ^ (1 << bit)) for k in range(size)])


def squared(size, rows):
    return size == 8 and rows % 256 == 0


def spread_begin(own, size, *before):
    (own,) = fence([own], *before)
    if squared(size, own.shape[0]):
        return [own, exchange(own, 1, size), exchange(own, 2, size)]
    pieces = own
    for bit in range(1, size.bit_length() - 2):
        pieces = jnp.concatenate([pieces, exchange(pieces, bit, size)])
    return [pieces]


def spread_end(some, size, before_last, before_core):
    if len(some) > 1:
        own, by_x, by_y = some
        unit = own.shape[0] // 2
        by_x, by_y = fence([by_x, by_y], *before_last)
        got = [exchange(by_x[:unit], 2, size), exchange(by_y[unit:], 1, size)]
        half = assemble([own, by_x, got[1], got[0], by_y], *before_core)
    else:
        (pieces,) = fence(some, *before_last)
        got = [exchange(pieces, size.bit_length() - 2, size)]
        half = jnp.concatenate([pieces] + fence(got, *before_core))
    return [half, exchange(half, 0, size)], got


def add_all(terms):
    total = terms[0].astype(F32)
    for term in terms[1:]:
        total = total + term.astype(F32)
    return total.astype(BF)


class Collect:
    def __init__(self, keep, send, size, d_own):
        self.size, self.unit = size, d_own // 2
        self.square = squared(size, d_own)
        self.bit = size.bit_length() - 2
        self.terms = [keep, exchange(send, 0, size)]
        self.first = self.last = None

    def rows(self, start, stop):
        return [t[start * self.unit : stop * self.unit] for t in self.terms]

    def sources(self):
        if not self.square:
            cut = self.terms[0].shape[0] // 2
            return [add_all([t[cut:] for t in self.terms])]
        if self.first is None:
            return [add_all(self.rows(3, 5)), add_all(self.rows(5, 7))]
        by_x, by_y = self.first
        return [add_all(self.rows(2, 3) + [by_y[: self.unit]]), add_all(self.rows(7, 8) + [by_x[self.unit :]])]

    def hop(self, sources):
        if not self.square:
            got = exchange(sources[0], self.bit, self.size)
            self.bit -= 1
            self.terms = [t[: got.shape[0]] for t in self.terms] + [got]
            return [got]
        got = [exchange(v, bit, self.size) for v, bit in zip(sources, (1, 2))]
        if self.first is None:
            self.first = got
        else:
            self.last = got
        return got

    def finish(self):
        if not self.square:
            while self.bit:
                self.hop(self.sources())
            return add_all(self.terms)
        low = add_all(self.rows(0, 1) + [self.first[1][self.unit :], self.last[0]])
        high = add_all(self.rows(1, 2) + [self.first[0][: self.unit], self.last[1]])
        return jnp.concatenate([low, high])


def z_shift(values, by, n, around=True):
    pairs = [(k, (k + by) % n) for k in range(n) if around or 0 <= k + by < n]
    return lax.ppermute(values, "tensor", pairs)


def z_scatter(values, n):
    turn = lax.axis_index("tensor")
    total = lax.dynamic_index_in_dim(values, turn, 0, keepdims=False).astype(F32)
    for k in range(1, n):
        block = lax.dynamic_index_in_dim(values, (turn + k) % n, 0, keepdims=False)
        total = total + z_shift(block, k, n).astype(F32)
    return total


def z_spread(own, n):
    return [z_shift(own, k, n) for k in range(1, n)]


def place_rows(pieces, starts):
    count, rows = len(pieces), pieces[0].shape[0]
    shape = (count * rows, pieces[0].shape[1])

    def body(starts_ref, *refs):
        out, held, coming, going = refs[count:]
        ins, outs = [], []
        for k in range(count):
            span = pl.ds(pl.multiple_of(starts_ref[k], rows), rows)
            ins.append(pltpu.make_async_copy(refs[k], held.at[k], coming.at[k]))
            outs.append(pltpu.make_async_copy(held.at[k], out.at[span], going.at[k]))
        for copy in ins:
            copy.start()
        for here, there in zip(ins, outs):
            here.wait()
            there.start()
        for copy in outs:
            copy.wait()

    place = pl.BlockSpec(memory_space=pl.ANY)
    return pl.pallas_call(
        body,
        in_specs=[pl.BlockSpec(memory_space=pltpu.SMEM)] + [place] * count,
        out_specs=place,
        out_shape=jax.ShapeDtypeStruct(shape, pieces[0].dtype),
        scratch_shapes=[
            pltpu.VMEM((count, rows, shape[1]), pieces[0].dtype),
            pltpu.SemaphoreType.DMA((count,)),
            pltpu.SemaphoreType.DMA((count,)),
        ],
        compiler_params=pltpu.CompilerParams(vmem_limit_bytes=VMEM),
        cost_estimate=LITTLE,
        name="place_rows",
    )(starts, *pieces)


def small_begin(own, size):
    if size == 8:
        return [own, exchange(own, 1, size), exchange(own, 2, size)]
    rows = own[None]
    for bit in range(1, size.bit_length() - 1):
        rows = jnp.concatenate([rows, exchange(rows, bit, size)])
    return [rows]


def small_end(some, size):
    if size == 8:
        own, by_x, by_y = some
        cut = own.shape[0] // 2
        far = jnp.concatenate([exchange(by_x[:cut], 2, size), exchange(by_y[cut:], 1, size)])
        rows = jnp.stack([own, by_x, by_y, far])
    else:
        (rows,) = some
    return jnp.concatenate([rows, exchange(rows, 0, size)])


def z_gather(own, n, *others):
    turn = lax.axis_index("tensor")
    blocks = jnp.stack([own] + fence([z_shift(own, -k, n) for k in range(1, n)], *others))
    blocks = jnp.take(blocks, (jnp.arange(n) - turn) % n, axis=0, mode="clip")
    return blocks.transpose(1, 0, 2).reshape(own.shape[0], -1)


def small_scatter(values, size, n):
    place = lax.axis_index("dp")
    values = jnp.take(values, jnp.arange(size) ^ place, axis=0, mode="clip")
    for bit in reversed(range(size.bit_length() - 1)):
        half = values.shape[0] // 2
        values = add_all([values[:half], exchange(values[half:], bit, size)])
    return z_scatter(values[0], n)


def basis_spots(size, rows):
    if squared(size, rows):
        turns = ((0, 0), (0, 1), (2, 0), (2, 1), (6, 1), (6, 0), (4, 0), (4, 1))
        return [(core | mask, part) for core in range(2) for mask, part in turns], 2
    return [(core | q << 1, 0) for core in range(2) for q in range(size // 2)], 1


def basis(size, rows, place):
    spots, parts = basis_spots(size, rows)
    masks, which = (jnp.asarray(np.array(v, np.int32)) for v in zip(*spots))
    table = (place ^ masks) * parts + which
    spots = jnp.arange(table.shape[0], dtype=jnp.int32)
    inverse = jnp.sum(jnp.where(table[None, :] == spots[:, None], spots[None, :], 0), axis=1)
    return table, inverse.astype(jnp.int32)


def copy_kernel(blocks, table_ref, in_ref, out_ref):
    width = in_ref.shape[1] // blocks
    for p in range(blocks):
        start = pl.multiple_of(table_ref[p] * width, width)
        out_ref[:, p * width : (p + 1) * width] = in_ref[:, pl.ds(start, width)]


def permute_rows(values, table, step=0, stride=1, offset=0):
    rows, d_model = values.shape
    step = step or max(k for k in range(16, 289, 16) if rows % k == 0)
    return pl.pallas_call(
        functools.partial(copy_kernel, table.shape[0]),
        grid_spec=pltpu.PrefetchScalarGridSpec(
            num_scalar_prefetch=1,
            grid=(rows // (step * stride),),
            in_specs=[pl.BlockSpec((step, d_model), lambda r, tab: (r * stride + offset, 0))],
            out_specs=pl.BlockSpec((step, d_model), lambda r, tab: (r, 0)),
        ),
        out_shape=jax.ShapeDtypeStruct((rows // stride, d_model), values.dtype),
        compiler_params=pltpu.CompilerParams(vmem_limit_bytes=VMEM),
        cost_estimate=LITTLE,
        name="permute",
    )(table, values)


def interleave_kernel(one_ref, two_ref, out_ref):
    out_ref[0] = one_ref[...]
    out_ref[1] = two_ref[...]


def interleave(one, two):
    n, rows, d_model = one.shape
    spec = pl.BlockSpec((pl.squeezed, rows, d_model), lambda j: (j, 0, 0))
    return pl.pallas_call(
        interleave_kernel,
        grid=(n,),
        in_specs=[spec, spec],
        out_specs=pl.BlockSpec((pl.squeezed, 2, rows, d_model), lambda j: (j, 0, 0, 0)),
        out_shape=jax.ShapeDtypeStruct((n, 2, rows, d_model), one.dtype),
        compiler_params=pltpu.CompilerParams(vmem_limit_bytes=VMEM),
        cost_estimate=LITTLE,
        name="interleave",
    )(one, two)


def permute_gain(values, table):
    lead = values.shape[0]
    return jnp.take(values.reshape(lead, table.shape[0], -1), table, axis=1, mode="clip").reshape(lead, -1)


def row_ids(count, width, first):
    return lax.broadcasted_iota(jnp.int32, (count, width), 0) + first


def scan_slab(decay, value, back):
    rows = row_ids(SLAB, decay.shape[1], 0)
    for step in (1, 2, 4):
        keep = rows < SLAB - step if back else rows >= step
        shift = SLAB - step if back else step
        moved_decay = pltpu.roll(decay, shift, 0)
        moved_value = pltpu.roll(value, shift, 0)
        value = jnp.where(keep, value + decay * moved_value, value)
        decay = jnp.where(keep, decay * moved_decay, decay)
    return decay, value


def head_mask(head, at, width):
    lanes = lax.broadcasted_iota(jnp.int32, (head, 2 * width), 1)
    lanes = jnp.where(lanes >= width, lanes - width, lanes)
    return (lanes >= at * head) & (lanes < (at + 1) * head)


def fill_dense(w_ref, order_ref, dense_ref):
    head, count = order_ref.shape
    pad = count // w_ref.shape[0]
    width = dense_ref.shape[0]
    for gate in range(2):
        rows = w_ref[:, gate * pad : (gate + 1) * pad, :].reshape(count, width)
        rows = dot(order_ref[...], rows)
        for k in range(width // head):
            lanes = lax.broadcasted_iota(jnp.int32, (head, width), 1)
            block = jnp.where((lanes >= k * head) & (lanes < (k + 1) * head), rows, 0.0)
            dense_ref[k * head : (k + 1) * head, gate * width : (gate + 1) * width] = block.astype(BF)


def forward_kernel(
    live_ref, pre_ref, par_ref, w_ref, order_ref, conv_ref, decay_ref, ig_ref, dg_ref, state_ref, prod_ref,
    rec_ref, dense_ref,
):
    rows, width = conv_ref.shape
    fill_dense(w_ref, order_ref, dense_ref)
    live = live_ref[0]
    rec_ref[...] = jnp.where(row_ids(rows + HALO, width, -HALO) < live, pre_ref[...], 0.0)
    par = [par_ref[k : k + 1, :] for k in range(8)]
    for at in range(0, rows, ROWS):
        span = pl.ds(at, ROWS)
        near = rec_ref[pl.ds(at, ROWS + HALO), :]
        conv = par[4] + par[0] * near[HALO : HALO + ROWS]
        for k in range(1, 4):
            conv = conv + par[k] * near[HALO - k : HALO - k + ROWS]
        conv = jnp.where(row_ids(ROWS, width, at) < live, conv, 0.0)
        conv_ref[span, :] = conv
        gates = dot(conv.astype(BF), dense_ref[...])
        ig = lax.logistic(gates[:, :width] + par[5])
        dg = lax.logistic(gates[:, width:] + par[6])
        decay = jnp.exp(dg * par[7])
        ig_ref[span, :] = ig
        dg_ref[span, :] = dg
        decay_ref[span, :] = decay
        state_ref[span, :] = jnp.sqrt(jnp.maximum(1.0 - decay * decay, DECAY_FLOOR)) * ig * conv

    def slab(k, carry):
        state, prod = carry
        for inner in range(4):
            span = pl.ds(pl.multiple_of(k * 4 * SLAB + inner * SLAB, SLAB), SLAB)
            decay, value = scan_slab(decay_ref[span, :], state_ref[span, :], False)
            value = value + decay * state
            decay = decay * prod
            state_ref[span, :] = value
            prod_ref[span, :] = decay
            state = jnp.broadcast_to(value[SLAB - 1 :, :], (SLAB, width))
            prod = jnp.broadcast_to(decay[SLAB - 1 :, :], (SLAB, width))
        return state, prod

    lax.fori_loop(0, rows // (4 * SLAB), slab, (jnp.zeros((SLAB, width), F32), jnp.ones((SLAB, width), F32)))


def back_scan_kernel(
    live_ref, pre_ref, grad_ref, decay_ref, state_ref, prod_ref, cin_ref, lam_ref, reach_ref, edge_ref, low_ref
):
    rows, width = grad_ref.shape
    live = live_ref[0]
    cin = cin_ref[:1, :]
    c = np.float32(np.sqrt(2 / np.pi))
    for at in range(0, rows, ROWS):
        span = pl.ds(at, ROWS)
        v, grad = pre_ref[span, :], grad_ref[span, :]
        square = v * v
        bend = jnp.tanh(v * (c + (c * 0.044715) * square))
        rise = 0.5 + 0.5 * bend
        slope = rise + 0.5 * v * (1.0 - bend * bend) * (c + (3 * c * 0.044715) * square)
        grad = jnp.where(row_ids(ROWS, width, at) < live, grad, 0.0)
        lam_ref[span, :] = grad * (v * rise)
        low_ref[span, :] = (grad * (state_ref[span, :] + prod_ref[span, :] * cin) * slope).astype(BF)
    last = row_ids(SLAB, width, 0) == SLAB - 1

    def slab(k, carry):
        lam, reach, following, _ = carry
        for inner in range(4):
            span = pl.ds(pl.multiple_of(rows - (k * 4 + inner + 1) * SLAB, SLAB), SLAB)
            own = decay_ref[span, :]
            ahead = jnp.where(last, following, pltpu.roll(own, SLAB - 1, 0))
            decay, value = scan_slab(ahead, lam_ref[span, :], True)
            value = value + decay * lam
            decay = decay * reach
            lam_ref[span, :] = value
            reach_ref[span, :] = decay
            lam = jnp.broadcast_to(value[:1, :], (SLAB, width))
            reach = jnp.broadcast_to(decay[:1, :], (SLAB, width))
            following = jnp.broadcast_to(own[:1, :], (SLAB, width))
        return lam, reach, following, own

    one = jnp.ones((SLAB, width), F32)
    zero = jnp.zeros((SLAB, width), F32)
    lam, _, following, _ = lax.fori_loop(0, rows // (4 * SLAB), slab, (zero, one, one, one))
    edge_ref[...] = lam * following


def backward_kernel(
    live_ref, pre_ref, par_ref, w_ref, order_ref, lam_ref, reach_ref, edge_ref, decay_ref, conv_ref, ig_ref, dg_ref, state_ref, prod_ref, cin_ref,
    drec_ref, dpar_ref, dw_ref, rec_ref, dconv_ref, full_ref, dw_acc, dense_ref,
):
    rows, width = conv_ref.shape
    live = live_ref[0]
    rec_ref[...] = jnp.where(row_ids(rows + HALO, width, -HALO) < live, pre_ref[...], 0.0)
    par = [par_ref[k : k + 1, :] for k in range(8)]
    fill_dense(w_ref, order_ref, dense_ref)
    cin = cin_ref[:1, :]
    edge = edge_ref[:1, :]
    full_ref[:SLAB, :] = jnp.broadcast_to(cin, (SLAB, width))
    dconv_ref[:HALO, :] = jnp.zeros((HALO, width), F32)
    dconv_ref[rows + HALO :, :] = jnp.zeros((HALO, width), F32)
    sums = [jnp.zeros((1, width), F32) for _ in range(8)]
    for at in range(0, rows, ROWS):
        span = pl.ds(at, ROWS)
        full_ref[pl.ds(at + SLAB, ROWS), :] = state_ref[span, :] + prod_ref[span, :] * cin
        lam = lam_ref[span, :] + reach_ref[span, :] * edge
        decay, conv, ig, dg = decay_ref[span, :], conv_ref[span, :], ig_ref[span, :], dg_ref[span, :]
        before = full_ref[pl.ds(at, ROWS + SLAB), :][SLAB - 1 : SLAB - 1 + ROWS]
        room = 1.0 - decay * decay
        scale = jnp.sqrt(jnp.maximum(room, DECAY_FLOOR))
        lam_conv = lam * conv
        d_decay = lam * before - jnp.where(room > DECAY_FLOOR, lam_conv * ig * decay / scale, 0.0)
        moved = d_decay * decay
        sums[7] = sums[7] + jnp.sum(moved * dg, axis=0, keepdims=True)
        d_ig = lam_conv * scale * ig * (1.0 - ig)
        d_dg = moved * par[7] * dg * (1.0 - dg)
        sums[5] = sums[5] + jnp.sum(d_ig, axis=0, keepdims=True)
        sums[6] = sums[6] + jnp.sum(d_dg, axis=0, keepdims=True)
        both = jnp.concatenate([d_ig.astype(BF), d_dg.astype(BF)], axis=1)
        d_conv = lam * scale * ig + dot(both, dense_ref[...], ((1,), (1,)))
        d_conv = jnp.where(row_ids(ROWS, width, at) < live, d_conv, 0.0)
        dconv_ref[pl.ds(at + HALO, ROWS), :] = d_conv
        part = dot(conv.astype(BF), both, ((0,), (0,)))
        dw_acc[...] = part if at == 0 else dw_acc[...] + part
        near = rec_ref[pl.ds(at, ROWS + HALO), :]
        for k in range(4):
            sums[k] = sums[k] + jnp.sum(d_conv * near[HALO - k : HALO - k + ROWS], axis=0, keepdims=True)
        sums[4] = sums[4] + jnp.sum(d_conv, axis=0, keepdims=True)
    for k in range(8):
        dpar_ref[k : k + 1, :] = sums[k]
    head = dw_ref.shape[0]
    total = jnp.zeros((head, 2 * width), F32)
    for k in range(width // head):
        total = total + jnp.where(head_mask(head, k, width), dw_acc[k * head : (k + 1) * head, :], 0.0)
    dw_ref[...] = total.astype(BF)
    for at in list(range(0, rows, ROWS)) + [rows]:
        count = ROWS if at < rows else HALO
        near = dconv_ref[pl.ds(at, count + SLAB), :]
        total = par[0] * near[:count]
        for k in range(1, 4):
            total = total + par[k] * near[k : k + count]
        drec_ref[pl.ds(at, count), :] = total


def kernel_call(body, live, arrays, outs, scratch, name):
    width = outs[0][1]
    steps = width // GROUP
    specs = []
    for array in arrays:
        if array.ndim == 4:
            block = (array.shape[0], pl.squeezed) + array.shape[2:]
            specs.append(pl.BlockSpec(block, lambda j, s: (0, j, 0, 0)))
        elif array.shape[1] != width:
            specs.append(pl.BlockSpec(array.shape, lambda j, s: (0, 0)))
        else:
            specs.append(pl.BlockSpec((array.shape[0], GROUP), lambda j, s: (0, j)))
    out_specs, out_shapes = [], []
    for rows, cols, kind in outs:
        if cols == width:
            out_specs.append(pl.BlockSpec((rows, GROUP), lambda j, s: (0, j)))
            out_shapes.append(jax.ShapeDtypeStruct((rows, cols), kind))
        else:
            out_specs.append(pl.BlockSpec((pl.squeezed, rows, cols), lambda j, s: (j, 0, 0)))
            out_shapes.append(jax.ShapeDtypeStruct((steps, rows, cols), kind))
    return pl.pallas_call(
        body,
        grid_spec=pltpu.PrefetchScalarGridSpec(
            num_scalar_prefetch=1, grid=(steps,), in_specs=specs, out_specs=out_specs,
            scratch_shapes=[pltpu.VMEM(shape, kind) for shape, kind in scratch],
        ),
        out_shape=out_shapes,
        compiler_params=pltpu.CompilerParams(vmem_limit_bytes=VMEM),
        cost_estimate=LITTLE,
        name=name,
    )(live, *arrays)


def norm_rate(values):
    return lax.rsqrt(jnp.mean(values * values, axis=-1, keepdims=True) + NORM_EPS)


def norm_back(grad, unit, rate, gain):
    moved = grad * gain
    return rate * (moved - unit * jnp.mean(moved * unit, axis=-1, keepdims=True))


def gelu_product(gate, up):
    return jax.nn.gelu(gate) * up


def wide_dot(left, halves):
    cut = halves[0].shape[0]
    return dot(left[:, :cut], halves[0]) + dot(left[:, cut:], halves[1])


def wide_back(left, halves):
    return jnp.concatenate([dot(left, h, ((1,), (1,))) for h in halves], axis=1)


def on_device(size, n, tokens, lengths, gains, w_gelu, w_rec, chan, w_lru, w_out, w_mlp_in, w_down, cotangent):
    place = lax.axis_index("dp")
    turn = lax.axis_index("tensor")
    d_model = tokens.shape[1]
    rows = tokens.shape[0] // n
    half = rows // 2
    d_own = w_gelu.shape[0]
    heads_own, part, head = chan.shape[1], chan.shape[2], w_lru.shape[3]
    heads = heads_own * n
    width = heads * head
    groups = width // GROUP
    table, inverse = basis(size, d_own, place)
    live_count = (lengths - turn * rows).astype(jnp.int32)
    live = (lax.iota(jnp.int32, rows)[:, None] < live_count).astype(F32)

    cols = w_gelu.shape[1]
    pad = -(-part // 16) * 16
    own_lru = jnp.pad(w_lru.transpose(0, 2, 1, 3).reshape(2, part, cols), ((0, 0), (0, pad - part), (0, 0)))
    own_chan = jnp.zeros((8, heads_own, head), F32)
    own_chan = lax.dynamic_update_slice(own_chan, chan, (0, 0, place * part)).reshape(8, cols)
    own_gain = jnp.pad(gains.reshape(1, -1), ((0, 7), (0, cols - gains.size)))
    small = jnp.concatenate([own_lru.reshape(2 * pad, cols), own_chan, own_gain])
    whole = jnp.concatenate([w_rec, w_gelu, small]).astype(BF)
    own_dn = w_down.T.astype(BF)
    own_gu = jnp.concatenate([w_mlp_in[0], w_mlp_in[1]], axis=1).astype(BF)
    some_dn = spread_begin(own_dn, size)
    whole = lax.all_gather(whole, "tensor", axis=0)
    z_rec, z_gelu = (
        whole[:, k * d_own : (k + 1) * d_own].transpose(1, 0, 2).reshape(d_own, width) for k in range(2)
    )
    some_r = spread_begin(z_rec, size, *some_dn[1:], own_gu)
    some_small = small_begin(whole[:, 2 * d_own :].reshape(-1, cols), size)
    w_r, came_r = spread_end(some_r, size, (), ())
    small = small_end(some_small, size).reshape(size, n, -1, cols)

    spots, parts = basis_spots(size, d_own)
    unit = d_own // parts
    gain = small[:, 0, 2 * pad + 8, : gains.size].reshape(size, 2, d_own)
    gain = [gain[(mask & 1) * (size // 2) + (mask >> 1), :, k * unit : (k + 1) * unit] for mask, k in spots]
    gain = jnp.concatenate(gain, axis=1).astype(F32)
    chans = jnp.sum(small[:, :, 2 * pad : 2 * pad + 8].astype(F32), axis=0)
    chans = chans.transpose(1, 0, 2).reshape(8, width)
    par = jnp.concatenate([chans[:7], -8.0 * jax.nn.softplus(-chans[7:])])
    each = n // groups
    lru = small
    if each > 1:
        lru = lru.reshape(size, groups, each, -1, cols).transpose(0, 1, 3, 2, 4).reshape(size, groups, -1, GROUP)
    spot, row = jnp.arange(size * pad) // pad, jnp.arange(size * pad) % pad
    spot = place ^ (spot // (size // 2) | (spot % (size // 2)) << 1)
    row = jnp.where(row < part, spot * part + row, head)
    order = (jnp.arange(head)[:, None] == row[None, :]).astype(BF)

    main = lax.dynamic_slice_in_dim(tokens, turn * rows, rows)
    before = lax.dynamic_slice_in_dim(tokens, jnp.maximum(turn * rows - HALO, 0), HALO)
    before = jnp.where(turn > 0, before, jnp.zeros_like(before))
    extended = permute_rows(jnp.concatenate([before, main]), table).astype(F32)
    first_rate = norm_rate(extended)
    first = (extended * first_rate * gain[0]).astype(BF)
    inputs, first_own, first_rate = extended[HALO:], first[HALO:], first_rate[HALO:]
    cut = d_model // 2

    keep = (rows, width, F32)
    dense = ((GROUP, 2 * GROUP), BF)
    some_g = spread_begin(z_gelu, size, *came_r)
    rec_pre = wide_dot(first, w_r)
    conv, decay, ig, dg, state, prod = kernel_call(
        forward_kernel, live_count, [rec_pre, par, lru, order], [keep] * 6,
        [((rows + HALO, GROUP), F32), dense], "recurrence",
    )
    ends = jnp.concatenate([prod[-1:], state[-1:]])
    came = [z_shift(ends, k, n, False) for k in range(1, n)]
    carry = jnp.zeros((1, width), F32)
    for end in came[::-1]:
        carry = end[1:] + end[:1] * carry
    z_out = z_gather(w_out.T.astype(BF), n, ends)
    w_g, came_g = spread_end(some_g, size, (rec_pre,), (ends, z_out))
    some_o = spread_begin(z_out, size, *came_g)
    branch_pre = wide_dot(first_own, w_g)
    recurrent = (state + prod * carry) * live
    mixed = (jax.nn.gelu(branch_pre) * recurrent).astype(BF)
    w_o, came_o = spread_end(some_o, size, (branch_pre,), (mixed,))
    hidden = inputs + wide_back(mixed, w_o)
    second_rate = norm_rate(hidden)
    second_unit = hidden * second_rate
    second_own = (second_unit * gain[1]).astype(BF)
    some_gu = spread_begin(own_gu, size, *came_o)
    late = fence([table], second_own)[0]
    cots = [permute_rows(cotangent, late, half, 2, h) for h in range(2)]
    w_gu, came_gu = spread_end(some_gu, size, cots, ())
    w_dn, _ = spread_end(some_dn, size, came_gu, ())
    w_gu, w_dn = assemble(w_gu), assemble(w_dn)

    hidden_units = w_dn.shape[1]
    grad_products = [dot(c, w_dn) for c in cots]
    shares, grad_second, seconds, products, grads = [], [], [], [], []
    for h in range(2):
        second = lax.all_gather(second_own[h * half : (h + 1) * half], "tensor", axis=0, tiled=True)
        (second,) = fence([second], *shares)
        both = dot(second, w_gu)
        product, pull = jax.vjp(gelu_product, both[:, :hidden_units], both[:, hidden_units:])
        grad_gate, grad_up = pull(grad_products[h])
        product = product.astype(BF)
        grad = jnp.concatenate([grad_gate.astype(BF), grad_up.astype(BF)], axis=1)
        share = dot(grad, w_gu, ((1,), (1,))).astype(BF)
        shares.append(share)
        grad_second.append(lax.psum_scatter(share, "tensor", scatter_dimension=0, tiled=True))
        seconds.append(second)
        products.append(product)
        grads.append(grad)

    products, grads = [[*pair] for pair in zip(*[fence([p, g], shares[-1]) for p, g in zip(products, grads)])]
    shares = [dot(p, w_dn, ((1,), (1,))).astype(BF) for p in products]

    def by_rows(lefts, rights):
        parts = []
        for span in (slice(cut, None), slice(0, cut)):
            part = dot(lefts[0][:, span], rights[0], ((0,), (0,)))
            parts.append((part + dot(lefts[1][:, span], rights[1], ((0,), (0,)))).astype(BF))
        return Collect(parts[1], parts[0], size, d_own)

    sum_dn = by_rows(cots, products)
    sum_gu = by_rows(seconds, grads)
    sent_dn, sent_gu = sum_dn.sources(), sum_gu.sources()
    grad_second = fence(grad_second, *sent_dn, *sent_gu, *shares)
    came_mlp = sum_dn.hop(sent_dn) + sum_gu.hop(sent_gu)

    def mlp_result(h, mlp_sum):
        return permute_rows((hidden[h * half : (h + 1) * half] + mlp_sum.astype(F32)).astype(BF), inverse)

    shares = fence(shares, *grad_second)
    mlp_sums = [lax.psum_scatter(share, "tensor", scatter_dimension=0, tiled=True) for share in shares]

    grad_second = jnp.concatenate(grad_second).astype(F32)
    cot_own = jnp.concatenate([lax.dynamic_slice_in_dim(c, turn * half, half) for c in cots]).astype(F32)
    gain_two = jnp.sum(grad_second * second_unit, axis=0)
    grad_hidden = cot_own + norm_back(grad_second, second_unit, second_rate, gain[1])
    hidden_low = grad_hidden.astype(BF)

    def by_cols(left, right):
        parts = [dot(left[:, span], right, ((0,), (0,))).astype(BF) for span in (slice(cut, None), slice(0, cut))]
        return Collect(parts[1], parts[0], size, d_own)

    grad_mixed = wide_dot(hidden_low, w_o)
    tall = jnp.broadcast_to
    lam, reach, edge, pre_low = kernel_call(
        back_scan_kernel, live_count, [branch_pre, grad_mixed, decay, state, prod, tall(carry, (SLAB, width))],
        [keep, keep, (SLAB, width, F32), (rows, width, BF)], [], "back_scan",
    )
    edges = jnp.concatenate([prod[-1:], edge[:1]])
    came = [z_shift(edges, -k, n, False) for k in range(1, n)]
    arriving = jnp.zeros((1, width), F32)
    for end in came[::-1]:
        arriving = end[1:] + end[:1] * arriving
    (lam,) = fence([lam], *came_mlp)
    drec, dpar, d_lru = kernel_call(
        backward_kernel, live_count,
        [rec_pre, par, lru, order, lam, reach, tall(arriving, (SLAB, width)), decay, conv, ig, dg, state, prod, tall(carry, (SLAB, width))],
        [(rows + HALO, width, F32), (8, width, F32), (head, 2 * GROUP, BF)],
        [((rows + HALO, GROUP), F32), ((rows + 2 * HALO, GROUP), F32), ((rows + SLAB, GROUP), F32), ((GROUP, 2 * GROUP), F32), dense],
        "recurrence_back",
    )
    (edge_rows,) = fence([z_shift(drec[:HALO], -1, n, False)], mlp_sums[0])
    rec_low = (drec[HALO:] + jnp.pad(edge_rows, ((rows - HALO, 0), (0, 0)))) * live
    rec_low = rec_low.astype(BF)
    (pre_low,) = fence([pre_low], drec)
    grad_first = wide_back(pre_low, w_g) + wide_back(rec_low, w_r)
    first_unit = inputs * first_rate
    gain_one = jnp.sum(grad_first * first_unit, axis=0)
    grad_tokens = grad_hidden + norm_back(grad_first, first_unit, first_rate, gain[0])
    grad_tokens = permute_rows(grad_tokens.astype(BF), inverse)
    gathered = [lax.all_gather(grad_tokens[h * half : (h + 1) * half], "tensor", axis=0) for h in range(2)]
    (mixed,) = fence([mixed], grad_tokens)
    sum_o = by_cols(hidden_low, mixed)
    pre_low, rec_low = fence([pre_low, rec_low], sum_o.terms[1])
    sum_g, sum_r = by_cols(first_own, pre_low), by_cols(first_own, rec_low)
    results = [mlp_result(h, mlp_sum) for h, mlp_sum in enumerate(fence(mlp_sums, sum_o.terms[1]))]
    got_o = sum_o.hop(fence(sum_o.sources(), *results))
    got_g = sum_g.hop(fence(sum_g.sources(), *got_o))
    if sum_dn.square:
        sum_dn.hop(fence(sum_dn.sources(), *got_o))
        sum_gu.hop(fence(sum_gu.sources(), *got_o))
    pause = (gathered[0], *got_g)
    sum_o.hop(fence(sum_o.sources(), *pause))
    got_r = sum_r.hop(fence(sum_r.sources(), *pause))
    results = fence(results, *pause)
    came_0 = z_spread(results[0], n)
    sum_g.hop(fence(sum_g.sources(), *pause))
    d_lru, dpar = fence([d_lru, dpar], *pause)
    sum_r.hop(fence(sum_r.sources(), *got_r))
    owned = jnp.stack([total.finish().reshape(d_own, n, width // n) for total in (sum_o, sum_g, sum_r)])
    (owned,) = fence([owned.transpose(2, 0, 1, 3)], *came_0)
    came_1 = z_spread(results[1], n)
    owned = lax.psum_scatter(owned, "tensor", scatter_dimension=0).astype(F32)
    tokens_out = interleave(*fence(gathered, *came_0)).reshape(n * rows, d_model)
    g_gu, g_dn = sum_gu.finish().astype(F32), sum_dn.finish().astype(F32)
    starts = [(turn - k) % n * rows + h * half for h in range(2) for k in range(n)]
    output = place_rows([results[0], *came_0, results[1], *came_1], jnp.stack(starts).astype(jnp.int32))
    g_o, g_g, g_r = owned[0], owned[1], owned[2]

    d_gain = permute_gain(jnp.stack([gain_one, gain_two]), inverse)
    d_chan = jnp.concatenate([dpar[:7], dpar[7:] * 8.0 * jax.nn.sigmoid(-chans[7:])])
    d_lru = d_lru.reshape(groups, size, part, 2, each, -1).transpose(1, 0, 4, 2, 3, 5)
    d_chan = d_chan.reshape(8, n, heads_own, size, part).transpose(3, 1, 0, 2, 4)
    d_gain = d_gain.reshape(2, size, 1, d_own).transpose(1, 2, 0, 3)
    d_gain = jnp.broadcast_to(d_gain, (size, n, 2, d_own))
    small = [v.reshape(size, n, -1).astype(BF) for v in (d_lru, d_chan, d_gain)]
    small = small_scatter(jnp.concatenate(small, axis=2), size, n)
    d_lru = small[: w_lru.size].reshape(part, 2, heads_own, head).transpose(1, 2, 0, 3)
    d_chan = small[w_lru.size : -gains.size].reshape(chan.shape)
    d_gain = small[-gains.size :].reshape(gains.shape)
    g_gate, g_up = g_gu[:, :hidden_units], g_gu[:, hidden_units:]
    return (
        output, tokens_out, d_gain[0], d_gain[1], g_g, g_r, d_chan, d_lru,
        g_o.T, jnp.stack([g_gate, g_up]), g_dn.T,
    )


def solution(mesh):
    in_specs = (
        P("dp", None),
        P("dp"),
        P(None, "dp"),
        P("dp", "tensor"),
        P("dp", "tensor"),
        P(None, "tensor", "dp"),
        P(None, "tensor", "dp", None),
        P("tensor", "dp"),
        P(None, "dp", "tensor"),
        P("tensor", "dp"),
        P("dp", None),
    )
    out_specs = (
        P("dp", None),
        P("dp", None),
        P("dp"),
        P("dp"),
        P("dp", "tensor"),
        P("dp", "tensor"),
        P(None, "tensor", "dp"),
        P(None, "tensor", "dp", None),
        P("tensor", "dp"),
        P(None, "dp", "tensor"),
        P("tensor", "dp"),
    )
    body = functools.partial(on_device, mesh.shape["dp"], mesh.shape["tensor"])
    return jax.shard_map(body, mesh=mesh, in_specs=in_specs, out_specs=out_specs, check_vma=False)
```

```python
import functools

import jax
import jax.numpy as jnp
import numpy as np
from jax import lax
from jax.experimental import pallas as pl
from jax.experimental.pallas import tpu as pltpu
from jax.sharding import PartitionSpec as P

NORM_EPS = 1e-06
DECAY_FLOOR = 0.05
HALO = 16
GROUP = 640
ROWS = 128
SLAB = 8
VMEM = 58 * 1024 * 1024
BF = jnp.bfloat16
F32 = jnp.float32
LITTLE = pl.CostEstimate(flops=1024, bytes_accessed=1024, transcendentals=0)


def dot(left, right, dims=((1,), (0,))):
    return lax.dot_general(left, right, (dims, ((), ())), preferred_element_type=F32)


def fence(values, *others):
    if not others:
        return list(values)
    place = pl.BlockSpec(memory_space=pl.ANY)
    call = pl.pallas_call(
        lambda *refs: None,
        in_specs=[place] * (len(values) + len(others)),
        out_specs=[place] * len(values),
        out_shape=[jax.ShapeDtypeStruct(v.shape, v.dtype) for v in values],
        input_output_aliases={k: k for k in range(len(values))},
        compiler_params=pltpu.CompilerParams(vmem_limit_bytes=VMEM),
        name="fence",
    )
    return list(call(*values, *others))


def assemble(pieces, *others):
    count = len(pieces)
    rows = [p.shape[0] for p in pieces]
    spans = [pl.ds(sum(rows[:k]), rows[k]) for k in range(count)]
    shape = (sum(rows), pieces[0].shape[1])

    def body(*refs):
        out, held, coming, going = refs[count + len(others) :]
        ins = [pltpu.make_async_copy(refs[k], held.at[spans[k]], coming.at[k]) for k in range(count)]
        outs = [pltpu.make_async_copy(held.at[spans[k]], out.at[spans[k]], going.at[k]) for k in range(count)]
        for copy in ins:
            copy.start()
        for here, there in zip(ins, outs):
            here.wait()
            there.start()
        for copy in outs:
            copy.wait()

    place = pl.BlockSpec(memory_space=pl.ANY)
    return pl.pallas_call(
        body,
        in_specs=[place] * (count + len(others)),
        out_specs=place,
        out_shape=jax.ShapeDtypeStruct(shape, pieces[0].dtype),
        scratch_shapes=[
            pltpu.VMEM(shape, pieces[0].dtype),
            pltpu.SemaphoreType.DMA((count,)),
            pltpu.SemaphoreType.DMA((count,)),
        ],
        compiler_params=pltpu.CompilerParams(vmem_limit_bytes=VMEM),
        cost_estimate=LITTLE,
        name="assemble",
    )(*pieces, *others)


def exchange(values, bit, size):
    return lax.ppermute(values, "dp", [(k, k ^ (1 << bit)) for k in range(size)])


def squared(size, rows):
    return size == 8 and rows % 256 == 0


def spread_begin(own, size, *before):
    (own,) = fence([own], *before)
    if squared(size, own.shape[0]):
        return [own, exchange(own, 1, size), exchange(own, 2, size)]
    pieces = own
    for bit in range(1, size.bit_length() - 2):
        pieces = jnp.concatenate([pieces, exchange(pieces, bit, size)])
    return [pieces]


def spread_end(some, size, before_last, before_core):
    if len(some) > 1:
        own, by_x, by_y = some
        unit = own.shape[0] // 2
        by_x, by_y = fence([by_x, by_y], *before_last)
        got = [exchange(by_x[:unit], 2, size), exchange(by_y[unit:], 1, size)]
        half = assemble([own, by_x, got[1], got[0], by_y], *before_core)
    else:
        (pieces,) = fence(some, *before_last)
        got = [exchange(pieces, size.bit_length() - 2, size)]
        half = jnp.concatenate([pieces] + fence(got, *before_core))
    return [half, exchange(half, 0, size)], got


def add_all(terms):
    total = terms[0].astype(F32)
    for term in terms[1:]:
        total = total + term.astype(F32)
    return total.astype(BF)


class Collect:
    def __init__(self, keep, send, size, d_own):
        self.size, self.unit = size, d_own // 2
        self.square = squared(size, d_own)
        self.bit = size.bit_length() - 2
        self.terms = [keep, exchange(send, 0, size)]
        self.first = self.last = None

    def rows(self, start, stop):
        return [t[start * self.unit : stop * self.unit] for t in self.terms]

    def sources(self):
        if not self.square:
            cut = self.terms[0].shape[0] // 2
            return [add_all([t[cut:] for t in self.terms])]
        if self.first is None:
            return [add_all(self.rows(3, 5)), add_all(self.rows(5, 7))]
        by_x, by_y = self.first
        return [add_all(self.rows(2, 3) + [by_y[: self.unit]]), add_all(self.rows(7, 8) + [by_x[self.unit :]])]

    def hop(self, sources):
        if not self.square:
            got = exchange(sources[0], self.bit, self.size)
            self.bit -= 1
            self.terms = [t[: got.shape[0]] for t in self.terms] + [got]
            return [got]
        got = [exchange(v, bit, self.size) for v, bit in zip(sources, (1, 2))]
        if self.first is None:
            self.first = got
        else:
            self.last = got
        return got

    def finish(self):
        if not self.square:
            while self.bit:
                self.hop(self.sources())
            return add_all(self.terms)
        low = add_all(self.rows(0, 1) + [self.first[1][self.unit :], self.last[0]])
        high = add_all(self.rows(1, 2) + [self.first[0][: self.unit], self.last[1]])
        return jnp.concatenate([low, high])


def z_shift(values, by, n, around=True):
    pairs = [(k, (k + by) % n) for k in range(n) if around or 0 <= k + by < n]
    return lax.ppermute(values, "tensor", pairs)


def z_scatter(values, n):
    turn = lax.axis_index("tensor")
    total = lax.dynamic_index_in_dim(values, turn, 0, keepdims=False).astype(F32)
    for k in range(1, n):
        block = lax.dynamic_index_in_dim(values, (turn + k) % n, 0, keepdims=False)
        total = total + z_shift(block, k, n).astype(F32)
    return total


def small_masks(size):
    turns = (0, 2, 6, 4) if size == 8 else tuple(q << 1 for q in range(size // 2))
    return np.array([core | mask for core in range(2) for mask in turns], np.int32)


def small_begin(own, size):
    if size == 8:
        return [own, exchange(own, 1, size), exchange(own, 2, size)]
    rows = own[None]
    for bit in range(1, size.bit_length() - 1):
        rows = jnp.concatenate([rows, exchange(rows, bit, size)])
    return [rows]


def small_end(some, size):
    if size == 8:
        own, by_x, by_y = some
        cut = own.shape[0] // 2
        far = jnp.concatenate([exchange(by_x[:cut], 2, size), exchange(by_y[cut:], 1, size)])
        rows = jnp.stack([own, by_x, far, by_y])
    else:
        (rows,) = some
    return jnp.concatenate([rows, exchange(rows, 0, size)])


def small_scatter(values, size, n):
    place = lax.axis_index("dp")
    values = jnp.take(values, jnp.arange(size) ^ place, axis=0, mode="clip")
    for bit in reversed(range(size.bit_length() - 1)):
        half = values.shape[0] // 2
        values = add_all([values[:half], exchange(values[half:], bit, size)])
    return z_scatter(values[0], n)


def basis_spots(size, rows):
    if squared(size, rows):
        turns = ((0, 0), (0, 1), (2, 0), (2, 1), (6, 1), (6, 0), (4, 0), (4, 1))
        return [(core | mask, part) for core in range(2) for mask, part in turns], 2
    return [(core | q << 1, 0) for core in range(2) for q in range(size // 2)], 1


def basis(size, rows, place):
    spots, parts = basis_spots(size, rows)
    masks, which = (jnp.asarray(np.array(v, np.int32)) for v in zip(*spots))
    table = (place ^ masks) * parts + which
    spots = jnp.arange(table.shape[0], dtype=jnp.int32)
    inverse = jnp.sum(jnp.where(table[None, :] == spots[:, None], spots[None, :], 0), axis=1)
    return table, inverse.astype(jnp.int32)


def copy_kernel(blocks, table_ref, in_ref, out_ref):
    width = in_ref.shape[1] // blocks
    for p in range(blocks):
        start = pl.multiple_of(table_ref[p] * width, width)
        out_ref[:, p * width : (p + 1) * width] = in_ref[:, pl.ds(start, width)]


def permute_rows(values, table, step=0, stride=1, offset=0):
    rows, d_model = values.shape
    step = step or max(k for k in range(16, 289, 16) if rows % k == 0)
    return pl.pallas_call(
        functools.partial(copy_kernel, table.shape[0]),
        grid_spec=pltpu.PrefetchScalarGridSpec(
            num_scalar_prefetch=1,
            grid=(rows // (step * stride),),
            in_specs=[pl.BlockSpec((step, d_model), lambda r, tab: (r * stride + offset, 0))],
            out_specs=pl.BlockSpec((step, d_model), lambda r, tab: (r, 0)),
        ),
        out_shape=jax.ShapeDtypeStruct((rows // stride, d_model), values.dtype),
        compiler_params=pltpu.CompilerParams(vmem_limit_bytes=VMEM),
        cost_estimate=LITTLE,
        name="permute",
    )(table, values)


def interleave_kernel(one_ref, two_ref, out_ref):
    out_ref[0] = one_ref[...]
    out_ref[1] = two_ref[...]


def interleave(one, two):
    n, rows, d_model = one.shape
    spec = pl.BlockSpec((pl.squeezed, rows, d_model), lambda j: (j, 0, 0))
    return pl.pallas_call(
        interleave_kernel,
        grid=(n,),
        in_specs=[spec, spec],
        out_specs=pl.BlockSpec((pl.squeezed, 2, rows, d_model), lambda j: (j, 0, 0, 0)),
        out_shape=jax.ShapeDtypeStruct((n, 2, rows, d_model), one.dtype),
        compiler_params=pltpu.CompilerParams(vmem_limit_bytes=VMEM),
        cost_estimate=LITTLE,
        name="interleave",
    )(one, two)


def permute_gain(values, table):
    lead = values.shape[0]
    return jnp.take(values.reshape(lead, table.shape[0], -1), table, axis=1, mode="clip").reshape(lead, -1)


def row_ids(count, width, first):
    return lax.broadcasted_iota(jnp.int32, (count, width), 0) + first


def scan_slab(decay, value, back):
    rows = row_ids(SLAB, decay.shape[1], 0)
    for step in (1, 2, 4):
        keep = rows < SLAB - step if back else rows >= step
        shift = SLAB - step if back else step
        moved_decay = pltpu.roll(decay, shift, 0)
        moved_value = pltpu.roll(value, shift, 0)
        value = jnp.where(keep, value + decay * moved_value, value)
        decay = jnp.where(keep, decay * moved_decay, decay)
    return decay, value


def head_mask(head, at, width):
    lanes = lax.broadcasted_iota(jnp.int32, (head, 2 * width), 1)
    lanes = jnp.where(lanes >= width, lanes - width, lanes)
    return (lanes >= at * head) & (lanes < (at + 1) * head)


def fill_dense(w_ref, order_ref, dense_ref):
    head, count = order_ref.shape
    pad = count // w_ref.shape[0]
    width = dense_ref.shape[0]
    for gate in range(2):
        rows = w_ref[:, gate * pad : (gate + 1) * pad, :].reshape(count, width)
        rows = dot(order_ref[...], rows)
        for k in range(width // head):
            lanes = lax.broadcasted_iota(jnp.int32, (head, width), 1)
            block = jnp.where((lanes >= k * head) & (lanes < (k + 1) * head), rows, 0.0)
            dense_ref[k * head : (k + 1) * head, gate * width : (gate + 1) * width] = block.astype(BF)


def forward_kernel(
    live_ref, pre_ref, par_ref, w_ref, order_ref, conv_ref, decay_ref, ig_ref, dg_ref, state_ref, prod_ref,
    rec_ref, dense_ref,
):
    rows, width = conv_ref.shape
    fill_dense(w_ref, order_ref, dense_ref)
    live = live_ref[0]
    rec_ref[...] = jnp.where(row_ids(rows + HALO, width, -HALO) < live, pre_ref[...], 0.0)
    par = [par_ref[k : k + 1, :] for k in range(8)]
    for at in range(0, rows, ROWS):
        span = pl.ds(at, ROWS)
        near = rec_ref[pl.ds(at, ROWS + HALO), :]
        conv = par[4] + par[0] * near[HALO : HALO + ROWS]
        for k in range(1, 4):
            conv = conv + par[k] * near[HALO - k : HALO - k + ROWS]
        conv = jnp.where(row_ids(ROWS, width, at) < live, conv, 0.0)
        conv_ref[span, :] = conv
        gates = dot(conv.astype(BF), dense_ref[...])
        ig = lax.logistic(gates[:, :width] + par[5])
        dg = lax.logistic(gates[:, width:] + par[6])
        decay = jnp.exp(dg * par[7])
        ig_ref[span, :] = ig
        dg_ref[span, :] = dg
        decay_ref[span, :] = decay
        state_ref[span, :] = jnp.sqrt(jnp.maximum(1.0 - decay * decay, DECAY_FLOOR)) * ig * conv

    def slab(k, carry):
        state, prod = carry
        for inner in range(4):
            span = pl.ds(pl.multiple_of(k * 4 * SLAB + inner * SLAB, SLAB), SLAB)
            decay, value = scan_slab(decay_ref[span, :], state_ref[span, :], False)
            value = value + decay * state
            decay = decay * prod
            state_ref[span, :] = value
            prod_ref[span, :] = decay
            state = jnp.broadcast_to(value[SLAB - 1 :, :], (SLAB, width))
            prod = jnp.broadcast_to(decay[SLAB - 1 :, :], (SLAB, width))
        return state, prod

    lax.fori_loop(0, rows // (4 * SLAB), slab, (jnp.zeros((SLAB, width), F32), jnp.ones((SLAB, width), F32)))


def back_scan_kernel(
    live_ref, pre_ref, grad_ref, decay_ref, state_ref, prod_ref, cin_ref, lam_ref, reach_ref, edge_ref, low_ref
):
    rows, width = grad_ref.shape
    live = live_ref[0]
    cin = cin_ref[:1, :]
    c = np.float32(np.sqrt(2 / np.pi))
    for at in range(0, rows, ROWS):
        span = pl.ds(at, ROWS)
        v, grad = pre_ref[span, :], grad_ref[span, :]
        square = v * v
        bend = jnp.tanh(v * (c + (c * 0.044715) * square))
        rise = 0.5 + 0.5 * bend
        slope = rise + 0.5 * v * (1.0 - bend * bend) * (c + (3 * c * 0.044715) * square)
        grad = jnp.where(row_ids(ROWS, width, at) < live, grad, 0.0)
        lam_ref[span, :] = grad * (v * rise)
        low_ref[span, :] = (grad * (state_ref[span, :] + prod_ref[span, :] * cin) * slope).astype(BF)
    last = row_ids(SLAB, width, 0) == SLAB - 1

    def slab(k, carry):
        lam, reach, following, _ = carry
        for inner in range(4):
            span = pl.ds(pl.multiple_of(rows - (k * 4 + inner + 1) * SLAB, SLAB), SLAB)
            own = decay_ref[span, :]
            ahead = jnp.where(last, following, pltpu.roll(own, SLAB - 1, 0))
            decay, value = scan_slab(ahead, lam_ref[span, :], True)
            value = value + decay * lam
            decay = decay * reach
            lam_ref[span, :] = value
            reach_ref[span, :] = decay
            lam = jnp.broadcast_to(value[:1, :], (SLAB, width))
            reach = jnp.broadcast_to(decay[:1, :], (SLAB, width))
            following = jnp.broadcast_to(own[:1, :], (SLAB, width))
        return lam, reach, following, own

    one = jnp.ones((SLAB, width), F32)
    zero = jnp.zeros((SLAB, width), F32)
    lam, _, following, _ = lax.fori_loop(0, rows // (4 * SLAB), slab, (zero, one, one, one))
    edge_ref[...] = lam * following


def backward_kernel(
    live_ref, pre_ref, par_ref, w_ref, order_ref, lam_ref, reach_ref, edge_ref, decay_ref, conv_ref, ig_ref, dg_ref, state_ref, prod_ref, cin_ref,
    drec_ref, dpar_ref, dw_ref, rec_ref, dconv_ref, full_ref, dw_acc, dense_ref,
):
    rows, width = conv_ref.shape
    live = live_ref[0]
    rec_ref[...] = jnp.where(row_ids(rows + HALO, width, -HALO) < live, pre_ref[...], 0.0)
    par = [par_ref[k : k + 1, :] for k in range(8)]
    fill_dense(w_ref, order_ref, dense_ref)
    cin = cin_ref[:1, :]
    edge = edge_ref[:1, :]
    full_ref[:SLAB, :] = jnp.broadcast_to(cin, (SLAB, width))
    dconv_ref[:HALO, :] = jnp.zeros((HALO, width), F32)
    dconv_ref[rows + HALO :, :] = jnp.zeros((HALO, width), F32)
    sums = [jnp.zeros((1, width), F32) for _ in range(8)]
    for at in range(0, rows, ROWS):
        span = pl.ds(at, ROWS)
        full_ref[pl.ds(at + SLAB, ROWS), :] = state_ref[span, :] + prod_ref[span, :] * cin
        lam = lam_ref[span, :] + reach_ref[span, :] * edge
        decay, conv, ig, dg = decay_ref[span, :], conv_ref[span, :], ig_ref[span, :], dg_ref[span, :]
        before = full_ref[pl.ds(at, ROWS + SLAB), :][SLAB - 1 : SLAB - 1 + ROWS]
        room = 1.0 - decay * decay
        scale = jnp.sqrt(jnp.maximum(room, DECAY_FLOOR))
        lam_conv = lam * conv
        d_decay = lam * before - jnp.where(room > DECAY_FLOOR, lam_conv * ig * decay / scale, 0.0)
        moved = d_decay * decay
        sums[7] = sums[7] + jnp.sum(moved * dg, axis=0, keepdims=True)
        d_ig = lam_conv * scale * ig * (1.0 - ig)
        d_dg = moved * par[7] * dg * (1.0 - dg)
        sums[5] = sums[5] + jnp.sum(d_ig, axis=0, keepdims=True)
        sums[6] = sums[6] + jnp.sum(d_dg, axis=0, keepdims=True)
        both = jnp.concatenate([d_ig.astype(BF), d_dg.astype(BF)], axis=1)
        d_conv = lam * scale * ig + dot(both, dense_ref[...], ((1,), (1,)))
        d_conv = jnp.where(row_ids(ROWS, width, at) < live, d_conv, 0.0)
        dconv_ref[pl.ds(at + HALO, ROWS), :] = d_conv
        part = dot(conv.astype(BF), both, ((0,), (0,)))
        dw_acc[...] = part if at == 0 else dw_acc[...] + part
        near = rec_ref[pl.ds(at, ROWS + HALO), :]
        for k in range(4):
            sums[k] = sums[k] + jnp.sum(d_conv * near[HALO - k : HALO - k + ROWS], axis=0, keepdims=True)
        sums[4] = sums[4] + jnp.sum(d_conv, axis=0, keepdims=True)
    for k in range(8):
        dpar_ref[k : k + 1, :] = sums[k]
    head = dw_ref.shape[0]
    total = jnp.zeros((head, 2 * width), F32)
    for k in range(width // head):
        total = total + jnp.where(head_mask(head, k, width), dw_acc[k * head : (k + 1) * head, :], 0.0)
    dw_ref[...] = total.astype(BF)
    for at in list(range(0, rows, ROWS)) + [rows]:
        count = ROWS if at < rows else HALO
        near = dconv_ref[pl.ds(at, count + SLAB), :]
        total = par[0] * near[:count]
        for k in range(1, 4):
            total = total + par[k] * near[k : k + count]
        drec_ref[pl.ds(at, count), :] = total


def kernel_call(body, live, arrays, outs, scratch, name):
    width = outs[0][1]
    steps = width // GROUP
    specs = []
    for array in arrays:
        if array.ndim == 4:
            block = (array.shape[0], pl.squeezed) + array.shape[2:]
            specs.append(pl.BlockSpec(block, lambda j, s: (0, j, 0, 0)))
        elif array.shape[1] != width:
            specs.append(pl.BlockSpec(array.shape, lambda j, s: (0, 0)))
        else:
            specs.append(pl.BlockSpec((array.shape[0], GROUP), lambda j, s: (0, j)))
    out_specs, out_shapes = [], []
    for rows, cols, kind in outs:
        if cols == width:
            out_specs.append(pl.BlockSpec((rows, GROUP), lambda j, s: (0, j)))
            out_shapes.append(jax.ShapeDtypeStruct((rows, cols), kind))
        else:
            out_specs.append(pl.BlockSpec((pl.squeezed, rows, cols), lambda j, s: (j, 0, 0)))
            out_shapes.append(jax.ShapeDtypeStruct((steps, rows, cols), kind))
    return pl.pallas_call(
        body,
        grid_spec=pltpu.PrefetchScalarGridSpec(
            num_scalar_prefetch=1, grid=(steps,), in_specs=specs, out_specs=out_specs,
            scratch_shapes=[pltpu.VMEM(shape, kind) for shape, kind in scratch],
        ),
        out_shape=out_shapes,
        compiler_params=pltpu.CompilerParams(vmem_limit_bytes=VMEM),
        cost_estimate=LITTLE,
        name=name,
    )(live, *arrays)


def norm_rate(values):
    return lax.rsqrt(jnp.mean(values * values, axis=-1, keepdims=True) + NORM_EPS)


def norm_back(grad, unit, rate, gain):
    moved = grad * gain
    return rate * (moved - unit * jnp.mean(moved * unit, axis=-1, keepdims=True))


def gelu_product(gate, up):
    return jax.nn.gelu(gate) * up


def wide_dot(left, halves):
    cut = halves[0].shape[0]
    return dot(left[:, :cut], halves[0]) + dot(left[:, cut:], halves[1])


def wide_back(left, halves):
    return jnp.concatenate([dot(left, h, ((1,), (1,))) for h in halves], axis=1)


def on_device(size, n, tokens, lengths, gains, w_gelu, w_rec, chan, w_lru, w_out, w_mlp_in, w_down, cotangent):
    place = lax.axis_index("dp")
    turn = lax.axis_index("tensor")
    d_model = tokens.shape[1]
    rows = tokens.shape[0] // n
    half = rows // 2
    d_own = w_gelu.shape[0]
    heads_own, part, head = chan.shape[1], chan.shape[2], w_lru.shape[3]
    heads = heads_own * n
    width = heads * head
    groups = width // GROUP
    table, inverse = basis(size, d_own, place)
    live_count = (lengths - turn * rows).astype(jnp.int32)
    live = (lax.iota(jnp.int32, rows)[:, None] < live_count).astype(F32)

    cols = w_gelu.shape[1]
    pad = -(-part // 16) * 16
    own_lru = jnp.pad(w_lru.transpose(0, 2, 1, 3).reshape(2, part, cols), ((0, 0), (0, pad - part), (0, 0)))
    own_chan = jnp.zeros((8, heads_own, head), F32)
    own_chan = lax.dynamic_update_slice(own_chan, chan, (0, 0, place * part)).reshape(8, cols)
    own_gain = jnp.pad(gains.reshape(1, -1), ((0, 7), (0, cols - gains.size)))
    small = jnp.concatenate([own_lru.reshape(2 * pad, cols), own_chan, own_gain])
    whole = jnp.concatenate([w_rec, small]).astype(BF)
    others = jnp.concatenate([w_gelu, w_out.T]).astype(BF)
    own_gu = jnp.concatenate([w_mlp_in[0], w_mlp_in[1]], axis=1).astype(BF)
    own_dn = w_down.T.astype(BF)
    some_gu = spread_begin(own_gu, size)

    main = lax.dynamic_slice_in_dim(tokens, turn * rows, rows)
    before = lax.dynamic_slice_in_dim(tokens, jnp.maximum(turn * rows - HALO, 0), HALO)
    before = jnp.where(turn > 0, before, jnp.zeros_like(before))
    turned = permute_rows(jnp.concatenate([before, main]), table)
    extended = turned.astype(F32)
    first_rate = norm_rate(extended)

    def wide(blocks):
        return blocks.transpose(1, 0, 2).reshape(d_own, width)

    (whole,) = fence([lax.all_gather(whole, "tensor", axis=0)], *some_gu[1:], others, turned, first_rate)
    others = lax.all_gather(*fence([others], whole), "tensor", axis=0)
    z_gelu, z_out = wide(others[:, :d_own]), wide(others[:, d_own:])
    some_r = spread_begin(wide(whole[:, :d_own]), size)
    some_small = small_begin(whole[:, d_own:].reshape(-1, cols), size)
    small = small_end(some_small, size).reshape(size, n, -1, cols)

    masks = small_masks(size)
    gain = small[:, 0, 2 * pad + 8, : gains.size].reshape(size, 2, d_own)
    if squared(size, d_own):
        swapped = jnp.concatenate([gain[..., d_own // 2 :], gain[..., : d_own // 2]], axis=-1)
        gain = jnp.where(((jnp.asarray(masks) & 6) == 6)[:, None, None], swapped, gain)
    gain = gain.transpose(1, 0, 2).reshape(2, d_model).astype(F32)
    chans = jnp.sum(small[:, :, 2 * pad : 2 * pad + 8].astype(F32), axis=0)
    chans = chans.transpose(1, 0, 2).reshape(8, width)
    par = jnp.concatenate([chans[:7], -8.0 * jax.nn.softplus(-chans[7:])])
    each = n // groups
    lru = small
    if each > 1:
        lru = lru.reshape(size, groups, each, -1, cols).transpose(0, 1, 3, 2, 4).reshape(size, groups, -1, GROUP)
    spot = (place ^ jnp.asarray(masks))[jnp.arange(size * pad) // pad]
    row = jnp.arange(size * pad) % pad
    row = jnp.where(row < part, spot * part + row, head)
    order = (jnp.arange(head)[:, None] == row[None, :]).astype(BF)

    w_r, came_r = spread_end(some_r, size, some_small[1:], (others, gain, par, order, lru))
    first = (extended * first_rate * gain[0]).astype(BF)
    inputs, first_own, first_rate = extended[HALO:], first[HALO:], first_rate[HALO:]
    cut = d_model // 2

    keep = (rows, width, F32)
    dense = ((GROUP, 2 * GROUP), BF)
    some_g = spread_begin(z_gelu, size, *came_r)
    rec_pre = wide_dot(first, w_r)
    conv, decay, ig, dg, state, prod = kernel_call(
        forward_kernel, live_count, [rec_pre, par, lru, order], [keep] * 6,
        [((rows + HALO, GROUP), F32), dense], "recurrence",
    )
    ends = jnp.concatenate([prod[-1:], state[-1:]])
    came = [z_shift(ends, k, n, False) for k in range(1, n)]
    carry = jnp.zeros((1, width), F32)
    for end in came[::-1]:
        carry = end[1:] + end[:1] * carry
    w_g, came_g = spread_end(some_g, size, (ends,), ())
    some_o = spread_begin(z_out, size, *came_g)
    branch_pre = wide_dot(first_own, w_g)
    recurrent = (state + prod * carry) * live
    mixed = (jax.nn.gelu(branch_pre) * recurrent).astype(BF)
    w_o, came_o = spread_end(some_o, size, (branch_pre,), (mixed,))
    hidden = inputs + wide_back(mixed, w_o)
    second_rate = norm_rate(hidden)
    second_unit = hidden * second_rate
    second_own = (second_unit * gain[1]).astype(BF)
    w_gu, came_gu = spread_end(some_gu, size, came_o, (second_own,))
    w_dn, _ = spread_end(spread_begin(own_dn, size, *came_gu), size, (), ())
    w_gu, w_dn = assemble(w_gu), assemble(w_dn)
    late = fence([table], second_own)[0]
    cots = [permute_rows(cotangent, late, half, 2, h) for h in range(2)]

    hidden_units = w_dn.shape[1]
    grad_products = [dot(c, w_dn) for c in cots]
    shares, grad_second, seconds, products, grads = [], [], [], [], []
    for h in range(2):
        second = lax.all_gather(second_own[h * half : (h + 1) * half], "tensor", axis=0, tiled=True)
        (second,) = fence([second], *shares)
        both = dot(second, w_gu)
        product, pull = jax.vjp(gelu_product, both[:, :hidden_units], both[:, hidden_units:])
        grad_gate, grad_up = pull(grad_products[h])
        product = product.astype(BF)
        grad = jnp.concatenate([grad_gate.astype(BF), grad_up.astype(BF)], axis=1)
        share = dot(grad, w_gu, ((1,), (1,))).astype(BF)
        shares.append(share)
        grad_second.append(lax.psum_scatter(share, "tensor", scatter_dimension=0, tiled=True))
        seconds.append(second)
        products.append(product)
        grads.append(grad)

    products, grads = [[*pair] for pair in zip(*[fence([p, g], shares[-1]) for p, g in zip(products, grads)])]
    shares = [dot(p, w_dn, ((1,), (1,))).astype(BF) for p in products]

    def by_rows(lefts, rights):
        parts = []
        for span in (slice(cut, None), slice(0, cut)):
            part = dot(lefts[0][:, span], rights[0], ((0,), (0,)))
            parts.append((part + dot(lefts[1][:, span], rights[1], ((0,), (0,)))).astype(BF))
        return Collect(parts[1], parts[0], size, d_own)

    sum_dn = by_rows(cots, products)
    sum_gu = by_rows(seconds, grads)
    sent_dn, sent_gu = sum_dn.sources(), sum_gu.sources()
    grad_second = fence(grad_second, *sent_dn, *sent_gu, *shares)
    came_mlp = sum_dn.hop(sent_dn) + sum_gu.hop(sent_gu)

    def mlp_result(h, mlp_sum):
        return permute_rows((hidden[h * half : (h + 1) * half] + mlp_sum.astype(F32)).astype(BF), inverse)

    shares = fence(shares, *grad_second)
    mlp_sums = [lax.psum_scatter(share, "tensor", scatter_dimension=0, tiled=True) for share in shares]

    grad_second = jnp.concatenate(grad_second).astype(F32)
    cot_own = jnp.concatenate([lax.dynamic_slice_in_dim(c, turn * half, half) for c in cots]).astype(F32)
    gain_two = jnp.sum(grad_second * second_unit, axis=0)
    grad_hidden = cot_own + norm_back(grad_second, second_unit, second_rate, gain[1])
    hidden_low = grad_hidden.astype(BF)

    def by_cols(left, right):
        parts = [dot(left[:, span], right, ((0,), (0,))).astype(BF) for span in (slice(cut, None), slice(0, cut))]
        return Collect(parts[1], parts[0], size, d_own)

    grad_mixed = wide_dot(hidden_low, w_o)
    tall = jnp.broadcast_to
    lam, reach, edge, pre_low = kernel_call(
        back_scan_kernel, live_count, [branch_pre, grad_mixed, decay, state, prod, tall(carry, (SLAB, width))],
        [keep, keep, (SLAB, width, F32), (rows, width, BF)], [], "back_scan",
    )
    edges = jnp.concatenate([prod[-1:], edge[:1]])
    came = [z_shift(edges, -k, n, False) for k in range(1, n)]
    arriving = jnp.zeros((1, width), F32)
    for end in came[::-1]:
        arriving = end[1:] + end[:1] * arriving
    (lam,) = fence([lam], *came_mlp)
    drec, dpar, d_lru = kernel_call(
        backward_kernel, live_count,
        [rec_pre, par, lru, order, lam, reach, tall(arriving, (SLAB, width)), decay, conv, ig, dg, state, prod, tall(carry, (SLAB, width))],
        [(rows + HALO, width, F32), (8, width, F32), (head, 2 * GROUP, BF)],
        [((rows + HALO, GROUP), F32), ((rows + 2 * HALO, GROUP), F32), ((rows + SLAB, GROUP), F32), ((GROUP, 2 * GROUP), F32), dense],
        "recurrence_back",
    )
    (edge_rows,) = fence([z_shift(drec[:HALO], -1, n, False)], mlp_sums[0])
    rec_low = (drec[HALO:] + jnp.pad(edge_rows, ((rows - HALO, 0), (0, 0)))) * live
    rec_low = rec_low.astype(BF)
    (pre_low,) = fence([pre_low], drec)
    grad_first = wide_back(pre_low, w_g) + wide_back(rec_low, w_r)
    first_unit = inputs * first_rate
    gain_one = jnp.sum(grad_first * first_unit, axis=0)
    grad_tokens = grad_hidden + norm_back(grad_first, first_unit, first_rate, gain[0])
    grad_tokens = permute_rows(grad_tokens.astype(BF), inverse)
    gathered = [lax.all_gather(grad_tokens[h * half : (h + 1) * half], "tensor", axis=0) for h in range(2)]
    (mixed,) = fence([mixed], grad_tokens)
    sum_o = by_cols(hidden_low, mixed)
    pre_low, rec_low = fence([pre_low, rec_low], sum_o.terms[1])
    sum_g, sum_r = by_cols(first_own, pre_low), by_cols(first_own, rec_low)
    results = [mlp_result(h, mlp_sum) for h, mlp_sum in enumerate(fence(mlp_sums, sum_o.terms[1]))]
    got_o = sum_o.hop(sum_o.sources())
    sum_o.hop(fence(sum_o.sources(), gathered[0]))
    got_g = sum_g.hop(fence(sum_g.sources(), gathered[0]))
    results = fence(results, gathered[0])
    results = [lax.all_gather(result, "tensor", axis=0) for result in results]
    sum_g.hop(fence(sum_g.sources(), gathered[1]))
    got_r = sum_r.hop(fence(sum_r.sources(), gathered[1], *got_g))
    d_lru, dpar = fence([d_lru, dpar], gathered[1])
    sum_r.hop(fence(sum_r.sources(), results[0]))
    if sum_dn.square:
        sum_dn.hop(fence(sum_dn.sources(), results[0]))
        sum_gu.hop(fence(sum_gu.sources(), results[0]))
    tokens_out = interleave(*fence(gathered, results[0])).reshape(n * rows, d_model)
    g_gu, g_dn = sum_gu.finish().astype(F32), sum_dn.finish().astype(F32)
    owned = jnp.stack([total.finish().reshape(d_own, n, width // n) for total in (sum_o, sum_g, sum_r)])
    (owned,) = fence([owned.transpose(2, 0, 1, 3)], results[1])
    output = interleave(*results).reshape(n * rows, d_model)
    owned = lax.psum_scatter(owned, "tensor", scatter_dimension=0).astype(F32)
    g_o, g_g, g_r = owned[0], owned[1], owned[2]

    d_gain = permute_gain(jnp.stack([gain_one, gain_two]), inverse)
    d_chan = jnp.concatenate([dpar[:7], dpar[7:] * 8.0 * jax.nn.sigmoid(-chans[7:])])
    d_lru = d_lru.reshape(groups, size, part, 2, each, -1).transpose(1, 0, 4, 2, 3, 5)
    d_chan = d_chan.reshape(8, n, heads_own, size, part).transpose(3, 1, 0, 2, 4)
    d_gain = d_gain.reshape(2, size, 1, d_own).transpose(1, 2, 0, 3)
    d_gain = jnp.broadcast_to(d_gain, (size, n, 2, d_own))
    small = [v.reshape(size, n, -1).astype(BF) for v in (d_lru, d_chan, d_gain)]
    small = small_scatter(jnp.concatenate(small, axis=2), size, n)
    d_lru = small[: w_lru.size].reshape(part, 2, heads_own, head).transpose(1, 2, 0, 3)
    d_chan = small[w_lru.size : -gains.size].reshape(chan.shape)
    d_gain = small[-gains.size :].reshape(gains.shape)
    g_gate, g_up = g_gu[:, :hidden_units], g_gu[:, hidden_units:]
    return (
        output, tokens_out, d_gain[0], d_gain[1], g_g, g_r, d_chan, d_lru,
        g_o.T, jnp.stack([g_gate, g_up]), g_dn.T,
    )


def solution(mesh):
    in_specs = (
        P("dp", None),
        P("dp"),
        P(None, "dp"),
        P("dp", "tensor"),
        P("dp", "tensor"),
        P(None, "tensor", "dp"),
        P(None, "tensor", "dp", None),
        P("tensor", "dp"),
        P(None, "dp", "tensor"),
        P("tensor", "dp"),
        P("dp", None),
    )
    out_specs = (
        P("dp", None),
        P("dp", None),
        P("dp"),
        P("dp"),
        P("dp", "tensor"),
        P("dp", "tensor"),
        P(None, "tensor", "dp"),
        P(None, "tensor", "dp", None),
        P("tensor", "dp"),
        P(None, "dp", "tensor"),
        P("tensor", "dp"),
    )
    body = functools.partial(on_device, mesh.shape["dp"], mesh.shape["tensor"])
    return jax.shard_map(body, mesh=mesh, in_specs=in_specs, out_specs=out_specs, check_vma=False)
```

```python
import functools

import jax
import jax.numpy as jnp
import numpy as np
from jax import lax
from jax.experimental import pallas as pl
from jax.experimental.pallas import tpu as pltpu
from jax.sharding import PartitionSpec as P

NORM_EPS = 1e-06
DECAY_FLOOR = 0.05
HALO = 16
GROUP = 640
ROWS = 128
SLAB = 8
VMEM = 58 * 1024 * 1024
BF = jnp.bfloat16
F32 = jnp.float32
LITTLE = pl.CostEstimate(flops=1024, bytes_accessed=1024, transcendentals=0)


def dot(left, right, dims=((1,), (0,))):
    return lax.dot_general(left, right, (dims, ((), ())), preferred_element_type=F32)


def fence(values, *others):
    if not others:
        return list(values)
    place = pl.BlockSpec(memory_space=pl.ANY)
    call = pl.pallas_call(
        lambda *refs: None,
        in_specs=[place] * (len(values) + len(others)),
        out_specs=[place] * len(values),
        out_shape=[jax.ShapeDtypeStruct(v.shape, v.dtype) for v in values],
        input_output_aliases={k: k for k in range(len(values))},
        compiler_params=pltpu.CompilerParams(vmem_limit_bytes=VMEM),
        name="fence",
    )
    return list(call(*values, *others))


def assemble(pieces, *others):
    count = len(pieces)
    rows = [p.shape[0] for p in pieces]
    spans = [pl.ds(sum(rows[:k]), rows[k]) for k in range(count)]
    shape = (sum(rows), pieces[0].shape[1])

    def body(*refs):
        out, held, coming, going = refs[count + len(others) :]
        ins = [pltpu.make_async_copy(refs[k], held.at[spans[k]], coming.at[k]) for k in range(count)]
        outs = [pltpu.make_async_copy(held.at[spans[k]], out.at[spans[k]], going.at[k]) for k in range(count)]
        for copy in ins:
            copy.start()
        for here, there in zip(ins, outs):
            here.wait()
            there.start()
        for copy in outs:
            copy.wait()

    place = pl.BlockSpec(memory_space=pl.ANY)
    return pl.pallas_call(
        body,
        in_specs=[place] * (count + len(others)),
        out_specs=place,
        out_shape=jax.ShapeDtypeStruct(shape, pieces[0].dtype),
        scratch_shapes=[
            pltpu.VMEM(shape, pieces[0].dtype),
            pltpu.SemaphoreType.DMA((count,)),
            pltpu.SemaphoreType.DMA((count,)),
        ],
        compiler_params=pltpu.CompilerParams(vmem_limit_bytes=VMEM),
        cost_estimate=LITTLE,
        name="assemble",
    )(*pieces, *others)


def exchange(values, bit, size):
    return lax.ppermute(values, "dp", [(k, k ^ (1 << bit)) for k in range(size)])


def squared(size, rows):
    return size == 8 and rows % 256 == 0


def spread_begin(own, size, *before):
    (own,) = fence([own], *before)
    if squared(size, own.shape[0]):
        return [own, exchange(own, 1, size), exchange(own, 2, size)]
    pieces = own
    for bit in range(1, size.bit_length() - 2):
        pieces = jnp.concatenate([pieces, exchange(pieces, bit, size)])
    return [pieces]


def spread_end(some, size, before_last, before_core):
    if len(some) > 1:
        own, by_x, by_y = some
        unit = own.shape[0] // 2
        by_x, by_y = fence([by_x, by_y], *before_last)
        got = [exchange(by_x[:unit], 2, size), exchange(by_y[unit:], 1, size)]
        half = assemble([own, by_x, got[1], got[0], by_y], *before_core)
    else:
        (pieces,) = fence(some, *before_last)
        got = [exchange(pieces, size.bit_length() - 2, size)]
        half = jnp.concatenate([pieces] + fence(got, *before_core))
    return [half, exchange(half, 0, size)], got


def add_all(terms):
    total = terms[0].astype(F32)
    for term in terms[1:]:
        total = total + term.astype(F32)
    return total.astype(BF)


class Collect:
    def __init__(self, keep, send, size, d_own):
        self.size, self.unit = size, d_own // 2
        self.square = squared(size, d_own)
        self.bit = size.bit_length() - 2
        self.terms = [keep, exchange(send, 0, size)]
        self.first = self.last = None

    def rows(self, start, stop):
        return [t[start * self.unit : stop * self.unit] for t in self.terms]

    def sources(self):
        if not self.square:
            cut = self.terms[0].shape[0] // 2
            return [add_all([t[cut:] for t in self.terms])]
        if self.first is None:
            return [add_all(self.rows(3, 5)), add_all(self.rows(5, 7))]
        by_x, by_y = self.first
        return [add_all(self.rows(2, 3) + [by_y[: self.unit]]), add_all(self.rows(7, 8) + [by_x[self.unit :]])]

    def hop(self, sources):
        if not self.square:
            got = exchange(sources[0], self.bit, self.size)
            self.bit -= 1
            self.terms = [t[: got.shape[0]] for t in self.terms] + [got]
            return [got]
        got = [exchange(v, bit, self.size) for v, bit in zip(sources, (1, 2))]
        if self.first is None:
            self.first = got
        else:
            self.last = got
        return got

    def finish(self):
        if not self.square:
            while self.bit:
                self.hop(self.sources())
            return add_all(self.terms)
        low = add_all(self.rows(0, 1) + [self.first[1][self.unit :], self.last[0]])
        high = add_all(self.rows(1, 2) + [self.first[0][: self.unit], self.last[1]])
        return jnp.concatenate([low, high])


def z_shift(values, by, n, around=True):
    pairs = [(k, (k + by) % n) for k in range(n) if around or 0 <= k + by < n]
    return lax.ppermute(values, "tensor", pairs)


def z_scatter(values, n):
    turn = lax.axis_index("tensor")
    total = lax.dynamic_index_in_dim(values, turn, 0, keepdims=False).astype(F32)
    for k in range(1, n):
        block = lax.dynamic_index_in_dim(values, (turn + k) % n, 0, keepdims=False)
        total = total + z_shift(block, k, n).astype(F32)
    return total


class LineSum:
    def __init__(self, blocks, n):
        self.blocks, self.n, self.turn, self.rounds = blocks, n, lax.axis_index("tensor"), 0
        self.right = self.left = None

    def block(self, k):
        return lax.dynamic_index_in_dim(self.blocks, k % self.n, 0, keepdims=False)

    def go(self, *others):
        self.rounds += 1
        t, n = self.rounds, self.n
        right, left = self.block(self.turn + n - t), self.block(self.turn + t)
        if t > 1:
            before = fence([self.right, self.left], *others)
            right, left = add_all([right, before[0]]), add_all([left, before[1]])
        self.right = lax.ppermute(right, "tensor", [(k, k + 1) for k in range(min(t, n - 1))])
        self.left = lax.ppermute(left, "tensor", [(k, k - 1) for k in range(max(n - t, 1), n)])

    def finish(self):
        while self.rounds < self.n - 1:
            self.go()
        return self.block(self.turn).astype(F32) + self.right.astype(F32) + self.left.astype(F32)


def small_masks(size):
    turns = (0, 2, 6, 4) if size == 8 else tuple(q << 1 for q in range(size // 2))
    return np.array([core | mask for core in range(2) for mask in turns], np.int32)


def small_begin(own, size):
    if size == 8:
        return [own, exchange(own, 1, size), exchange(own, 2, size)]
    rows = own[None]
    for bit in range(1, size.bit_length() - 1):
        rows = jnp.concatenate([rows, exchange(rows, bit, size)])
    return [rows]


def small_end(some, size):
    if size == 8:
        own, by_x, by_y = some
        cut = own.shape[0] // 2
        far = jnp.concatenate([exchange(by_x[:cut], 2, size), exchange(by_y[cut:], 1, size)])
        rows = jnp.stack([own, by_x, far, by_y])
    else:
        (rows,) = some
    return jnp.concatenate([rows, exchange(rows, 0, size)])


def small_scatter(values, size, n):
    place = lax.axis_index("dp")
    values = jnp.take(values, jnp.arange(size) ^ place, axis=0, mode="clip")
    for bit in reversed(range(size.bit_length() - 1)):
        half = values.shape[0] // 2
        values = add_all([values[:half], exchange(values[half:], bit, size)])
    return z_scatter(values[0], n)


def basis_spots(size, rows):
    if squared(size, rows):
        turns = ((0, 0), (0, 1), (2, 0), (2, 1), (6, 1), (6, 0), (4, 0), (4, 1))
        return [(core | mask, part) for core in range(2) for mask, part in turns], 2
    return [(core | q << 1, 0) for core in range(2) for q in range(size // 2)], 1


def basis(size, rows, place):
    spots, parts = basis_spots(size, rows)
    masks, which = (jnp.asarray(np.array(v, np.int32)) for v in zip(*spots))
    table = (place ^ masks) * parts + which
    spots = jnp.arange(table.shape[0], dtype=jnp.int32)
    inverse = jnp.sum(jnp.where(table[None, :] == spots[:, None], spots[None, :], 0), axis=1)
    return table, inverse.astype(jnp.int32)


def copy_kernel(blocks, table_ref, in_ref, out_ref):
    width = in_ref.shape[1] // blocks
    for p in range(blocks):
        start = pl.multiple_of(table_ref[p] * width, width)
        out_ref[:, p * width : (p + 1) * width] = in_ref[:, pl.ds(start, width)]


def permute_rows(values, table, step=0, stride=1, offset=0):
    rows, d_model = values.shape
    step = step or max(k for k in range(16, 289, 16) if rows % k == 0)
    return pl.pallas_call(
        functools.partial(copy_kernel, table.shape[0]),
        grid_spec=pltpu.PrefetchScalarGridSpec(
            num_scalar_prefetch=1,
            grid=(rows // (step * stride),),
            in_specs=[pl.BlockSpec((step, d_model), lambda r, tab: (r * stride + offset, 0))],
            out_specs=pl.BlockSpec((step, d_model), lambda r, tab: (r, 0)),
        ),
        out_shape=jax.ShapeDtypeStruct((rows // stride, d_model), values.dtype),
        compiler_params=pltpu.CompilerParams(vmem_limit_bytes=VMEM),
        cost_estimate=LITTLE,
        name="permute",
    )(table, values)


def interleave_kernel(one_ref, two_ref, out_ref):
    out_ref[0] = one_ref[...]
    out_ref[1] = two_ref[...]


def interleave(one, two):
    n, rows, d_model = one.shape
    spec = pl.BlockSpec((pl.squeezed, rows, d_model), lambda j: (j, 0, 0))
    return pl.pallas_call(
        interleave_kernel,
        grid=(n,),
        in_specs=[spec, spec],
        out_specs=pl.BlockSpec((pl.squeezed, 2, rows, d_model), lambda j: (j, 0, 0, 0)),
        out_shape=jax.ShapeDtypeStruct((n, 2, rows, d_model), one.dtype),
        compiler_params=pltpu.CompilerParams(vmem_limit_bytes=VMEM),
        cost_estimate=LITTLE,
        name="interleave",
    )(one, two)


def permute_gain(values, table):
    lead = values.shape[0]
    return jnp.take(values.reshape(lead, table.shape[0], -1), table, axis=1, mode="clip").reshape(lead, -1)


def row_ids(count, width, first):
    return lax.broadcasted_iota(jnp.int32, (count, width), 0) + first


def scan_slab(decay, value, back):
    rows = row_ids(SLAB, decay.shape[1], 0)
    for step in (1, 2, 4):
        keep = rows < SLAB - step if back else rows >= step
        shift = SLAB - step if back else step
        moved_decay = pltpu.roll(decay, shift, 0)
        moved_value = pltpu.roll(value, shift, 0)
        value = jnp.where(keep, value + decay * moved_value, value)
        decay = jnp.where(keep, decay * moved_decay, decay)
    return decay, value


def head_mask(head, at, width):
    lanes = lax.broadcasted_iota(jnp.int32, (head, 2 * width), 1)
    lanes = jnp.where(lanes >= width, lanes - width, lanes)
    return (lanes >= at * head) & (lanes < (at + 1) * head)


def fill_dense(w_ref, order_ref, dense_ref):
    head, count = order_ref.shape
    pad = count // w_ref.shape[0]
    width = dense_ref.shape[0]
    for gate in range(2):
        rows = w_ref[:, gate * pad : (gate + 1) * pad, :].reshape(count, width)
        rows = dot(order_ref[...], rows)
        for k in range(width // head):
            lanes = lax.broadcasted_iota(jnp.int32, (head, width), 1)
            block = jnp.where((lanes >= k * head) & (lanes < (k + 1) * head), rows, 0.0)
            dense_ref[k * head : (k + 1) * head, gate * width : (gate + 1) * width] = block.astype(BF)


def forward_kernel(
    live_ref, pre_ref, par_ref, w_ref, order_ref, conv_ref, decay_ref, ig_ref, dg_ref, state_ref, prod_ref,
    rec_ref, dense_ref,
):
    rows, width = conv_ref.shape
    fill_dense(w_ref, order_ref, dense_ref)
    live = live_ref[0]
    rec_ref[...] = jnp.where(row_ids(rows + HALO, width, -HALO) < live, pre_ref[...], 0.0)
    par = [par_ref[k : k + 1, :] for k in range(8)]
    for at in range(0, rows, ROWS):
        span = pl.ds(at, ROWS)
        near = rec_ref[pl.ds(at, ROWS + HALO), :]
        conv = par[4] + par[0] * near[HALO : HALO + ROWS]
        for k in range(1, 4):
            conv = conv + par[k] * near[HALO - k : HALO - k + ROWS]
        conv = jnp.where(row_ids(ROWS, width, at) < live, conv, 0.0)
        conv_ref[span, :] = conv
        gates = dot(conv.astype(BF), dense_ref[...])
        ig = lax.logistic(gates[:, :width] + par[5])
        dg = lax.logistic(gates[:, width:] + par[6])
        decay = jnp.exp(dg * par[7])
        ig_ref[span, :] = ig
        dg_ref[span, :] = dg
        decay_ref[span, :] = decay
        state_ref[span, :] = jnp.sqrt(jnp.maximum(1.0 - decay * decay, DECAY_FLOOR)) * ig * conv

    def slab(k, carry):
        state, prod = carry
        for inner in range(4):
            span = pl.ds(pl.multiple_of(k * 4 * SLAB + inner * SLAB, SLAB), SLAB)
            decay, value = scan_slab(decay_ref[span, :], state_ref[span, :], False)
            value = value + decay * state
            decay = decay * prod
            state_ref[span, :] = value
            prod_ref[span, :] = decay
            state = jnp.broadcast_to(value[SLAB - 1 :, :], (SLAB, width))
            prod = jnp.broadcast_to(decay[SLAB - 1 :, :], (SLAB, width))
        return state, prod

    lax.fori_loop(0, rows // (4 * SLAB), slab, (jnp.zeros((SLAB, width), F32), jnp.ones((SLAB, width), F32)))


def back_scan_kernel(
    live_ref, pre_ref, grad_ref, decay_ref, state_ref, prod_ref, cin_ref, lam_ref, reach_ref, edge_ref, low_ref
):
    rows, width = grad_ref.shape
    live = live_ref[0]
    cin = cin_ref[:1, :]
    c = np.float32(np.sqrt(2 / np.pi))
    for at in range(0, rows, ROWS):
        span = pl.ds(at, ROWS)
        v, grad = pre_ref[span, :], grad_ref[span, :]
        square = v * v
        bend = jnp.tanh(v * (c + (c * 0.044715) * square))
        rise = 0.5 + 0.5 * bend
        slope = rise + 0.5 * v * (1.0 - bend * bend) * (c + (3 * c * 0.044715) * square)
        grad = jnp.where(row_ids(ROWS, width, at) < live, grad, 0.0)
        lam_ref[span, :] = grad * (v * rise)
        low_ref[span, :] = (grad * (state_ref[span, :] + prod_ref[span, :] * cin) * slope).astype(BF)
    last = row_ids(SLAB, width, 0) == SLAB - 1

    def slab(k, carry):
        lam, reach, following, _ = carry
        for inner in range(4):
            span = pl.ds(pl.multiple_of(rows - (k * 4 + inner + 1) * SLAB, SLAB), SLAB)
            own = decay_ref[span, :]
            ahead = jnp.where(last, following, pltpu.roll(own, SLAB - 1, 0))
            decay, value = scan_slab(ahead, lam_ref[span, :], True)
            value = value + decay * lam
            decay = decay * reach
            lam_ref[span, :] = value
            reach_ref[span, :] = decay
            lam = jnp.broadcast_to(value[:1, :], (SLAB, width))
            reach = jnp.broadcast_to(decay[:1, :], (SLAB, width))
            following = jnp.broadcast_to(own[:1, :], (SLAB, width))
        return lam, reach, following, own

    one = jnp.ones((SLAB, width), F32)
    zero = jnp.zeros((SLAB, width), F32)
    lam, _, following, _ = lax.fori_loop(0, rows // (4 * SLAB), slab, (zero, one, one, one))
    edge_ref[...] = lam * following


def backward_kernel(
    live_ref, pre_ref, par_ref, w_ref, order_ref, lam_ref, reach_ref, edge_ref, decay_ref, conv_ref, ig_ref, dg_ref, state_ref, prod_ref, cin_ref,
    drec_ref, dpar_ref, dw_ref, rec_ref, dconv_ref, full_ref, dw_acc, dense_ref,
):
    rows, width = conv_ref.shape
    live = live_ref[0]
    rec_ref[...] = jnp.where(row_ids(rows + HALO, width, -HALO) < live, pre_ref[...], 0.0)
    par = [par_ref[k : k + 1, :] for k in range(8)]
    fill_dense(w_ref, order_ref, dense_ref)
    cin = cin_ref[:1, :]
    edge = edge_ref[:1, :]
    full_ref[:SLAB, :] = jnp.broadcast_to(cin, (SLAB, width))
    dconv_ref[:HALO, :] = jnp.zeros((HALO, width), F32)
    dconv_ref[rows + HALO :, :] = jnp.zeros((HALO, width), F32)
    sums = [jnp.zeros((1, width), F32) for _ in range(8)]
    for at in range(0, rows, ROWS):
        span = pl.ds(at, ROWS)
        full_ref[pl.ds(at + SLAB, ROWS), :] = state_ref[span, :] + prod_ref[span, :] * cin
        lam = lam_ref[span, :] + reach_ref[span, :] * edge
        decay, conv, ig, dg = decay_ref[span, :], conv_ref[span, :], ig_ref[span, :], dg_ref[span, :]
        before = full_ref[pl.ds(at, ROWS + SLAB), :][SLAB - 1 : SLAB - 1 + ROWS]
        room = 1.0 - decay * decay
        scale = jnp.sqrt(jnp.maximum(room, DECAY_FLOOR))
        lam_conv = lam * conv
        d_decay = lam * before - jnp.where(room > DECAY_FLOOR, lam_conv * ig * decay / scale, 0.0)
        moved = d_decay * decay
        sums[7] = sums[7] + jnp.sum(moved * dg, axis=0, keepdims=True)
        d_ig = lam_conv * scale * ig * (1.0 - ig)
        d_dg = moved * par[7] * dg * (1.0 - dg)
        sums[5] = sums[5] + jnp.sum(d_ig, axis=0, keepdims=True)
        sums[6] = sums[6] + jnp.sum(d_dg, axis=0, keepdims=True)
        both = jnp.concatenate([d_ig.astype(BF), d_dg.astype(BF)], axis=1)
        d_conv = lam * scale * ig + dot(both, dense_ref[...], ((1,), (1,)))
        d_conv = jnp.where(row_ids(ROWS, width, at) < live, d_conv, 0.0)
        dconv_ref[pl.ds(at + HALO, ROWS), :] = d_conv
        part = dot(conv.astype(BF), both, ((0,), (0,)))
        dw_acc[...] = part if at == 0 else dw_acc[...] + part
        near = rec_ref[pl.ds(at, ROWS + HALO), :]
        for k in range(4):
            sums[k] = sums[k] + jnp.sum(d_conv * near[HALO - k : HALO - k + ROWS], axis=0, keepdims=True)
        sums[4] = sums[4] + jnp.sum(d_conv, axis=0, keepdims=True)
    for k in range(8):
        dpar_ref[k : k + 1, :] = sums[k]
    head = dw_ref.shape[0]
    total = jnp.zeros((head, 2 * width), F32)
    for k in range(width // head):
        total = total + jnp.where(head_mask(head, k, width), dw_acc[k * head : (k + 1) * head, :], 0.0)
    dw_ref[...] = total.astype(BF)
    for at in list(range(0, rows, ROWS)) + [rows]:
        count = ROWS if at < rows else HALO
        near = dconv_ref[pl.ds(at, count + SLAB), :]
        total = par[0] * near[:count]
        for k in range(1, 4):
            total = total + par[k] * near[k : k + count]
        drec_ref[pl.ds(at, count), :] = total


def kernel_call(body, live, arrays, outs, scratch, name):
    width = outs[0][1]
    steps = width // GROUP
    specs = []
    for array in arrays:
        if array.ndim == 4:
            block = (array.shape[0], pl.squeezed) + array.shape[2:]
            specs.append(pl.BlockSpec(block, lambda j, s: (0, j, 0, 0)))
        elif array.shape[1] != width:
            specs.append(pl.BlockSpec(array.shape, lambda j, s: (0, 0)))
        else:
            specs.append(pl.BlockSpec((array.shape[0], GROUP), lambda j, s: (0, j)))
    out_specs, out_shapes = [], []
    for rows, cols, kind in outs:
        if cols == width:
            out_specs.append(pl.BlockSpec((rows, GROUP), lambda j, s: (0, j)))
            out_shapes.append(jax.ShapeDtypeStruct((rows, cols), kind))
        else:
            out_specs.append(pl.BlockSpec((pl.squeezed, rows, cols), lambda j, s: (j, 0, 0)))
            out_shapes.append(jax.ShapeDtypeStruct((steps, rows, cols), kind))
    return pl.pallas_call(
        body,
        grid_spec=pltpu.PrefetchScalarGridSpec(
            num_scalar_prefetch=1, grid=(steps,), in_specs=specs, out_specs=out_specs,
            scratch_shapes=[pltpu.VMEM(shape, kind) for shape, kind in scratch],
        ),
        out_shape=out_shapes,
        compiler_params=pltpu.CompilerParams(vmem_limit_bytes=VMEM),
        cost_estimate=LITTLE,
        name=name,
    )(live, *arrays)


def norm_rate(values):
    return lax.rsqrt(jnp.mean(values * values, axis=-1, keepdims=True) + NORM_EPS)


def norm_back(grad, unit, rate, gain):
    moved = grad * gain
    return rate * (moved - unit * jnp.mean(moved * unit, axis=-1, keepdims=True))


def gelu_product(gate, up):
    return jax.nn.gelu(gate) * up


def wide_dot(left, halves):
    cut = halves[0].shape[0]
    return dot(left[:, :cut], halves[0]) + dot(left[:, cut:], halves[1])


def wide_back(left, halves):
    return jnp.concatenate([dot(left, h, ((1,), (1,))) for h in halves], axis=1)


def on_device(size, n, tokens, lengths, gains, w_gelu, w_rec, chan, w_lru, w_out, w_mlp_in, w_down, cotangent):
    place = lax.axis_index("dp")
    turn = lax.axis_index("tensor")
    d_model = tokens.shape[1]
    rows = tokens.shape[0] // n
    half = rows // 2
    d_own = w_gelu.shape[0]
    heads_own, part, head = chan.shape[1], chan.shape[2], w_lru.shape[3]
    heads = heads_own * n
    width = heads * head
    groups = width // GROUP
    table, inverse = basis(size, d_own, place)
    live_count = (lengths - turn * rows).astype(jnp.int32)
    live = (lax.iota(jnp.int32, rows)[:, None] < live_count).astype(F32)

    cols = w_gelu.shape[1]
    pad = -(-part // 16) * 16
    own_lru = jnp.pad(w_lru.transpose(0, 2, 1, 3).reshape(2, part, cols), ((0, 0), (0, pad - part), (0, 0)))
    own_chan = jnp.zeros((8, heads_own, head), F32)
    own_chan = lax.dynamic_update_slice(own_chan, chan, (0, 0, place * part)).reshape(8, cols)
    own_gain = jnp.pad(gains.reshape(1, -1), ((0, 7), (0, cols - gains.size)))
    small = jnp.concatenate([own_lru.reshape(2 * pad, cols), own_chan, own_gain])
    whole = jnp.concatenate([w_rec, small]).astype(BF)
    others = jnp.concatenate([w_gelu, w_out.T]).astype(BF)
    own_gu = jnp.concatenate([w_mlp_in[0], w_mlp_in[1]], axis=1).astype(BF)
    own_dn = w_down.T.astype(BF)
    some_gu = spread_begin(own_gu, size)

    main = lax.dynamic_slice_in_dim(tokens, turn * rows, rows)
    before = lax.dynamic_slice_in_dim(tokens, jnp.maximum(turn * rows - HALO, 0), HALO)
    before = jnp.where(turn > 0, before, jnp.zeros_like(before))
    turned = permute_rows(jnp.concatenate([before, main]), table)
    extended = turned.astype(F32)
    first_rate = norm_rate(extended)

    def wide(blocks):
        return blocks.transpose(1, 0, 2).reshape(d_own, width)

    (whole,) = fence([lax.all_gather(whole, "tensor", axis=0)], *some_gu[1:], others, turned, first_rate)
    others = lax.all_gather(*fence([others], whole), "tensor", axis=0)
    z_gelu, z_out = wide(others[:, :d_own]), wide(others[:, d_own:])
    some_r = spread_begin(wide(whole[:, :d_own]), size)
    some_small = small_begin(whole[:, d_own:].reshape(-1, cols), size)
    small = small_end(some_small, size).reshape(size, n, -1, cols)

    masks = small_masks(size)
    gain = small[:, 0, 2 * pad + 8, : gains.size].reshape(size, 2, d_own)
    if squared(size, d_own):
        swapped = jnp.concatenate([gain[..., d_own // 2 :], gain[..., : d_own // 2]], axis=-1)
        gain = jnp.where(((jnp.asarray(masks) & 6) == 6)[:, None, None], swapped, gain)
    gain = gain.transpose(1, 0, 2).reshape(2, d_model).astype(F32)
    chans = jnp.sum(small[:, :, 2 * pad : 2 * pad + 8].astype(F32), axis=0)
    chans = chans.transpose(1, 0, 2).reshape(8, width)
    par = jnp.concatenate([chans[:7], -8.0 * jax.nn.softplus(-chans[7:])])
    each = n // groups
    lru = small
    if each > 1:
        lru = lru.reshape(size, groups, each, -1, cols).transpose(0, 1, 3, 2, 4).reshape(size, groups, -1, GROUP)
    spot = (place ^ jnp.asarray(masks))[jnp.arange(size * pad) // pad]
    row = jnp.arange(size * pad) % pad
    row = jnp.where(row < part, spot * part + row, head)
    order = (jnp.arange(head)[:, None] == row[None, :]).astype(BF)

    w_r, came_r = spread_end(some_r, size, (), (others, order))
    first = (extended * first_rate * gain[0]).astype(BF)
    inputs, first_own, first_rate = extended[HALO:], first[HALO:], first_rate[HALO:]
    cut = d_model // 2

    keep = (rows, width, F32)
    dense = ((GROUP, 2 * GROUP), BF)
    some_g = spread_begin(z_gelu, size, *came_r)
    rec_pre = wide_dot(first, w_r)
    conv, decay, ig, dg, state, prod = kernel_call(
        forward_kernel, live_count, [rec_pre, par, lru, order], [keep] * 6,
        [((rows + HALO, GROUP), F32), dense], "recurrence",
    )
    ends = jnp.concatenate([prod[-1:], state[-1:]])
    came = [z_shift(ends, k, n, False) for k in range(1, n)]
    w_g, came_g = spread_end(some_g, size, (ends,), came)
    carry = jnp.zeros((1, width), F32)
    for end in came[::-1]:
        carry = end[1:] + end[:1] * carry
    some_o = spread_begin(z_out, size, *came_g)
    branch_pre = wide_dot(first_own, w_g)
    recurrent = (state + prod * carry) * live
    mixed = (jax.nn.gelu(branch_pre) * recurrent).astype(BF)
    w_o, came_o = spread_end(some_o, size, (branch_pre,), (mixed,))
    hidden = inputs + wide_back(mixed, w_o)
    second_rate = norm_rate(hidden)
    second_unit = hidden * second_rate
    second_own = (second_unit * gain[1]).astype(BF)
    w_gu, came_gu = spread_end(some_gu, size, came_o, (second_own,))
    w_dn, _ = spread_end(spread_begin(own_dn, size, *came_gu), size, (), ())
    w_gu, w_dn = assemble(w_gu), assemble(w_dn)
    late = fence([table], second_own)[0]
    cots = [permute_rows(cotangent, late, half, 2, h) for h in range(2)]

    hidden_units = w_dn.shape[1]
    grad_products = [dot(c, w_dn) for c in cots]
    shares, grad_second, seconds, products, grads = [], [], [], [], []
    for h in range(2):
        second = lax.all_gather(second_own[h * half : (h + 1) * half], "tensor", axis=0, tiled=True)
        (second,) = fence([second], *shares)
        both = dot(second, w_gu)
        product, pull = jax.vjp(gelu_product, both[:, :hidden_units], both[:, hidden_units:])
        grad_gate, grad_up = pull(grad_products[h])
        product = product.astype(BF)
        grad = jnp.concatenate([grad_gate.astype(BF), grad_up.astype(BF)], axis=1)
        share = dot(grad, w_gu, ((1,), (1,))).astype(BF)
        shares.append(share)
        grad_second.append(lax.psum_scatter(share, "tensor", scatter_dimension=0, tiled=True))
        seconds.append(second)
        products.append(product)
        grads.append(grad)

    products, grads = [[*pair] for pair in zip(*[fence([p, g], shares[-1]) for p, g in zip(products, grads)])]
    shares = [dot(p, w_dn, ((1,), (1,))).astype(BF) for p in products]

    def by_rows(lefts, rights):
        parts = []
        for span in (slice(cut, None), slice(0, cut)):
            part = dot(lefts[0][:, span], rights[0], ((0,), (0,)))
            parts.append((part + dot(lefts[1][:, span], rights[1], ((0,), (0,)))).astype(BF))
        return Collect(parts[1], parts[0], size, d_own)

    sum_dn = by_rows(cots, products)
    sum_gu = by_rows(seconds, grads)
    sent_dn, sent_gu = sum_dn.sources(), sum_gu.sources()
    grad_second = fence(grad_second, *sent_dn, *sent_gu, *shares)
    came_mlp = sum_dn.hop(sent_dn) + sum_gu.hop(sent_gu)

    def mlp_result(h, mlp_sum):
        return permute_rows((hidden[h * half : (h + 1) * half] + mlp_sum.astype(F32)).astype(BF), inverse)

    shares = fence(shares, *grad_second)
    mlp_sums = [lax.psum_scatter(share, "tensor", scatter_dimension=0, tiled=True) for share in shares]

    grad_second = jnp.concatenate(grad_second).astype(F32)
    cot_own = jnp.concatenate([lax.dynamic_slice_in_dim(c, turn * half, half) for c in cots]).astype(F32)
    gain_two = jnp.sum(grad_second * second_unit, axis=0)
    grad_hidden = cot_own + norm_back(grad_second, second_unit, second_rate, gain[1])
    hidden_low = grad_hidden.astype(BF)

    def by_cols(left, right):
        parts = [dot(left[:, span], right, ((0,), (0,))).astype(BF) for span in (slice(cut, None), slice(0, cut))]
        return Collect(parts[1], parts[0], size, d_own)

    grad_mixed = wide_dot(hidden_low, w_o)
    tall = jnp.broadcast_to
    lam, reach, edge, pre_low = kernel_call(
        back_scan_kernel, live_count, [branch_pre, grad_mixed, decay, state, prod, tall(carry, (SLAB, width))],
        [keep, keep, (SLAB, width, F32), (rows, width, BF)], [], "back_scan",
    )
    edges = jnp.concatenate([prod[-1:], edge[:1]])
    came = [z_shift(edges, -k, n, False) for k in range(1, n)]
    arriving = jnp.zeros((1, width), F32)
    for end in came[::-1]:
        arriving = end[1:] + end[:1] * arriving
    (lam,) = fence([lam], *came_mlp)
    drec, dpar, d_lru = kernel_call(
        backward_kernel, live_count,
        [rec_pre, par, lru, order, lam, reach, tall(arriving, (SLAB, width)), decay, conv, ig, dg, state, prod, tall(carry, (SLAB, width))],
        [(rows + HALO, width, F32), (8, width, F32), (head, 2 * GROUP, BF)],
        [((rows + HALO, GROUP), F32), ((rows + 2 * HALO, GROUP), F32), ((rows + SLAB, GROUP), F32), ((GROUP, 2 * GROUP), F32), dense],
        "recurrence_back",
    )
    (edge_rows,) = fence([z_shift(drec[:HALO], -1, n, False)], mlp_sums[0])
    rec_low = (drec[HALO:] + jnp.pad(edge_rows, ((rows - HALO, 0), (0, 0)))) * live
    rec_low = rec_low.astype(BF)
    (pre_low,) = fence([pre_low], drec)
    grad_first = wide_back(pre_low, w_g) + wide_back(rec_low, w_r)
    first_unit = inputs * first_rate
    gain_one = jnp.sum(grad_first * first_unit, axis=0)
    grad_tokens = grad_hidden + norm_back(grad_first, first_unit, first_rate, gain[0])
    grad_tokens = permute_rows(grad_tokens.astype(BF), inverse)
    gathered = [lax.all_gather(grad_tokens[h * half : (h + 1) * half], "tensor", axis=0) for h in range(2)]
    (mixed,) = fence([mixed], grad_tokens)
    sum_o = by_cols(hidden_low, mixed)
    pre_low, rec_low = fence([pre_low, rec_low], sum_o.terms[1])
    sum_g, sum_r = by_cols(first_own, pre_low), by_cols(first_own, rec_low)
    results = [mlp_result(h, mlp_sum) for h, mlp_sum in enumerate(fence(mlp_sums, sum_o.terms[1]))]
    got_o = sum_o.hop(sum_o.sources())
    got_g = sum_g.hop(fence(sum_g.sources(), *got_o))
    pause = (gathered[0], *got_g)
    sum_o.hop(fence(sum_o.sources(), *pause))
    got_r = sum_r.hop(fence(sum_r.sources(), *pause))
    results = fence(results, gathered[0], *got_g)
    results = [lax.all_gather(result, "tensor", axis=0) for result in results]
    sum_g.hop(fence(sum_g.sources(), *pause))
    got_r = sum_r.hop(fence(sum_r.sources(), *got_r))
    owned = jnp.stack([total.finish().reshape(d_own, n, width // n) for total in (sum_o, sum_g, sum_r)])
    owned = LineSum(owned.transpose(2, 0, 1, 3), n)
    owned.go()
    pause = (gathered[1], owned.right, owned.left)
    d_lru, dpar = fence([d_lru, dpar], *pause)
    if sum_dn.square:
        sum_dn.hop(fence(sum_dn.sources(), *pause))
        sum_gu.hop(fence(sum_gu.sources(), *pause))
    owned.go(gathered[1])
    tokens_out = interleave(*fence(gathered, owned.right)).reshape(n * rows, d_model)
    if n > 3:
        owned.go(results[0])
    g_gu, g_dn = sum_gu.finish().astype(F32), sum_dn.finish().astype(F32)
    g_all = owned.finish()
    output = interleave(*fence(results, owned.right, owned.left)).reshape(n * rows, d_model)
    g_o, g_g, g_r = g_all[0], g_all[1], g_all[2]

    d_gain = permute_gain(jnp.stack([gain_one, gain_two]), inverse)
    d_chan = jnp.concatenate([dpar[:7], dpar[7:] * 8.0 * jax.nn.sigmoid(-chans[7:])])
    d_lru = d_lru.reshape(groups, size, part, 2, each, -1).transpose(1, 0, 4, 2, 3, 5)
    d_chan = d_chan.reshape(8, n, heads_own, size, part).transpose(3, 1, 0, 2, 4)
    d_gain = d_gain.reshape(2, size, 1, d_own).transpose(1, 2, 0, 3)
    d_gain = jnp.broadcast_to(d_gain, (size, n, 2, d_own))
    small = [v.reshape(size, n, -1).astype(BF) for v in (d_lru, d_chan, d_gain)]
    small = small_scatter(jnp.concatenate(small, axis=2), size, n)
    d_lru = small[: w_lru.size].reshape(part, 2, heads_own, head).transpose(1, 2, 0, 3)
    d_chan = small[w_lru.size : -gains.size].reshape(chan.shape)
    d_gain = small[-gains.size :].reshape(gains.shape)
    g_gate, g_up = g_gu[:, :hidden_units], g_gu[:, hidden_units:]
    return (
        output, tokens_out, d_gain[0], d_gain[1], g_g, g_r, d_chan, d_lru,
        g_o.T, jnp.stack([g_gate, g_up]), g_dn.T,
    )


def solution(mesh):
    in_specs = (
        P("dp", None),
        P("dp"),
        P(None, "dp"),
        P("dp", "tensor"),
        P("dp", "tensor"),
        P(None, "tensor", "dp"),
        P(None, "tensor", "dp", None),
        P("tensor", "dp"),
        P(None, "dp", "tensor"),
        P("tensor", "dp"),
        P("dp", None),
    )
    out_specs = (
        P("dp", None),
        P("dp", None),
        P("dp"),
        P("dp"),
        P("dp", "tensor"),
        P("dp", "tensor"),
        P(None, "tensor", "dp"),
        P(None, "tensor", "dp", None),
        P("tensor", "dp"),
        P(None, "dp", "tensor"),
        P("tensor", "dp"),
    )
    body = functools.partial(on_device, mesh.shape["dp"], mesh.shape["tensor"])
    return jax.shard_map(body, mesh=mesh, in_specs=in_specs, out_specs=out_specs, check_vma=False)
```

```python
import functools

import jax
import jax.numpy as jnp
import numpy as np
from jax import lax
from jax.experimental import pallas as pl
from jax.experimental.pallas import tpu as pltpu
from jax.sharding import PartitionSpec as P

NORM_EPS = 1e-06
DECAY_FLOOR = 0.05
HALO = 16
GROUP = 640
ROWS = 128
SLAB = 8
VMEM = 58 * 1024 * 1024
BF = jnp.bfloat16
F32 = jnp.float32
LITTLE = pl.CostEstimate(flops=1024, bytes_accessed=1024, transcendentals=0)


def dot(left, right, dims=((1,), (0,))):
    return lax.dot_general(left, right, (dims, ((), ())), preferred_element_type=F32)


def fence(values, *others):
    if not others:
        return list(values)
    place = pl.BlockSpec(memory_space=pl.ANY)
    call = pl.pallas_call(
        lambda *refs: None,
        in_specs=[place] * (len(values) + len(others)),
        out_specs=[place] * len(values),
        out_shape=[jax.ShapeDtypeStruct(v.shape, v.dtype) for v in values],
        input_output_aliases={k: k for k in range(len(values))},
        compiler_params=pltpu.CompilerParams(vmem_limit_bytes=VMEM),
        name="fence",
    )
    return list(call(*values, *others))


def assemble(pieces, *others):
    count = len(pieces)
    rows = [p.shape[0] for p in pieces]
    spans = [pl.ds(sum(rows[:k]), rows[k]) for k in range(count)]
    shape = (sum(rows), pieces[0].shape[1])

    def body(*refs):
        out, held, coming, going = refs[count + len(others) :]
        ins = [pltpu.make_async_copy(refs[k], held.at[spans[k]], coming.at[k]) for k in range(count)]
        outs = [pltpu.make_async_copy(held.at[spans[k]], out.at[spans[k]], going.at[k]) for k in range(count)]
        for copy in ins:
            copy.start()
        for here, there in zip(ins, outs):
            here.wait()
            there.start()
        for copy in outs:
            copy.wait()

    place = pl.BlockSpec(memory_space=pl.ANY)
    return pl.pallas_call(
        body,
        in_specs=[place] * (count + len(others)),
        out_specs=place,
        out_shape=jax.ShapeDtypeStruct(shape, pieces[0].dtype),
        scratch_shapes=[
            pltpu.VMEM(shape, pieces[0].dtype),
            pltpu.SemaphoreType.DMA((count,)),
            pltpu.SemaphoreType.DMA((count,)),
        ],
        compiler_params=pltpu.CompilerParams(vmem_limit_bytes=VMEM),
        cost_estimate=LITTLE,
        name="assemble",
    )(*pieces, *others)


def swap(values, mask, size):
    return lax.ppermute(values, "dp", [(k, k ^ mask) for k in range(size)])


def exchange(values, bit, size):
    return swap(values, 1 << bit, size)


def squared(size, rows):
    return size == 8 and rows % 256 == 0


def spread_begin(own, size, *before):
    (own,) = fence([own], *before)
    if squared(size, own.shape[0]):
        return [own, exchange(own, 1, size), exchange(own, 2, size)]
    pieces = own
    for bit in range(1, size.bit_length() - 2):
        pieces = jnp.concatenate([pieces, exchange(pieces, bit, size)])
    return [pieces]


def spread_end(some, size, before_last, before_core):
    if len(some) > 1:
        own, by_x, by_y = some
        unit = own.shape[0] // 2
        by_x, by_y = fence([by_x, by_y], *before_last)
        got = [exchange(by_x[:unit], 2, size), exchange(by_y[unit:], 1, size)]
        half = assemble([own, by_x, got[1], got[0], by_y], *before_core)
    else:
        (pieces,) = fence(some, *before_last)
        got = [exchange(pieces, size.bit_length() - 2, size)]
        half = jnp.concatenate([pieces] + fence(got, *before_core))
    return [half, exchange(half, 0, size)], got


def add_all(terms):
    total = terms[0].astype(F32)
    for term in terms[1:]:
        total = total + term.astype(F32)
    return total.astype(BF)


class Collect:
    def __init__(self, keep, send, size, d_own):
        self.size, self.unit = size, d_own // 2
        self.square = squared(size, d_own)
        self.bit = size.bit_length() - 2
        self.terms = [keep, exchange(send, 0, size)]
        self.first = self.last = None

    def rows(self, start, stop):
        return [t[start * self.unit : stop * self.unit] for t in self.terms]

    def sources(self):
        if not self.square:
            cut = self.terms[0].shape[0] // 2
            return [add_all([t[cut:] for t in self.terms])]
        if self.first is None:
            return [add_all(self.rows(3, 5)), add_all(self.rows(5, 7))]
        by_x, by_y = self.first
        return [add_all(self.rows(2, 3) + [by_y[: self.unit]]), add_all(self.rows(7, 8) + [by_x[self.unit :]])]

    def hop(self, sources):
        if not self.square:
            got = exchange(sources[0], self.bit, self.size)
            self.bit -= 1
            self.terms = [t[: got.shape[0]] for t in self.terms] + [got]
            return [got]
        got = [exchange(v, bit, self.size) for v, bit in zip(sources, (1, 2))]
        if self.first is None:
            self.first = got
        else:
            self.last = got
        return got

    def finish(self):
        if not self.square:
            while self.bit:
                self.hop(self.sources())
            return add_all(self.terms)
        low = add_all(self.rows(0, 1) + [self.first[1][self.unit :], self.last[0]])
        high = add_all(self.rows(1, 2) + [self.first[0][: self.unit], self.last[1]])
        return jnp.concatenate([low, high])


def z_shift(values, by, n, around=True):
    pairs = [(k, (k + by) % n) for k in range(n) if around or 0 <= k + by < n]
    return lax.ppermute(values, "tensor", pairs)


def z_scatter(values, n):
    turn = lax.axis_index("tensor")
    total = lax.dynamic_index_in_dim(values, turn, 0, keepdims=False).astype(F32)
    for k in range(1, n):
        block = lax.dynamic_index_in_dim(values, (turn + k) % n, 0, keepdims=False)
        total = total + z_shift(block, k, n).astype(F32)
    return total


class LineSum:
    def __init__(self, blocks, n):
        self.blocks, self.n, self.turn, self.rounds = blocks, n, lax.axis_index("tensor"), 0
        self.right = self.left = None

    def block(self, k):
        return lax.dynamic_index_in_dim(self.blocks, k % self.n, 0, keepdims=False)

    def go(self, *others):
        self.rounds += 1
        t, n = self.rounds, self.n
        right, left = self.block(self.turn + n - t), self.block(self.turn + t)
        if t > 1:
            before = fence([self.right, self.left], *others)
            right, left = add_all([right, before[0]]), add_all([left, before[1]])
        self.right = lax.ppermute(right, "tensor", [(k, k + 1) for k in range(min(t, n - 1))])
        self.left = lax.ppermute(left, "tensor", [(k, k - 1) for k in range(max(n - t, 1), n)])

    def finish(self):
        while self.rounds < self.n - 1:
            self.go()
        return self.block(self.turn).astype(F32) + self.right.astype(F32) + self.left.astype(F32)


def small_masks(size):
    turns = (0, 2, 6, 4) if size == 8 else tuple(q << 1 for q in range(size // 2))
    return np.array([core | mask for core in range(2) for mask in turns], np.int32)


def small_begin(own, size):
    if size == 8:
        return [own] + [swap(own, mask, size) for mask in (2, 6, 4)]
    rows = own[None]
    for bit in range(1, size.bit_length() - 1):
        rows = jnp.concatenate([rows, exchange(rows, bit, size)])
    return [rows]


def small_end(some, size):
    if size == 8:
        rows = jnp.stack(some)
    else:
        (rows,) = some
    return jnp.concatenate([rows, exchange(rows, 0, size)])


def small_scatter(values, size, n):
    place = lax.axis_index("dp")
    values = jnp.take(values, jnp.arange(size) ^ place, axis=0, mode="clip")
    for bit in reversed(range(size.bit_length() - 1)):
        half = values.shape[0] // 2
        values = add_all([values[:half], exchange(values[half:], bit, size)])
    return z_scatter(values[0], n)


def basis_spots(size, rows):
    if squared(size, rows):
        turns = ((0, 0), (0, 1), (2, 0), (2, 1), (6, 1), (6, 0), (4, 0), (4, 1))
        return [(core | mask, part) for core in range(2) for mask, part in turns], 2
    return [(core | q << 1, 0) for core in range(2) for q in range(size // 2)], 1


def basis(size, rows, place):
    spots, parts = basis_spots(size, rows)
    masks, which = (jnp.asarray(np.array(v, np.int32)) for v in zip(*spots))
    table = (place ^ masks) * parts + which
    spots = jnp.arange(table.shape[0], dtype=jnp.int32)
    inverse = jnp.sum(jnp.where(table[None, :] == spots[:, None], spots[None, :], 0), axis=1)
    return table, inverse.astype(jnp.int32)


def copy_kernel(blocks, table_ref, in_ref, out_ref):
    width = in_ref.shape[1] // blocks
    for p in range(blocks):
        start = pl.multiple_of(table_ref[p] * width, width)
        out_ref[:, p * width : (p + 1) * width] = in_ref[:, pl.ds(start, width)]


def permute_rows(values, table, step=0, stride=1, offset=0):
    rows, d_model = values.shape
    step = step or max(k for k in range(16, 289, 16) if rows % k == 0)
    return pl.pallas_call(
        functools.partial(copy_kernel, table.shape[0]),
        grid_spec=pltpu.PrefetchScalarGridSpec(
            num_scalar_prefetch=1,
            grid=(rows // (step * stride),),
            in_specs=[pl.BlockSpec((step, d_model), lambda r, tab: (r * stride + offset, 0))],
            out_specs=pl.BlockSpec((step, d_model), lambda r, tab: (r, 0)),
        ),
        out_shape=jax.ShapeDtypeStruct((rows // stride, d_model), values.dtype),
        compiler_params=pltpu.CompilerParams(vmem_limit_bytes=VMEM),
        cost_estimate=LITTLE,
        name="permute",
    )(table, values)


def interleave_kernel(one_ref, two_ref, out_ref):
    out_ref[0] = one_ref[...]
    out_ref[1] = two_ref[...]


def interleave(one, two):
    n, rows, d_model = one.shape
    spec = pl.BlockSpec((pl.squeezed, rows, d_model), lambda j: (j, 0, 0))
    return pl.pallas_call(
        interleave_kernel,
        grid=(n,),
        in_specs=[spec, spec],
        out_specs=pl.BlockSpec((pl.squeezed, 2, rows, d_model), lambda j: (j, 0, 0, 0)),
        out_shape=jax.ShapeDtypeStruct((n, 2, rows, d_model), one.dtype),
        compiler_params=pltpu.CompilerParams(vmem_limit_bytes=VMEM),
        cost_estimate=LITTLE,
        name="interleave",
    )(one, two)


def permute_gain(values, table):
    lead = values.shape[0]
    return jnp.take(values.reshape(lead, table.shape[0], -1), table, axis=1, mode="clip").reshape(lead, -1)


def row_ids(count, width, first):
    return lax.broadcasted_iota(jnp.int32, (count, width), 0) + first


def scan_slab(decay, value, back):
    rows = row_ids(SLAB, decay.shape[1], 0)
    for step in (1, 2, 4):
        keep = rows < SLAB - step if back else rows >= step
        shift = SLAB - step if back else step
        moved_decay = pltpu.roll(decay, shift, 0)
        moved_value = pltpu.roll(value, shift, 0)
        value = jnp.where(keep, value + decay * moved_value, value)
        decay = jnp.where(keep, decay * moved_decay, decay)
    return decay, value


def head_mask(head, at, width):
    lanes = lax.broadcasted_iota(jnp.int32, (head, 2 * width), 1)
    lanes = jnp.where(lanes >= width, lanes - width, lanes)
    return (lanes >= at * head) & (lanes < (at + 1) * head)


def fill_dense(w_ref, order_ref, dense_ref):
    head, count = order_ref.shape
    pad = count // w_ref.shape[0]
    width = dense_ref.shape[0]
    for gate in range(2):
        rows = w_ref[:, gate * pad : (gate + 1) * pad, :].reshape(count, width)
        rows = dot(order_ref[...], rows)
        for k in range(width // head):
            lanes = lax.broadcasted_iota(jnp.int32, (head, width), 1)
            block = jnp.where((lanes >= k * head) & (lanes < (k + 1) * head), rows, 0.0)
            dense_ref[k * head : (k + 1) * head, gate * width : (gate + 1) * width] = block.astype(BF)


def forward_kernel(
    live_ref, pre_ref, par_ref, w_ref, order_ref, conv_ref, decay_ref, ig_ref, dg_ref, state_ref, prod_ref,
    rec_ref, dense_ref,
):
    rows, width = conv_ref.shape
    fill_dense(w_ref, order_ref, dense_ref)
    live = live_ref[0]
    rec_ref[...] = jnp.where(row_ids(rows + HALO, width, -HALO) < live, pre_ref[...], 0.0)
    par = [par_ref[k : k + 1, :] for k in range(8)]
    for at in range(0, rows, ROWS):
        span = pl.ds(at, ROWS)
        near = rec_ref[pl.ds(at, ROWS + HALO), :]
        conv = par[4] + par[0] * near[HALO : HALO + ROWS]
        for k in range(1, 4):
            conv = conv + par[k] * near[HALO - k : HALO - k + ROWS]
        conv = jnp.where(row_ids(ROWS, width, at) < live, conv, 0.0)
        conv_ref[span, :] = conv
        gates = dot(conv.astype(BF), dense_ref[...])
        ig = lax.logistic(gates[:, :width] + par[5])
        dg = lax.logistic(gates[:, width:] + par[6])
        decay = jnp.exp(dg * par[7])
        ig_ref[span, :] = ig
        dg_ref[span, :] = dg
        decay_ref[span, :] = decay
        state_ref[span, :] = jnp.sqrt(jnp.maximum(1.0 - decay * decay, DECAY_FLOOR)) * ig * conv

    def slab(k, carry):
        state, prod = carry
        for inner in range(4):
            span = pl.ds(pl.multiple_of(k * 4 * SLAB + inner * SLAB, SLAB), SLAB)
            decay, value = scan_slab(decay_ref[span, :], state_ref[span, :], False)
            value = value + decay * state
            decay = decay * prod
            state_ref[span, :] = value
            prod_ref[span, :] = decay
            state = jnp.broadcast_to(value[SLAB - 1 :, :], (SLAB, width))
            prod = jnp.broadcast_to(decay[SLAB - 1 :, :], (SLAB, width))
        return state, prod

    lax.fori_loop(0, rows // (4 * SLAB), slab, (jnp.zeros((SLAB, width), F32), jnp.ones((SLAB, width), F32)))


def back_scan_kernel(
    live_ref, pre_ref, grad_ref, decay_ref, state_ref, prod_ref, cin_ref, lam_ref, reach_ref, edge_ref, low_ref
):
    rows, width = grad_ref.shape
    live = live_ref[0]
    cin = cin_ref[:1, :]
    c = np.float32(np.sqrt(2 / np.pi))
    for at in range(0, rows, ROWS):
        span = pl.ds(at, ROWS)
        v, grad = pre_ref[span, :], grad_ref[span, :]
        square = v * v
        bend = jnp.tanh(v * (c + (c * 0.044715) * square))
        rise = 0.5 + 0.5 * bend
        slope = rise + 0.5 * v * (1.0 - bend * bend) * (c + (3 * c * 0.044715) * square)
        grad = jnp.where(row_ids(ROWS, width, at) < live, grad, 0.0)
        lam_ref[span, :] = grad * (v * rise)
        low_ref[span, :] = (grad * (state_ref[span, :] + prod_ref[span, :] * cin) * slope).astype(BF)
    last = row_ids(SLAB, width, 0) == SLAB - 1

    def slab(k, carry):
        lam, reach, following, _ = carry
        for inner in range(4):
            span = pl.ds(pl.multiple_of(rows - (k * 4 + inner + 1) * SLAB, SLAB), SLAB)
            own = decay_ref[span, :]
            ahead = jnp.where(last, following, pltpu.roll(own, SLAB - 1, 0))
            decay, value = scan_slab(ahead, lam_ref[span, :], True)
            value = value + decay * lam
            decay = decay * reach
            lam_ref[span, :] = value
            reach_ref[span, :] = decay
            lam = jnp.broadcast_to(value[:1, :], (SLAB, width))
            reach = jnp.broadcast_to(decay[:1, :], (SLAB, width))
            following = jnp.broadcast_to(own[:1, :], (SLAB, width))
        return lam, reach, following, own

    one = jnp.ones((SLAB, width), F32)
    zero = jnp.zeros((SLAB, width), F32)
    lam, _, following, _ = lax.fori_loop(0, rows // (4 * SLAB), slab, (zero, one, one, one))
    edge_ref[...] = lam * following


def backward_kernel(
    live_ref, pre_ref, par_ref, w_ref, order_ref, lam_ref, reach_ref, edge_ref, decay_ref, conv_ref, ig_ref, dg_ref, state_ref, prod_ref, cin_ref,
    drec_ref, dpar_ref, dw_ref, rec_ref, dconv_ref, full_ref, dw_acc, dense_ref,
):
    rows, width = conv_ref.shape
    live = live_ref[0]
    rec_ref[...] = jnp.where(row_ids(rows + HALO, width, -HALO) < live, pre_ref[...], 0.0)
    par = [par_ref[k : k + 1, :] for k in range(8)]
    fill_dense(w_ref, order_ref, dense_ref)
    cin = cin_ref[:1, :]
    edge = edge_ref[:1, :]
    full_ref[:SLAB, :] = jnp.broadcast_to(cin, (SLAB, width))
    dconv_ref[:HALO, :] = jnp.zeros((HALO, width), F32)
    dconv_ref[rows + HALO :, :] = jnp.zeros((HALO, width), F32)
    sums = [jnp.zeros((1, width), F32) for _ in range(8)]
    for at in range(0, rows, ROWS):
        span = pl.ds(at, ROWS)
        full_ref[pl.ds(at + SLAB, ROWS), :] = state_ref[span, :] + prod_ref[span, :] * cin
        lam = lam_ref[span, :] + reach_ref[span, :] * edge
        decay, conv, ig, dg = decay_ref[span, :], conv_ref[span, :], ig_ref[span, :], dg_ref[span, :]
        before = full_ref[pl.ds(at, ROWS + SLAB), :][SLAB - 1 : SLAB - 1 + ROWS]
        room = 1.0 - decay * decay
        scale = jnp.sqrt(jnp.maximum(room, DECAY_FLOOR))
        lam_conv = lam * conv
        d_decay = lam * before - jnp.where(room > DECAY_FLOOR, lam_conv * ig * decay / scale, 0.0)
        moved = d_decay * decay
        sums[7] = sums[7] + jnp.sum(moved * dg, axis=0, keepdims=True)
        d_ig = lam_conv * scale * ig * (1.0 - ig)
        d_dg = moved * par[7] * dg * (1.0 - dg)
        sums[5] = sums[5] + jnp.sum(d_ig, axis=0, keepdims=True)
        sums[6] = sums[6] + jnp.sum(d_dg, axis=0, keepdims=True)
        both = jnp.concatenate([d_ig.astype(BF), d_dg.astype(BF)], axis=1)
        d_conv = lam * scale * ig + dot(both, dense_ref[...], ((1,), (1,)))
        d_conv = jnp.where(row_ids(ROWS, width, at) < live, d_conv, 0.0)
        dconv_ref[pl.ds(at + HALO, ROWS), :] = d_conv
        part = dot(conv.astype(BF), both, ((0,), (0,)))
        dw_acc[...] = part if at == 0 else dw_acc[...] + part
        near = rec_ref[pl.ds(at, ROWS + HALO), :]
        for k in range(4):
            sums[k] = sums[k] + jnp.sum(d_conv * near[HALO - k : HALO - k + ROWS], axis=0, keepdims=True)
        sums[4] = sums[4] + jnp.sum(d_conv, axis=0, keepdims=True)
    for k in range(8):
        dpar_ref[k : k + 1, :] = sums[k]
    head = dw_ref.shape[0]
    total = jnp.zeros((head, 2 * width), F32)
    for k in range(width // head):
        total = total + jnp.where(head_mask(head, k, width), dw_acc[k * head : (k + 1) * head, :], 0.0)
    dw_ref[...] = total.astype(BF)
    for at in list(range(0, rows, ROWS)) + [rows]:
        count = ROWS if at < rows else HALO
        near = dconv_ref[pl.ds(at, count + SLAB), :]
        total = par[0] * near[:count]
        for k in range(1, 4):
            total = total + par[k] * near[k : k + count]
        drec_ref[pl.ds(at, count), :] = total


def kernel_call(body, live, arrays, outs, scratch, name):
    width = outs[0][1]
    steps = width // GROUP
    specs = []
    for array in arrays:
        if array.ndim == 4:
            block = (array.shape[0], pl.squeezed) + array.shape[2:]
            specs.append(pl.BlockSpec(block, lambda j, s: (0, j, 0, 0)))
        elif array.shape[1] != width:
            specs.append(pl.BlockSpec(array.shape, lambda j, s: (0, 0)))
        else:
            specs.append(pl.BlockSpec((array.shape[0], GROUP), lambda j, s: (0, j)))
    out_specs, out_shapes = [], []
    for rows, cols, kind in outs:
        if cols == width:
            out_specs.append(pl.BlockSpec((rows, GROUP), lambda j, s: (0, j)))
            out_shapes.append(jax.ShapeDtypeStruct((rows, cols), kind))
        else:
            out_specs.append(pl.BlockSpec((pl.squeezed, rows, cols), lambda j, s: (j, 0, 0)))
            out_shapes.append(jax.ShapeDtypeStruct((steps, rows, cols), kind))
    return pl.pallas_call(
        body,
        grid_spec=pltpu.PrefetchScalarGridSpec(
            num_scalar_prefetch=1, grid=(steps,), in_specs=specs, out_specs=out_specs,
            scratch_shapes=[pltpu.VMEM(shape, kind) for shape, kind in scratch],
        ),
        out_shape=out_shapes,
        compiler_params=pltpu.CompilerParams(vmem_limit_bytes=VMEM),
        cost_estimate=LITTLE,
        name=name,
    )(live, *arrays)


def norm_rate(values):
    return lax.rsqrt(jnp.mean(values * values, axis=-1, keepdims=True) + NORM_EPS)


def norm_back(grad, unit, rate, gain):
    moved = grad * gain
    return rate * (moved - unit * jnp.mean(moved * unit, axis=-1, keepdims=True))


def gelu_product(gate, up):
    return jax.nn.gelu(gate) * up


def wide_dot(left, halves):
    cut = halves[0].shape[0]
    return dot(left[:, :cut], halves[0]) + dot(left[:, cut:], halves[1])


def wide_back(left, halves):
    return jnp.concatenate([dot(left, h, ((1,), (1,))) for h in halves], axis=1)


def on_device(size, n, tokens, lengths, gains, w_gelu, w_rec, chan, w_lru, w_out, w_mlp_in, w_down, cotangent):
    place = lax.axis_index("dp")
    turn = lax.axis_index("tensor")
    d_model = tokens.shape[1]
    rows = tokens.shape[0] // n
    half = rows // 2
    d_own = w_gelu.shape[0]
    heads_own, part, head = chan.shape[1], chan.shape[2], w_lru.shape[3]
    heads = heads_own * n
    width = heads * head
    groups = width // GROUP
    table, inverse = basis(size, d_own, place)
    live_count = (lengths - turn * rows).astype(jnp.int32)
    live = (lax.iota(jnp.int32, rows)[:, None] < live_count).astype(F32)

    cols = w_gelu.shape[1]
    pad = -(-part // 16) * 16
    own_lru = jnp.pad(w_lru.transpose(0, 2, 1, 3).reshape(2, part, cols), ((0, 0), (0, pad - part), (0, 0)))
    own_chan = jnp.zeros((8, heads_own, head), F32)
    own_chan = lax.dynamic_update_slice(own_chan, chan, (0, 0, place * part)).reshape(8, cols)
    own_gain = jnp.pad(gains.reshape(1, -1), ((0, 7), (0, cols - gains.size)))
    small = jnp.concatenate([own_lru.reshape(2 * pad, cols), own_chan, own_gain])
    whole = jnp.concatenate([w_rec, small]).astype(BF)
    others = jnp.concatenate([w_gelu, w_out.T]).astype(BF)
    own_gu = jnp.concatenate([w_mlp_in[0], w_mlp_in[1]], axis=1).astype(BF)
    own_dn = w_down.T.astype(BF)
    some_gu = spread_begin(own_gu, size)

    main = lax.dynamic_slice_in_dim(tokens, turn * rows, rows)
    before = lax.dynamic_slice_in_dim(tokens, jnp.maximum(turn * rows - HALO, 0), HALO)
    before = jnp.where(turn > 0, before, jnp.zeros_like(before))
    turned = permute_rows(jnp.concatenate([before, main]), table)
    extended = turned.astype(F32)
    first_rate = norm_rate(extended)

    def wide(blocks):
        return blocks.transpose(1, 0, 2).reshape(d_own, width)

    (whole,) = fence([lax.all_gather(whole, "tensor", axis=0)], *some_gu[1:], others, turned, first_rate)
    others = lax.all_gather(*fence([others], whole), "tensor", axis=0)
    z_gelu, z_out = wide(others[:, :d_own]), wide(others[:, d_own:])
    some_r = spread_begin(wide(whole[:, :d_own]), size)
    some_small = small_begin(whole[:, d_own:].reshape(-1, cols), size)
    small = small_end(some_small, size).reshape(size, n, -1, cols)

    masks = small_masks(size)
    gain = small[:, 0, 2 * pad + 8, : gains.size].reshape(size, 2, d_own)
    if squared(size, d_own):
        swapped = jnp.concatenate([gain[..., d_own // 2 :], gain[..., : d_own // 2]], axis=-1)
        gain = jnp.where(((jnp.asarray(masks) & 6) == 6)[:, None, None], swapped, gain)
    gain = gain.transpose(1, 0, 2).reshape(2, d_model).astype(F32)
    chans = jnp.sum(small[:, :, 2 * pad : 2 * pad + 8].astype(F32), axis=0)
    chans = chans.transpose(1, 0, 2).reshape(8, width)
    par = jnp.concatenate([chans[:7], -8.0 * jax.nn.softplus(-chans[7:])])
    each = n // groups
    lru = small
    if each > 1:
        lru = lru.reshape(size, groups, each, -1, cols).transpose(0, 1, 3, 2, 4).reshape(size, groups, -1, GROUP)
    spot = (place ^ jnp.asarray(masks))[jnp.arange(size * pad) // pad]
    row = jnp.arange(size * pad) % pad
    row = jnp.where(row < part, spot * part + row, head)
    order = (jnp.arange(head)[:, None] == row[None, :]).astype(BF)

    w_r, came_r = spread_end(some_r, size, (), (z_gelu, order))
    first = (extended * first_rate * gain[0]).astype(BF)
    inputs, first_own, first_rate = extended[HALO:], first[HALO:], first_rate[HALO:]
    cut = d_model // 2

    keep = (rows, width, F32)
    dense = ((GROUP, 2 * GROUP), BF)
    some_g = spread_begin(z_gelu, size, *came_r)
    rec_pre = dot(first[:, :cut], w_r[0])
    w_r[1:] = fence(w_r[1:], *some_g[1:], rec_pre)
    rec_pre = rec_pre + dot(first[:, cut:], w_r[1])
    conv, decay, ig, dg, state, prod = kernel_call(
        forward_kernel, live_count, [rec_pre, par, lru, order], [keep] * 6,
        [((rows + HALO, GROUP), F32), dense], "recurrence",
    )
    ends = jnp.concatenate([prod[-1:], state[-1:]])
    came = [z_shift(ends, k, n, False) for k in range(1, n)]
    w_g, came_g = spread_end(some_g, size, (), came)
    carry = jnp.zeros((1, width), F32)
    for end in came[::-1]:
        carry = end[1:] + end[:1] * carry
    some_o = spread_begin(z_out, size, *came_g)
    branch_pre = wide_dot(first_own, w_g)
    recurrent = (state + prod * carry) * live
    mixed = (jax.nn.gelu(branch_pre) * recurrent).astype(BF)
    w_o, came_o = spread_end(some_o, size, (branch_pre,), (mixed,))
    hidden = inputs + wide_back(mixed, w_o)
    second_rate = norm_rate(hidden)
    second_unit = hidden * second_rate
    second_own = (second_unit * gain[1]).astype(BF)
    w_gu, came_gu = spread_end(some_gu, size, came_o, (second_own,))
    w_dn, _ = spread_end(spread_begin(own_dn, size, *came_gu), size, (), ())
    w_gu, w_dn = assemble(w_gu), assemble(w_dn)
    late = fence([table], second_own)[0]
    cots = [permute_rows(cotangent, late, half, 2, h) for h in range(2)]

    hidden_units = w_dn.shape[1]
    grad_products = [dot(c, w_dn) for c in cots]
    shares, grad_second, seconds, products, grads = [], [], [], [], []
    for h in range(2):
        second = lax.all_gather(second_own[h * half : (h + 1) * half], "tensor", axis=0, tiled=True)
        (second,) = fence([second], *shares)
        both = dot(second, w_gu)
        product, pull = jax.vjp(gelu_product, both[:, :hidden_units], both[:, hidden_units:])
        grad_gate, grad_up = pull(grad_products[h])
        product = product.astype(BF)
        grad = jnp.concatenate([grad_gate.astype(BF), grad_up.astype(BF)], axis=1)
        share = dot(grad, w_gu, ((1,), (1,))).astype(BF)
        shares.append(share)
        grad_second.append(lax.psum_scatter(share, "tensor", scatter_dimension=0, tiled=True))
        seconds.append(second)
        products.append(product)
        grads.append(grad)

    products, grads = [[*pair] for pair in zip(*[fence([p, g], shares[-1]) for p, g in zip(products, grads)])]
    shares = [dot(p, w_dn, ((1,), (1,))).astype(BF) for p in products]

    def by_rows(lefts, rights):
        parts = []
        for span in (slice(cut, None), slice(0, cut)):
            part = dot(lefts[0][:, span], rights[0], ((0,), (0,)))
            parts.append((part + dot(lefts[1][:, span], rights[1], ((0,), (0,)))).astype(BF))
        return Collect(parts[1], parts[0], size, d_own)

    sum_dn = by_rows(cots, products)
    sum_gu = by_rows(seconds, grads)
    sent_dn, sent_gu = sum_dn.sources(), sum_gu.sources()
    grad_second = fence(grad_second, *sent_dn, *sent_gu, *shares)
    came_mlp = sum_dn.hop(sent_dn) + sum_gu.hop(sent_gu)

    def mlp_result(h, mlp_sum):
        return permute_rows((hidden[h * half : (h + 1) * half] + mlp_sum.astype(F32)).astype(BF), inverse)

    shares = fence(shares, *grad_second)
    mlp_sums = [lax.psum_scatter(share, "tensor", scatter_dimension=0, tiled=True) for share in shares]

    grad_second = jnp.concatenate(grad_second).astype(F32)
    cot_own = jnp.concatenate([lax.dynamic_slice_in_dim(c, turn * half, half) for c in cots]).astype(F32)
    gain_two = jnp.sum(grad_second * second_unit, axis=0)
    grad_hidden = cot_own + norm_back(grad_second, second_unit, second_rate, gain[1])
    hidden_low = grad_hidden.astype(BF)

    def by_cols(left, right):
        parts = [dot(left[:, span], right, ((0,), (0,))).astype(BF) for span in (slice(cut, None), slice(0, cut))]
        return Collect(parts[1], parts[0], size, d_own)

    grad_mixed = wide_dot(hidden_low, w_o)
    tall = jnp.broadcast_to
    lam, reach, edge, pre_low = kernel_call(
        back_scan_kernel, live_count, [branch_pre, grad_mixed, decay, state, prod, tall(carry, (SLAB, width))],
        [keep, keep, (SLAB, width, F32), (rows, width, BF)], [], "back_scan",
    )
    edges = jnp.concatenate([prod[-1:], edge[:1]])
    came = [z_shift(edges, -k, n, False) for k in range(1, n)]
    arriving = jnp.zeros((1, width), F32)
    for end in came[::-1]:
        arriving = end[1:] + end[:1] * arriving
    (lam,) = fence([lam], *came_mlp)
    drec, dpar, d_lru = kernel_call(
        backward_kernel, live_count,
        [rec_pre, par, lru, order, lam, reach, tall(arriving, (SLAB, width)), decay, conv, ig, dg, state, prod, tall(carry, (SLAB, width))],
        [(rows + HALO, width, F32), (8, width, F32), (head, 2 * GROUP, BF)],
        [((rows + HALO, GROUP), F32), ((rows + 2 * HALO, GROUP), F32), ((rows + SLAB, GROUP), F32), ((GROUP, 2 * GROUP), F32), dense],
        "recurrence_back",
    )
    (edge_rows,) = fence([z_shift(drec[:HALO], -1, n, False)], mlp_sums[0])
    rec_low = (drec[HALO:] + jnp.pad(edge_rows, ((rows - HALO, 0), (0, 0)))) * live
    rec_low = rec_low.astype(BF)
    (pre_low,) = fence([pre_low], drec)
    grad_first = wide_back(pre_low, w_g) + wide_back(rec_low, w_r)
    first_unit = inputs * first_rate
    gain_one = jnp.sum(grad_first * first_unit, axis=0)
    grad_tokens = grad_hidden + norm_back(grad_first, first_unit, first_rate, gain[0])
    grad_tokens = permute_rows(grad_tokens.astype(BF), inverse)
    gathered = [lax.all_gather(grad_tokens[h * half : (h + 1) * half], "tensor", axis=0) for h in range(2)]
    (mixed,) = fence([mixed], grad_tokens)
    sum_o = by_cols(hidden_low, mixed)
    pre_low, rec_low = fence([pre_low, rec_low], sum_o.terms[1])
    sum_g, sum_r = by_cols(first_own, pre_low), by_cols(first_own, rec_low)
    results = [mlp_result(h, mlp_sum) for h, mlp_sum in enumerate(fence(mlp_sums, sum_o.terms[1]))]
    got_o = sum_o.hop(sum_o.sources())
    got_g = sum_g.hop(fence(sum_g.sources(), *got_o))
    pause = (gathered[0], *got_g)
    sum_o.hop(fence(sum_o.sources(), *pause))
    got_r = sum_r.hop(fence(sum_r.sources(), *pause))
    results = fence(results, gathered[0], *got_g)
    results = [lax.all_gather(result, "tensor", axis=0) for result in results]
    sum_g.hop(fence(sum_g.sources(), *pause))
    got_r = sum_r.hop(fence(sum_r.sources(), *got_r))
    owned = jnp.stack([total.finish().reshape(d_own, n, width // n) for total in (sum_o, sum_g, sum_r)])
    owned = LineSum(owned.transpose(2, 0, 1, 3), n)
    owned.go()
    pause = (gathered[1], owned.right, owned.left)
    d_lru, dpar = fence([d_lru, dpar], *pause)
    if sum_dn.square:
        sum_dn.hop(fence(sum_dn.sources(), *pause))
        sum_gu.hop(fence(sum_gu.sources(), *pause))
    owned.go(gathered[1])
    tokens_out = interleave(*fence(gathered, owned.right)).reshape(n * rows, d_model)
    if n > 3:
        owned.go(results[0])
    g_gu, g_dn = sum_gu.finish().astype(F32), sum_dn.finish().astype(F32)
    g_all = owned.finish()
    output = interleave(*fence(results, owned.right, owned.left)).reshape(n * rows, d_model)
    g_o, g_g, g_r = g_all[0], g_all[1], g_all[2]

    d_gain = permute_gain(jnp.stack([gain_one, gain_two]), inverse)
    d_chan = jnp.concatenate([dpar[:7], dpar[7:] * 8.0 * jax.nn.sigmoid(-chans[7:])])
    d_lru = d_lru.reshape(groups, size, part, 2, each, -1).transpose(1, 0, 4, 2, 3, 5)
    d_chan = d_chan.reshape(8, n, heads_own, size, part).transpose(3, 1, 0, 2, 4)
    d_gain = d_gain.reshape(2, size, 1, d_own).transpose(1, 2, 0, 3)
    d_gain = jnp.broadcast_to(d_gain, (size, n, 2, d_own))
    small = [v.reshape(size, n, -1).astype(BF) for v in (d_lru, d_chan, d_gain)]
    small = small_scatter(jnp.concatenate(small, axis=2), size, n)
    d_lru = small[: w_lru.size].reshape(part, 2, heads_own, head).transpose(1, 2, 0, 3)
    d_chan = small[w_lru.size : -gains.size].reshape(chan.shape)
    d_gain = small[-gains.size :].reshape(gains.shape)
    g_gate, g_up = g_gu[:, :hidden_units], g_gu[:, hidden_units:]
    return (
        output, tokens_out, d_gain[0], d_gain[1], g_g, g_r, d_chan, d_lru,
        g_o.T, jnp.stack([g_gate, g_up]), g_dn.T,
    )


def solution(mesh):
    in_specs = (
        P("dp", None),
        P("dp"),
        P(None, "dp"),
        P("dp", "tensor"),
        P("dp", "tensor"),
        P(None, "tensor", "dp"),
        P(None, "tensor", "dp", None),
        P("tensor", "dp"),
        P(None, "dp", "tensor"),
        P("tensor", "dp"),
        P("dp", None),
    )
    out_specs = (
        P("dp", None),
        P("dp", None),
        P("dp"),
        P("dp"),
        P("dp", "tensor"),
        P("dp", "tensor"),
        P(None, "tensor", "dp"),
        P(None, "tensor", "dp", None),
        P("tensor", "dp"),
        P(None, "dp", "tensor"),
        P("tensor", "dp"),
    )
    body = functools.partial(on_device, mesh.shape["dp"], mesh.shape["tensor"])
    return jax.shard_map(body, mesh=mesh, in_specs=in_specs, out_specs=out_specs, check_vma=False)
```

```python
import functools

import jax
import jax.numpy as jnp
import numpy as np
from jax import lax
from jax.experimental import pallas as pl
from jax.experimental.pallas import tpu as pltpu
from jax.sharding import PartitionSpec as P

NORM_EPS = 1e-06
DECAY_FLOOR = 0.05
HALO = 16
GROUP = 640
ROWS = 128
SLAB = 8
VMEM = 58 * 1024 * 1024
BF = jnp.bfloat16
F32 = jnp.float32
EARLY = pl.CostEstimate(flops=14 * 10**9, bytes_accessed=1024, transcendentals=0)
LITTLE = pl.CostEstimate(flops=1024, bytes_accessed=1024, transcendentals=0)


def dot(left, right, dims=((1,), (0,))):
    return lax.dot_general(left, right, (dims, ((), ())), preferred_element_type=F32)


def fence(values, *others, cost=LITTLE):
    if not others:
        return list(values)
    place = pl.BlockSpec(memory_space=pl.ANY)
    call = pl.pallas_call(
        lambda *refs: None,
        in_specs=[place] * (len(values) + len(others)),
        out_specs=[place] * len(values),
        out_shape=[jax.ShapeDtypeStruct(v.shape, v.dtype) for v in values],
        input_output_aliases={k: k for k in range(len(values))},
        compiler_params=pltpu.CompilerParams(vmem_limit_bytes=VMEM),
        cost_estimate=cost,
        name="fence",
    )
    return list(call(*values, *others))


def assemble(pieces, *others):
    count = len(pieces)
    rows = [p.shape[0] for p in pieces]
    spans = [pl.ds(sum(rows[:k]), rows[k]) for k in range(count)]
    shape = (sum(rows), pieces[0].shape[1])

    def body(*refs):
        out, held, coming, going = refs[count + len(others) :]
        ins = [pltpu.make_async_copy(refs[k], held.at[spans[k]], coming.at[k]) for k in range(count)]
        outs = [pltpu.make_async_copy(held.at[spans[k]], out.at[spans[k]], going.at[k]) for k in range(count)]
        for copy in ins:
            copy.start()
        for here, there in zip(ins, outs):
            here.wait()
            there.start()
        for copy in outs:
            copy.wait()

    place = pl.BlockSpec(memory_space=pl.ANY)
    return pl.pallas_call(
        body,
        in_specs=[place] * (count + len(others)),
        out_specs=place,
        out_shape=jax.ShapeDtypeStruct(shape, pieces[0].dtype),
        scratch_shapes=[
            pltpu.VMEM(shape, pieces[0].dtype),
            pltpu.SemaphoreType.DMA((count,)),
            pltpu.SemaphoreType.DMA((count,)),
        ],
        compiler_params=pltpu.CompilerParams(vmem_limit_bytes=VMEM),
        cost_estimate=LITTLE,
        name="assemble",
    )(*pieces, *others)


def swap(values, mask, size):
    return lax.ppermute(values, "dp", [(k, k ^ mask) for k in range(size)])


def exchange(values, bit, size):
    return swap(values, 1 << bit, size)


def squared(size, rows):
    return size == 8 and rows % 256 == 0


def spread_begin(own, size, *before):
    (own,) = fence([own], *before)
    if squared(size, own.shape[0]):
        return [own, exchange(own, 1, size), exchange(own, 2, size)]
    pieces = own
    for bit in range(1, size.bit_length() - 2):
        pieces = jnp.concatenate([pieces, exchange(pieces, bit, size)])
    return [pieces]


def spread_end(some, size, before_last, before_core, cost=LITTLE):
    if len(some) > 1:
        own, by_x, by_y = some
        unit = own.shape[0] // 2
        by_x, by_y = fence([by_x, by_y], *before_last, cost=cost)
        got = [exchange(by_x[:unit], 2, size), exchange(by_y[unit:], 1, size)]
        half = assemble([own, by_x, got[1], got[0], by_y], *before_core)
    else:
        (pieces,) = fence(some, *before_last)
        got = [exchange(pieces, size.bit_length() - 2, size)]
        half = jnp.concatenate([pieces] + fence(got, *before_core))
    return [half, exchange(half, 0, size)], got


def add_all(terms):
    total = terms[0].astype(F32)
    for term in terms[1:]:
        total = total + term.astype(F32)
    return total.astype(BF)


class Collect:
    def __init__(self, keep, send, size, d_own):
        self.size, self.unit = size, d_own // 2
        self.square = squared(size, d_own)
        self.bit = size.bit_length() - 2
        self.terms = [keep, exchange(send, 0, size)]
        self.first = self.last = None

    def rows(self, start, stop):
        return [t[start * self.unit : stop * self.unit] for t in self.terms]

    def sources(self):
        if not self.square:
            cut = self.terms[0].shape[0] // 2
            return [add_all([t[cut:] for t in self.terms])]
        if self.first is None:
            return [add_all(self.rows(3, 5)), add_all(self.rows(5, 7))]
        by_x, by_y = self.first
        return [add_all(self.rows(2, 3) + [by_y[: self.unit]]), add_all(self.rows(7, 8) + [by_x[self.unit :]])]

    def hop(self, sources):
        if not self.square:
            got = exchange(sources[0], self.bit, self.size)
            self.bit -= 1
            self.terms = [t[: got.shape[0]] for t in self.terms] + [got]
            return [got]
        got = [exchange(v, bit, self.size) for v, bit in zip(sources, (1, 2))]
        if self.first is None:
            self.first = got
        else:
            self.last = got
        return got

    def finish(self):
        if not self.square:
            while self.bit:
                self.hop(self.sources())
            return add_all(self.terms)
        low = add_all(self.rows(0, 1) + [self.first[1][self.unit :], self.last[0]])
        high = add_all(self.rows(1, 2) + [self.first[0][: self.unit], self.last[1]])
        return jnp.concatenate([low, high])


def z_shift(values, by, n, around=True):
    pairs = [(k, (k + by) % n) for k in range(n) if around or 0 <= k + by < n]
    return lax.ppermute(values, "tensor", pairs)


def z_scatter(values, n):
    turn = lax.axis_index("tensor")
    total = lax.dynamic_index_in_dim(values, turn, 0, keepdims=False).astype(F32)
    for k in range(1, n):
        block = lax.dynamic_index_in_dim(values, (turn + k) % n, 0, keepdims=False)
        total = total + z_shift(block, k, n).astype(F32)
    return total


class LineSum:
    def __init__(self, blocks, n):
        self.blocks, self.n, self.turn, self.rounds = blocks, n, lax.axis_index("tensor"), 0
        self.right = self.left = None

    def block(self, k):
        return lax.dynamic_index_in_dim(self.blocks, k % self.n, 0, keepdims=False)

    def go(self, *others):
        self.rounds += 1
        t, n = self.rounds, self.n
        right, left = self.block(self.turn + n - t), self.block(self.turn + t)
        if t > 1:
            before = fence([self.right, self.left], *others)
            right, left = add_all([right, before[0]]), add_all([left, before[1]])
        self.right = lax.ppermute(right, "tensor", [(k, k + 1) for k in range(min(t, n - 1))])
        self.left = lax.ppermute(left, "tensor", [(k, k - 1) for k in range(max(n - t, 1), n)])

    def finish(self):
        while self.rounds < self.n - 1:
            self.go()
        return self.block(self.turn).astype(F32) + self.right.astype(F32) + self.left.astype(F32)


def small_masks(size):
    turns = (0, 2, 6, 4) if size == 8 else tuple(q << 1 for q in range(size // 2))
    return np.array([core | mask for core in range(2) for mask in turns], np.int32)


def small_begin(own, size):
    if size == 8:
        return [own] + [swap(own, mask, size) for mask in (2, 6, 4)]
    rows = own[None]
    for bit in range(1, size.bit_length() - 1):
        rows = jnp.concatenate([rows, exchange(rows, bit, size)])
    return [rows]


def small_end(some, size):
    if size == 8:
        rows = jnp.stack(some)
    else:
        (rows,) = some
    return jnp.concatenate([rows, exchange(rows, 0, size)])


def small_scatter(values, size, n):
    place = lax.axis_index("dp")
    values = jnp.take(values, jnp.arange(size) ^ place, axis=0, mode="clip")
    for bit in reversed(range(size.bit_length() - 1)):
        half = values.shape[0] // 2
        values = add_all([values[:half], exchange(values[half:], bit, size)])
    return z_scatter(values[0], n)


def basis_spots(size, rows):
    if squared(size, rows):
        turns = ((0, 0), (0, 1), (2, 0), (2, 1), (6, 1), (6, 0), (4, 0), (4, 1))
        return [(core | mask, part) for core in range(2) for mask, part in turns], 2
    return [(core | q << 1, 0) for core in range(2) for q in range(size // 2)], 1


def basis(size, rows, place):
    spots, parts = basis_spots(size, rows)
    masks, which = (jnp.asarray(np.array(v, np.int32)) for v in zip(*spots))
    table = (place ^ masks) * parts + which
    spots = jnp.arange(table.shape[0], dtype=jnp.int32)
    inverse = jnp.sum(jnp.where(table[None, :] == spots[:, None], spots[None, :], 0), axis=1)
    return table, inverse.astype(jnp.int32)


def copy_kernel(blocks, table_ref, in_ref, out_ref):
    width = in_ref.shape[1] // blocks
    for p in range(blocks):
        start = pl.multiple_of(table_ref[p] * width, width)
        out_ref[:, p * width : (p + 1) * width] = in_ref[:, pl.ds(start, width)]


def permute_rows(values, table, step=0, stride=1, offset=0):
    rows, d_model = values.shape
    step = step or max(k for k in range(16, 289, 16) if rows % k == 0)
    return pl.pallas_call(
        functools.partial(copy_kernel, table.shape[0]),
        grid_spec=pltpu.PrefetchScalarGridSpec(
            num_scalar_prefetch=1,
            grid=(rows // (step * stride),),
            in_specs=[pl.BlockSpec((step, d_model), lambda r, tab: (r * stride + offset, 0))],
            out_specs=pl.BlockSpec((step, d_model), lambda r, tab: (r, 0)),
        ),
        out_shape=jax.ShapeDtypeStruct((rows // stride, d_model), values.dtype),
        compiler_params=pltpu.CompilerParams(vmem_limit_bytes=VMEM),
        cost_estimate=LITTLE,
        name="permute",
    )(table, values)


def interleave_kernel(one_ref, two_ref, out_ref):
    out_ref[0] = one_ref[...]
    out_ref[1] = two_ref[...]


def interleave(one, two):
    n, rows, d_model = one.shape
    spec = pl.BlockSpec((pl.squeezed, rows, d_model), lambda j: (j, 0, 0))
    return pl.pallas_call(
        interleave_kernel,
        grid=(n,),
        in_specs=[spec, spec],
        out_specs=pl.BlockSpec((pl.squeezed, 2, rows, d_model), lambda j: (j, 0, 0, 0)),
        out_shape=jax.ShapeDtypeStruct((n, 2, rows, d_model), one.dtype),
        compiler_params=pltpu.CompilerParams(vmem_limit_bytes=VMEM),
        cost_estimate=LITTLE,
        name="interleave",
    )(one, two)


def permute_gain(values, table):
    lead = values.shape[0]
    return jnp.take(values.reshape(lead, table.shape[0], -1), table, axis=1, mode="clip").reshape(lead, -1)


def row_ids(count, width, first):
    return lax.broadcasted_iota(jnp.int32, (count, width), 0) + first


def scan_slab(decay, value, back):
    rows = row_ids(SLAB, decay.shape[1], 0)
    for step in (1, 2, 4):
        keep = rows < SLAB - step if back else rows >= step
        shift = SLAB - step if back else step
        moved_decay = pltpu.roll(decay, shift, 0)
        moved_value = pltpu.roll(value, shift, 0)
        value = jnp.where(keep, value + decay * moved_value, value)
        decay = jnp.where(keep, decay * moved_decay, decay)
    return decay, value


def head_mask(head, at, width):
    lanes = lax.broadcasted_iota(jnp.int32, (head, 2 * width), 1)
    lanes = jnp.where(lanes >= width, lanes - width, lanes)
    return (lanes >= at * head) & (lanes < (at + 1) * head)


def fill_dense(w_ref, order_ref, dense_ref):
    head, count = order_ref.shape
    pad = count // w_ref.shape[0]
    width = dense_ref.shape[0]
    for gate in range(2):
        rows = w_ref[:, gate * pad : (gate + 1) * pad, :].reshape(count, width)
        rows = dot(order_ref[...], rows)
        for k in range(width // head):
            lanes = lax.broadcasted_iota(jnp.int32, (head, width), 1)
            block = jnp.where((lanes >= k * head) & (lanes < (k + 1) * head), rows, 0.0)
            dense_ref[k * head : (k + 1) * head, gate * width : (gate + 1) * width] = block.astype(BF)


def forward_kernel(
    live_ref, pre_ref, par_ref, w_ref, order_ref, conv_ref, decay_ref, ig_ref, dg_ref, state_ref, prod_ref,
    rec_ref, dense_ref,
):
    rows, width = conv_ref.shape
    fill_dense(w_ref, order_ref, dense_ref)
    live = live_ref[0]
    rec_ref[...] = jnp.where(row_ids(rows + HALO, width, -HALO) < live, pre_ref[...], 0.0)
    par = [par_ref[k : k + 1, :] for k in range(8)]
    for at in range(0, rows, ROWS):
        span = pl.ds(at, ROWS)
        near = rec_ref[pl.ds(at, ROWS + HALO), :]
        conv = par[4] + par[0] * near[HALO : HALO + ROWS]
        for k in range(1, 4):
            conv = conv + par[k] * near[HALO - k : HALO - k + ROWS]
        conv = jnp.where(row_ids(ROWS, width, at) < live, conv, 0.0)
        conv_ref[span, :] = conv
        gates = dot(conv.astype(BF), dense_ref[...])
        ig = lax.logistic(gates[:, :width] + par[5])
        dg = lax.logistic(gates[:, width:] + par[6])
        decay = jnp.exp(dg * par[7])
        ig_ref[span, :] = ig
        dg_ref[span, :] = dg
        decay_ref[span, :] = decay
        state_ref[span, :] = jnp.sqrt(jnp.maximum(1.0 - decay * decay, DECAY_FLOOR)) * ig * conv

    def slab(k, carry):
        state, prod = carry
        for inner in range(4):
            span = pl.ds(pl.multiple_of(k * 4 * SLAB + inner * SLAB, SLAB), SLAB)
            decay, value = scan_slab(decay_ref[span, :], state_ref[span, :], False)
            value = value + decay * state
            decay = decay * prod
            state_ref[span, :] = value
            prod_ref[span, :] = decay
            state = jnp.broadcast_to(value[SLAB - 1 :, :], (SLAB, width))
            prod = jnp.broadcast_to(decay[SLAB - 1 :, :], (SLAB, width))
        return state, prod

    lax.fori_loop(0, rows // (4 * SLAB), slab, (jnp.zeros((SLAB, width), F32), jnp.ones((SLAB, width), F32)))


def back_scan_kernel(
    live_ref, pre_ref, grad_ref, decay_ref, state_ref, prod_ref, cin_ref, lam_ref, reach_ref, edge_ref, low_ref
):
    rows, width = grad_ref.shape
    live = live_ref[0]
    cin = cin_ref[:1, :]
    c = np.float32(np.sqrt(2 / np.pi))
    for at in range(0, rows, ROWS):
        span = pl.ds(at, ROWS)
        v, grad = pre_ref[span, :], grad_ref[span, :]
        square = v * v
        bend = jnp.tanh(v * (c + (c * 0.044715) * square))
        rise = 0.5 + 0.5 * bend
        slope = rise + 0.5 * v * (1.0 - bend * bend) * (c + (3 * c * 0.044715) * square)
        grad = jnp.where(row_ids(ROWS, width, at) < live, grad, 0.0)
        lam_ref[span, :] = grad * (v * rise)
        low_ref[span, :] = (grad * (state_ref[span, :] + prod_ref[span, :] * cin) * slope).astype(BF)
    last = row_ids(SLAB, width, 0) == SLAB - 1

    def slab(k, carry):
        lam, reach, following, _ = carry
        for inner in range(4):
            span = pl.ds(pl.multiple_of(rows - (k * 4 + inner + 1) * SLAB, SLAB), SLAB)
            own = decay_ref[span, :]
            ahead = jnp.where(last, following, pltpu.roll(own, SLAB - 1, 0))
            decay, value = scan_slab(ahead, lam_ref[span, :], True)
            value = value + decay * lam
            decay = decay * reach
            lam_ref[span, :] = value
            reach_ref[span, :] = decay
            lam = jnp.broadcast_to(value[:1, :], (SLAB, width))
            reach = jnp.broadcast_to(decay[:1, :], (SLAB, width))
            following = jnp.broadcast_to(own[:1, :], (SLAB, width))
        return lam, reach, following, own

    one = jnp.ones((SLAB, width), F32)
    zero = jnp.zeros((SLAB, width), F32)
    lam, _, following, _ = lax.fori_loop(0, rows // (4 * SLAB), slab, (zero, one, one, one))
    edge_ref[...] = lam * following


def backward_kernel(
    live_ref, pre_ref, par_ref, w_ref, order_ref, lam_ref, reach_ref, edge_ref, decay_ref, conv_ref, ig_ref, dg_ref, state_ref, prod_ref, cin_ref,
    drec_ref, dpar_ref, dw_ref, rec_ref, dconv_ref, full_ref, dw_acc, dense_ref,
):
    rows, width = conv_ref.shape
    live = live_ref[0]
    rec_ref[...] = jnp.where(row_ids(rows + HALO, width, -HALO) < live, pre_ref[...], 0.0)
    par = [par_ref[k : k + 1, :] for k in range(8)]
    fill_dense(w_ref, order_ref, dense_ref)
    cin = cin_ref[:1, :]
    edge = edge_ref[:1, :]
    full_ref[:SLAB, :] = jnp.broadcast_to(cin, (SLAB, width))
    dconv_ref[:HALO, :] = jnp.zeros((HALO, width), F32)
    dconv_ref[rows + HALO :, :] = jnp.zeros((HALO, width), F32)
    sums = [jnp.zeros((1, width), F32) for _ in range(8)]
    for at in range(0, rows, ROWS):
        span = pl.ds(at, ROWS)
        full_ref[pl.ds(at + SLAB, ROWS), :] = state_ref[span, :] + prod_ref[span, :] * cin
        lam = lam_ref[span, :] + reach_ref[span, :] * edge
        decay, conv, ig, dg = decay_ref[span, :], conv_ref[span, :], ig_ref[span, :], dg_ref[span, :]
        before = full_ref[pl.ds(at, ROWS + SLAB), :][SLAB - 1 : SLAB - 1 + ROWS]
        room = 1.0 - decay * decay
        scale = jnp.sqrt(jnp.maximum(room, DECAY_FLOOR))
        lam_conv = lam * conv
        d_decay = lam * before - jnp.where(room > DECAY_FLOOR, lam_conv * ig * decay / scale, 0.0)
        moved = d_decay * decay
        sums[7] = sums[7] + jnp.sum(moved * dg, axis=0, keepdims=True)
        d_ig = lam_conv * scale * ig * (1.0 - ig)
        d_dg = moved * par[7] * dg * (1.0 - dg)
        sums[5] = sums[5] + jnp.sum(d_ig, axis=0, keepdims=True)
        sums[6] = sums[6] + jnp.sum(d_dg, axis=0, keepdims=True)
        both = jnp.concatenate([d_ig.astype(BF), d_dg.astype(BF)], axis=1)
        d_conv = lam * scale * ig + dot(both, dense_ref[...], ((1,), (1,)))
        d_conv = jnp.where(row_ids(ROWS, width, at) < live, d_conv, 0.0)
        dconv_ref[pl.ds(at + HALO, ROWS), :] = d_conv
        part = dot(conv.astype(BF), both, ((0,), (0,)))
        dw_acc[...] = part if at == 0 else dw_acc[...] + part
        near = rec_ref[pl.ds(at, ROWS + HALO), :]
        for k in range(4):
            sums[k] = sums[k] + jnp.sum(d_conv * near[HALO - k : HALO - k + ROWS], axis=0, keepdims=True)
        sums[4] = sums[4] + jnp.sum(d_conv, axis=0, keepdims=True)
    for k in range(8):
        dpar_ref[k : k + 1, :] = sums[k]
    head = dw_ref.shape[0]
    total = jnp.zeros((head, 2 * width), F32)
    for k in range(width // head):
        total = total + jnp.where(head_mask(head, k, width), dw_acc[k * head : (k + 1) * head, :], 0.0)
    dw_ref[...] = total.astype(BF)
    for at in list(range(0, rows, ROWS)) + [rows]:
        count = ROWS if at < rows else HALO
        near = dconv_ref[pl.ds(at, count + SLAB), :]
        total = par[0] * near[:count]
        for k in range(1, 4):
            total = total + par[k] * near[k : k + count]
        drec_ref[pl.ds(at, count), :] = total


def kernel_call(body, live, arrays, outs, scratch, name):
    width = outs[0][1]
    steps = width // GROUP
    specs = []
    for array in arrays:
        if array.ndim == 4:
            block = (array.shape[0], pl.squeezed) + array.shape[2:]
            specs.append(pl.BlockSpec(block, lambda j, s: (0, j, 0, 0)))
        elif array.shape[1] != width:
            specs.append(pl.BlockSpec(array.shape, lambda j, s: (0, 0)))
        else:
            specs.append(pl.BlockSpec((array.shape[0], GROUP), lambda j, s: (0, j)))
    out_specs, out_shapes = [], []
    for rows, cols, kind in outs:
        if cols == width:
            out_specs.append(pl.BlockSpec((rows, GROUP), lambda j, s: (0, j)))
            out_shapes.append(jax.ShapeDtypeStruct((rows, cols), kind))
        else:
            out_specs.append(pl.BlockSpec((pl.squeezed, rows, cols), lambda j, s: (j, 0, 0)))
            out_shapes.append(jax.ShapeDtypeStruct((steps, rows, cols), kind))
    return pl.pallas_call(
        body,
        grid_spec=pltpu.PrefetchScalarGridSpec(
            num_scalar_prefetch=1, grid=(steps,), in_specs=specs, out_specs=out_specs,
            scratch_shapes=[pltpu.VMEM(shape, kind) for shape, kind in scratch],
        ),
        out_shape=out_shapes,
        compiler_params=pltpu.CompilerParams(vmem_limit_bytes=VMEM),
        cost_estimate=LITTLE,
        name=name,
    )(live, *arrays)


def norm_rate(values):
    return lax.rsqrt(jnp.mean(values * values, axis=-1, keepdims=True) + NORM_EPS)


def norm_back(grad, unit, rate, gain):
    moved = grad * gain
    return rate * (moved - unit * jnp.mean(moved * unit, axis=-1, keepdims=True))


def gelu_product(gate, up):
    return jax.nn.gelu(gate) * up


def wide_dot(left, halves):
    cut = halves[0].shape[0]
    return dot(left[:, :cut], halves[0]) + dot(left[:, cut:], halves[1])


def wide_back(left, halves):
    return jnp.concatenate([dot(left, h, ((1,), (1,))) for h in halves], axis=1)


def on_device(size, n, tokens, lengths, gains, w_gelu, w_rec, chan, w_lru, w_out, w_mlp_in, w_down, cotangent):
    place = lax.axis_index("dp")
    turn = lax.axis_index("tensor")
    d_model = tokens.shape[1]
    rows = tokens.shape[0] // n
    half = rows // 2
    d_own = w_gelu.shape[0]
    heads_own, part, head = chan.shape[1], chan.shape[2], w_lru.shape[3]
    heads = heads_own * n
    width = heads * head
    groups = width // GROUP
    table, inverse = basis(size, d_own, place)
    live_count = (lengths - turn * rows).astype(jnp.int32)
    live = (lax.iota(jnp.int32, rows)[:, None] < live_count).astype(F32)

    cols = w_gelu.shape[1]
    pad = -(-part // 16) * 16
    own_lru = jnp.pad(w_lru.transpose(0, 2, 1, 3).reshape(2, part, cols), ((0, 0), (0, pad - part), (0, 0)))
    own_chan = jnp.zeros((8, heads_own, head), F32)
    own_chan = lax.dynamic_update_slice(own_chan, chan, (0, 0, place * part)).reshape(8, cols)
    own_gain = jnp.pad(gains.reshape(1, -1), ((0, 7), (0, cols - gains.size)))
    small = jnp.concatenate([own_lru.reshape(2 * pad, cols), own_chan, own_gain])
    whole = jnp.concatenate([w_rec, small]).astype(BF)
    others = jnp.concatenate([w_gelu, w_out.T]).astype(BF)
    own_gu = jnp.concatenate([w_mlp_in[0], w_mlp_in[1]], axis=1).astype(BF)
    own_dn = w_down.T.astype(BF)
    some_gu = spread_begin(own_gu, size)

    main = lax.dynamic_slice_in_dim(tokens, turn * rows, rows)
    before = lax.dynamic_slice_in_dim(tokens, jnp.maximum(turn * rows - HALO, 0), HALO)
    before = jnp.where(turn > 0, before, jnp.zeros_like(before))
    turned = permute_rows(jnp.concatenate([before, main]), table)
    extended = turned.astype(F32)
    first_rate = norm_rate(extended)

    def wide(blocks):
        return blocks.transpose(1, 0, 2).reshape(d_own, width)

    (whole,) = fence([lax.all_gather(whole, "tensor", axis=0)], *some_gu[1:], others, turned, first_rate)
    others = lax.all_gather(*fence([others], whole), "tensor", axis=0)
    z_gelu, z_out = wide(others[:, :d_own]), wide(others[:, d_own:])
    some_r = spread_begin(wide(whole[:, :d_own]), size)
    some_small = small_begin(whole[:, d_own:].reshape(-1, cols), size)
    small = small_end(some_small, size).reshape(size, n, -1, cols)

    masks = small_masks(size)
    gain = small[:, 0, 2 * pad + 8, : gains.size].reshape(size, 2, d_own)
    if squared(size, d_own):
        swapped = jnp.concatenate([gain[..., d_own // 2 :], gain[..., : d_own // 2]], axis=-1)
        gain = jnp.where(((jnp.asarray(masks) & 6) == 6)[:, None, None], swapped, gain)
    gain = gain.transpose(1, 0, 2).reshape(2, d_model).astype(F32)
    chans = jnp.sum(small[:, :, 2 * pad : 2 * pad + 8].astype(F32), axis=0)
    chans = chans.transpose(1, 0, 2).reshape(8, width)
    par = jnp.concatenate([chans[:7], -8.0 * jax.nn.softplus(-chans[7:])])
    each = n // groups
    lru = small
    if each > 1:
        lru = lru.reshape(size, groups, each, -1, cols).transpose(0, 1, 3, 2, 4).reshape(size, groups, -1, GROUP)
    spot = (place ^ jnp.asarray(masks))[jnp.arange(size * pad) // pad]
    row = jnp.arange(size * pad) % pad
    row = jnp.where(row < part, spot * part + row, head)
    order = (jnp.arange(head)[:, None] == row[None, :]).astype(BF)

    w_r, came_r = spread_end(some_r, size, (table,), (z_gelu, order, gain, par, lru), EARLY)
    first = (extended * first_rate * gain[0]).astype(BF)
    inputs, first_own, first_rate = extended[HALO:], first[HALO:], first_rate[HALO:]
    cut = d_model // 2

    keep = (rows, width, F32)
    dense = ((GROUP, 2 * GROUP), BF)
    some_g = spread_begin(z_gelu, size, *came_r)
    rec_pre = wide_dot(first, w_r)
    conv, decay, ig, dg, state, prod = kernel_call(
        forward_kernel, live_count, [rec_pre, par, lru, order], [keep] * 6,
        [((rows + HALO, GROUP), F32), dense], "recurrence",
    )
    ends = jnp.concatenate([prod[-1:], state[-1:]])
    came = [z_shift(ends, k, n, False) for k in range(1, n)]
    w_g, came_g = spread_end(some_g, size, (ends,), came)
    carry = jnp.zeros((1, width), F32)
    for end in came[::-1]:
        carry = end[1:] + end[:1] * carry
    some_o = spread_begin(z_out, size, *came_g)
    branch_pre = wide_dot(first_own, w_g)
    recurrent = (state + prod * carry) * live
    mixed = (jax.nn.gelu(branch_pre) * recurrent).astype(BF)
    w_o, came_o = spread_end(some_o, size, (branch_pre,), (mixed,))
    hidden = inputs + wide_back(mixed, w_o)
    second_rate = norm_rate(hidden)
    second_unit = hidden * second_rate
    second_own = (second_unit * gain[1]).astype(BF)
    w_gu, came_gu = spread_end(some_gu, size, came_o, (second_own,))
    w_dn, _ = spread_end(spread_begin(own_dn, size, *came_gu), size, (), ())
    w_gu, w_dn = assemble(w_gu), assemble(w_dn)
    late = fence([table], second_own)[0]
    cots = [permute_rows(cotangent, late, half, 2, h) for h in range(2)]

    hidden_units = w_dn.shape[1]
    grad_products = [dot(c, w_dn) for c in cots]
    shares, grad_second, seconds, products, grads = [], [], [], [], []
    for h in range(2):
        second = lax.all_gather(second_own[h * half : (h + 1) * half], "tensor", axis=0, tiled=True)
        (second,) = fence([second], *shares)
        both = dot(second, w_gu)
        product, pull = jax.vjp(gelu_product, both[:, :hidden_units], both[:, hidden_units:])
        grad_gate, grad_up = pull(grad_products[h])
        product = product.astype(BF)
        grad = jnp.concatenate([grad_gate.astype(BF), grad_up.astype(BF)], axis=1)
        share = dot(grad, w_gu, ((1,), (1,))).astype(BF)
        shares.append(share)
        grad_second.append(lax.psum_scatter(share, "tensor", scatter_dimension=0, tiled=True))
        seconds.append(second)
        products.append(product)
        grads.append(grad)

    products, grads = [[*pair] for pair in zip(*[fence([p, g], shares[-1]) for p, g in zip(products, grads)])]
    shares = [dot(p, w_dn, ((1,), (1,))).astype(BF) for p in products]

    def by_rows(lefts, rights):
        parts = []
        for span in (slice(cut, None), slice(0, cut)):
            part = dot(lefts[0][:, span], rights[0], ((0,), (0,)))
            parts.append((part + dot(lefts[1][:, span], rights[1], ((0,), (0,)))).astype(BF))
        return Collect(parts[1], parts[0], size, d_own)

    sum_dn = by_rows(cots, products)
    sum_gu = by_rows(seconds, grads)
    sent_dn, sent_gu = sum_dn.sources(), sum_gu.sources()
    grad_second = fence(grad_second, *sent_dn, *sent_gu, *shares)
    came_mlp = sum_dn.hop(sent_dn) + sum_gu.hop(sent_gu)

    def mlp_result(h, mlp_sum):
        return permute_rows((hidden[h * half : (h + 1) * half] + mlp_sum.astype(F32)).astype(BF), inverse)

    shares = fence(shares, *grad_second)
    mlp_sums = [lax.psum_scatter(share, "tensor", scatter_dimension=0, tiled=True) for share in shares]

    grad_second = jnp.concatenate(grad_second).astype(F32)
    cot_own = jnp.concatenate([lax.dynamic_slice_in_dim(c, turn * half, half) for c in cots]).astype(F32)
    gain_two = jnp.sum(grad_second * second_unit, axis=0)
    grad_hidden = cot_own + norm_back(grad_second, second_unit, second_rate, gain[1])
    hidden_low = grad_hidden.astype(BF)

    def by_cols(left, right):
        parts = [dot(left[:, span], right, ((0,), (0,))).astype(BF) for span in (slice(cut, None), slice(0, cut))]
        return Collect(parts[1], parts[0], size, d_own)

    grad_mixed = wide_dot(hidden_low, w_o)
    tall = jnp.broadcast_to
    lam, reach, edge, pre_low = kernel_call(
        back_scan_kernel, live_count, [branch_pre, grad_mixed, decay, state, prod, tall(carry, (SLAB, width))],
        [keep, keep, (SLAB, width, F32), (rows, width, BF)], [], "back_scan",
    )
    edges = jnp.concatenate([prod[-1:], edge[:1]])
    came = [z_shift(edges, -k, n, False) for k in range(1, n)]
    arriving = jnp.zeros((1, width), F32)
    for end in came[::-1]:
        arriving = end[1:] + end[:1] * arriving
    (lam,) = fence([lam], *came_mlp)
    drec, dpar, d_lru = kernel_call(
        backward_kernel, live_count,
        [rec_pre, par, lru, order, lam, reach, tall(arriving, (SLAB, width)), decay, conv, ig, dg, state, prod, tall(carry, (SLAB, width))],
        [(rows + HALO, width, F32), (8, width, F32), (head, 2 * GROUP, BF)],
        [((rows + HALO, GROUP), F32), ((rows + 2 * HALO, GROUP), F32), ((rows + SLAB, GROUP), F32), ((GROUP, 2 * GROUP), F32), dense],
        "recurrence_back",
    )
    (edge_rows,) = fence([z_shift(drec[:HALO], -1, n, False)], mlp_sums[0])
    rec_low = (drec[HALO:] + jnp.pad(edge_rows, ((rows - HALO, 0), (0, 0)))) * live
    rec_low = rec_low.astype(BF)
    (pre_low,) = fence([pre_low], drec)
    grad_first = wide_back(pre_low, w_g) + wide_back(rec_low, w_r)
    first_unit = inputs * first_rate
    gain_one = jnp.sum(grad_first * first_unit, axis=0)
    grad_tokens = grad_hidden + norm_back(grad_first, first_unit, first_rate, gain[0])
    grad_tokens = permute_rows(grad_tokens.astype(BF), inverse)
    gathered = [lax.all_gather(grad_tokens[h * half : (h + 1) * half], "tensor", axis=0) for h in range(2)]
    (mixed,) = fence([mixed], grad_tokens)
    sum_o = by_cols(hidden_low, mixed)
    pre_low, rec_low = fence([pre_low, rec_low], sum_o.terms[1])
    sum_g, sum_r = by_cols(first_own, pre_low), by_cols(first_own, rec_low)
    results = [mlp_result(h, mlp_sum) for h, mlp_sum in enumerate(fence(mlp_sums, sum_o.terms[1]))]
    got_o = sum_o.hop(sum_o.sources())
    got_g = sum_g.hop(fence(sum_g.sources(), *got_o))
    pause = (gathered[0], *got_g)
    sum_o.hop(fence(sum_o.sources(), *pause))
    got_r = sum_r.hop(fence(sum_r.sources(), *pause))
    results = fence(results, gathered[0], *got_g)
    results = [lax.all_gather(result, "tensor", axis=0) for result in results]
    sum_g.hop(fence(sum_g.sources(), *pause))
    got_r = sum_r.hop(fence(sum_r.sources(), *got_r))
    owned = jnp.stack([total.finish().reshape(d_own, n, width // n) for total in (sum_o, sum_g, sum_r)])
    owned = LineSum(owned.transpose(2, 0, 1, 3), n)
    owned.go()
    pause = (gathered[1], owned.right, owned.left)
    d_lru, dpar = fence([d_lru, dpar], *pause)
    if sum_dn.square:
        sum_dn.hop(fence(sum_dn.sources(), *pause))
        sum_gu.hop(fence(sum_gu.sources(), *pause))
    owned.go(gathered[1])
    tokens_out = interleave(*fence(gathered, owned.right)).reshape(n * rows, d_model)
    if n > 3:
        owned.go(results[0])
    g_gu, g_dn = sum_gu.finish().astype(F32), sum_dn.finish().astype(F32)
    g_all = owned.finish()
    output = interleave(*fence(results, owned.right, owned.left)).reshape(n * rows, d_model)
    g_o, g_g, g_r = g_all[0], g_all[1], g_all[2]

    d_gain = permute_gain(jnp.stack([gain_one, gain_two]), inverse)
    d_chan = jnp.concatenate([dpar[:7], dpar[7:] * 8.0 * jax.nn.sigmoid(-chans[7:])])
    d_lru = d_lru.reshape(groups, size, part, 2, each, -1).transpose(1, 0, 4, 2, 3, 5)
    d_chan = d_chan.reshape(8, n, heads_own, size, part).transpose(3, 1, 0, 2, 4)
    d_gain = d_gain.reshape(2, size, 1, d_own).transpose(1, 2, 0, 3)
    d_gain = jnp.broadcast_to(d_gain, (size, n, 2, d_own))
    small = [v.reshape(size, n, -1).astype(BF) for v in (d_lru, d_chan, d_gain)]
    small = small_scatter(jnp.concatenate(small, axis=2), size, n)
    d_lru = small[: w_lru.size].reshape(part, 2, heads_own, head).transpose(1, 2, 0, 3)
    d_chan = small[w_lru.size : -gains.size].reshape(chan.shape)
    d_gain = small[-gains.size :].reshape(gains.shape)
    g_gate, g_up = g_gu[:, :hidden_units], g_gu[:, hidden_units:]
    return (
        output, tokens_out, d_gain[0], d_gain[1], g_g, g_r, d_chan, d_lru,
        g_o.T, jnp.stack([g_gate, g_up]), g_dn.T,
    )


def solution(mesh):
    in_specs = (
        P("dp", None),
        P("dp"),
        P(None, "dp"),
        P("dp", "tensor"),
        P("dp", "tensor"),
        P(None, "tensor", "dp"),
        P(None, "tensor", "dp", None),
        P("tensor", "dp"),
        P(None, "dp", "tensor"),
        P("tensor", "dp"),
        P("dp", None),
    )
    out_specs = (
        P("dp", None),
        P("dp", None),
        P("dp"),
        P("dp"),
        P("dp", "tensor"),
        P("dp", "tensor"),
        P(None, "tensor", "dp"),
        P(None, "tensor", "dp", None),
        P("tensor", "dp"),
        P(None, "dp", "tensor"),
        P("tensor", "dp"),
    )
    body = functools.partial(on_device, mesh.shape["dp"], mesh.shape["tensor"])
    return jax.shard_map(body, mesh=mesh, in_specs=in_specs, out_specs=out_specs, check_vma=False)
```

```python
import functools

import jax
import jax.numpy as jnp
import numpy as np
from jax import lax
from jax.experimental import pallas as pl
from jax.experimental.pallas import tpu as pltpu
from jax.sharding import PartitionSpec as P

NORM_EPS = 1e-06
DECAY_FLOOR = 0.05
HALO = 16
GROUP = 640
ROWS = 128
SLAB = 8
VMEM = 58 * 1024 * 1024
BF = jnp.bfloat16
F32 = jnp.float32
MUCH = pl.CostEstimate(flops=60 * 10**9, bytes_accessed=1024, transcendentals=0)
LITTLE = pl.CostEstimate(flops=1024, bytes_accessed=1024, transcendentals=0)


def dot(left, right, dims=((1,), (0,))):
    return lax.dot_general(left, right, (dims, ((), ())), preferred_element_type=F32)


def fence(values, *others, cost=LITTLE):
    if not others:
        return list(values)
    place = pl.BlockSpec(memory_space=pl.ANY)
    call = pl.pallas_call(
        lambda *refs: None,
        in_specs=[place] * (len(values) + len(others)),
        out_specs=[place] * len(values),
        out_shape=[jax.ShapeDtypeStruct(v.shape, v.dtype) for v in values],
        input_output_aliases={k: k for k in range(len(values))},
        compiler_params=pltpu.CompilerParams(vmem_limit_bytes=VMEM),
        cost_estimate=cost,
        name="fence",
    )
    return list(call(*values, *others))


def assemble(pieces, *others):
    count = len(pieces)
    rows = [p.shape[0] for p in pieces]
    spans = [pl.ds(sum(rows[:k]), rows[k]) for k in range(count)]
    shape = (sum(rows), pieces[0].shape[1])

    def body(*refs):
        out, held, coming, going = refs[count + len(others) :]
        ins = [pltpu.make_async_copy(refs[k], held.at[spans[k]], coming.at[k]) for k in range(count)]
        outs = [pltpu.make_async_copy(held.at[spans[k]], out.at[spans[k]], going.at[k]) for k in range(count)]
        for copy in ins:
            copy.start()
        for here, there in zip(ins, outs):
            here.wait()
            there.start()
        for copy in outs:
            copy.wait()

    place = pl.BlockSpec(memory_space=pl.ANY)
    return pl.pallas_call(
        body,
        in_specs=[place] * (count + len(others)),
        out_specs=place,
        out_shape=jax.ShapeDtypeStruct(shape, pieces[0].dtype),
        scratch_shapes=[
            pltpu.VMEM(shape, pieces[0].dtype),
            pltpu.SemaphoreType.DMA((count,)),
            pltpu.SemaphoreType.DMA((count,)),
        ],
        compiler_params=pltpu.CompilerParams(vmem_limit_bytes=VMEM),
        cost_estimate=LITTLE,
        name="assemble",
    )(*pieces, *others)


def exchange(values, bit, size):
    return lax.ppermute(values, "dp", [(k, k ^ (1 << bit)) for k in range(size)])


def squared(size, rows):
    return size == 8 and rows % 256 == 0


def spread_begin(own, size, *before):
    (own,) = fence([own], *before)
    if squared(size, own.shape[0]):
        return [own, exchange(own, 1, size), exchange(own, 2, size)]
    pieces = own
    for bit in range(1, size.bit_length() - 2):
        pieces = jnp.concatenate([pieces, exchange(pieces, bit, size)])
    return [pieces]


def spread_end(some, size, before_last, before_core):
    if len(some) > 1:
        own, by_x, by_y = some
        unit = own.shape[0] // 2
        by_x, by_y = fence([by_x, by_y], *before_last)
        got = [exchange(by_x[:unit], 2, size), exchange(by_y[unit:], 1, size)]
        half = assemble([own, by_x, got[1], got[0], by_y], *before_core)
    else:
        (pieces,) = fence(some, *before_last)
        got = [exchange(pieces, size.bit_length() - 2, size)]
        half = jnp.concatenate([pieces] + fence(got, *before_core))
    return [half, exchange(half, 0, size)], got


def add_all(terms):
    total = terms[0].astype(F32)
    for term in terms[1:]:
        total = total + term.astype(F32)
    return total.astype(BF)


class Collect:
    def __init__(self, keep, send, size, d_own):
        self.size, self.unit = size, d_own // 2
        self.square = squared(size, d_own)
        self.bit = size.bit_length() - 2
        self.terms = [keep, exchange(send, 0, size)]
        self.first = self.last = None

    def rows(self, start, stop):
        return [t[start * self.unit : stop * self.unit] for t in self.terms]

    def sources(self):
        if not self.square:
            cut = self.terms[0].shape[0] // 2
            return [add_all([t[cut:] for t in self.terms])]
        if self.first is None:
            return [add_all(self.rows(3, 5)), add_all(self.rows(5, 7))]
        by_x, by_y = self.first
        return [add_all(self.rows(2, 3) + [by_y[: self.unit]]), add_all(self.rows(7, 8) + [by_x[self.unit :]])]

    def hop(self, sources):
        if not self.square:
            got = exchange(sources[0], self.bit, self.size)
            self.bit -= 1
            self.terms = [t[: got.shape[0]] for t in self.terms] + [got]
            return [got]
        got = [exchange(v, bit, self.size) for v, bit in zip(sources, (1, 2))]
        if self.first is None:
            self.first = got
        else:
            self.last = got
        return got

    def finish(self):
        if not self.square:
            while self.bit:
                self.hop(self.sources())
            return add_all(self.terms)
        low = add_all(self.rows(0, 1) + [self.first[1][self.unit :], self.last[0]])
        high = add_all(self.rows(1, 2) + [self.first[0][: self.unit], self.last[1]])
        return jnp.concatenate([low, high])


def z_shift(values, by, n, around=True):
    pairs = [(k, (k + by) % n) for k in range(n) if around or 0 <= k + by < n]
    return lax.ppermute(values, "tensor", pairs)


def z_scatter(values, n):
    turn = lax.axis_index("tensor")
    total = lax.dynamic_index_in_dim(values, turn, 0, keepdims=False).astype(F32)
    for k in range(1, n):
        block = lax.dynamic_index_in_dim(values, (turn + k) % n, 0, keepdims=False)
        total = total + z_shift(block, k, n).astype(F32)
    return total


class LineSum:
    def __init__(self, blocks, n):
        self.blocks, self.n, self.turn, self.rounds = blocks, n, lax.axis_index("tensor"), 0
        self.right = self.left = None

    def block(self, k):
        return lax.dynamic_index_in_dim(self.blocks, k % self.n, 0, keepdims=False)

    def go(self, *others):
        self.rounds += 1
        t, n = self.rounds, self.n
        right, left = self.block(self.turn + n - t), self.block(self.turn + t)
        if t > 1:
            before = fence([self.right, self.left], *others)
            right, left = add_all([right, before[0]]), add_all([left, before[1]])
        self.right = lax.ppermute(right, "tensor", [(k, k + 1) for k in range(min(t, n - 1))])
        self.left = lax.ppermute(left, "tensor", [(k, k - 1) for k in range(max(n - t, 1), n)])

    def finish(self):
        while self.rounds < self.n - 1:
            self.go()
        return self.block(self.turn).astype(F32) + self.right.astype(F32) + self.left.astype(F32)


def small_masks(size):
    turns = (0, 2, 6, 4) if size == 8 else tuple(q << 1 for q in range(size // 2))
    return np.array([core | mask for core in range(2) for mask in turns], np.int32)


def small_begin(own, size):
    if size == 8:
        return [own, exchange(own, 1, size), exchange(own, 2, size)]
    rows = own[None]
    for bit in range(1, size.bit_length() - 1):
        rows = jnp.concatenate([rows, exchange(rows, bit, size)])
    return [rows]


def small_end(some, size):
    if size == 8:
        own, by_x, by_y = some
        cut = own.shape[0] // 2
        far = jnp.concatenate([exchange(by_x[:cut], 2, size), exchange(by_y[cut:], 1, size)])
        rows = jnp.stack([own, by_x, far, by_y])
    else:
        (rows,) = some
    return jnp.concatenate([rows, exchange(rows, 0, size)])


def small_scatter(values, size, n):
    place = lax.axis_index("dp")
    values = jnp.take(values, jnp.arange(size) ^ place, axis=0, mode="clip")
    for bit in reversed(range(size.bit_length() - 1)):
        half = values.shape[0] // 2
        values = add_all([values[:half], exchange(values[half:], bit, size)])
    return z_scatter(values[0], n)


def basis_spots(size, rows):
    if squared(size, rows):
        turns = ((0, 0), (0, 1), (2, 0), (2, 1), (6, 1), (6, 0), (4, 0), (4, 1))
        return [(core | mask, part) for core in range(2) for mask, part in turns], 2
    return [(core | q << 1, 0) for core in range(2) for q in range(size // 2)], 1


def basis(size, rows, place):
    spots, parts = basis_spots(size, rows)
    masks, which = (jnp.asarray(np.array(v, np.int32)) for v in zip(*spots))
    table = (place ^ masks) * parts + which
    spots = jnp.arange(table.shape[0], dtype=jnp.int32)
    inverse = jnp.sum(jnp.where(table[None, :] == spots[:, None], spots[None, :], 0), axis=1)
    return table, inverse.astype(jnp.int32)


def copy_kernel(blocks, table_ref, in_ref, out_ref):
    width = in_ref.shape[1] // blocks
    for p in range(blocks):
        start = pl.multiple_of(table_ref[p] * width, width)
        out_ref[:, p * width : (p + 1) * width] = in_ref[:, pl.ds(start, width)]


def permute_rows(values, table, step=0, stride=1, offset=0):
    rows, d_model = values.shape
    step = step or max(k for k in range(16, 289, 16) if rows % k == 0)
    return pl.pallas_call(
        functools.partial(copy_kernel, table.shape[0]),
        grid_spec=pltpu.PrefetchScalarGridSpec(
            num_scalar_prefetch=1,
            grid=(rows // (step * stride),),
            in_specs=[pl.BlockSpec((step, d_model), lambda r, tab: (r * stride + offset, 0))],
            out_specs=pl.BlockSpec((step, d_model), lambda r, tab: (r, 0)),
        ),
        out_shape=jax.ShapeDtypeStruct((rows // stride, d_model), values.dtype),
        compiler_params=pltpu.CompilerParams(vmem_limit_bytes=VMEM),
        cost_estimate=LITTLE,
        name="permute",
    )(table, values)


def permute_gain(values, table):
    lead = values.shape[0]
    return jnp.take(values.reshape(lead, table.shape[0], -1), table, axis=1, mode="clip").reshape(lead, -1)


def row_ids(count, width, first):
    return lax.broadcasted_iota(jnp.int32, (count, width), 0) + first


def scan_slab(decay, value, back):
    rows = row_ids(SLAB, decay.shape[1], 0)
    for step in (1, 2, 4):
        keep = rows < SLAB - step if back else rows >= step
        shift = SLAB - step if back else step
        moved_decay = pltpu.roll(decay, shift, 0)
        moved_value = pltpu.roll(value, shift, 0)
        value = jnp.where(keep, value + decay * moved_value, value)
        decay = jnp.where(keep, decay * moved_decay, decay)
    return decay, value


def head_mask(head, at, width):
    lanes = lax.broadcasted_iota(jnp.int32, (head, 2 * width), 1)
    lanes = jnp.where(lanes >= width, lanes - width, lanes)
    return (lanes >= at * head) & (lanes < (at + 1) * head)


def fill_dense(w_ref, order_ref, dense_ref):
    head, count = order_ref.shape
    pad = count // w_ref.shape[0]
    width = dense_ref.shape[0]
    for gate in range(2):
        rows = w_ref[:, gate * pad : (gate + 1) * pad, :].reshape(count, width)
        rows = dot(order_ref[...], rows)
        for k in range(width // head):
            lanes = lax.broadcasted_iota(jnp.int32, (head, width), 1)
            block = jnp.where((lanes >= k * head) & (lanes < (k + 1) * head), rows, 0.0)
            dense_ref[k * head : (k + 1) * head, gate * width : (gate + 1) * width] = block.astype(BF)


def forward_kernel(
    live_ref, pre_ref, par_ref, w_ref, order_ref, conv_ref, decay_ref, ig_ref, dg_ref, state_ref, prod_ref,
    rec_ref, dense_ref,
):
    rows, width = conv_ref.shape
    fill_dense(w_ref, order_ref, dense_ref)
    live = live_ref[0]
    rec_ref[...] = jnp.where(row_ids(rows + HALO, width, -HALO) < live, pre_ref[...], 0.0)
    par = [par_ref[k : k + 1, :] for k in range(8)]
    for at in range(0, rows, ROWS):
        span = pl.ds(at, ROWS)
        near = rec_ref[pl.ds(at, ROWS + HALO), :]
        conv = par[4] + par[0] * near[HALO : HALO + ROWS]
        for k in range(1, 4):
            conv = conv + par[k] * near[HALO - k : HALO - k + ROWS]
        conv = jnp.where(row_ids(ROWS, width, at) < live, conv, 0.0)
        conv_ref[span, :] = conv
        gates = dot(conv.astype(BF), dense_ref[...])
        ig = lax.logistic(gates[:, :width] + par[5])
        dg = lax.logistic(gates[:, width:] + par[6])
        decay = jnp.exp(dg * par[7])
        ig_ref[span, :] = ig
        dg_ref[span, :] = dg
        decay_ref[span, :] = decay
        state_ref[span, :] = jnp.sqrt(jnp.maximum(1.0 - decay * decay, DECAY_FLOOR)) * ig * conv

    def slab(k, carry):
        state, prod = carry
        for inner in range(4):
            span = pl.ds(pl.multiple_of(k * 4 * SLAB + inner * SLAB, SLAB), SLAB)
            decay, value = scan_slab(decay_ref[span, :], state_ref[span, :], False)
            value = value + decay * state
            decay = decay * prod
            state_ref[span, :] = value
            prod_ref[span, :] = decay
            state = jnp.broadcast_to(value[SLAB - 1 :, :], (SLAB, width))
            prod = jnp.broadcast_to(decay[SLAB - 1 :, :], (SLAB, width))
        return state, prod

    lax.fori_loop(0, rows // (4 * SLAB), slab, (jnp.zeros((SLAB, width), F32), jnp.ones((SLAB, width), F32)))


def back_scan_kernel(
    live_ref, pre_ref, grad_ref, decay_ref, state_ref, prod_ref, cin_ref, lam_ref, reach_ref, edge_ref, low_ref
):
    rows, width = grad_ref.shape
    live = live_ref[0]
    cin = cin_ref[:1, :]
    c = np.float32(np.sqrt(2 / np.pi))
    for at in range(0, rows, ROWS):
        span = pl.ds(at, ROWS)
        v, grad = pre_ref[span, :], grad_ref[span, :]
        square = v * v
        bend = jnp.tanh(v * (c + (c * 0.044715) * square))
        rise = 0.5 + 0.5 * bend
        slope = rise + 0.5 * v * (1.0 - bend * bend) * (c + (3 * c * 0.044715) * square)
        grad = jnp.where(row_ids(ROWS, width, at) < live, grad, 0.0)
        lam_ref[span, :] = grad * (v * rise)
        low_ref[span, :] = (grad * (state_ref[span, :] + prod_ref[span, :] * cin) * slope).astype(BF)
    last = row_ids(SLAB, width, 0) == SLAB - 1

    def slab(k, carry):
        lam, reach, following, _ = carry
        for inner in range(4):
            span = pl.ds(pl.multiple_of(rows - (k * 4 + inner + 1) * SLAB, SLAB), SLAB)
            own = decay_ref[span, :]
            ahead = jnp.where(last, following, pltpu.roll(own, SLAB - 1, 0))
            decay, value = scan_slab(ahead, lam_ref[span, :], True)
            value = value + decay * lam
            decay = decay * reach
            lam_ref[span, :] = value
            reach_ref[span, :] = decay
            lam = jnp.broadcast_to(value[:1, :], (SLAB, width))
            reach = jnp.broadcast_to(decay[:1, :], (SLAB, width))
            following = jnp.broadcast_to(own[:1, :], (SLAB, width))
        return lam, reach, following, own

    one = jnp.ones((SLAB, width), F32)
    zero = jnp.zeros((SLAB, width), F32)
    lam, _, following, _ = lax.fori_loop(0, rows // (4 * SLAB), slab, (zero, one, one, one))
    edge_ref[...] = lam * following


def backward_kernel(
    live_ref, pre_ref, par_ref, w_ref, order_ref, lam_ref, reach_ref, edge_ref, decay_ref, conv_ref, ig_ref, dg_ref, state_ref, prod_ref, cin_ref,
    drec_ref, dpar_ref, dw_ref, rec_ref, dconv_ref, full_ref, dw_acc, dense_ref,
):
    rows, width = conv_ref.shape
    live = live_ref[0]
    rec_ref[...] = jnp.where(row_ids(rows + HALO, width, -HALO) < live, pre_ref[...], 0.0)
    par = [par_ref[k : k + 1, :] for k in range(8)]
    fill_dense(w_ref, order_ref, dense_ref)
    cin = cin_ref[:1, :]
    edge = edge_ref[:1, :]
    full_ref[:SLAB, :] = jnp.broadcast_to(cin, (SLAB, width))
    dconv_ref[:HALO, :] = jnp.zeros((HALO, width), F32)
    dconv_ref[rows + HALO :, :] = jnp.zeros((HALO, width), F32)
    sums = [jnp.zeros((1, width), F32) for _ in range(8)]
    for at in range(0, rows, ROWS):
        span = pl.ds(at, ROWS)
        full_ref[pl.ds(at + SLAB, ROWS), :] = state_ref[span, :] + prod_ref[span, :] * cin
        lam = lam_ref[span, :] + reach_ref[span, :] * edge
        decay, conv, ig, dg = decay_ref[span, :], conv_ref[span, :], ig_ref[span, :], dg_ref[span, :]
        before = full_ref[pl.ds(at, ROWS + SLAB), :][SLAB - 1 : SLAB - 1 + ROWS]
        room = 1.0 - decay * decay
        scale = jnp.sqrt(jnp.maximum(room, DECAY_FLOOR))
        lam_conv = lam * conv
        d_decay = lam * before - jnp.where(room > DECAY_FLOOR, lam_conv * ig * decay / scale, 0.0)
        moved = d_decay * decay
        sums[7] = sums[7] + jnp.sum(moved * dg, axis=0, keepdims=True)
        d_ig = lam_conv * scale * ig * (1.0 - ig)
        d_dg = moved * par[7] * dg * (1.0 - dg)
        sums[5] = sums[5] + jnp.sum(d_ig, axis=0, keepdims=True)
        sums[6] = sums[6] + jnp.sum(d_dg, axis=0, keepdims=True)
        both = jnp.concatenate([d_ig.astype(BF), d_dg.astype(BF)], axis=1)
        d_conv = lam * scale * ig + dot(both, dense_ref[...], ((1,), (1,)))
        d_conv = jnp.where(row_ids(ROWS, width, at) < live, d_conv, 0.0)
        dconv_ref[pl.ds(at + HALO, ROWS), :] = d_conv
        part = dot(conv.astype(BF), both, ((0,), (0,)))
        dw_acc[...] = part if at == 0 else dw_acc[...] + part
        near = rec_ref[pl.ds(at, ROWS + HALO), :]
        for k in range(4):
            sums[k] = sums[k] + jnp.sum(d_conv * near[HALO - k : HALO - k + ROWS], axis=0, keepdims=True)
        sums[4] = sums[4] + jnp.sum(d_conv, axis=0, keepdims=True)
    for k in range(8):
        dpar_ref[k : k + 1, :] = sums[k]
    head = dw_ref.shape[0]
    total = jnp.zeros((head, 2 * width), F32)
    for k in range(width // head):
        total = total + jnp.where(head_mask(head, k, width), dw_acc[k * head : (k + 1) * head, :], 0.0)
    dw_ref[...] = total.astype(BF)
    for at in list(range(0, rows, ROWS)) + [rows]:
        count = ROWS if at < rows else HALO
        near = dconv_ref[pl.ds(at, count + SLAB), :]
        total = par[0] * near[:count]
        for k in range(1, 4):
            total = total + par[k] * near[k : k + count]
        drec_ref[pl.ds(at, count), :] = total


def kernel_call(body, live, arrays, outs, scratch, name):
    width = outs[0][1]
    steps = width // GROUP
    specs = []
    for array in arrays:
        if array.ndim == 4:
            block = (array.shape[0], pl.squeezed) + array.shape[2:]
            specs.append(pl.BlockSpec(block, lambda j, s: (0, j, 0, 0)))
        elif array.shape[1] != width:
            specs.append(pl.BlockSpec(array.shape, lambda j, s: (0, 0)))
        else:
            specs.append(pl.BlockSpec((array.shape[0], GROUP), lambda j, s: (0, j)))
    out_specs, out_shapes = [], []
    for rows, cols, kind in outs:
        if cols == width:
            out_specs.append(pl.BlockSpec((rows, GROUP), lambda j, s: (0, j)))
            out_shapes.append(jax.ShapeDtypeStruct((rows, cols), kind))
        else:
            out_specs.append(pl.BlockSpec((pl.squeezed, rows, cols), lambda j, s: (j, 0, 0)))
            out_shapes.append(jax.ShapeDtypeStruct((steps, rows, cols), kind))
    return pl.pallas_call(
        body,
        grid_spec=pltpu.PrefetchScalarGridSpec(
            num_scalar_prefetch=1, grid=(steps,), in_specs=specs, out_specs=out_specs,
            scratch_shapes=[pltpu.VMEM(shape, kind) for shape, kind in scratch],
        ),
        out_shape=out_shapes,
        compiler_params=pltpu.CompilerParams(vmem_limit_bytes=VMEM),
        cost_estimate=LITTLE,
        name=name,
    )(live, *arrays)


def norm_rate(values):
    return lax.rsqrt(jnp.mean(values * values, axis=-1, keepdims=True) + NORM_EPS)


def norm_back(grad, unit, rate, gain):
    moved = grad * gain
    return rate * (moved - unit * jnp.mean(moved * unit, axis=-1, keepdims=True))


def gelu_product(gate, up):
    return jax.nn.gelu(gate) * up


def wide_dot(left, halves):
    cut = halves[0].shape[0]
    return dot(left[:, :cut], halves[0]) + dot(left[:, cut:], halves[1])


def wide_back(left, halves):
    return jnp.concatenate([dot(left, h, ((1,), (1,))) for h in halves], axis=1)


def on_device(size, n, tokens, lengths, gains, w_gelu, w_rec, chan, w_lru, w_out, w_mlp_in, w_down, cotangent):
    place = lax.axis_index("dp")
    turn = lax.axis_index("tensor")
    d_model = tokens.shape[1]
    rows = tokens.shape[0] // n
    half = rows // 2
    d_own = w_gelu.shape[0]
    heads_own, part, head = chan.shape[1], chan.shape[2], w_lru.shape[3]
    heads = heads_own * n
    width = heads * head
    groups = width // GROUP
    table, inverse = basis(size, d_own, place)
    live_count = (lengths - turn * rows).astype(jnp.int32)
    live = (lax.iota(jnp.int32, rows)[:, None] < live_count).astype(F32)

    cols = w_gelu.shape[1]
    pad = -(-part // 16) * 16
    own_lru = jnp.pad(w_lru.transpose(0, 2, 1, 3).reshape(2, part, cols), ((0, 0), (0, pad - part), (0, 0)))
    own_chan = jnp.zeros((8, heads_own, head), F32)
    own_chan = lax.dynamic_update_slice(own_chan, chan, (0, 0, place * part)).reshape(8, cols)
    own_gain = jnp.pad(gains.reshape(1, -1), ((0, 7), (0, cols - gains.size)))
    small = jnp.concatenate([own_lru.reshape(2 * pad, cols), own_chan, own_gain])
    whole = jnp.concatenate([w_rec, small]).astype(BF)
    others = jnp.concatenate([w_gelu, w_out.T]).astype(BF)
    own_gu = jnp.concatenate([w_mlp_in[0], w_mlp_in[1]], axis=1).astype(BF)
    own_dn = w_down.T.astype(BF)
    some_gu = spread_begin(own_gu, size)

    main = lax.dynamic_slice_in_dim(tokens, turn * rows, rows)
    before = lax.dynamic_slice_in_dim(tokens, jnp.maximum(turn * rows - HALO, 0), HALO)
    before = jnp.where(turn > 0, before, jnp.zeros_like(before))
    turned = permute_rows(jnp.concatenate([before, main]), table)
    extended = turned.astype(F32)
    first_rate = norm_rate(extended)

    def wide(blocks):
        return blocks.transpose(1, 0, 2).reshape(d_own, width)

    (whole,) = fence([lax.all_gather(whole, "tensor", axis=0)], *some_gu[1:], others, turned, first_rate)
    others = lax.all_gather(*fence([others], whole), "tensor", axis=0)
    z_gelu, z_out = wide(others[:, :d_own]), wide(others[:, d_own:])
    some_r = spread_begin(wide(whole[:, :d_own]), size)
    some_small = small_begin(whole[:, d_own:].reshape(-1, cols), size)
    small = small_end(some_small, size).reshape(size, n, -1, cols)

    masks = small_masks(size)
    gain = small[:, 0, 2 * pad + 8, : gains.size].reshape(size, 2, d_own)
    if squared(size, d_own):
        swapped = jnp.concatenate([gain[..., d_own // 2 :], gain[..., : d_own // 2]], axis=-1)
        gain = jnp.where(((jnp.asarray(masks) & 6) == 6)[:, None, None], swapped, gain)
    gain = gain.transpose(1, 0, 2).reshape(2, d_model).astype(F32)
    chans = jnp.sum(small[:, :, 2 * pad : 2 * pad + 8].astype(F32), axis=0)
    chans = chans.transpose(1, 0, 2).reshape(8, width)
    par = jnp.concatenate([chans[:7], -8.0 * jax.nn.softplus(-chans[7:])])
    each = n // groups
    lru = small
    if each > 1:
        lru = lru.reshape(size, groups, each, -1, cols).transpose(0, 1, 3, 2, 4).reshape(size, groups, -1, GROUP)
    spot = (place ^ jnp.asarray(masks))[jnp.arange(size * pad) // pad]
    row = jnp.arange(size * pad) % pad
    row = jnp.where(row < part, spot * part + row, head)
    order = (jnp.arange(head)[:, None] == row[None, :]).astype(BF)

    w_r, came_r = spread_end(some_r, size, (), (others, order))
    first = (extended * first_rate * gain[0]).astype(BF)
    inputs, first_own, first_rate = extended[HALO:], first[HALO:], first_rate[HALO:]
    cut = d_model // 2

    keep = (rows, width, F32)
    dense = ((GROUP, 2 * GROUP), BF)
    some_g = spread_begin(z_gelu, size, *came_r)
    rec_pre = wide_dot(first, w_r)
    conv, decay, ig, dg, state, prod = kernel_call(
        forward_kernel, live_count, [rec_pre, par, lru, order], [keep] * 6,
        [((rows + HALO, GROUP), F32), dense], "recurrence",
    )
    ends = jnp.concatenate([prod[-1:], state[-1:]])
    came = [z_shift(ends, k, n, False) for k in range(1, n)]
    w_g, came_g = spread_end(some_g, size, (ends,), came)
    carry = jnp.zeros((1, width), F32)
    for end in came[::-1]:
        carry = end[1:] + end[:1] * carry
    some_o = spread_begin(z_out, size, *came_g)
    branch_pre = wide_dot(first_own, w_g)
    recurrent = (state + prod * carry) * live
    mixed = (jax.nn.gelu(branch_pre) * recurrent).astype(BF)
    w_o, came_o = spread_end(some_o, size, (branch_pre,), (mixed,))
    hidden = inputs + wide_back(mixed, w_o)
    second_rate = norm_rate(hidden)
    second_unit = hidden * second_rate
    second_own = (second_unit * gain[1]).astype(BF)
    w_gu, came_gu = spread_end(some_gu, size, came_o, (second_own,))
    w_dn, _ = spread_end(spread_begin(own_dn, size, *came_gu), size, (), ())
    w_gu, w_dn = assemble(w_gu), assemble(w_dn)
    late = fence([table], second_own)[0]
    cots = [permute_rows(cotangent, late, half, 2, h) for h in range(2)]

    hidden_units = w_dn.shape[1]
    grad_products = [dot(c, w_dn) for c in cots]
    shares, grad_second, seconds, products, grads = [], [], [], [], []
    for h in range(2):
        second = lax.all_gather(second_own[h * half : (h + 1) * half], "tensor", axis=0, tiled=True)
        (second,) = fence([second], *shares)
        both = dot(second, w_gu)
        product, pull = jax.vjp(gelu_product, both[:, :hidden_units], both[:, hidden_units:])
        grad_gate, grad_up = pull(grad_products[h])
        product = product.astype(BF)
        grad = jnp.concatenate([grad_gate.astype(BF), grad_up.astype(BF)], axis=1)
        share = dot(grad, w_gu, ((1,), (1,))).astype(BF)
        shares.append(share)
        grad_second.append(lax.psum_scatter(share, "tensor", scatter_dimension=0, tiled=True))
        seconds.append(second)
        products.append(product)
        grads.append(grad)

    products, grads = [[*pair] for pair in zip(*[fence([p, g], shares[-1]) for p, g in zip(products, grads)])]
    shares = [dot(p, w_dn, ((1,), (1,))).astype(BF) for p in products]

    def by_rows(lefts, rights):
        parts = []
        for span in (slice(cut, None), slice(0, cut)):
            part = dot(lefts[0][:, span], rights[0], ((0,), (0,)))
            parts.append((part + dot(lefts[1][:, span], rights[1], ((0,), (0,)))).astype(BF))
        return Collect(parts[1], parts[0], size, d_own)

    sum_dn = by_rows(cots, products)
    sum_gu = by_rows(seconds, grads)
    sent_dn, sent_gu = sum_dn.sources(), sum_gu.sources()
    grad_second = fence(grad_second, *sent_dn, *sent_gu, *shares)
    came_mlp = sum_dn.hop(sent_dn) + sum_gu.hop(sent_gu)

    shares = fence(shares, *grad_second)
    mlp_sums = [lax.psum_scatter(share, "tensor", scatter_dimension=0, tiled=True) for share in shares]

    grad_second = jnp.concatenate(grad_second).astype(F32)
    cot_own = jnp.concatenate([lax.dynamic_slice_in_dim(c, turn * half, half) for c in cots]).astype(F32)
    gain_two = jnp.sum(grad_second * second_unit, axis=0)
    grad_hidden = cot_own + norm_back(grad_second, second_unit, second_rate, gain[1])
    hidden_low = grad_hidden.astype(BF)

    def by_cols(left, right):
        parts = [dot(left[:, span], right, ((0,), (0,))).astype(BF) for span in (slice(cut, None), slice(0, cut))]
        return Collect(parts[1], parts[0], size, d_own)

    grad_mixed = wide_dot(hidden_low, w_o)
    tall = jnp.broadcast_to
    lam, reach, edge, pre_low = kernel_call(
        back_scan_kernel, live_count, [branch_pre, grad_mixed, decay, state, prod, tall(carry, (SLAB, width))],
        [keep, keep, (SLAB, width, F32), (rows, width, BF)], [], "back_scan",
    )
    edges = jnp.concatenate([prod[-1:], edge[:1]])
    came = [z_shift(edges, -k, n, False) for k in range(1, n)]
    arriving = jnp.zeros((1, width), F32)
    for end in came[::-1]:
        arriving = end[1:] + end[:1] * arriving
    (lam,) = fence([lam], *came_mlp)
    drec, dpar, d_lru = kernel_call(
        backward_kernel, live_count,
        [rec_pre, par, lru, order, lam, reach, tall(arriving, (SLAB, width)), decay, conv, ig, dg, state, prod, tall(carry, (SLAB, width))],
        [(rows + HALO, width, F32), (8, width, F32), (head, 2 * GROUP, BF)],
        [((rows + HALO, GROUP), F32), ((rows + 2 * HALO, GROUP), F32), ((rows + SLAB, GROUP), F32), ((GROUP, 2 * GROUP), F32), dense],
        "recurrence_back",
    )
    (edge_rows,) = fence([z_shift(drec[:HALO], -1, n, False)], mlp_sums[0])
    rec_low = (drec[HALO:] + jnp.pad(edge_rows, ((rows - HALO, 0), (0, 0)))) * live
    rec_low = rec_low.astype(BF)
    (pre_low,) = fence([pre_low], drec)
    grad_first = wide_back(pre_low, w_g) + wide_back(rec_low, w_r)
    first_unit = inputs * first_rate
    gain_one = jnp.sum(grad_first * first_unit, axis=0)
    grad_tokens = grad_hidden + norm_back(grad_first, first_unit, first_rate, gain[0])
    grad_tokens = permute_rows(grad_tokens.astype(BF), inverse)
    gathered = lax.all_gather(grad_tokens, "tensor", axis=0, tiled=True)
    (mixed,) = fence([mixed], grad_tokens)
    sum_o = by_cols(hidden_low, mixed)
    pre_low, rec_low = fence([pre_low, rec_low], sum_o.terms[1])
    sum_g, sum_r = by_cols(first_own, pre_low), by_cols(first_own, rec_low)
    mlp_sum = jnp.concatenate(fence(mlp_sums, sum_o.terms[1])).astype(F32)
    result = permute_rows((hidden + mlp_sum).astype(BF), inverse)
    got_o = sum_o.hop(fence(sum_o.sources(), result))
    result = lax.all_gather(result, "tensor", axis=0, tiled=True)
    got_g = sum_g.hop(fence(sum_g.sources(), *got_o))
    sum_o.hop(fence(sum_o.sources(), *got_g))
    got_r = sum_r.hop(fence(sum_r.sources(), *got_g))
    sum_g.hop(fence(sum_g.sources(), *got_g))
    got_r = sum_r.hop(fence(sum_r.sources(), *got_r))
    (tokens_out,) = fence([gathered], *got_r, cost=MUCH)
    owned = jnp.stack([total.finish().reshape(d_own, n, width // n) for total in (sum_o, sum_g, sum_r)])
    owned = LineSum(owned.transpose(2, 0, 1, 3), n)
    owned.go()
    d_lru, dpar = fence([d_lru, dpar], *got_r)
    if sum_dn.square:
        sum_dn.hop(fence(sum_dn.sources(), *got_r))
        sum_gu.hop(fence(sum_gu.sources(), *got_r))
    g_gu, g_dn = sum_gu.finish().astype(F32), sum_dn.finish().astype(F32)
    g_all = owned.finish()
    (output,) = fence([result], owned.right, owned.left, g_gu, g_dn, cost=MUCH)
    g_o, g_g, g_r = g_all[0], g_all[1], g_all[2]

    d_gain = permute_gain(jnp.stack([gain_one, gain_two]), inverse)
    d_chan = jnp.concatenate([dpar[:7], dpar[7:] * 8.0 * jax.nn.sigmoid(-chans[7:])])
    d_lru = d_lru.reshape(groups, size, part, 2, each, -1).transpose(1, 0, 4, 2, 3, 5)
    d_chan = d_chan.reshape(8, n, heads_own, size, part).transpose(3, 1, 0, 2, 4)
    d_gain = d_gain.reshape(2, size, 1, d_own).transpose(1, 2, 0, 3)
    d_gain = jnp.broadcast_to(d_gain, (size, n, 2, d_own))
    small = [v.reshape(size, n, -1).astype(BF) for v in (d_lru, d_chan, d_gain)]
    small = small_scatter(jnp.concatenate(small, axis=2), size, n)
    d_lru = small[: w_lru.size].reshape(part, 2, heads_own, head).transpose(1, 2, 0, 3)
    d_chan = small[w_lru.size : -gains.size].reshape(chan.shape)
    d_gain = small[-gains.size :].reshape(gains.shape)
    g_gate, g_up = g_gu[:, :hidden_units], g_gu[:, hidden_units:]
    return (
        output, tokens_out, d_gain[0], d_gain[1], g_g, g_r, d_chan, d_lru,
        g_o.T, jnp.stack([g_gate, g_up]), g_dn.T,
    )


def solution(mesh):
    in_specs = (
        P("dp", None),
        P("dp"),
        P(None, "dp"),
        P("dp", "tensor"),
        P("dp", "tensor"),
        P(None, "tensor", "dp"),
        P(None, "tensor", "dp", None),
        P("tensor", "dp"),
        P(None, "dp", "tensor"),
        P("tensor", "dp"),
        P("dp", None),
    )
    out_specs = (
        P("dp", None),
        P("dp", None),
        P("dp"),
        P("dp"),
        P("dp", "tensor"),
        P("dp", "tensor"),
        P(None, "tensor", "dp"),
        P(None, "tensor", "dp", None),
        P("tensor", "dp"),
        P(None, "dp", "tensor"),
        P("tensor", "dp"),
    )
    body = functools.partial(on_device, mesh.shape["dp"], mesh.shape["tensor"])
    return jax.shard_map(body, mesh=mesh, in_specs=in_specs, out_specs=out_specs, check_vma=False)
```

```python
import functools

import jax
import jax.numpy as jnp
import numpy as np
from jax import lax
from jax.experimental import pallas as pl
from jax.experimental.pallas import tpu as pltpu
from jax.sharding import PartitionSpec as P

NORM_EPS = 1e-06
DECAY_FLOOR = 0.05
HALO = 16
GROUP = 640
ROWS = 128
SLAB = 8
VMEM = 58 * 1024 * 1024
BF = jnp.bfloat16
F32 = jnp.float32
MUCH = pl.CostEstimate(flops=60 * 10**9, bytes_accessed=1024, transcendentals=0)
LITTLE = pl.CostEstimate(flops=1024, bytes_accessed=1024, transcendentals=0)


def dot(left, right, dims=((1,), (0,))):
    return lax.dot_general(left, right, (dims, ((), ())), preferred_element_type=F32)


def fence(values, *others, cost=LITTLE):
    if not others:
        return list(values)
    place = pl.BlockSpec(memory_space=pl.ANY)
    call = pl.pallas_call(
        lambda *refs: None,
        in_specs=[place] * (len(values) + len(others)),
        out_specs=[place] * len(values),
        out_shape=[jax.ShapeDtypeStruct(v.shape, v.dtype) for v in values],
        input_output_aliases={k: k for k in range(len(values))},
        compiler_params=pltpu.CompilerParams(vmem_limit_bytes=VMEM),
        cost_estimate=cost,
        name="fence",
    )
    return list(call(*values, *others))


def assemble(pieces, *others):
    count = len(pieces)
    rows = [p.shape[0] for p in pieces]
    spans = [pl.ds(sum(rows[:k]), rows[k]) for k in range(count)]
    shape = (sum(rows), pieces[0].shape[1])

    def body(*refs):
        out, held, coming, going = refs[count + len(others) :]
        ins = [pltpu.make_async_copy(refs[k], held.at[spans[k]], coming.at[k]) for k in range(count)]
        outs = [pltpu.make_async_copy(held.at[spans[k]], out.at[spans[k]], going.at[k]) for k in range(count)]
        for copy in ins:
            copy.start()
        for here, there in zip(ins, outs):
            here.wait()
            there.start()
        for copy in outs:
            copy.wait()

    place = pl.BlockSpec(memory_space=pl.ANY)
    return pl.pallas_call(
        body,
        in_specs=[place] * (count + len(others)),
        out_specs=place,
        out_shape=jax.ShapeDtypeStruct(shape, pieces[0].dtype),
        scratch_shapes=[
            pltpu.VMEM(shape, pieces[0].dtype),
            pltpu.SemaphoreType.DMA((count,)),
            pltpu.SemaphoreType.DMA((count,)),
        ],
        compiler_params=pltpu.CompilerParams(vmem_limit_bytes=VMEM),
        cost_estimate=LITTLE,
        name="assemble",
    )(*pieces, *others)


def exchange(values, bit, size):
    return lax.ppermute(values, "dp", [(k, k ^ (1 << bit)) for k in range(size)])


def squared(size, rows):
    return size == 8 and rows % 256 == 0


def spread_begin(own, size, *before):
    (own,) = fence([own], *before)
    if squared(size, own.shape[0]):
        return [own, exchange(own, 1, size), exchange(own, 2, size)]
    pieces = own
    for bit in range(1, size.bit_length() - 2):
        pieces = jnp.concatenate([pieces, exchange(pieces, bit, size)])
    return [pieces]


def spread_end(some, size, before_last, before_core):
    if len(some) > 1:
        own, by_x, by_y = some
        unit = own.shape[0] // 2
        by_x, by_y = fence([by_x, by_y], *before_last)
        got = [exchange(by_x[:unit], 2, size), exchange(by_y[unit:], 1, size)]
        half = assemble([own, by_x, got[1], got[0], by_y], *before_core)
    else:
        (pieces,) = fence(some, *before_last)
        got = [exchange(pieces, size.bit_length() - 2, size)]
        half = jnp.concatenate([pieces] + fence(got, *before_core))
    return [half, exchange(half, 0, size)], got


def add_all(terms):
    total = terms[0].astype(F32)
    for term in terms[1:]:
        total = total + term.astype(F32)
    return total.astype(BF)


class Collect:
    def __init__(self, keep, send, size, d_own):
        self.size, self.unit = size, d_own // 2
        self.square = squared(size, d_own)
        self.bit = size.bit_length() - 2
        self.terms = [keep, exchange(send, 0, size)]
        self.first = self.last = None

    def rows(self, start, stop):
        return [t[start * self.unit : stop * self.unit] for t in self.terms]

    def sources(self):
        if not self.square:
            cut = self.terms[0].shape[0] // 2
            return [add_all([t[cut:] for t in self.terms])]
        if self.first is None:
            return [add_all(self.rows(3, 5)), add_all(self.rows(5, 7))]
        by_x, by_y = self.first
        return [add_all(self.rows(2, 3) + [by_y[: self.unit]]), add_all(self.rows(7, 8) + [by_x[self.unit :]])]

    def hop(self, sources):
        if not self.square:
            got = exchange(sources[0], self.bit, self.size)
            self.bit -= 1
            self.terms = [t[: got.shape[0]] for t in self.terms] + [got]
            return [got]
        got = [exchange(v, bit, self.size) for v, bit in zip(sources, (1, 2))]
        if self.first is None:
            self.first = got
        else:
            self.last = got
        return got

    def finish(self):
        if not self.square:
            while self.bit:
                self.hop(self.sources())
            return add_all(self.terms)
        low = add_all(self.rows(0, 1) + [self.first[1][self.unit :], self.last[0]])
        high = add_all(self.rows(1, 2) + [self.first[0][: self.unit], self.last[1]])
        return jnp.concatenate([low, high])


def z_shift(values, by, n, around=True):
    pairs = [(k, (k + by) % n) for k in range(n) if around or 0 <= k + by < n]
    return lax.ppermute(values, "tensor", pairs)


def z_scatter(values, n):
    turn = lax.axis_index("tensor")
    total = lax.dynamic_index_in_dim(values, turn, 0, keepdims=False).astype(F32)
    for k in range(1, n):
        block = lax.dynamic_index_in_dim(values, (turn + k) % n, 0, keepdims=False)
        total = total + z_shift(block, k, n).astype(F32)
    return total


class LineSum:
    def __init__(self, blocks, n):
        self.blocks, self.n, self.turn, self.rounds = blocks, n, lax.axis_index("tensor"), 0
        self.right = self.left = None

    def block(self, k):
        return lax.dynamic_index_in_dim(self.blocks, k % self.n, 0, keepdims=False)

    def go(self, *others):
        self.rounds += 1
        t, n = self.rounds, self.n
        right, left = self.block(self.turn + n - t), self.block(self.turn + t)
        if t > 1:
            before = fence([self.right, self.left], self.blocks, *others)
            right, left = add_all([right, before[0]]), add_all([left, before[1]])
        self.right = lax.ppermute(right, "tensor", [(k, k + 1) for k in range(min(t, n - 1))])
        self.left = lax.ppermute(left, "tensor", [(k, k - 1) for k in range(max(n - t, 1), n)])

    def finish(self):
        while self.rounds < self.n - 1:
            self.go()
        return self.block(self.turn).astype(F32) + self.right.astype(F32) + self.left.astype(F32)


def small_masks(size):
    turns = (0, 2, 6, 4) if size == 8 else tuple(q << 1 for q in range(size // 2))
    return np.array([core | mask for core in range(2) for mask in turns], np.int32)


def small_begin(own, size):
    if size == 8:
        return [own, exchange(own, 1, size), exchange(own, 2, size)]
    rows = own[None]
    for bit in range(1, size.bit_length() - 1):
        rows = jnp.concatenate([rows, exchange(rows, bit, size)])
    return [rows]


def small_end(some, size):
    if size == 8:
        own, by_x, by_y = some
        cut = own.shape[0] // 2
        far = jnp.concatenate([exchange(by_x[:cut], 2, size), exchange(by_y[cut:], 1, size)])
        rows = jnp.stack([own, by_x, far, by_y])
    else:
        (rows,) = some
    return jnp.concatenate([rows, exchange(rows, 0, size)])


def small_scatter(values, size, n):
    place = lax.axis_index("dp")
    values = jnp.take(values, jnp.arange(size) ^ place, axis=0, mode="clip")
    for bit in reversed(range(size.bit_length() - 1)):
        half = values.shape[0] // 2
        values = add_all([values[:half], exchange(values[half:], bit, size)])
    return z_scatter(values[0], n)


def basis_spots(size, rows):
    if squared(size, rows):
        turns = ((0, 0), (0, 1), (2, 0), (2, 1), (6, 1), (6, 0), (4, 0), (4, 1))
        return [(core | mask, part) for core in range(2) for mask, part in turns], 2
    return [(core | q << 1, 0) for core in range(2) for q in range(size // 2)], 1


def basis(size, rows, place):
    spots, parts = basis_spots(size, rows)
    masks, which = (jnp.asarray(np.array(v, np.int32)) for v in zip(*spots))
    table = (place ^ masks) * parts + which
    spots = jnp.arange(table.shape[0], dtype=jnp.int32)
    inverse = jnp.sum(jnp.where(table[None, :] == spots[:, None], spots[None, :], 0), axis=1)
    return table, inverse.astype(jnp.int32)


def copy_kernel(blocks, table_ref, in_ref, out_ref):
    width = in_ref.shape[1] // blocks
    for p in range(blocks):
        start = pl.multiple_of(table_ref[p] * width, width)
        out_ref[:, p * width : (p + 1) * width] = in_ref[:, pl.ds(start, width)]


def permute_rows(values, table, step=0, stride=1, offset=0):
    rows, d_model = values.shape
    step = step or max(k for k in range(16, 289, 16) if rows % k == 0)
    return pl.pallas_call(
        functools.partial(copy_kernel, table.shape[0]),
        grid_spec=pltpu.PrefetchScalarGridSpec(
            num_scalar_prefetch=1,
            grid=(rows // (step * stride),),
            in_specs=[pl.BlockSpec((step, d_model), lambda r, tab: (r * stride + offset, 0))],
            out_specs=pl.BlockSpec((step, d_model), lambda r, tab: (r, 0)),
        ),
        out_shape=jax.ShapeDtypeStruct((rows // stride, d_model), values.dtype),
        compiler_params=pltpu.CompilerParams(vmem_limit_bytes=VMEM),
        cost_estimate=LITTLE,
        name="permute",
    )(table, values)


def move_kernel(in_ref, out_ref):
    out_ref[...] = in_ref[...]


def move(values):
    rows, d_model = values.shape
    spec = pl.BlockSpec((max(k for k in range(16, 289, 16) if rows % k == 0), d_model), lambda r: (r, 0))
    return pl.pallas_call(
        move_kernel,
        grid=(rows // spec.block_shape[0],),
        in_specs=[spec],
        out_specs=spec,
        out_shape=jax.ShapeDtypeStruct(values.shape, values.dtype),
        compiler_params=pltpu.CompilerParams(vmem_limit_bytes=VMEM),
        cost_estimate=LITTLE,
        name="move",
    )(values)


def permute_gain(values, table):
    lead = values.shape[0]
    return jnp.take(values.reshape(lead, table.shape[0], -1), table, axis=1, mode="clip").reshape(lead, -1)


def row_ids(count, width, first):
    return lax.broadcasted_iota(jnp.int32, (count, width), 0) + first


def scan_slab(decay, value, back):
    rows = row_ids(SLAB, decay.shape[1], 0)
    for step in (1, 2, 4):
        keep = rows < SLAB - step if back else rows >= step
        shift = SLAB - step if back else step
        moved_decay = pltpu.roll(decay, shift, 0)
        moved_value = pltpu.roll(value, shift, 0)
        value = jnp.where(keep, value + decay * moved_value, value)
        decay = jnp.where(keep, decay * moved_decay, decay)
    return decay, value


def head_mask(head, at, width):
    lanes = lax.broadcasted_iota(jnp.int32, (head, 2 * width), 1)
    lanes = jnp.where(lanes >= width, lanes - width, lanes)
    return (lanes >= at * head) & (lanes < (at + 1) * head)


def fill_dense(w_ref, order_ref, dense_ref):
    head, count = order_ref.shape
    pad = count // w_ref.shape[0]
    width = dense_ref.shape[0]
    for gate in range(2):
        rows = w_ref[:, gate * pad : (gate + 1) * pad, :].reshape(count, width)
        rows = dot(order_ref[...], rows)
        for k in range(width // head):
            lanes = lax.broadcasted_iota(jnp.int32, (head, width), 1)
            block = jnp.where((lanes >= k * head) & (lanes < (k + 1) * head), rows, 0.0)
            dense_ref[k * head : (k + 1) * head, gate * width : (gate + 1) * width] = block.astype(BF)


def forward_kernel(
    live_ref, pre_ref, par_ref, w_ref, order_ref, conv_ref, decay_ref, ig_ref, dg_ref, state_ref, prod_ref,
    rec_ref, dense_ref,
):
    rows, width = conv_ref.shape
    fill_dense(w_ref, order_ref, dense_ref)
    live = live_ref[0]
    rec_ref[...] = jnp.where(row_ids(rows + HALO, width, -HALO) < live, pre_ref[...], 0.0)
    par = [par_ref[k : k + 1, :] for k in range(8)]
    for at in range(0, rows, ROWS):
        span = pl.ds(at, ROWS)
        near = rec_ref[pl.ds(at, ROWS + HALO), :]
        conv = par[4] + par[0] * near[HALO : HALO + ROWS]
        for k in range(1, 4):
            conv = conv + par[k] * near[HALO - k : HALO - k + ROWS]
        conv = jnp.where(row_ids(ROWS, width, at) < live, conv, 0.0)
        conv_ref[span, :] = conv
        gates = dot(conv.astype(BF), dense_ref[...])
        ig = lax.logistic(gates[:, :width] + par[5])
        dg = lax.logistic(gates[:, width:] + par[6])
        decay = jnp.exp(dg * par[7])
        ig_ref[span, :] = ig
        dg_ref[span, :] = dg
        decay_ref[span, :] = decay
        state_ref[span, :] = jnp.sqrt(jnp.maximum(1.0 - decay * decay, DECAY_FLOOR)) * ig * conv

    def slab(k, carry):
        state, prod = carry
        for inner in range(4):
            span = pl.ds(pl.multiple_of(k * 4 * SLAB + inner * SLAB, SLAB), SLAB)
            decay, value = scan_slab(decay_ref[span, :], state_ref[span, :], False)
            value = value + decay * state
            decay = decay * prod
            state_ref[span, :] = value
            prod_ref[span, :] = decay
            state = jnp.broadcast_to(value[SLAB - 1 :, :], (SLAB, width))
            prod = jnp.broadcast_to(decay[SLAB - 1 :, :], (SLAB, width))
        return state, prod

    lax.fori_loop(0, rows // (4 * SLAB), slab, (jnp.zeros((SLAB, width), F32), jnp.ones((SLAB, width), F32)))


def back_scan_kernel(
    live_ref, pre_ref, grad_ref, decay_ref, state_ref, prod_ref, cin_ref, lam_ref, reach_ref, edge_ref, low_ref
):
    rows, width = grad_ref.shape
    live = live_ref[0]
    cin = cin_ref[:1, :]
    c = np.float32(np.sqrt(2 / np.pi))
    for at in range(0, rows, ROWS):
        span = pl.ds(at, ROWS)
        v, grad = pre_ref[span, :], grad_ref[span, :]
        square = v * v
        bend = jnp.tanh(v * (c + (c * 0.044715) * square))
        rise = 0.5 + 0.5 * bend
        slope = rise + 0.5 * v * (1.0 - bend * bend) * (c + (3 * c * 0.044715) * square)
        grad = jnp.where(row_ids(ROWS, width, at) < live, grad, 0.0)
        lam_ref[span, :] = grad * (v * rise)
        low_ref[span, :] = (grad * (state_ref[span, :] + prod_ref[span, :] * cin) * slope).astype(BF)
    last = row_ids(SLAB, width, 0) == SLAB - 1

    def slab(k, carry):
        lam, reach, following, _ = carry
        for inner in range(4):
            span = pl.ds(pl.multiple_of(rows - (k * 4 + inner + 1) * SLAB, SLAB), SLAB)
            own = decay_ref[span, :]
            ahead = jnp.where(last, following, pltpu.roll(own, SLAB - 1, 0))
            decay, value = scan_slab(ahead, lam_ref[span, :], True)
            value = value + decay * lam
            decay = decay * reach
            lam_ref[span, :] = value
            reach_ref[span, :] = decay
            lam = jnp.broadcast_to(value[:1, :], (SLAB, width))
            reach = jnp.broadcast_to(decay[:1, :], (SLAB, width))
            following = jnp.broadcast_to(own[:1, :], (SLAB, width))
        return lam, reach, following, own

    one = jnp.ones((SLAB, width), F32)
    zero = jnp.zeros((SLAB, width), F32)
    lam, _, following, _ = lax.fori_loop(0, rows // (4 * SLAB), slab, (zero, one, one, one))
    edge_ref[...] = lam * following


def backward_kernel(
    live_ref, pre_ref, par_ref, w_ref, order_ref, lam_ref, reach_ref, edge_ref, decay_ref, conv_ref, ig_ref, dg_ref, state_ref, prod_ref, cin_ref,
    drec_ref, dpar_ref, dw_ref, rec_ref, dconv_ref, full_ref, dw_acc, dense_ref,
):
    rows, width = conv_ref.shape
    live = live_ref[0]
    rec_ref[...] = jnp.where(row_ids(rows + HALO, width, -HALO) < live, pre_ref[...], 0.0)
    par = [par_ref[k : k + 1, :] for k in range(8)]
    fill_dense(w_ref, order_ref, dense_ref)
    cin = cin_ref[:1, :]
    edge = edge_ref[:1, :]
    full_ref[:SLAB, :] = jnp.broadcast_to(cin, (SLAB, width))
    dconv_ref[:HALO, :] = jnp.zeros((HALO, width), F32)
    dconv_ref[rows + HALO :, :] = jnp.zeros((HALO, width), F32)
    sums = [jnp.zeros((1, width), F32) for _ in range(8)]
    for at in range(0, rows, ROWS):
        span = pl.ds(at, ROWS)
        full_ref[pl.ds(at + SLAB, ROWS), :] = state_ref[span, :] + prod_ref[span, :] * cin
        lam = lam_ref[span, :] + reach_ref[span, :] * edge
        decay, conv, ig, dg = decay_ref[span, :], conv_ref[span, :], ig_ref[span, :], dg_ref[span, :]
        before = full_ref[pl.ds(at, ROWS + SLAB), :][SLAB - 1 : SLAB - 1 + ROWS]
        room = 1.0 - decay * decay
        scale = jnp.sqrt(jnp.maximum(room, DECAY_FLOOR))
        lam_conv = lam * conv
        d_decay = lam * before - jnp.where(room > DECAY_FLOOR, lam_conv * ig * decay / scale, 0.0)
        moved = d_decay * decay
        sums[7] = sums[7] + jnp.sum(moved * dg, axis=0, keepdims=True)
        d_ig = lam_conv * scale * ig * (1.0 - ig)
        d_dg = moved * par[7] * dg * (1.0 - dg)
        sums[5] = sums[5] + jnp.sum(d_ig, axis=0, keepdims=True)
        sums[6] = sums[6] + jnp.sum(d_dg, axis=0, keepdims=True)
        both = jnp.concatenate([d_ig.astype(BF), d_dg.astype(BF)], axis=1)
        d_conv = lam * scale * ig + dot(both, dense_ref[...], ((1,), (1,)))
        d_conv = jnp.where(row_ids(ROWS, width, at) < live, d_conv, 0.0)
        dconv_ref[pl.ds(at + HALO, ROWS), :] = d_conv
        part = dot(conv.astype(BF), both, ((0,), (0,)))
        dw_acc[...] = part if at == 0 else dw_acc[...] + part
        near = rec_ref[pl.ds(at, ROWS + HALO), :]
        for k in range(4):
            sums[k] = sums[k] + jnp.sum(d_conv * near[HALO - k : HALO - k + ROWS], axis=0, keepdims=True)
        sums[4] = sums[4] + jnp.sum(d_conv, axis=0, keepdims=True)
    for k in range(8):
        dpar_ref[k : k + 1, :] = sums[k]
    head = dw_ref.shape[0]
    total = jnp.zeros((head, 2 * width), F32)
    for k in range(width // head):
        total = total + jnp.where(head_mask(head, k, width), dw_acc[k * head : (k + 1) * head, :], 0.0)
    dw_ref[...] = total.astype(BF)
    for at in list(range(0, rows, ROWS)) + [rows]:
        count = ROWS if at < rows else HALO
        near = dconv_ref[pl.ds(at, count + SLAB), :]
        total = par[0] * near[:count]
        for k in range(1, 4):
            total = total + par[k] * near[k : k + count]
        drec_ref[pl.ds(at, count), :] = total


def kernel_call(body, live, arrays, outs, scratch, name):
    width = outs[0][1]
    steps = width // GROUP
    specs = []
    for array in arrays:
        if array.ndim == 4:
            block = (array.shape[0], pl.squeezed) + array.shape[2:]
            specs.append(pl.BlockSpec(block, lambda j, s: (0, j, 0, 0)))
        elif array.shape[1] != width:
            specs.append(pl.BlockSpec(array.shape, lambda j, s: (0, 0)))
        else:
            specs.append(pl.BlockSpec((array.shape[0], GROUP), lambda j, s: (0, j)))
    out_specs, out_shapes = [], []
    for rows, cols, kind in outs:
        if cols == width:
            out_specs.append(pl.BlockSpec((rows, GROUP), lambda j, s: (0, j)))
            out_shapes.append(jax.ShapeDtypeStruct((rows, cols), kind))
        else:
            out_specs.append(pl.BlockSpec((pl.squeezed, rows, cols), lambda j, s: (j, 0, 0)))
            out_shapes.append(jax.ShapeDtypeStruct((steps, rows, cols), kind))
    return pl.pallas_call(
        body,
        grid_spec=pltpu.PrefetchScalarGridSpec(
            num_scalar_prefetch=1, grid=(steps,), in_specs=specs, out_specs=out_specs,
            scratch_shapes=[pltpu.VMEM(shape, kind) for shape, kind in scratch],
        ),
        out_shape=out_shapes,
        compiler_params=pltpu.CompilerParams(vmem_limit_bytes=VMEM),
        cost_estimate=LITTLE,
        name=name,
    )(live, *arrays)


def norm_rate(values):
    return lax.rsqrt(jnp.mean(values * values, axis=-1, keepdims=True) + NORM_EPS)


def norm_back(grad, unit, rate, gain):
    moved = grad * gain
    return rate * (moved - unit * jnp.mean(moved * unit, axis=-1, keepdims=True))


def gelu_product(gate, up):
    return jax.nn.gelu(gate) * up


def wide_dot(left, halves):
    cut = halves[0].shape[0]
    return dot(left[:, :cut], halves[0]) + dot(left[:, cut:], halves[1])


def wide_back(left, halves):
    return jnp.concatenate([dot(left, h, ((1,), (1,))) for h in halves], axis=1)


def on_device(size, n, tokens, lengths, gains, w_gelu, w_rec, chan, w_lru, w_out, w_mlp_in, w_down, cotangent):
    place = lax.axis_index("dp")
    turn = lax.axis_index("tensor")
    d_model = tokens.shape[1]
    rows = tokens.shape[0] // n
    half = rows // 2
    d_own = w_gelu.shape[0]
    heads_own, part, head = chan.shape[1], chan.shape[2], w_lru.shape[3]
    heads = heads_own * n
    width = heads * head
    groups = width // GROUP
    table, inverse = basis(size, d_own, place)
    live_count = (lengths - turn * rows).astype(jnp.int32)
    live = (lax.iota(jnp.int32, rows)[:, None] < live_count).astype(F32)

    cols = w_gelu.shape[1]
    pad = -(-part // 16) * 16
    own_lru = jnp.pad(w_lru.transpose(0, 2, 1, 3).reshape(2, part, cols), ((0, 0), (0, pad - part), (0, 0)))
    own_chan = jnp.zeros((8, heads_own, head), F32)
    own_chan = lax.dynamic_update_slice(own_chan, chan, (0, 0, place * part)).reshape(8, cols)
    own_gain = jnp.pad(gains.reshape(1, -1), ((0, 7), (0, cols - gains.size)))
    small = jnp.concatenate([own_lru.reshape(2 * pad, cols), own_chan, own_gain])
    whole = jnp.concatenate([w_rec, small]).astype(BF)
    others = jnp.concatenate([w_gelu, w_out.T]).astype(BF)
    own_gu = jnp.concatenate([w_mlp_in[0], w_mlp_in[1]], axis=1).astype(BF)
    own_dn = w_down.T.astype(BF)
    some_gu = spread_begin(own_gu, size)

    main = lax.dynamic_slice_in_dim(tokens, turn * rows, rows)
    before = lax.dynamic_slice_in_dim(tokens, jnp.maximum(turn * rows - HALO, 0), HALO)
    before = jnp.where(turn > 0, before, jnp.zeros_like(before))
    turned = permute_rows(jnp.concatenate([before, main]), table)
    extended = turned.astype(F32)
    first_rate = norm_rate(extended)

    def wide(blocks):
        return blocks.transpose(1, 0, 2).reshape(d_own, width)

    (whole,) = fence([lax.all_gather(whole, "tensor", axis=0)], *some_gu[1:], others, turned, first_rate)
    others = lax.all_gather(*fence([others], whole), "tensor", axis=0)
    z_gelu, z_out = wide(others[:, :d_own]), wide(others[:, d_own:])
    some_r = spread_begin(wide(whole[:, :d_own]), size)
    some_small = small_begin(whole[:, d_own:].reshape(-1, cols), size)
    small = small_end(some_small, size).reshape(size, n, -1, cols)

    masks = small_masks(size)
    gain = small[:, 0, 2 * pad + 8, : gains.size].reshape(size, 2, d_own)
    if squared(size, d_own):
        swapped = jnp.concatenate([gain[..., d_own // 2 :], gain[..., : d_own // 2]], axis=-1)
        gain = jnp.where(((jnp.asarray(masks) & 6) == 6)[:, None, None], swapped, gain)
    gain = gain.transpose(1, 0, 2).reshape(2, d_model).astype(F32)
    chans = jnp.sum(small[:, :, 2 * pad : 2 * pad + 8].astype(F32), axis=0)
    chans = chans.transpose(1, 0, 2).reshape(8, width)
    par = jnp.concatenate([chans[:7], -8.0 * jax.nn.softplus(-chans[7:])])
    each = n // groups
    lru = small
    if each > 1:
        lru = lru.reshape(size, groups, each, -1, cols).transpose(0, 1, 3, 2, 4).reshape(size, groups, -1, GROUP)
    spot = (place ^ jnp.asarray(masks))[jnp.arange(size * pad) // pad]
    row = jnp.arange(size * pad) % pad
    row = jnp.where(row < part, spot * part + row, head)
    order = (jnp.arange(head)[:, None] == row[None, :]).astype(BF)

    w_r, came_r = spread_end(some_r, size, (), (others, order))
    first = (extended * first_rate * gain[0]).astype(BF)
    inputs, first_own, first_rate = extended[HALO:], first[HALO:], first_rate[HALO:]
    cut = d_model // 2

    keep = (rows, width, F32)
    dense = ((GROUP, 2 * GROUP), BF)
    some_g = spread_begin(z_gelu, size, *came_r)
    rec_pre = wide_dot(first, w_r)
    conv, decay, ig, dg, state, prod = kernel_call(
        forward_kernel, live_count, [rec_pre, par, lru, order], [keep] * 6,
        [((rows + HALO, GROUP), F32), dense], "recurrence",
    )
    ends = jnp.concatenate([prod[-1:], state[-1:]])
    came = [z_shift(ends, k, n, False) for k in range(1, n)]
    w_g, came_g = spread_end(some_g, size, (ends,), came)
    carry = jnp.zeros((1, width), F32)
    for end in came[::-1]:
        carry = end[1:] + end[:1] * carry
    some_o = spread_begin(z_out, size, *came_g)
    branch_pre = wide_dot(first_own, w_g)
    recurrent = (state + prod * carry) * live
    mixed = (jax.nn.gelu(branch_pre) * recurrent).astype(BF)
    w_o, came_o = spread_end(some_o, size, (branch_pre,), (mixed,))
    hidden = inputs + wide_back(mixed, w_o)
    second_rate = norm_rate(hidden)
    second_unit = hidden * second_rate
    second_own = (second_unit * gain[1]).astype(BF)
    w_gu, came_gu = spread_end(some_gu, size, came_o, (second_own,))
    w_dn, _ = spread_end(spread_begin(own_dn, size, *came_gu), size, (), ())
    w_gu, w_dn = assemble(w_gu), assemble(w_dn)
    late = fence([table], second_own)[0]
    cots = [permute_rows(cotangent, late, half, 2, h) for h in range(2)]

    hidden_units = w_dn.shape[1]
    grad_products = [dot(c, w_dn) for c in cots]
    shares, grad_second, seconds, products, grads = [], [], [], [], []
    for h in range(2):
        second = lax.all_gather(second_own[h * half : (h + 1) * half], "tensor", axis=0, tiled=True)
        (second,) = fence([second], *shares)
        both = dot(second, w_gu)
        product, pull = jax.vjp(gelu_product, both[:, :hidden_units], both[:, hidden_units:])
        grad_gate, grad_up = pull(grad_products[h])
        product = product.astype(BF)
        grad = jnp.concatenate([grad_gate.astype(BF), grad_up.astype(BF)], axis=1)
        share = dot(grad, w_gu, ((1,), (1,))).astype(BF)
        shares.append(share)
        grad_second.append(lax.psum_scatter(share, "tensor", scatter_dimension=0, tiled=True))
        seconds.append(second)
        products.append(product)
        grads.append(grad)

    products, grads = [[*pair] for pair in zip(*[fence([p, g], shares[-1]) for p, g in zip(products, grads)])]
    shares = [dot(p, w_dn, ((1,), (1,))).astype(BF) for p in products]

    def by_rows(lefts, rights):
        parts = []
        for span in (slice(cut, None), slice(0, cut)):
            part = dot(lefts[0][:, span], rights[0], ((0,), (0,)))
            parts.append((part + dot(lefts[1][:, span], rights[1], ((0,), (0,)))).astype(BF))
        return Collect(parts[1], parts[0], size, d_own)

    sum_dn = by_rows(cots, products)
    sum_gu = by_rows(seconds, grads)
    sent_dn, sent_gu = sum_dn.sources(), sum_gu.sources()
    grad_second = fence(grad_second, *sent_dn, *sent_gu, *shares)
    came_mlp = sum_dn.hop(sent_dn) + sum_gu.hop(sent_gu)

    shares = fence(shares, *grad_second)
    mlp_sums = [lax.psum_scatter(share, "tensor", scatter_dimension=0, tiled=True) for share in shares]

    grad_second = jnp.concatenate(grad_second).astype(F32)
    cot_own = jnp.concatenate([lax.dynamic_slice_in_dim(c, turn * half, half) for c in cots]).astype(F32)
    gain_two = jnp.sum(grad_second * second_unit, axis=0)
    grad_hidden = cot_own + norm_back(grad_second, second_unit, second_rate, gain[1])
    hidden_low = grad_hidden.astype(BF)

    def by_cols(left, right):
        parts = [dot(left[:, span], right, ((0,), (0,))).astype(BF) for span in (slice(cut, None), slice(0, cut))]
        return Collect(parts[1], parts[0], size, d_own)

    grad_mixed = wide_dot(hidden_low, w_o)
    tall = jnp.broadcast_to
    lam, reach, edge, pre_low = kernel_call(
        back_scan_kernel, live_count, [branch_pre, grad_mixed, decay, state, prod, tall(carry, (SLAB, width))],
        [keep, keep, (SLAB, width, F32), (rows, width, BF)], [], "back_scan",
    )
    edges = jnp.concatenate([prod[-1:], edge[:1]])
    came = [z_shift(edges, -k, n, False) for k in range(1, n)]
    arriving = jnp.zeros((1, width), F32)
    for end in came[::-1]:
        arriving = end[1:] + end[:1] * arriving
    (lam,) = fence([lam], *came_mlp)
    drec, dpar, d_lru = kernel_call(
        backward_kernel, live_count,
        [rec_pre, par, lru, order, lam, reach, tall(arriving, (SLAB, width)), decay, conv, ig, dg, state, prod, tall(carry, (SLAB, width))],
        [(rows + HALO, width, F32), (8, width, F32), (head, 2 * GROUP, BF)],
        [((rows + HALO, GROUP), F32), ((rows + 2 * HALO, GROUP), F32), ((rows + SLAB, GROUP), F32), ((GROUP, 2 * GROUP), F32), dense],
        "recurrence_back",
    )
    (edge_rows,) = fence([z_shift(drec[:HALO], -1, n, False)], mlp_sums[0])
    rec_low = (drec[HALO:] + jnp.pad(edge_rows, ((rows - HALO, 0), (0, 0)))) * live
    rec_low = rec_low.astype(BF)
    (pre_low,) = fence([pre_low], drec)
    grad_first = wide_back(pre_low, w_g) + wide_back(rec_low, w_r)
    first_unit = inputs * first_rate
    gain_one = jnp.sum(grad_first * first_unit, axis=0)
    grad_tokens = grad_hidden + norm_back(grad_first, first_unit, first_rate, gain[0])
    grad_tokens = permute_rows(grad_tokens.astype(BF), inverse)
    gathered = lax.all_gather(grad_tokens, "tensor", axis=0, tiled=True)
    (mixed,) = fence([mixed], grad_tokens)
    sum_o = by_cols(hidden_low, mixed)
    pre_low, rec_low = fence([pre_low, rec_low], sum_o.terms[1])
    sum_g, sum_r = by_cols(first_own, pre_low), by_cols(first_own, rec_low)
    mlp_sum = jnp.concatenate(fence(mlp_sums, sum_o.terms[1])).astype(F32)
    result = permute_rows((hidden + mlp_sum).astype(BF), inverse)
    got_o = sum_o.hop(fence(sum_o.sources(), result))
    result = lax.all_gather(result, "tensor", axis=0, tiled=True)
    got_g = sum_g.hop(fence(sum_g.sources(), *got_o))
    sum_o.hop(fence(sum_o.sources(), *got_g))
    got_r = sum_r.hop(fence(sum_r.sources(), *got_g))
    sum_g.hop(fence(sum_g.sources(), *got_g))
    got_r = sum_r.hop(fence(sum_r.sources(), *got_r))
    (tokens_out,) = fence([gathered], *got_r, cost=MUCH)
    owned = jnp.stack([total.finish().reshape(d_own, n, width // n) for total in (sum_o, sum_g, sum_r)])
    owned = LineSum(owned.transpose(2, 0, 1, 3), n)
    owned.go()
    tokens_out = move(tokens_out)
    if n > 2:
        owned.go(tokens_out)
    d_lru, dpar = fence([d_lru, dpar], *got_r)
    if sum_dn.square:
        sum_dn.hop(fence(sum_dn.sources(), *got_r))
        sum_gu.hop(fence(sum_gu.sources(), *got_r))
    g_gu, g_dn = sum_gu.finish().astype(F32), sum_dn.finish().astype(F32)
    g_all = owned.finish()
    (output,) = fence([result], owned.right, owned.left, g_gu, g_dn, cost=MUCH)
    output = move(output)
    g_o, g_g, g_r = g_all[0], g_all[1], g_all[2]

    d_gain = permute_gain(jnp.stack([gain_one, gain_two]), inverse)
    d_chan = jnp.concatenate([dpar[:7], dpar[7:] * 8.0 * jax.nn.sigmoid(-chans[7:])])
    d_lru = d_lru.reshape(groups, size, part, 2, each, -1).transpose(1, 0, 4, 2, 3, 5)
    d_chan = d_chan.reshape(8, n, heads_own, size, part).transpose(3, 1, 0, 2, 4)
    d_gain = d_gain.reshape(2, size, 1, d_own).transpose(1, 2, 0, 3)
    d_gain = jnp.broadcast_to(d_gain, (size, n, 2, d_own))
    small = [v.reshape(size, n, -1).astype(BF) for v in (d_lru, d_chan, d_gain)]
    small = small_scatter(jnp.concatenate(small, axis=2), size, n)
    d_lru = small[: w_lru.size].reshape(part, 2, heads_own, head).transpose(1, 2, 0, 3)
    d_chan = small[w_lru.size : -gains.size].reshape(chan.shape)
    d_gain = small[-gains.size :].reshape(gains.shape)
    g_gate, g_up = g_gu[:, :hidden_units], g_gu[:, hidden_units:]
    return (
        output, tokens_out, d_gain[0], d_gain[1], g_g, g_r, d_chan, d_lru,
        g_o.T, jnp.stack([g_gate, g_up]), g_dn.T,
    )


def solution(mesh):
    in_specs = (
        P("dp", None),
        P("dp"),
        P(None, "dp"),
        P("dp", "tensor"),
        P("dp", "tensor"),
        P(None, "tensor", "dp"),
        P(None, "tensor", "dp", None),
        P("tensor", "dp"),
        P(None, "dp", "tensor"),
        P("tensor", "dp"),
        P("dp", None),
    )
    out_specs = (
        P("dp", None),
        P("dp", None),
        P("dp"),
        P("dp"),
        P("dp", "tensor"),
        P("dp", "tensor"),
        P(None, "tensor", "dp"),
        P(None, "tensor", "dp", None),
        P("tensor", "dp"),
        P(None, "dp", "tensor"),
        P("tensor", "dp"),
    )
    body = functools.partial(on_device, mesh.shape["dp"], mesh.shape["tensor"])
    return jax.shard_map(body, mesh=mesh, in_specs=in_specs, out_specs=out_specs, check_vma=False)
```

```python
import functools

import jax
import jax.numpy as jnp
import numpy as np
from jax import lax
from jax.experimental import pallas as pl
from jax.experimental.pallas import tpu as pltpu
from jax.sharding import PartitionSpec as P

NORM_EPS = 1e-06
DECAY_FLOOR = 0.05
HALO = 16
GROUP = 640
ROWS = 128
SLAB = 8
VMEM = 58 * 1024 * 1024
BF = jnp.bfloat16
F32 = jnp.float32
MUCH = pl.CostEstimate(flops=60 * 10**9, bytes_accessed=1024, transcendentals=0)
LITTLE = pl.CostEstimate(flops=1024, bytes_accessed=1024, transcendentals=0)


def dot(left, right, dims=((1,), (0,))):
    return lax.dot_general(left, right, (dims, ((), ())), preferred_element_type=F32)


def fence(values, *others, cost=LITTLE):
    if not others:
        return list(values)
    place = pl.BlockSpec(memory_space=pl.ANY)
    call = pl.pallas_call(
        lambda *refs: None,
        in_specs=[place] * (len(values) + len(others)),
        out_specs=[place] * len(values),
        out_shape=[jax.ShapeDtypeStruct(v.shape, v.dtype) for v in values],
        input_output_aliases={k: k for k in range(len(values))},
        compiler_params=pltpu.CompilerParams(vmem_limit_bytes=VMEM),
        cost_estimate=cost,
        name="fence",
    )
    return list(call(*values, *others))


def assemble(pieces, *others):
    count = len(pieces)
    rows = [p.shape[0] for p in pieces]
    spans = [pl.ds(sum(rows[:k]), rows[k]) for k in range(count)]
    shape = (sum(rows), pieces[0].shape[1])

    def body(*refs):
        out, held, coming, going = refs[count + len(others) :]
        ins = [pltpu.make_async_copy(refs[k], held.at[spans[k]], coming.at[k]) for k in range(count)]
        outs = [pltpu.make_async_copy(held.at[spans[k]], out.at[spans[k]], going.at[k]) for k in range(count)]
        for copy in ins:
            copy.start()
        for here, there in zip(ins, outs):
            here.wait()
            there.start()
        for copy in outs:
            copy.wait()

    place = pl.BlockSpec(memory_space=pl.ANY)
    return pl.pallas_call(
        body,
        in_specs=[place] * (count + len(others)),
        out_specs=place,
        out_shape=jax.ShapeDtypeStruct(shape, pieces[0].dtype),
        scratch_shapes=[
            pltpu.VMEM(shape, pieces[0].dtype),
            pltpu.SemaphoreType.DMA((count,)),
            pltpu.SemaphoreType.DMA((count,)),
        ],
        compiler_params=pltpu.CompilerParams(vmem_limit_bytes=VMEM),
        cost_estimate=LITTLE,
        name="assemble",
    )(*pieces, *others)


def exchange(values, bit, size):
    return lax.ppermute(values, "dp", [(k, k ^ (1 << bit)) for k in range(size)])


def squared(size, rows):
    return size == 8 and rows % 256 == 0


def spread_begin(own, size, *before):
    (own,) = fence([own], *before)
    if squared(size, own.shape[0]):
        return [own, exchange(own, 1, size), exchange(own, 2, size)]
    pieces = own
    for bit in range(1, size.bit_length() - 2):
        pieces = jnp.concatenate([pieces, exchange(pieces, bit, size)])
    return [pieces]


def spread_end(some, size, before_last, before_core):
    if len(some) > 1:
        own, by_x, by_y = some
        unit = own.shape[0] // 2
        by_x, by_y = fence([by_x, by_y], *before_last)
        got = [exchange(by_x[:unit], 2, size), exchange(by_y[unit:], 1, size)]
        half = assemble([own, by_x, got[1], got[0], by_y], *before_core)
    else:
        (pieces,) = fence(some, *before_last)
        got = [exchange(pieces, size.bit_length() - 2, size)]
        half = jnp.concatenate([pieces] + fence(got, *before_core))
    return [half, exchange(half, 0, size)], got


def add_all(terms):
    total = terms[0].astype(F32)
    for term in terms[1:]:
        total = total + term.astype(F32)
    return total.astype(BF)


class Collect:
    def __init__(self, keep, send, size, d_own):
        self.size, self.unit = size, d_own // 2
        self.square = squared(size, d_own)
        self.bit = size.bit_length() - 2
        self.terms = [keep, exchange(send, 0, size)]
        self.first = self.last = None

    def rows(self, start, stop):
        return [t[start * self.unit : stop * self.unit] for t in self.terms]

    def sources(self):
        if not self.square:
            cut = self.terms[0].shape[0] // 2
            return [add_all([t[cut:] for t in self.terms])]
        if self.first is None:
            return [add_all(self.rows(3, 5)), add_all(self.rows(5, 7))]
        by_x, by_y = self.first
        return [add_all(self.rows(2, 3) + [by_y[: self.unit]]), add_all(self.rows(7, 8) + [by_x[self.unit :]])]

    def hop(self, sources):
        if not self.square:
            got = exchange(sources[0], self.bit, self.size)
            self.bit -= 1
            self.terms = [t[: got.shape[0]] for t in self.terms] + [got]
            return [got]
        got = [exchange(v, bit, self.size) for v, bit in zip(sources, (1, 2))]
        if self.first is None:
            self.first = got
        else:
            self.last = got
        return got

    def finish(self):
        if not self.square:
            while self.bit:
                self.hop(self.sources())
            return add_all(self.terms)
        low = add_all(self.rows(0, 1) + [self.first[1][self.unit :], self.last[0]])
        high = add_all(self.rows(1, 2) + [self.first[0][: self.unit], self.last[1]])
        return jnp.concatenate([low, high])


def z_shift(values, by, n, around=True):
    pairs = [(k, (k + by) % n) for k in range(n) if around or 0 <= k + by < n]
    return lax.ppermute(values, "tensor", pairs)


def z_scatter(values, n):
    turn = lax.axis_index("tensor")
    total = lax.dynamic_index_in_dim(values, turn, 0, keepdims=False).astype(F32)
    for k in range(1, n):
        block = lax.dynamic_index_in_dim(values, (turn + k) % n, 0, keepdims=False)
        total = total + z_shift(block, k, n).astype(F32)
    return total


class LineSum:
    def __init__(self, blocks, n):
        self.blocks, self.n, self.turn, self.rounds = blocks, n, lax.axis_index("tensor"), 0
        self.right = self.left = None

    def block(self, k):
        return lax.dynamic_index_in_dim(self.blocks, k % self.n, 0, keepdims=False)

    def go(self, *others):
        self.rounds += 1
        t, n = self.rounds, self.n
        right, left = self.block(self.turn + n - t), self.block(self.turn + t)
        if t > 1:
            before = fence([self.right, self.left], self.blocks, *others)
            right, left = add_all([right, before[0]]), add_all([left, before[1]])
        self.right = lax.ppermute(right, "tensor", [(k, k + 1) for k in range(min(t, n - 1))])
        self.left = lax.ppermute(left, "tensor", [(k, k - 1) for k in range(max(n - t, 1), n)])

    def finish(self):
        while self.rounds < self.n - 1:
            self.go()
        return self.block(self.turn).astype(F32) + self.right.astype(F32) + self.left.astype(F32)


def small_masks(size):
    turns = (0, 2, 6, 4) if size == 8 else tuple(q << 1 for q in range(size // 2))
    return np.array([core | mask for core in range(2) for mask in turns], np.int32)


def small_begin(own, size):
    if size == 8:
        return [own, exchange(own, 1, size), exchange(own, 2, size)]
    rows = own[None]
    for bit in range(1, size.bit_length() - 1):
        rows = jnp.concatenate([rows, exchange(rows, bit, size)])
    return [rows]


def small_end(some, size):
    if size == 8:
        own, by_x, by_y = some
        cut = own.shape[0] // 2
        far = jnp.concatenate([exchange(by_x[:cut], 2, size), exchange(by_y[cut:], 1, size)])
        rows = jnp.stack([own, by_x, far, by_y])
    else:
        (rows,) = some
    return jnp.concatenate([rows, exchange(rows, 0, size)])


def small_scatter(values, size, n):
    place = lax.axis_index("dp")
    values = jnp.take(values, jnp.arange(size) ^ place, axis=0, mode="clip")
    for bit in reversed(range(size.bit_length() - 1)):
        half = values.shape[0] // 2
        values = add_all([values[:half], exchange(values[half:], bit, size)])
    return z_scatter(values[0], n)


def basis_spots(size, rows):
    if squared(size, rows):
        turns = ((0, 0), (0, 1), (2, 0), (2, 1), (6, 1), (6, 0), (4, 0), (4, 1))
        return [(core | mask, part) for core in range(2) for mask, part in turns], 2
    return [(core | q << 1, 0) for core in range(2) for q in range(size // 2)], 1


def basis(size, rows, place):
    spots, parts = basis_spots(size, rows)
    masks, which = (jnp.asarray(np.array(v, np.int32)) for v in zip(*spots))
    table = (place ^ masks) * parts + which
    spots = jnp.arange(table.shape[0], dtype=jnp.int32)
    inverse = jnp.sum(jnp.where(table[None, :] == spots[:, None], spots[None, :], 0), axis=1)
    return table, inverse.astype(jnp.int32)


def copy_kernel(blocks, table_ref, in_ref, out_ref):
    width = in_ref.shape[1] // blocks
    for p in range(blocks):
        start = pl.multiple_of(table_ref[p] * width, width)
        out_ref[:, p * width : (p + 1) * width] = in_ref[:, pl.ds(start, width)]


def permute_rows(values, table, step=0, stride=1, offset=0):
    rows, d_model = values.shape
    step = step or max(k for k in range(16, 289, 16) if rows % k == 0)
    return pl.pallas_call(
        functools.partial(copy_kernel, table.shape[0]),
        grid_spec=pltpu.PrefetchScalarGridSpec(
            num_scalar_prefetch=1,
            grid=(rows // (step * stride),),
            in_specs=[pl.BlockSpec((step, d_model), lambda r, tab: (r * stride + offset, 0))],
            out_specs=pl.BlockSpec((step, d_model), lambda r, tab: (r, 0)),
        ),
        out_shape=jax.ShapeDtypeStruct((rows // stride, d_model), values.dtype),
        compiler_params=pltpu.CompilerParams(vmem_limit_bytes=VMEM),
        cost_estimate=LITTLE,
        name="permute",
    )(table, values)


def move_kernel(in_ref, out_ref):
    out_ref[...] = in_ref[...]


def move(values):
    rows, d_model = values.shape
    spec = pl.BlockSpec((max(k for k in range(16, 289, 16) if rows % k == 0), d_model), lambda r: (r, 0))
    return pl.pallas_call(
        move_kernel,
        grid=(rows // spec.block_shape[0],),
        in_specs=[spec],
        out_specs=spec,
        out_shape=jax.ShapeDtypeStruct(values.shape, values.dtype),
        compiler_params=pltpu.CompilerParams(vmem_limit_bytes=VMEM),
        cost_estimate=LITTLE,
        name="move",
    )(values)


def permute_gain(values, table):
    lead = values.shape[0]
    return jnp.take(values.reshape(lead, table.shape[0], -1), table, axis=1, mode="clip").reshape(lead, -1)


def row_ids(count, width, first):
    return lax.broadcasted_iota(jnp.int32, (count, width), 0) + first


def scan_slab(decay, value, back):
    rows = row_ids(SLAB, decay.shape[1], 0)
    for step in (1, 2, 4):
        keep = rows < SLAB - step if back else rows >= step
        shift = SLAB - step if back else step
        moved_decay = pltpu.roll(decay, shift, 0)
        moved_value = pltpu.roll(value, shift, 0)
        value = jnp.where(keep, value + decay * moved_value, value)
        decay = jnp.where(keep, decay * moved_decay, decay)
    return decay, value


def head_mask(head, at, width):
    lanes = lax.broadcasted_iota(jnp.int32, (head, 2 * width), 1)
    lanes = jnp.where(lanes >= width, lanes - width, lanes)
    return (lanes >= at * head) & (lanes < (at + 1) * head)


def fill_dense(w_ref, order_ref, dense_ref):
    head, count = order_ref.shape
    pad = count // w_ref.shape[0]
    width = dense_ref.shape[0]
    for gate in range(2):
        rows = w_ref[:, gate * pad : (gate + 1) * pad, :].reshape(count, width)
        rows = dot(order_ref[...], rows)
        for k in range(width // head):
            lanes = lax.broadcasted_iota(jnp.int32, (head, width), 1)
            block = jnp.where((lanes >= k * head) & (lanes < (k + 1) * head), rows, 0.0)
            dense_ref[k * head : (k + 1) * head, gate * width : (gate + 1) * width] = block.astype(BF)


def forward_kernel(
    live_ref, pre_ref, par_ref, w_ref, order_ref, conv_ref, decay_ref, ig_ref, dg_ref, state_ref, prod_ref,
    rec_ref, dense_ref,
):
    rows, width = conv_ref.shape
    fill_dense(w_ref, order_ref, dense_ref)
    live = live_ref[0]
    rec_ref[...] = jnp.where(row_ids(rows + HALO, width, -HALO) < live, pre_ref[...], 0.0)
    par = [par_ref[k : k + 1, :] for k in range(8)]
    for at in range(0, rows, ROWS):
        span = pl.ds(at, ROWS)
        near = rec_ref[pl.ds(at, ROWS + HALO), :]
        conv = par[4] + par[0] * near[HALO : HALO + ROWS]
        for k in range(1, 4):
            conv = conv + par[k] * near[HALO - k : HALO - k + ROWS]
        conv = jnp.where(row_ids(ROWS, width, at) < live, conv, 0.0)
        conv_ref[span, :] = conv
        gates = dot(conv.astype(BF), dense_ref[...])
        ig = lax.logistic(gates[:, :width] + par[5])
        dg = lax.logistic(gates[:, width:] + par[6])
        decay = jnp.exp(dg * par[7])
        ig_ref[span, :] = ig
        dg_ref[span, :] = dg
        decay_ref[span, :] = decay
        state_ref[span, :] = jnp.sqrt(jnp.maximum(1.0 - decay * decay, DECAY_FLOOR)) * ig * conv

    def slab(k, carry):
        state, prod = carry
        for inner in range(4):
            span = pl.ds(pl.multiple_of(k * 4 * SLAB + inner * SLAB, SLAB), SLAB)
            decay, value = scan_slab(decay_ref[span, :], state_ref[span, :], False)
            value = value + decay * state
            decay = decay * prod
            state_ref[span, :] = value
            prod_ref[span, :] = decay
            state = jnp.broadcast_to(value[SLAB - 1 :, :], (SLAB, width))
            prod = jnp.broadcast_to(decay[SLAB - 1 :, :], (SLAB, width))
        return state, prod

    lax.fori_loop(0, rows // (4 * SLAB), slab, (jnp.zeros((SLAB, width), F32), jnp.ones((SLAB, width), F32)))


def back_scan_kernel(
    live_ref, pre_ref, grad_ref, decay_ref, state_ref, prod_ref, cin_ref, lam_ref, reach_ref, edge_ref, low_ref
):
    rows, width = grad_ref.shape
    live = live_ref[0]
    cin = cin_ref[:1, :]
    c = np.float32(np.sqrt(2 / np.pi))
    for at in range(0, rows, ROWS):
        span = pl.ds(at, ROWS)
        v, grad = pre_ref[span, :], grad_ref[span, :]
        square = v * v
        bend = jnp.tanh(v * (c + (c * 0.044715) * square))
        rise = 0.5 + 0.5 * bend
        slope = rise + 0.5 * v * (1.0 - bend * bend) * (c + (3 * c * 0.044715) * square)
        grad = jnp.where(row_ids(ROWS, width, at) < live, grad, 0.0)
        lam_ref[span, :] = grad * (v * rise)
        low_ref[span, :] = (grad * (state_ref[span, :] + prod_ref[span, :] * cin) * slope).astype(BF)
    last = row_ids(SLAB, width, 0) == SLAB - 1

    def slab(k, carry):
        lam, reach, following, _ = carry
        for inner in range(4):
            span = pl.ds(pl.multiple_of(rows - (k * 4 + inner + 1) * SLAB, SLAB), SLAB)
            own = decay_ref[span, :]
            ahead = jnp.where(last, following, pltpu.roll(own, SLAB - 1, 0))
            decay, value = scan_slab(ahead, lam_ref[span, :], True)
            value = value + decay * lam
            decay = decay * reach
            lam_ref[span, :] = value
            reach_ref[span, :] = decay
            lam = jnp.broadcast_to(value[:1, :], (SLAB, width))
            reach = jnp.broadcast_to(decay[:1, :], (SLAB, width))
            following = jnp.broadcast_to(own[:1, :], (SLAB, width))
        return lam, reach, following, own

    one = jnp.ones((SLAB, width), F32)
    zero = jnp.zeros((SLAB, width), F32)
    lam, _, following, _ = lax.fori_loop(0, rows // (4 * SLAB), slab, (zero, one, one, one))
    edge_ref[...] = lam * following


def backward_kernel(
    live_ref, pre_ref, par_ref, w_ref, order_ref, lam_ref, reach_ref, edge_ref, decay_ref, conv_ref, ig_ref, dg_ref, state_ref, prod_ref, cin_ref,
    drec_ref, dpar_ref, dw_ref, rec_ref, dconv_ref, full_ref, dw_acc, dense_ref,
):
    rows, width = conv_ref.shape
    live = live_ref[0]
    rec_ref[...] = jnp.where(row_ids(rows + HALO, width, -HALO) < live, pre_ref[...], 0.0)
    par = [par_ref[k : k + 1, :] for k in range(8)]
    fill_dense(w_ref, order_ref, dense_ref)
    cin = cin_ref[:1, :]
    edge = edge_ref[:1, :]
    full_ref[:SLAB, :] = jnp.broadcast_to(cin, (SLAB, width))
    dconv_ref[:HALO, :] = jnp.zeros((HALO, width), F32)
    dconv_ref[rows + HALO :, :] = jnp.zeros((HALO, width), F32)
    sums = [jnp.zeros((1, width), F32) for _ in range(8)]
    for at in range(0, rows, ROWS):
        span = pl.ds(at, ROWS)
        full_ref[pl.ds(at + SLAB, ROWS), :] = state_ref[span, :] + prod_ref[span, :] * cin
        lam = lam_ref[span, :] + reach_ref[span, :] * edge
        decay, conv, ig, dg = decay_ref[span, :], conv_ref[span, :], ig_ref[span, :], dg_ref[span, :]
        before = full_ref[pl.ds(at, ROWS + SLAB), :][SLAB - 1 : SLAB - 1 + ROWS]
        room = 1.0 - decay * decay
        scale = jnp.sqrt(jnp.maximum(room, DECAY_FLOOR))
        lam_conv = lam * conv
        d_decay = lam * before - jnp.where(room > DECAY_FLOOR, lam_conv * ig * decay / scale, 0.0)
        moved = d_decay * decay
        sums[7] = sums[7] + jnp.sum(moved * dg, axis=0, keepdims=True)
        d_ig = lam_conv * scale * ig * (1.0 - ig)
        d_dg = moved * par[7] * dg * (1.0 - dg)
        sums[5] = sums[5] + jnp.sum(d_ig, axis=0, keepdims=True)
        sums[6] = sums[6] + jnp.sum(d_dg, axis=0, keepdims=True)
        both = jnp.concatenate([d_ig.astype(BF), d_dg.astype(BF)], axis=1)
        d_conv = lam * scale * ig + dot(both, dense_ref[...], ((1,), (1,)))
        d_conv = jnp.where(row_ids(ROWS, width, at) < live, d_conv, 0.0)
        dconv_ref[pl.ds(at + HALO, ROWS), :] = d_conv
        part = dot(conv.astype(BF), both, ((0,), (0,)))
        dw_acc[...] = part if at == 0 else dw_acc[...] + part
        near = rec_ref[pl.ds(at, ROWS + HALO), :]
        for k in range(4):
            sums[k] = sums[k] + jnp.sum(d_conv * near[HALO - k : HALO - k + ROWS], axis=0, keepdims=True)
        sums[4] = sums[4] + jnp.sum(d_conv, axis=0, keepdims=True)
    for k in range(8):
        dpar_ref[k : k + 1, :] = sums[k]
    head = dw_ref.shape[0]
    total = jnp.zeros((head, 2 * width), F32)
    for k in range(width // head):
        total = total + jnp.where(head_mask(head, k, width), dw_acc[k * head : (k + 1) * head, :], 0.0)
    dw_ref[...] = total.astype(BF)
    for at in list(range(0, rows, ROWS)) + [rows]:
        count = ROWS if at < rows else HALO
        near = dconv_ref[pl.ds(at, count + SLAB), :]
        total = par[0] * near[:count]
        for k in range(1, 4):
            total = total + par[k] * near[k : k + count]
        drec_ref[pl.ds(at, count), :] = total


def kernel_call(body, live, arrays, outs, scratch, name):
    width = outs[0][1]
    steps = width // GROUP
    specs = []
    for array in arrays:
        if array.ndim == 4:
            block = (array.shape[0], pl.squeezed) + array.shape[2:]
            specs.append(pl.BlockSpec(block, lambda j, s: (0, j, 0, 0)))
        elif array.shape[1] != width:
            specs.append(pl.BlockSpec(array.shape, lambda j, s: (0, 0)))
        else:
            specs.append(pl.BlockSpec((array.shape[0], GROUP), lambda j, s: (0, j)))
    out_specs, out_shapes = [], []
    for rows, cols, kind in outs:
        if cols == width:
            out_specs.append(pl.BlockSpec((rows, GROUP), lambda j, s: (0, j)))
            out_shapes.append(jax.ShapeDtypeStruct((rows, cols), kind))
        else:
            out_specs.append(pl.BlockSpec((pl.squeezed, rows, cols), lambda j, s: (j, 0, 0)))
            out_shapes.append(jax.ShapeDtypeStruct((steps, rows, cols), kind))
    return pl.pallas_call(
        body,
        grid_spec=pltpu.PrefetchScalarGridSpec(
            num_scalar_prefetch=1, grid=(steps,), in_specs=specs, out_specs=out_specs,
            scratch_shapes=[pltpu.VMEM(shape, kind) for shape, kind in scratch],
        ),
        out_shape=out_shapes,
        compiler_params=pltpu.CompilerParams(vmem_limit_bytes=VMEM),
        cost_estimate=LITTLE,
        name=name,
    )(live, *arrays)


def norm_rate(values):
    return lax.rsqrt(jnp.mean(values * values, axis=-1, keepdims=True) + NORM_EPS)


def norm_back(grad, unit, rate, gain):
    moved = grad * gain
    return rate * (moved - unit * jnp.mean(moved * unit, axis=-1, keepdims=True))


def gelu_product(gate, up):
    return jax.nn.gelu(gate) * up


def wide_dot(left, halves):
    cut = halves[0].shape[0]
    return dot(left[:, :cut], halves[0]) + dot(left[:, cut:], halves[1])


def wide_back(left, halves):
    return jnp.concatenate([dot(left, h, ((1,), (1,))) for h in halves], axis=1)


def on_device(size, n, tokens, lengths, gains, w_gelu, w_rec, chan, w_lru, w_out, w_mlp_in, w_down, cotangent):
    place = lax.axis_index("dp")
    turn = lax.axis_index("tensor")
    d_model = tokens.shape[1]
    rows = tokens.shape[0] // n
    half = rows // 2
    d_own = w_gelu.shape[0]
    heads_own, part, head = chan.shape[1], chan.shape[2], w_lru.shape[3]
    heads = heads_own * n
    width = heads * head
    groups = width // GROUP
    table, inverse = basis(size, d_own, place)
    live_count = (lengths - turn * rows).astype(jnp.int32)
    live = (lax.iota(jnp.int32, rows)[:, None] < live_count).astype(F32)

    cols = w_gelu.shape[1]
    pad = -(-part // 16) * 16
    own_lru = jnp.pad(w_lru.transpose(0, 2, 1, 3).reshape(2, part, cols), ((0, 0), (0, pad - part), (0, 0)))
    own_chan = jnp.zeros((8, heads_own, head), F32)
    own_chan = lax.dynamic_update_slice(own_chan, chan, (0, 0, place * part)).reshape(8, cols)
    own_gain = jnp.pad(gains.reshape(1, -1), ((0, 7), (0, cols - gains.size)))
    small = jnp.concatenate([own_lru.reshape(2 * pad, cols), own_chan, own_gain])
    whole = jnp.concatenate([w_rec, small]).astype(BF)
    others = jnp.concatenate([w_gelu, w_out.T]).astype(BF)
    own_gu = jnp.concatenate([w_mlp_in[0], w_mlp_in[1]], axis=1).astype(BF)
    own_dn = w_down.T.astype(BF)
    some_gu = spread_begin(own_gu, size)

    main = lax.dynamic_slice_in_dim(tokens, turn * rows, rows)
    before = lax.dynamic_slice_in_dim(tokens, jnp.maximum(turn * rows - HALO, 0), HALO)
    before = jnp.where(turn > 0, before, jnp.zeros_like(before))
    turned = permute_rows(jnp.concatenate([before, main]), table)
    extended = turned.astype(F32)
    first_rate = norm_rate(extended)

    def wide(blocks):
        return blocks.transpose(1, 0, 2).reshape(d_own, width)

    (whole,) = fence([lax.all_gather(whole, "tensor", axis=0)], *some_gu[1:], others, turned, first_rate)
    others = lax.all_gather(*fence([others], whole), "tensor", axis=0)
    z_gelu, z_out = wide(others[:, :d_own]), wide(others[:, d_own:])
    some_r = spread_begin(wide(whole[:, :d_own]), size)
    some_small = small_begin(whole[:, d_own:].reshape(-1, cols), size)
    small = small_end(some_small, size).reshape(size, n, -1, cols)

    masks = small_masks(size)
    gain = small[:, 0, 2 * pad + 8, : gains.size].reshape(size, 2, d_own)
    if squared(size, d_own):
        swapped = jnp.concatenate([gain[..., d_own // 2 :], gain[..., : d_own // 2]], axis=-1)
        gain = jnp.where(((jnp.asarray(masks) & 6) == 6)[:, None, None], swapped, gain)
    gain = gain.transpose(1, 0, 2).reshape(2, d_model).astype(F32)
    chans = jnp.sum(small[:, :, 2 * pad : 2 * pad + 8].astype(F32), axis=0)
    chans = chans.transpose(1, 0, 2).reshape(8, width)
    par = jnp.concatenate([chans[:7], -8.0 * jax.nn.softplus(-chans[7:])])
    each = n // groups
    lru = small
    if each > 1:
        lru = lru.reshape(size, groups, each, -1, cols).transpose(0, 1, 3, 2, 4).reshape(size, groups, -1, GROUP)
    spot = (place ^ jnp.asarray(masks))[jnp.arange(size * pad) // pad]
    row = jnp.arange(size * pad) % pad
    row = jnp.where(row < part, spot * part + row, head)
    order = (jnp.arange(head)[:, None] == row[None, :]).astype(BF)

    w_r, came_r = spread_end(some_r, size, (), (others, order))
    first = (extended * first_rate * gain[0]).astype(BF)
    inputs, first_own, first_rate = extended[HALO:], first[HALO:], first_rate[HALO:]
    cut = d_model // 2

    keep = (rows, width, F32)
    dense = ((GROUP, 2 * GROUP), BF)
    some_g = spread_begin(z_gelu, size, *came_r)
    rec_pre = wide_dot(first, w_r)
    conv, decay, ig, dg, state, prod = kernel_call(
        forward_kernel, live_count, [rec_pre, par, lru, order], [keep] * 6,
        [((rows + HALO, GROUP), F32), dense], "recurrence",
    )
    ends = jnp.concatenate([prod[-1:], state[-1:]])
    came = [z_shift(ends, k, n, False) for k in range(1, n)]
    w_g, came_g = spread_end(some_g, size, (ends,), came)
    carry = jnp.zeros((1, width), F32)
    for end in came[::-1]:
        carry = end[1:] + end[:1] * carry
    some_o = spread_begin(z_out, size, *came_g)
    branch_pre = wide_dot(first_own, w_g)
    recurrent = (state + prod * carry) * live
    mixed = (jax.nn.gelu(branch_pre) * recurrent).astype(BF)
    w_o, came_o = spread_end(some_o, size, (branch_pre,), (mixed,))
    hidden = inputs + wide_back(mixed, w_o)
    second_rate = norm_rate(hidden)
    second_unit = hidden * second_rate
    second_own = (second_unit * gain[1]).astype(BF)
    w_gu, came_gu = spread_end(some_gu, size, came_o, (second_own,))
    w_dn, _ = spread_end(spread_begin(own_dn, size, *came_gu), size, (), ())
    w_gu, w_dn = assemble(w_gu), assemble(w_dn)
    late = fence([table], second_own)[0]
    cots = [permute_rows(cotangent, late, half, 2, h) for h in range(2)]

    hidden_units = w_dn.shape[1]
    grad_products = [dot(c, w_dn) for c in cots]
    shares, grad_second, seconds, products, grads = [], [], [], [], []
    for h in range(2):
        second = lax.all_gather(second_own[h * half : (h + 1) * half], "tensor", axis=0, tiled=True)
        (second,) = fence([second], *shares)
        both = dot(second, w_gu)
        product, pull = jax.vjp(gelu_product, both[:, :hidden_units], both[:, hidden_units:])
        grad_gate, grad_up = pull(grad_products[h])
        product = product.astype(BF)
        grad = jnp.concatenate([grad_gate.astype(BF), grad_up.astype(BF)], axis=1)
        share = dot(grad, w_gu, ((1,), (1,))).astype(BF)
        shares.append(share)
        grad_second.append(lax.psum_scatter(share, "tensor", scatter_dimension=0, tiled=True))
        seconds.append(second)
        products.append(product)
        grads.append(grad)

    products, grads = [[*pair] for pair in zip(*[fence([p, g], shares[-1]) for p, g in zip(products, grads)])]
    shares = [dot(p, w_dn, ((1,), (1,))).astype(BF) for p in products]

    def by_rows(lefts, rights):
        parts = []
        for span in (slice(cut, None), slice(0, cut)):
            part = dot(lefts[0][:, span], rights[0], ((0,), (0,)))
            parts.append((part + dot(lefts[1][:, span], rights[1], ((0,), (0,)))).astype(BF))
        return Collect(parts[1], parts[0], size, d_own)

    sum_dn = by_rows(cots, products)
    sum_gu = by_rows(seconds, grads)
    sent_dn, sent_gu = sum_dn.sources(), sum_gu.sources()
    grad_second = fence(grad_second, *sent_dn, *sent_gu, *shares)
    came_mlp = sum_dn.hop(sent_dn) + sum_gu.hop(sent_gu)

    shares = fence(shares, *grad_second)
    mlp_sums = [lax.psum_scatter(share, "tensor", scatter_dimension=0, tiled=True) for share in shares]

    grad_second = jnp.concatenate(grad_second).astype(F32)
    cot_own = jnp.concatenate([lax.dynamic_slice_in_dim(c, turn * half, half) for c in cots]).astype(F32)
    gain_two = jnp.sum(grad_second * second_unit, axis=0)
    grad_hidden = cot_own + norm_back(grad_second, second_unit, second_rate, gain[1])
    hidden_low = grad_hidden.astype(BF)

    def by_cols(left, right):
        parts = [dot(left[:, span], right, ((0,), (0,))).astype(BF) for span in (slice(cut, None), slice(0, cut))]
        return Collect(parts[1], parts[0], size, d_own)

    grad_mixed = wide_dot(hidden_low, w_o)
    tall = jnp.broadcast_to
    lam, reach, edge, pre_low = kernel_call(
        back_scan_kernel, live_count, [branch_pre, grad_mixed, decay, state, prod, tall(carry, (SLAB, width))],
        [keep, keep, (SLAB, width, F32), (rows, width, BF)], [], "back_scan",
    )
    edges = jnp.concatenate([prod[-1:], edge[:1]])
    came = [z_shift(edges, -k, n, False) for k in range(1, n)]
    arriving = jnp.zeros((1, width), F32)
    for end in came[::-1]:
        arriving = end[1:] + end[:1] * arriving
    (lam,) = fence([lam], *came_mlp)
    drec, dpar, d_lru = kernel_call(
        backward_kernel, live_count,
        [rec_pre, par, lru, order, lam, reach, tall(arriving, (SLAB, width)), decay, conv, ig, dg, state, prod, tall(carry, (SLAB, width))],
        [(rows + HALO, width, F32), (8, width, F32), (head, 2 * GROUP, BF)],
        [((rows + HALO, GROUP), F32), ((rows + 2 * HALO, GROUP), F32), ((rows + SLAB, GROUP), F32), ((GROUP, 2 * GROUP), F32), dense],
        "recurrence_back",
    )
    (edge_rows,) = fence([z_shift(drec[:HALO], -1, n, False)], mlp_sums[0])
    rec_low = (drec[HALO:] + jnp.pad(edge_rows, ((rows - HALO, 0), (0, 0)))) * live
    rec_low = rec_low.astype(BF)
    (pre_low,) = fence([pre_low], drec)
    grad_first = wide_back(pre_low, w_g) + wide_back(rec_low, w_r)
    first_unit = inputs * first_rate
    gain_one = jnp.sum(grad_first * first_unit, axis=0)
    grad_tokens = grad_hidden + norm_back(grad_first, first_unit, first_rate, gain[0])
    grad_tokens = permute_rows(grad_tokens.astype(BF), inverse)
    gathered = lax.all_gather(grad_tokens, "tensor", axis=0, tiled=True)
    (mixed,) = fence([mixed], grad_tokens)
    sum_o = by_cols(hidden_low, mixed)
    pre_low, rec_low = fence([pre_low, rec_low], sum_o.terms[1])
    sum_g, sum_r = by_cols(first_own, pre_low), by_cols(first_own, rec_low)
    mlp_sum = jnp.concatenate(fence(mlp_sums, sum_o.terms[1])).astype(F32)
    result = permute_rows((hidden + mlp_sum).astype(BF), inverse)
    got_o = sum_o.hop(fence(sum_o.sources(), result))
    result = lax.all_gather(result, "tensor", axis=0, tiled=True)
    got_g = sum_g.hop(fence(sum_g.sources(), *got_o))
    sum_o.hop(fence(sum_o.sources(), *got_g))
    got_r = sum_r.hop(fence(sum_r.sources(), *got_g))
    sum_g.hop(fence(sum_g.sources(), *got_g))
    got_r = sum_r.hop(fence(sum_r.sources(), *got_r))
    (tokens_out,) = fence([gathered], *got_r, cost=MUCH)
    owned = jnp.stack([total.finish().reshape(d_own, n, width // n) for total in (sum_o, sum_g, sum_r)])
    owned = LineSum(owned.transpose(2, 0, 1, 3), n)
    owned.go()
    pause = (owned.right, owned.left)
    tokens_out = move(tokens_out)
    if n > 2:
        owned.go(tokens_out)
    d_lru, dpar = fence([d_lru, dpar], *pause)
    if sum_dn.square:
        sum_dn.hop(fence(sum_dn.sources(), *pause))
        sum_gu.hop(fence(sum_gu.sources(), *pause))
    g_gu, g_dn = sum_gu.finish().astype(F32), sum_dn.finish().astype(F32)
    g_all = owned.finish()
    (output,) = fence([result], owned.right, owned.left, g_gu, g_dn, cost=MUCH)
    output = move(output)
    g_o, g_g, g_r = g_all[0], g_all[1], g_all[2]

    d_gain = permute_gain(jnp.stack([gain_one, gain_two]), inverse)
    d_chan = jnp.concatenate([dpar[:7], dpar[7:] * 8.0 * jax.nn.sigmoid(-chans[7:])])
    d_lru = d_lru.reshape(groups, size, part, 2, each, -1).transpose(1, 0, 4, 2, 3, 5)
    d_chan = d_chan.reshape(8, n, heads_own, size, part).transpose(3, 1, 0, 2, 4)
    d_gain = d_gain.reshape(2, size, 1, d_own).transpose(1, 2, 0, 3)
    d_gain = jnp.broadcast_to(d_gain, (size, n, 2, d_own))
    small = [v.reshape(size, n, -1).astype(BF) for v in (d_lru, d_chan, d_gain)]
    small = small_scatter(jnp.concatenate(small, axis=2), size, n)
    d_lru = small[: w_lru.size].reshape(part, 2, heads_own, head).transpose(1, 2, 0, 3)
    d_chan = small[w_lru.size : -gains.size].reshape(chan.shape)
    d_gain = small[-gains.size :].reshape(gains.shape)
    g_gate, g_up = g_gu[:, :hidden_units], g_gu[:, hidden_units:]
    return (
        output, tokens_out, d_gain[0], d_gain[1], g_g, g_r, d_chan, d_lru,
        g_o.T, jnp.stack([g_gate, g_up]), g_dn.T,
    )


def solution(mesh):
    in_specs = (
        P("dp", None),
        P("dp"),
        P(None, "dp"),
        P("dp", "tensor"),
        P("dp", "tensor"),
        P(None, "tensor", "dp"),
        P(None, "tensor", "dp", None),
        P("tensor", "dp"),
        P(None, "dp", "tensor"),
        P("tensor", "dp"),
        P("dp", None),
    )
    out_specs = (
        P("dp", None),
        P("dp", None),
        P("dp"),
        P("dp"),
        P("dp", "tensor"),
        P("dp", "tensor"),
        P(None, "tensor", "dp"),
        P(None, "tensor", "dp", None),
        P("tensor", "dp"),
        P(None, "dp", "tensor"),
        P("tensor", "dp"),
    )
    body = functools.partial(on_device, mesh.shape["dp"], mesh.shape["tensor"])
    return jax.shard_map(body, mesh=mesh, in_specs=in_specs, out_specs=out_specs, check_vma=False)
```
